32 devices in a mesh: dp: 2 (over core), ctx: 16 (over z, y, x).
Axes of the slice: x: 2, y: 2, z: 4, core: 2. Of those that a mesh axis runs over, the one named last changes fastest.
Arguments:
- tokens: bfloat16 [2, 2048, 1024], P('dp', 'ctx'), may hold values from -6 to 6
- cotangent: bfloat16 [2, 2048, 1024], P('dp', 'ctx'), may hold values from -6 to 6
- block_order: int32 [32], replicated, may hold values from 0 to 31, each once
- doc_lengths: int32 [2, 8], P('dp'), may hold values from 1 to 1024, 2048 in all within a row
- routes: int32 [2, 2048, 1], P('dp', 'ctx'), may hold values from 0 to 15; in each aligned block of 128 rows (0 to 127, 128 to 255, ..., all dimensions but the last counted through in order) at most 16 rows name the same one
- w_qkv: float32 [1024, 3072], P(('dp', 'ctx')), may hold values from -0.1875 to 0.1875
- w_out: float32 [1024, 1024], P(('dp', 'ctx')), may hold values from -3 to 3
- w_up: float32 [1024, 4096], P(('dp', 'ctx')), may hold values from -0.1875 to 0.1875
- w_down: float32 [4096, 1024], P(('dp', 'ctx')), may hold values from -0.09375 to 0.09375
- router: float32 [1024, 18], P(('dp', 'ctx')), may hold values from -0.09375 to 0.09375
- norm_gains: float32 [2, 1024], P(None, ('dp', 'ctx')), may hold values from 0.5 to 1.5
- norm_biases: float32 [2, 1024], P(None, ('dp', 'ctx')), may hold values from -1 to 1
- expert_up: bfloat16 [16, 1024, 4096], P('ctx', None, 'dp'), may hold values from -0.1875 to 0.1875
- expert_down: bfloat16 [16, 4096, 1024], P('ctx', 'dp'), may hold values from -8 to 8
Outputs:
- layer_out: bfloat16 [2, 2048, 1024], P('dp', 'ctx')
- grad_tokens: bfloat16 [2, 2048, 1024], P('dp', 'ctx')
- grad_w_qkv: float32 [1024, 3072], P(('dp', 'ctx'))
- grad_w_out: float32 [1024, 1024], P(('dp', 'ctx'))
- grad_w_up: float32 [1024, 4096], P(('dp', 'ctx'))
- grad_w_down: float32 [4096, 1024], P(('dp', 'ctx'))
- grad_router: float32 [1024, 18], P(('dp', 'ctx'))
- grad_norm_gains: float32 [2, 1024], P(None, ('dp', 'ctx'))
- grad_norm_biases: float32 [2, 1024], P(None, ('dp', 'ctx'))
- grad_expert_up: float32 [16, 1024, 4096], P('ctx', None, 'dp')
- grad_expert_down: float32 [16, 4096, 1024], P('ctx', 'dp')
The draws below stay inside these ranges and needn't reach their ends.
Inputs may be any that keep to these rules, and one draw needn't show every extreme that they name: `block_order`: each value appears once; entry i is the initial block place, in blocks of 64 tokens, of rows i * 64 to (i + 1) * 64 - 1 of every packed sequence. `doc_lengths`: A packed sequence's document lengths sum to 2048; the longest is exactly 1024. `routes`: among the 128 rows of a packed sequence that one index of ctx holds, no expert is named more than 16 times, a bound that some block reaches.
All inputs are finite; a program needn't handle non-finite values.
Results may differ from the reference program's by a relative error of at most 0.014.
Values may be sent and summed in bfloat16 or wider, within the bound.
A program may use at most 320 MiB of HBM per device.

```python
import math
import jax
import jax.numpy as jnp
import numpy as np
from jax import lax

D = 1024
HEADS = 16
HEAD_DIM = 64
FF = 4096
EXPERT_FF = 4096
TOK_DEV = 128
DOCS = 8
SEQS = 2
LENGTH = 2048
BLOCKS = 32
MAXDOC = 1024
EXPERTS = 16
CAP = 16


def level_of(stream_key, extent, split, low, high):
    def one(dim, parts):
        steps = jax.random.uniform(jax.random.fold_in(jax.random.fold_in(stream_key, 6), dim), (parts,), jnp.float32, low / len(split), high / len(split))
        return jnp.repeat(jnp.exp(steps), extent[dim] // parts).reshape((-1,) + (1,) * (len(extent) - dim - 1))

    factor_of = one(*split[0])
    for cut in split[1:]:
        factor_of = factor_of * one(*cut)
    return factor_of


def length_profile(count, total, limit, skew):
    loads = [(1 << 20) // math.isqrt(standing ** skew) + 1 for standing in range(2, count + 1)]
    spare, holding = total - limit - (count - 1), [1] * (count - 1)
    while spare > 0:
        free = [i for i in range(count - 1) if holding[i] < limit]
        pool, left = sum([loads[i] for i in free]), spare
        for i in free:
            more = min(limit - holding[i], max(1, left * loads[i] // pool), spare)
            holding[i] = holding[i] + more
            spare = spare - more
    return np.array([limit] + holding)


def ragged_sizes(rng, amount, total, most, slope):
    if amount == 2:
        one = jax.random.randint(rng, (), max(1, total - most), min(most, total - 1) + 1)
        return jnp.stack([one, total - one])
    tallies = jnp.asarray(length_profile(amount, total, most, slope), jnp.int32)
    couples = (amount - 1) // 2
    giver, sink = tallies[1:1 + 2 * couples:2], tallies[2:2 + 2 * couples:2]
    slack = jnp.minimum(giver - 1, most - sink)
    moved = jax.random.randint(jax.random.fold_in(rng, 1), (couples,), 0, 1 << 20) % (slack + 1)
    tallies = tallies.at[1:1 + 2 * couples:2].set(giver - moved).at[2:2 + 2 * couples:2].set(sink + moved)
    return tallies[jax.random.permutation(jax.random.fold_in(rng, 2), amount)]


def deal_out(stream_key, own, number, rows, amount, top, reach, lean):
    order = jax.random.permutation(stream_key, amount)
    crowded, usual = portions_of(amount, rows * top, reach, lean, True), portions_of(amount, rows * top, reach, lean, False)
    places = jnp.arange(amount)

    def named(lengths, offset_by):
        used = int((lengths > 0).sum())
        fixed = max(1, used // 4)
        shifted = fixed + (places - fixed + offset_by * (used - fixed)) % max(1, amount - fixed)
        return jnp.zeros((amount,), jnp.int32).at[order[jnp.where(places < fixed, places, shifted)]].set(jnp.asarray(lengths, jnp.int32))

    lengths = jnp.where(number % 4 == 0, named(crowded, number // 4), named(usual, number - number // 4 - 1))
    mixed = jax.random.permutation(jax.random.fold_in(own, 3), amount)
    source_of, sink = mixed[0:amount // 2 * 2:2], mixed[1:amount // 2 * 2:2]
    room = jnp.minimum(lengths[source_of] - 1, reach - lengths[sink]) // 2
    room = jnp.where((source_of == order[0]) | (sink == order[0]) | (lengths[sink] == 0), 0, jnp.maximum(room, 0))
    shifted = jax.random.randint(jax.random.fold_in(own, 4), (amount // 2,), 0, 1 << 20) % (room + 1)
    lengths = lengths.at[source_of].add(-shifted).at[sink].add(shifted)
    items = jnp.searchsorted(jnp.cumsum(lengths), jnp.arange(rows * top), side="right").astype(jnp.int32)
    listing = items.reshape(top, rows).T
    listing = listing[jax.random.permutation(jax.random.fold_in(own, 1), rows)]
    offset_by = jax.random.randint(jax.random.fold_in(own, 2), (rows, 1), 0, top)
    return jnp.take_along_axis(listing, (jnp.arange(top)[None, :] + offset_by) % top, axis=1)


def portions_of(amount, total, bound, slope, full):
    weights = [(1 << 20) // math.isqrt(grade ** slope) + 1 for grade in range(1, amount + 1)]
    largest = bound if full else min(bound, max(-(-total // amount), total * weights[0] // sum(weights)))
    least = 1 if total - largest >= amount - 1 else 0
    given, surplus = [largest] + [least] * (amount - 1), total - largest - least * (amount - 1)
    while surplus > 0:
        movable = [i for i in range(1, amount) if given[i] < largest] or [i for i in range(1, amount) if given[i] < bound]
        whole, left = sum([weights[i] for i in movable]), surplus
        for i in movable:
            addition = min(bound - given[i], max(1, left * weights[i] // whole), surplus)
            given[i] = given[i] + addition
            surplus = surplus - addition
    return np.array(given)


def centred(own_key, dims, deviation, bound, cuts=(), held_as=jnp.bfloat16):
    values = deviation * jax.random.normal(own_key, dims, jnp.float32)
    if cuts:
        values = values * level_of(own_key, dims, cuts, -0.22, 0.18)
    return jnp.clip(values, -bound, bound).astype(held_as)


def setup_inputs(seed: int = 0) -> dict:
    splits = jax.random.split(jax.random.key(seed), 15)
    tokens = centred(splits[0], (SEQS, LENGTH, D), 1.0, 6.0, ((0, 2), (1, 16)))
    cotangent = centred(splits[1], (SEQS, LENGTH, D), 1.0, 6.0, ((0, 2), (1, 16)))
    block_order = jax.random.permutation(splits[2], BLOCKS).astype(jnp.int32)
    doc_lengths = jax.vmap(lambda own: ragged_sizes(own, DOCS, LENGTH, MAXDOC, 2))(jax.random.split(splits[3], SEQS)).reshape((SEQS, DOCS)).astype(jnp.int32)
    routes_keys = jax.random.split(jax.random.fold_in(splits[4], 1), SEQS * LENGTH // TOK_DEV)
    routes_turns = jax.random.permutation(jax.random.fold_in(splits[4], 3), SEQS * LENGTH // TOK_DEV)
    routes = jax.vmap(lambda own, number: deal_out(jax.random.fold_in(splits[4], 2), own, number, TOK_DEV, EXPERTS, 1, CAP, 2))(routes_keys, routes_turns).reshape((SEQS, LENGTH, 1))
    w_qkv = centred(splits[5], (D, 3 * D), D ** -0.5, 0.1875, ((0, 32),), jnp.float32)
    w_out = centred(splits[6], (D, D), (max(1, D // 256)) ** -0.5, 3.0, ((0, 32),), jnp.float32)
    w_up = centred(splits[7], (D, FF), D ** -0.5, 0.1875, ((0, 32),), jnp.float32)
    w_down = centred(splits[8], (FF, D), FF ** -0.5, 0.09375, ((0, 32),), jnp.float32)
    router = centred(splits[9], (D, EXPERTS + 2), (4 * D) ** -0.5, 0.09375, ((0, 32),), jnp.float32)
    norm_gains = jnp.clip(1.0 + 0.1 * jax.random.normal(splits[10], (2, D), jnp.float32), 0.5, 1.5)
    norm_biases = centred(splits[11], (2, D), 0.2, 1.0, ((1, 32),), jnp.float32)
    expert_up = centred(splits[12], (EXPERTS, D, EXPERT_FF), D ** -0.5, 0.1875, ((0, 16), (2, 2)))
    expert_down = centred(splits[13], (EXPERTS, EXPERT_FF, D), (5 * EXPERTS * EXPERT_FF ** -0.5), 8.0, ((0, 16), (1, 2)))
    return {"tokens": tokens, "cotangent": cotangent, "block_order": block_order, "doc_lengths": doc_lengths, "routes": routes, "w_qkv": w_qkv, "w_out": w_out, "w_up": w_up, "w_down": w_down, "router": router, "norm_gains": norm_gains, "norm_biases": norm_biases, "expert_up": expert_up, "expert_down": expert_down}


@jax.custom_vjp
def lower_precision(v):
    return lax.optimization_barrier(v.astype(jnp.bfloat16)).astype(jnp.float32)

@jax.custom_vjp
def lower_backward(v):
    return v

def low_keep(v):
    return (lower_precision(v), None)

def low_pass(kept, grad):
    return (grad,)

def back_keep(v):
    return (v, None)

def back_low(kept, grad):
    return (lower_precision(grad),)
lower_precision.defvjp(low_keep, low_pass)
lower_backward.defvjp(back_keep, back_low)
UPPER_PRECISION = lax.Precision.HIGHEST
EPS = 1e-05
NEG = -1e+30
SCALE = 0.125

def layer_norm(values, gain, shift):
    center = values - lax.optimization_barrier(jnp.mean(values, axis=-1, keepdims=True))
    spread = lax.optimization_barrier(jnp.mean(center * center, axis=-1, keepdims=True))
    return center * lax.rsqrt(spread + EPS) * gain + shift

def gelu_tanh(values):
    return jax.nn.gelu(values, approximate=True)

def place_rows(rows, block_order, block_rows, doc_ends):
    blocks = rows // block_rows
    marks = blocks[:, None] == jnp.arange(block_order.shape[0], dtype=jnp.int32)[None, :]
    anchor = lax.optimization_barrier(jnp.sum(jnp.where(marks, block_order[None, :], 0), axis=1)).astype(jnp.int32)
    place = anchor * block_rows + rows % block_rows
    document = lax.optimization_barrier(jnp.sum((doc_ends[None, :] <= place[:, None]).astype(jnp.int32), axis=1))
    return (place, document)

def attend_whole(queries, keys, values, place, document):
    length = queries.shape[0]
    block = math.gcd(length, 512)
    count = length // block

    def one_block(args):
        query_part, query_place, query_doc = args
        raw = lower_backward(jnp.einsum('qhd,khd->hqk', query_part, keys, precision=UPPER_PRECISION))
        allowed = (place[None, :] <= query_place[:, None]) & (document[None, :] == query_doc[:, None])
        scores = jnp.where(allowed[None], raw * SCALE, NEG)
        chances = lower_precision(jax.nn.softmax(scores, axis=-1))
        return jnp.einsum('hqk,khd->qhd', chances, values, precision=UPPER_PRECISION)
    result = lax.map(jax.checkpoint(one_block), (queries.reshape(count, block, HEADS, HEAD_DIM), place.reshape(count, block), document.reshape(count, block)))
    return result.reshape(length, HEADS * HEAD_DIM)

def reference(tokens, cotangent, block_order, doc_lengths, routes, w_qkv, w_out, w_up, w_down, router, norm_gains, norm_biases, expert_up, expert_down):
    seq_count, length, width = tokens.shape
    block_rows = length // block_order.shape[0]
    rows_all = jnp.arange(length, dtype=jnp.int32)
    places = []
    documents = []
    for index in range(seq_count):
        place, document = place_rows(rows_all, block_order, block_rows, jnp.cumsum(doc_lengths[index]).astype(jnp.int32))
        places.append(place)
        documents.append(document)
    route_flat = routes[..., 0].reshape(-1).astype(jnp.int32)
    total_rows = seq_count * length
    block_count = total_rows // TOK_DEV
    route_hot = (route_flat[:, None] == jnp.arange(EXPERTS, dtype=jnp.int32)[None, :]).astype(jnp.int32)
    shaped_hot = route_hot.reshape(block_count, TOK_DEV, EXPERTS)
    ranks = jnp.cumsum(shaped_hot, axis=1) - 1
    slot_in = lax.optimization_barrier(jnp.sum(jnp.where(shaped_hot > 0, ranks, 0), axis=2)).reshape(-1).astype(jnp.int32)
    owner = jnp.arange(total_rows, dtype=jnp.int32) // TOK_DEV
    slot_of_row = ((route_flat * block_count + owner) * CAP + slot_in).astype(jnp.int32)
    source_row = jnp.zeros((EXPERTS * block_count * CAP,), jnp.int32).at[slot_of_row].set(jnp.arange(total_rows, dtype=jnp.int32) + 1) - 1
    filled = source_row >= 0
    source_row = jnp.maximum(source_row, 0).astype(jnp.int32)
    gate_hot = route_hot.astype(jnp.float32).reshape(seq_count, length, EXPERTS)

    def forward(inputs, query_key_value_master, output_weight_master, up_weight_master, down_weight_master, router_weight_master, gain_master, bias_master, up_experts, down_experts):
        gains = lower_precision(gain_master)
        shifts = lower_precision(bias_master)
        normalized_input = lower_precision(layer_norm(inputs, gains[0], shifts[0]))
        mixed_output = lower_precision(lower_backward(jnp.einsum('ogt,tr->ogr', normalized_input, lower_precision(query_key_value_master), precision=UPPER_PRECISION)))
        pieces = []
        for index in range(seq_count):
            queries = mixed_output[index, :, :width].reshape(length, HEADS, HEAD_DIM)
            keys = mixed_output[index, :, width:2 * width].reshape(length, HEADS, HEAD_DIM)
            values = mixed_output[index, :, 2 * width:].reshape(length, HEADS, HEAD_DIM)
            pieces.append(attend_whole(queries, keys, values, places[index], documents[index]))
        attention_output = lower_precision(lower_backward(jnp.stack(pieces)))
        expert_branch = lower_backward(jnp.einsum('ogt,tr->ogr', attention_output, lower_precision(output_weight_master), precision=UPPER_PRECISION))
        middle = inputs + expert_branch
        second_normalized = lower_precision(layer_norm(middle, gains[1], shifts[1]))
        upper_residual = lower_backward(jnp.einsum('awe,eu->awu', second_normalized, lower_precision(up_weight_master), precision=UPPER_PRECISION))
        active_rows = lower_precision(gelu_tanh(upper_residual))
        dense_output = lower_backward(jnp.einsum('pxz,zn->pxn', active_rows, lower_precision(down_weight_master), precision=UPPER_PRECISION))
        router_logits = lower_backward(jnp.einsum('ogt,tr->ogr', second_normalized, lower_precision(router_weight_master), precision=UPPER_PRECISION))
        gate = lax.optimization_barrier(jnp.sum(jax.nn.softmax(router_logits[..., :EXPERTS], axis=-1) * gate_hot, axis=-1))
        mixing = jax.nn.softmax(router_logits[..., EXPERTS:], axis=-1)
        flat = second_normalized.reshape(total_rows, width)
        slots = jnp.where(filled[:, None], jnp.take(flat, source_row, axis=0), 0.0).reshape(EXPERTS, block_count * CAP, width)

        def run_expert(args):
            rows, up_weight, down_weight = args
            hidden = lower_backward(jnp.dot(rows, up_weight, precision=UPPER_PRECISION))
            return jnp.dot(lower_precision(gelu_tanh(hidden)), down_weight, precision=UPPER_PRECISION)
        expert_out = lax.map(jax.checkpoint(run_expert), (slots, up_experts, down_experts))
        routed = lower_backward(jnp.take(expert_out.reshape(-1, width), slot_of_row, axis=0).reshape(seq_count, length, width))
        return middle + mixing[..., :1] * dense_output + (mixing[..., 1] * gate)[..., None] * routed
    primals = (tokens.astype(jnp.float32), w_qkv, w_out, w_up, w_down, router, norm_gains, norm_biases, expert_up.astype(jnp.float32), expert_down.astype(jnp.float32))
    result, pullback = jax.vjp(forward, *primals)
    grads = pullback(cotangent.astype(jnp.float32))
    return (result.astype(jnp.bfloat16), grads[0].astype(jnp.bfloat16), grads[1], grads[2], grads[3], grads[4], grads[5], grads[6], grads[7], grads[8], grads[9])
```

```python
import functools
import math

import jax
import jax.numpy as jnp
from jax import lax
from jax.experimental import pallas as pl
from jax.experimental.pallas import tpu as pltpu
from jax.sharding import PartitionSpec as P

HEADS = 16
HEAD_DIM = 64

EPS = 1e-05
NEG = -1e30
SCALE = 0.125
TILE = 256
BF = jnp.bfloat16
F32 = jnp.float32
MESH = pl.DeviceIdType.MESH


def layer_norm(values, gain, shift):
    center = values - jnp.mean(values, axis=-1, keepdims=True)
    spread = jnp.mean(center * center, axis=-1, keepdims=True)
    return center * lax.rsqrt(spread + EPS) * gain + shift


def gelu_tanh(values):
    return jax.nn.gelu(values, approximate=True)


def router_heads(router_logits, route_hot, experts):
    chances = jax.nn.softmax(router_logits[:, :experts], axis=-1)
    gate = jnp.sum(chances * route_hot, axis=-1)
    mixing = jax.nn.softmax(router_logits[:, experts:], axis=-1)
    return (gate, mixing[:, 0], mixing[:, 1])


def dot_f32(left, right):
    return jnp.dot(left, right, preferred_element_type=F32)


def contract_rows(left, right):
    return lax.dot_general(left, right, (((0,), (0,)), ((), ())), preferred_element_type=F32)


def contract_cols(left, right):
    return lax.dot_general(left, right, (((1,), (1,)), ((), ())), preferred_element_type=F32)


class Move:
    def __init__(self, step, src, dst, after=None):
        self.step, self.src, self.dst, self.after = step, src, dst, after


def exchange(name, cid, sizes, ins, outs, build):
    two, groups, team = sizes

    def kernel(*refs):
        in_refs, out_refs = refs[: len(ins)], refs[len(ins) : len(ins) + len(outs)]
        send_sem, recv_sem, local_sem = refs[len(ins) + len(outs) :]
        c = lax.axis_index("dp")
        i = lax.axis_index("ctx")
        g, t = lax.div(i, team), lax.rem(i, team)

        def device(step):
            dc, dg, dt = step
            return (
                lax.rem(c + dc, two),
                lax.rem(g + dg, groups) * team + lax.rem(t + dt, team),
            )

        locals_, moves = build((c, g, t), in_refs, out_refs)
        steps = sorted({m.step for m in moves})
        greet = sorted(
            set(steps) | {((-a) % two, (-b) % groups, (-d) % team) for a, b, d in steps}
        )
        barrier = pltpu.get_barrier_semaphore()
        for step in greet:
            pl.semaphore_signal(barrier, inc=1, device_id=device(step), device_id_type=MESH)
        pl.semaphore_wait(barrier, len(greet))

        copies = {}
        arrived = set()
        for k, (src, dst) in enumerate(locals_):
            copies[("local", k)] = pltpu.make_async_copy(src, dst, local_sem.at[k])
        for k, m in enumerate(moves):
            copies[k] = pltpu.make_async_remote_copy(
                src_ref=m.src,
                dst_ref=m.dst,
                send_sem=send_sem.at[k],
                recv_sem=recv_sem.at[k],
                device_id=device(m.step),
                device_id_type=MESH,
            )
        for k, m in enumerate(moves):
            if m.after is None:
                copies[k].start()
        for k in range(len(locals_)):
            copies[("local", k)].start()
        for k, m in enumerate(moves):
            if m.after is not None:
                if m.after not in arrived:
                    arrived.add(m.after)
                    if isinstance(m.after, tuple):
                        copies[m.after].wait()
                    else:
                        copies[m.after].wait_recv()
                copies[k].start()
        for k in range(len(locals_)):
            if ("local", k) not in arrived:
                copies[("local", k)].wait()
        for k in range(len(moves)):
            if k not in arrived:
                copies[k].wait_recv()
        for k in range(len(moves)):
            copies[k].wait_send()

    count = []

    def trace_counts():
        class Probe:
            def __getattr__(self, name):
                return self

            def __getitem__(self, index):
                return self

        locals_, moves = build((0, 0, 0), [Probe() for _ in ins], [Probe() for _ in outs])
        count.extend((len(locals_), len(moves)))

    trace_counts()
    return pl.pallas_call(
        kernel,
        name=name,
        out_shape=tuple(jax.ShapeDtypeStruct(s, d) for s, d in outs),
        in_specs=[pl.BlockSpec(memory_space=pl.ANY)] * len(ins),
        out_specs=tuple(pl.BlockSpec(memory_space=pl.ANY) for _ in outs),
        scratch_shapes=[
            pltpu.SemaphoreType.DMA((max(1, count[1]),)),
            pltpu.SemaphoreType.DMA((max(1, count[1]),)),
            pltpu.SemaphoreType.DMA((max(1, count[0]),)),
        ],
        compiler_params=pltpu.CompilerParams(collective_id=cid, has_side_effects=True),
    )(*ins)


def mask_of(kt, key_place, query_place, query_low):
    return (key_place <= query_place) & (key_place >= query_low)


def key_places(sorted_rows, kt, place_ref):
    if sorted_rows:
        return lax.broadcasted_iota(jnp.int32, (TILE, TILE), 0) + kt * TILE
    return place_ref[pl.ds(pl.multiple_of(kt * TILE, TILE), TILE), :]


def attend_kernel(
    sorted_rows, bounds, meta_ref, place_ref, q_ref, rows_ref, kvt_ref, out_ref, lse_ref
):
    step = pl.program_id(0)
    queries = q_ref[...]
    place, low = meta_ref[0:1, :], meta_ref[1:2, :]

    def body(kt, carry):
        peak, total, acc = carry
        at = pl.ds(pl.multiple_of(kt * TILE, TILE), TILE)
        scores = dot_f32(rows_ref[at, :], queries)
        allowed = mask_of(kt, key_places(sorted_rows, kt, place_ref), place, low)
        scores = jnp.where(allowed, scores, NEG)
        new_peak = jnp.maximum(peak, jnp.max(scores, axis=0, keepdims=True))
        weights = jnp.exp(scores - new_peak)
        fade = jnp.exp(peak - new_peak)
        total = total * fade + jnp.sum(weights, axis=0, keepdims=True)
        acc = acc * fade + dot_f32(kvt_ref[HEAD_DIM:, at], weights.astype(BF))
        return new_peak, total, acc

    start = (
        jnp.full((1, TILE), NEG, F32),
        jnp.zeros((1, TILE), F32),
        jnp.zeros((HEAD_DIM, TILE), F32),
    )
    peak, total, acc = lax.fori_loop(bounds[step, 0], bounds[step, 1], body, start)
    out_ref[...] = acc / total
    lse_ref[...] = peak + jnp.log(total)


def attend_back_kernel(
    sorted_rows,
    tiles,
    bounds,
    meta_ref,
    place_ref,
    q_ref,
    do_ref,
    out_ref,
    lse_ref,
    rows_ref,
    kvt_ref,
    dq_ref,
    dkv_ref,
    acc_ref,
):
    step = pl.program_id(0)

    @pl.when(step == 0)
    def _():
        acc_ref[...] = jnp.zeros_like(acc_ref)

    queries, flows = q_ref[...], do_ref[...]
    place, low = meta_ref[0:1, :], meta_ref[1:2, :]
    log_total = lse_ref[...]
    delta = jnp.sum(flows[HEAD_DIM:, :].astype(F32) * out_ref[...], axis=0, keepdims=True)

    def body(kt, dq):
        at = pl.ds(pl.multiple_of(kt * TILE, TILE), TILE)
        rows = rows_ref[at, :]
        scores = dot_f32(rows, queries)
        allowed = mask_of(kt, key_places(sorted_rows, kt, place_ref), place, low)
        chances = jnp.exp(jnp.where(allowed, scores - log_total, NEG))
        flow = dot_f32(rows, flows)
        score_grad = (chances * (flow - delta)).astype(BF)
        dq = dq + dot_f32(kvt_ref[:HEAD_DIM, at], score_grad)
        acc_ref[:HEAD_DIM, at] += contract_cols(queries[:HEAD_DIM, :], score_grad)
        acc_ref[HEAD_DIM:, at] += contract_cols(flows[HEAD_DIM:, :], chances.astype(BF))
        return dq

    dq = lax.fori_loop(
        bounds[step, 0], bounds[step, 1], body, jnp.zeros((HEAD_DIM, TILE), F32)
    )
    dq_ref[...] = (dq * SCALE).astype(BF)

    @pl.when(step == tiles - 1)
    def _():
        dkv_ref[...] = acc_ref[...].astype(BF)


def attention_specs(length, query_length):
    def whole(shape):
        return pl.BlockSpec(shape, lambda i: (0, 0))

    def tile(rows):
        return pl.BlockSpec((rows, TILE), lambda i: (0, i))

    return whole, tile


def attend(sorted_rows, bounds, meta, place_col, q_pad, kv_rows, kv_t):
    length, query_length = kv_rows.shape[0], q_pad.shape[1]
    whole, tile = attention_specs(length, query_length)
    return pl.pallas_call(
        functools.partial(attend_kernel, sorted_rows),
        name="attend",
        grid=(query_length // TILE,),
        in_specs=[
            pl.BlockSpec(memory_space=pltpu.SMEM),
            tile(8),
            whole(place_col.shape),
            tile(2 * HEAD_DIM),
            whole((length, 2 * HEAD_DIM)),
            whole((2 * HEAD_DIM, length)),
        ],
        out_specs=(tile(HEAD_DIM), tile(1)),
        out_shape=(
            jax.ShapeDtypeStruct((HEAD_DIM, query_length), F32),
            jax.ShapeDtypeStruct((1, query_length), F32),
        ),
        compiler_params=pltpu.CompilerParams(vmem_limit_bytes=40 * 2**20),
    )(bounds, meta, place_col, q_pad, kv_rows, kv_t)


def attend_back(sorted_rows, bounds, meta, place_col, q_pad, do_pad, out, lse, kv_rows, kv_t):
    length, query_length = kv_rows.shape[0], q_pad.shape[1]
    whole, tile = attention_specs(length, query_length)
    return pl.pallas_call(
        functools.partial(attend_back_kernel, sorted_rows, query_length // TILE),
        name="attend_back",
        grid=(query_length // TILE,),
        in_specs=[
            pl.BlockSpec(memory_space=pltpu.SMEM),
            tile(8),
            whole(place_col.shape),
            tile(2 * HEAD_DIM),
            tile(2 * HEAD_DIM),
            tile(HEAD_DIM),
            tile(1),
            whole((length, 2 * HEAD_DIM)),
            whole((2 * HEAD_DIM, length)),
        ],
        out_specs=(tile(HEAD_DIM), whole((2 * HEAD_DIM, length))),
        out_shape=(
            jax.ShapeDtypeStruct((HEAD_DIM, query_length), BF),
            jax.ShapeDtypeStruct((2 * HEAD_DIM, length), BF),
        ),
        scratch_shapes=[pltpu.VMEM((2 * HEAD_DIM, length), F32)],
        compiler_params=pltpu.CompilerParams(vmem_limit_bytes=40 * 2**20),
    )(bounds, meta, place_col, q_pad, do_pad, out, lse, kv_rows, kv_t)


def tall(chunk):
    rows, cols = chunk.shape[-2:]
    factor = 1
    while (rows * factor) % 16:
        factor *= 2
    return chunk.reshape(chunk.shape[:-2] + (rows * factor, cols // factor))


def per_device(
    tokens,
    cotangent,
    block_order,
    doc_lengths,
    routes,
    w_qkv,
    w_out,
    w_up,
    w_down,
    router,
    norm_gains,
    norm_biases,
    expert_up,
    expert_down,
):
    rows, width = tokens.shape[1], tokens.shape[2]
    ctx_count = lax.axis_size("ctx")
    two = lax.axis_size("dp")
    team = math.gcd(4, ctx_count)
    groups = ctx_count // team
    sizes = (two, groups, team)
    team_heads = HEADS // team
    reps = groups // team_heads
    length = rows * ctx_count
    group_rows = rows * team
    experts = ctx_count * expert_up.shape[0]
    capacity = max(2, 2 * rows // experts)
    block_rows = length // block_order.shape[0]
    hidden = w_up.shape[1]
    hidden_dev = w_down.shape[0]
    wr = w_qkv.shape[0]
    qkv_cols = 3 * width // team
    up_cols = hidden // team
    core = lax.axis_index("dp")
    ctx = lax.axis_index("ctx")
    group, member = lax.div(ctx, team), lax.rem(ctx, team)
    team_steps = [(0, 0, k) for k in range(1, team)]
    group_steps = [(0, k, 0) for k in range(1, groups)]
    by_group = [[g * team + t for g in range(groups)] for t in range(team)]
    by_team = [[g * team + t for t in range(team)] for g in range(groups)]
    swap = [(d, (d + 1) % two) for d in range(two)]

    small_flat = jnp.concatenate(
        [router.reshape(-1), norm_gains.reshape(-1), norm_biases.reshape(-1)]
    )
    small_size = -(-small_flat.shape[0] // 2048) * 2048
    small = jnp.pad(small_flat, (0, small_size - small_flat.shape[0])).astype(BF)
    small = small.reshape(-1, 128)

    heads_first = (
        w_qkv.reshape(wr, 3, team, team_heads, HEAD_DIM)
        .transpose(2, 0, 3, 1, 4)
        .reshape(team, wr, qkv_cols)
        .astype(BF)
    )
    up_first = (
        w_up.reshape(wr, two * groups, team, hidden_dev)
        .transpose(2, 0, 1, 3)
        .reshape(team, wr, up_cols)
        .astype(BF)
    )
    heads_first, up_first = tall(heads_first), tall(up_first)
    route_row = jnp.broadcast_to(routes[0, :, 0][None, :], (8, rows))

    def first(coords, ins, outs):
        c, g, t = coords
        moves, local = [], []
        for s in team_steps:
            to = lax.rem(t + s[2], team)
            moves.append(Move(s, ins[0], outs[0].at[t]))
            moves.append(Move(s, ins[1].at[to], outs[1].at[t]))
            moves.append(Move(s, ins[3], outs[3].at[t]))
            moves.append(Move(s, ins[4], outs[4].at[t]))
            moves.append(Move(s, ins[2].at[to], outs[2].at[t]))
        local.append((ins[0], outs[0].at[t]))
        local.append((ins[1].at[t], outs[1].at[t]))
        local.append((ins[2].at[t], outs[2].at[t]))
        local.append((ins[3], outs[3].at[t]))
        local.append((ins[4], outs[4].at[t]))
        return local, moves

    token_rows, qkv_part, up_part, small_part, route_all = exchange(
        "first",
        1,
        sizes,
        (tokens[0], heads_first, up_first, small, route_row),
        [
            ((team, rows, width), BF),
            (heads_first.shape, BF),
            (up_first.shape, BF),
            ((team,) + small.shape, BF),
            ((team, 8, rows), jnp.int32),
        ],
        first,
    )

    def second_build(coords, ins, outs):
        c, g, t = coords
        moves, local = [], []
        for k, s in enumerate(group_steps):
            moves.append(Move(s, ins[0], outs[0].at[c, g]))
            moves.append(Move(s, ins[1], outs[1].at[c, g]))
        for s in team_steps:
            moves.append(Move(s, ins[2], outs[2].at[t]))
        local.append((ins[0], outs[0].at[c, g]))
        local.append((ins[1], outs[1].at[c, g]))
        local.append((ins[2], outs[2].at[t]))
        other = (1, 0, 0)
        for n in range(2):
            moves.append(Move(other, outs[n].at[c, g], outs[n].at[c, g], after=("local", n)))
        for k, s in enumerate(group_steps):
            source = lax.rem(g + groups - s[1], groups)
            for n in range(2):
                moves.append(
                    Move(other, outs[n].at[c, source], outs[n].at[c, source], after=2 * k + n)
                )
        return local, moves

    qkv_all, small_all, cot_rows = exchange(
        "second",
        2,
        sizes,
        (qkv_part, small_part, cotangent[0]),
        [
            ((two, groups) + qkv_part.shape, BF),
            ((two, groups) + small_part.shape, BF),
            ((team, rows, width), BF),
        ],
        second_build,
    )
    qkv_weight = qkv_all.reshape(width, qkv_cols)
    small_rows = small_all.reshape(two * ctx_count, -1)
    router_cols = router.shape[1]
    router_weight = small_rows[:, : wr * router_cols].reshape(width, router_cols)
    vectors = small_rows[:, wr * router_cols : small_flat.shape[0]].reshape(
        two * ctx_count, 4, wr
    )
    vectors = vectors.transpose(1, 0, 2).reshape(4, width).astype(F32)
    gains, shifts = vectors[:2], vectors[2:]

    ff_part = jnp.concatenate(
        [up_part.reshape(team * wr, up_cols), w_down.astype(BF).reshape(team * wr, -1)], axis=1
    )
    ff_half = lax.all_gather(ff_part, "ctx", axis=0, tiled=False, axis_index_groups=by_group)
    out_half = lax.all_gather(w_out.astype(BF), "ctx", axis=0, tiled=True)

    def both(half):
        other = lax.ppermute(half, "dp", swap)
        return jnp.where(core == 0, jnp.stack([half, other]), jnp.stack([other, half]))

    out_weight = both(out_half).reshape(width, width)
    up_weight = both(ff_half[:, :, :up_cols]).reshape(width, up_cols)
    down_weight = both(ff_half[:, :, up_cols:]).reshape(up_cols, width)

    doc_id = jnp.arange(doc_lengths.shape[1], dtype=jnp.int32)
    doc_ends = jnp.sum(
        jnp.where(doc_id[:, None] <= doc_id[None, :], doc_lengths[0][:, None], 0), axis=0
    )
    all_rows = jnp.arange(length, dtype=jnp.int32)
    marks = (all_rows // block_rows)[:, None] == jnp.arange(
        block_order.shape[0], dtype=jnp.int32
    )[None, :]
    anchor = jnp.sum(jnp.where(marks, block_order[None, :], 0), axis=1)
    all_place = anchor * block_rows + all_rows % block_rows

    def low_of(place):
        return jnp.max(
            jnp.where(doc_ends[None, :] <= place[:, None], doc_ends[None, :], 0), axis=1
        )

    sorted_rows = reps == 1
    query_length = length // reps
    tiles = query_length // TILE
    if sorted_rows:
        query_place = all_rows
        order = (all_place[:, None] == all_rows[None, :]).astype(BF)
        lows = low_of(all_rows)
        start = lows[::TILE] // TILE
        bounds = jnp.stack([start, jnp.arange(1, tiles + 1, dtype=jnp.int32)], axis=1)
    else:
        part = lax.rem(group, reps)
        query_place = lax.dynamic_slice(all_place, (part * query_length,), (query_length,))
        lows = low_of(query_place)
        bounds = jnp.broadcast_to(
            jnp.array([[0, length // TILE]], dtype=jnp.int32), (tiles, 2)
        )
    meta = jnp.concatenate(
        [query_place[None], lows[None], jnp.zeros((6, query_length), jnp.int32)], axis=0
    )
    place_col = all_place[:, None] if not sorted_rows else jnp.zeros((8, 128), jnp.int32)

    token_rows = token_rows.reshape(group_rows, width)
    inputs = token_rows.astype(F32)
    normed_low = layer_norm(inputs, gains[0], shifts[0]).astype(BF)
    mixed_t = lax.dot_general(
        qkv_weight, normed_low, (((0,), (1,)), ((), ())), preferred_element_type=F32
    ).astype(BF)
    mixed_t = mixed_t.reshape(team_heads, 3 * HEAD_DIM, group_rows)

    def spread_heads(coords, ins, outs):
        c, g, t = coords
        moves = [
            Move(s, ins[0].at[lax.div(lax.rem(g + s[1], groups), reps)], outs[0].at[g])
            for s in group_steps
        ]
        return [(ins[0].at[lax.div(g, reps)], outs[0].at[g])], moves

    [head_parts] = exchange(
        "heads",
        3,
        sizes,
        (mixed_t,),
        [((groups, 3 * HEAD_DIM, group_rows), BF)],
        spread_heads,
    )
    head_t = head_parts.transpose(1, 0, 2).reshape(3 * HEAD_DIM, length)
    zeros = jnp.zeros((HEAD_DIM, query_length), BF)
    if sorted_rows:
        sorted_t = dot_f32(head_t, order).astype(BF)
        kv_rows = lax.dot_general(
            order, head_t[HEAD_DIM:], (((0,), (1,)), ((), ())), preferred_element_type=F32
        ).astype(BF)
        kv_t = sorted_t[HEAD_DIM:]
        q_t = sorted_t[:HEAD_DIM]
    else:
        kv_t = head_t[HEAD_DIM:]
        kv_rows = kv_t.T
        q_t = lax.dynamic_slice(
            head_t[:HEAD_DIM], (0, part * query_length), (HEAD_DIM, query_length)
        )
    q_pad = jnp.concatenate([q_t * jnp.asarray(SCALE, BF), zeros], axis=0)
    attention_t, log_total = attend(sorted_rows, bounds, meta, place_col, q_pad, kv_rows, kv_t)
    low_t = attention_t.astype(BF)
    if sorted_rows:
        low_t = contract_cols(low_t, order).astype(BF)
    else:
        low_t = lax.dynamic_update_slice(
            jnp.zeros((HEAD_DIM, length), BF), low_t, (0, part * query_length)
        )
    low_t = low_t.reshape(HEAD_DIM, groups, group_rows).transpose(1, 0, 2)

    def gather_heads(coords, ins, outs):
        c, g, t = coords
        moves = [
            Move(s, ins[0].at[lax.rem(g + s[1], groups)], outs[0].at[t, g]) for s in group_steps
        ]
        local = [(ins[0].at[g], outs[0].at[t, g])]
        for s in team_steps:
            moves.append(Move(s, outs[0].at[t, g], outs[0].at[t, g], after=("local", 0)))
        for k, s in enumerate(group_steps):
            source = lax.rem(g + groups - s[1], groups)
            for e in team_steps:
                moves.append(Move(e, outs[0].at[t, source], outs[0].at[t, source], after=k))
        return local, moves

    [attended] = exchange(
        "attended",
        4,
        sizes,
        (low_t,),
        [((team, groups, HEAD_DIM, group_rows), BF)],
        gather_heads,
    )
    if reps > 1:
        chosen = jnp.arange(team_heads) * reps + lax.div(group, groups // reps)
        attended = jnp.take(attended, chosen, axis=1)
    attended_t = attended.reshape(width, group_rows)

    middle = inputs + contract_rows(attended_t, out_weight)
    second_low = layer_norm(middle, gains[1], shifts[1]).astype(BF)
    router_logits = dot_f32(second_low, router_weight)
    route = route_all[:, 0, :]
    earlier = jnp.arange(rows)[None, :] < jnp.arange(rows)[:, None]
    same = (route[:, :, None] == route[:, None, :]) & earlier[None]
    rank = jnp.sum(same.astype(jnp.int32), axis=2)
    route_flat = route.reshape(group_rows)
    route_hot = (route_flat[:, None] == jnp.arange(experts, dtype=jnp.int32)[None, :]).astype(F32)
    gate, mix_dense, mix_expert = router_heads(router_logits, route_hot, experts)
    scaled_gate = mix_expert * gate
    out_grad = cot_rows.reshape(group_rows, width).astype(F32)
    dense_grad = (out_grad * mix_dense[:, None]).astype(BF)
    expert_grad = (out_grad * scaled_gate[:, None]).astype(BF)
    slots = team * capacity
    slot = (jnp.arange(team, dtype=jnp.int32)[:, None] * capacity + rank).reshape(group_rows)
    target = jnp.where(
        route_flat % team == member, (route_flat // team) * slots + slot, groups * slots
    )
    select = (
        jnp.arange(groups * slots, dtype=jnp.int32)[:, None] == target[None, :]
    ).astype(BF)
    send = jnp.concatenate(
        [dot_f32(select, second_low).astype(BF), dot_f32(select, expert_grad).astype(BF)], axis=1
    ).reshape(groups, slots, 2 * width)

    def dispatch(coords, ins, outs):
        c, g, t = coords
        other = (1, 0, 0)
        moves = [
            Move(s, ins[0].at[lax.rem(g + s[1], groups)], outs[0].at[c, g]) for s in group_steps
        ]
        local = [(ins[0].at[g], outs[0].at[c, g])]
        moves.append(Move(other, outs[0].at[c, g], outs[0].at[c, g], after=("local", 0)))
        for k, s in enumerate(group_steps):
            source = lax.rem(g + groups - s[1], groups)
            moves.append(Move(other, outs[0].at[c, source], outs[0].at[c, source], after=k))
        return local, moves

    [arrived] = exchange(
        "dispatch", 5, sizes, (send,), [((two, groups, slots, 2 * width), BF)], dispatch
    )
    arrived = arrived.reshape(two * groups * slots, 2 * width)
    arrived_in, arrived_grad = arrived[:, :width], arrived[:, width:]

    expert_hidden = dot_f32(arrived_in, expert_up[0])
    expert_active = gelu_tanh(expert_hidden).astype(BF)
    partial_out = dot_f32(expert_active, expert_down[0])
    hidden_pull = jax.vjp(gelu_tanh, expert_hidden)[1]
    hidden_grad = hidden_pull(contract_cols(arrived_grad, expert_down[0]))[0].astype(BF)
    input_part = contract_cols(hidden_grad, expert_up[0])
    partial = jnp.concatenate([partial_out, input_part], axis=1).reshape(
        two, groups * slots, 2 * width
    )
    mine = lax.dynamic_index_in_dim(partial, core, 0, keepdims=False)
    theirs = lax.dynamic_index_in_dim(partial, 1 - core, 0, keepdims=False)
    back = (mine + lax.ppermute(theirs, "dp", swap)).astype(BF).reshape(groups, slots, 2 * width)

    def spread(coords, ins, outs):
        c, g, t = coords
        moves = [
            Move(s, ins[0].at[lax.rem(g + s[1], groups)], outs[0].at[g]) for s in group_steps
        ]
        return [(ins[0].at[g], outs[0].at[g])], moves

    [returned] = exchange("returned", 6, sizes, (back,), [(back.shape, BF)], spread)
    returned = returned.reshape(groups * slots, 2 * width)
    expert_down_grad = contract_rows(expert_active, arrived_grad)
    expert_up_grad = contract_rows(arrived_in, hidden_grad)

    upper_residual = dot_f32(second_low, up_weight)
    active_low = gelu_tanh(upper_residual).astype(BF)
    dense_output = dot_f32(active_low, down_weight)
    upper_pull = jax.vjp(gelu_tanh, upper_residual)[1]
    upper_grad = upper_pull(contract_cols(dense_grad, down_weight))[0].astype(BF)
    second_part = contract_cols(upper_grad, up_weight)
    down_term = contract_rows(active_low, dense_grad)
    up_term = contract_rows(second_low, upper_grad)

    picked = contract_rows(select, returned)
    expert_rows, expert_back = picked[:, :width], picked[:, width:]
    layer_part = mix_dense[:, None] * dense_output + scaled_gate[:, None] * expert_rows
    sums_part = jnp.stack(
        [jnp.sum(out_grad * dense_output, axis=1), jnp.sum(out_grad * expert_rows, axis=1)]
    )
    sums_part = jnp.pad(
        sums_part.reshape(2, team, rows).transpose(1, 0, 2), ((0, 0), (0, 6), (0, 0))
    )
    both_part = (
        jnp.concatenate([layer_part, second_part + expert_back], axis=1)
        .astype(BF)
        .reshape(team, rows, 2 * width)
    )

    def to_owner(coords, ins, outs):
        c, g, t = coords
        moves, local = [], []
        for n in range(len(ins)):
            for s in team_steps:
                moves.append(Move(s, ins[n].at[lax.rem(t + s[2], team)], outs[n].at[t]))
            local.append((ins[n].at[t], outs[n].at[t]))
        return local, moves

    both_own, sums_own = exchange(
        "owner",
        7,
        sizes,
        (both_part, sums_part),
        [(both_part.shape, BF), (sums_part.shape, F32)],
        to_owner,
    )
    both_own = jnp.sum(both_own.astype(F32), axis=0)
    sums_own = jnp.sum(sums_own, axis=0)

    def own(array):
        return lax.dynamic_slice_in_dim(array, member * rows, rows, axis=0)

    middle_own, logits_own, hot_own, second_own = (
        own(middle),
        own(router_logits),
        own(route_hot),
        own(second_low),
    )
    out_grad_own = cotangent[0].astype(F32)
    layer_out = middle_own + both_own[:, :width]
    (gate_own, mix_dense_own, mix_expert_own), router_pull = jax.vjp(
        lambda values: router_heads(values, hot_own, experts), logits_own
    )
    logit_grad = router_pull(
        (sums_own[1] * mix_expert_own, sums_own[0], sums_own[1] * gate_own)
    )[0].astype(BF)
    router_term = contract_rows(second_own, logit_grad)
    second_grad = both_own[:, width:] + contract_cols(logit_grad, router_weight)
    middle_part, gain_second, bias_second = jax.vjp(layer_norm, middle_own, gains[1], shifts[1])[1](
        second_grad
    )
    middle_grad = out_grad_own + middle_part
    branch_grad = middle_grad.astype(BF)
    attended_own = lax.dynamic_slice_in_dim(attended_t, member * rows, rows, axis=1)
    out_term = dot_f32(attended_own, branch_grad)
    flow_t = contract_cols(out_weight, branch_grad).astype(BF)
    flow_t = flow_t.reshape(team, team_heads, HEAD_DIM, rows)

    def spread_flow(coords, ins, outs):
        c, g, t = coords
        moves = []
        for dg in range(groups):
            for dt in range(team):
                if dg or dt:
                    to_g, to_t = lax.rem(g + dg, groups), lax.rem(t + dt, team)
                    moves.append(
                        Move((0, dg, dt), ins[0].at[to_t, lax.div(to_g, reps)], outs[0].at[g, t])
                    )
        return [(ins[0].at[t, lax.div(g, reps)], outs[0].at[g, t])], moves

    [flow_parts] = exchange(
        "flow", 8, sizes, (flow_t,), [((groups, team, HEAD_DIM, rows), BF)], spread_flow
    )
    flow_all = flow_parts.transpose(2, 0, 1, 3).reshape(HEAD_DIM, length)
    if sorted_rows:
        flow_all = dot_f32(flow_all, order).astype(BF)
    else:
        flow_all = lax.dynamic_slice(
            flow_all, (0, part * query_length), (HEAD_DIM, query_length)
        )
    do_pad = jnp.concatenate([zeros, flow_all], axis=0)
    query_grad, pair_grad = attend_back(
        sorted_rows,
        bounds,
        meta,
        place_col,
        q_pad,
        do_pad,
        attention_t,
        log_total,
        kv_rows,
        kv_t,
    )
    if not sorted_rows:
        query_grad = lax.dynamic_update_slice(
            jnp.zeros((HEAD_DIM, length), BF), query_grad, (0, part * query_length)
        )
    grad_t = jnp.concatenate([query_grad, pair_grad], axis=0)
    if sorted_rows:
        grad_t = contract_cols(grad_t, order).astype(BF)
    grad_t = grad_t.reshape(3 * HEAD_DIM, groups, group_rows).transpose(1, 0, 2)
    [grad_parts] = exchange("mixed", 9, sizes, (grad_t,), [(grad_t.shape, BF)], spread)
    if reps > 1:
        grad_parts = jnp.sum(
            grad_parts.reshape(team_heads, reps, 3 * HEAD_DIM, group_rows).astype(F32), axis=1
        ).astype(BF)
    mixed_grad_t = grad_parts.reshape(qkv_cols, group_rows)
    normed_part = (
        lax.dot_general(
            mixed_grad_t, qkv_weight, (((0,), (1,)), ((), ())), preferred_element_type=F32
        )
        .astype(BF)
        .reshape(team, rows, width)
    )
    qkv_term = lax.dot_general(
        normed_low, mixed_grad_t, (((0,), (1,)), ((), ())), preferred_element_type=F32
    )
    [normed_own] = exchange(
        "normed", 10, sizes, (normed_part,), [(normed_part.shape, BF)], to_owner
    )
    normed_grad = jnp.sum(normed_own.astype(F32), axis=0)
    input_part_grad, gain_first, bias_first = jax.vjp(
        layer_norm, tokens[0].astype(F32), gains[0], shifts[0]
    )[1](normed_grad)
    input_grad = middle_grad + input_part_grad

    def core_half(term):
        halves = term.reshape((two, term.shape[0] // two) + term.shape[1:])
        keep = lax.dynamic_index_in_dim(halves, core, 0, keepdims=False)
        give = lax.dynamic_index_in_dim(halves, 1 - core, 0, keepdims=False)
        return keep + lax.ppermute(give.astype(BF), "dp", swap).astype(F32)

    def over_groups(term):
        return lax.psum_scatter(
            core_half(term).astype(BF),
            "ctx",
            scatter_dimension=0,
            tiled=True,
            axis_index_groups=by_group,
        )

    down_sum = over_groups(down_term).astype(F32)
    up_sum = over_groups(up_term).reshape(team, wr, up_cols)
    out_sum = lax.psum_scatter(
        core_half(out_term).astype(BF), "ctx", scatter_dimension=0, tiled=True
    ).astype(F32)
    qkv_sum = over_groups(qkv_term).reshape(team, wr, qkv_cols)
    up_own, qkv_own = exchange(
        "owners",
        11,
        sizes,
        (tall(up_sum), tall(qkv_sum)),
        [(tall(up_sum).shape, BF), (tall(qkv_sum).shape, BF)],
        to_owner,
    )
    up_own = (
        up_own.reshape(team, wr, two * groups, hidden_dev)
        .transpose(1, 2, 0, 3)
        .reshape(wr, hidden)
        .astype(F32)
    )
    qkv_own = (
        qkv_own.reshape(team, wr, team_heads, 3, HEAD_DIM)
        .transpose(1, 3, 0, 2, 4)
        .reshape(wr, 3 * width)
        .astype(F32)
    )
    small_term = jnp.concatenate(
        [
            router_term,
            gain_first[:, None],
            gain_second[:, None],
            bias_first[:, None],
            bias_second[:, None],
        ],
        axis=1,
    )
    small_sum = lax.psum_scatter(small_term, ("dp", "ctx"), scatter_dimension=0, tiled=True)
    vector_sums = small_sum[:, router_cols:].T
    return (
        layer_out[None].astype(BF),
        input_grad[None].astype(BF),
        qkv_own,
        out_sum,
        up_own,
        down_sum,
        small_sum[:, :router_cols],
        vector_sums[:2],
        vector_sums[2:],
        expert_up_grad[None],
        expert_down_grad[None],
    )


def solution(mesh):
    in_specs = (
        P("dp", "ctx", None),
        P("dp", "ctx", None),
        P(),
        P("dp", None),
        P("dp", "ctx", None),
        P(("dp", "ctx"), None),
        P(("dp", "ctx"), None),
        P(("dp", "ctx"), None),
        P(("dp", "ctx"), None),
        P(("dp", "ctx"), None),
        P(None, ("dp", "ctx")),
        P(None, ("dp", "ctx")),
        P("ctx", None, "dp"),
        P("ctx", "dp", None),
    )
    out_specs = (
        P("dp", "ctx", None),
        P("dp", "ctx", None),
        P(("dp", "ctx"), None),
        P(("dp", "ctx"), None),
        P(("dp", "ctx"), None),
        P(("dp", "ctx"), None),
        P(("dp", "ctx"), None),
        P(None, ("dp", "ctx")),
        P(None, ("dp", "ctx")),
        P("ctx", None, "dp"),
        P("ctx", "dp", None),
    )
    return jax.shard_map(
        per_device, mesh=mesh, in_specs=in_specs, out_specs=out_specs, check_vma=False
    )
```

```python
import functools
import math

import jax
import jax.numpy as jnp
from jax import lax
from jax.experimental import pallas as pl
from jax.experimental.pallas import tpu as pltpu
from jax.sharding import PartitionSpec as P

HEADS = 16
HEAD_DIM = 64

EPS = 1e-05
NEG = -1e30
SCALE = 0.125
TILE = 256
BF = jnp.bfloat16
F32 = jnp.float32
MESH = pl.DeviceIdType.MESH


def layer_norm(values, gain, shift):
    center = values - jnp.mean(values, axis=-1, keepdims=True)
    spread = jnp.mean(center * center, axis=-1, keepdims=True)
    return center * lax.rsqrt(spread + EPS) * gain + shift


def gelu_tanh(values):
    return jax.nn.gelu(values, approximate=True)


def router_heads(router_logits, route_hot, experts):
    chances = jax.nn.softmax(router_logits[:, :experts], axis=-1)
    gate = jnp.sum(chances * route_hot, axis=-1)
    mixing = jax.nn.softmax(router_logits[:, experts:], axis=-1)
    return (gate, mixing[:, 0], mixing[:, 1])


def dot_f32(left, right):
    return jnp.dot(left, right, preferred_element_type=F32)


def contract_rows(left, right):
    return lax.dot_general(left, right, (((0,), (0,)), ((), ())), preferred_element_type=F32)


def contract_cols(left, right):
    return lax.dot_general(left, right, (((1,), (1,)), ((), ())), preferred_element_type=F32)


class Move:
    def __init__(self, step, src, dst, after=None):
        self.step, self.src, self.dst, self.after = step, src, dst, after


def exchange(name, cid, sizes, ins, outs, build, micros=20):
    two, groups, team = sizes

    def kernel(*refs):
        in_refs, out_refs = refs[: len(ins)], refs[len(ins) : len(ins) + len(outs)]
        send_sem, recv_sem, local_sem = refs[len(ins) + len(outs) :]
        c = lax.axis_index("dp")
        i = lax.axis_index("ctx")
        g, t = lax.div(i, team), lax.rem(i, team)

        def device(step):
            dc, dg, dt = step
            return (
                lax.rem(c + dc, two),
                lax.rem(g + dg, groups) * team + lax.rem(t + dt, team),
            )

        locals_, moves = build((c, g, t), in_refs, out_refs)
        steps = sorted({m.step for m in moves})
        greet = sorted(
            set(steps) | {((-a) % two, (-b) % groups, (-d) % team) for a, b, d in steps}
        )
        barrier = pltpu.get_barrier_semaphore()
        for step in greet:
            pl.semaphore_signal(barrier, inc=1, device_id=device(step), device_id_type=MESH)
        pl.semaphore_wait(barrier, len(greet))

        copies = {}
        arrived = set()
        for k, (src, dst) in enumerate(locals_):
            copies[("local", k)] = pltpu.make_async_copy(src, dst, local_sem.at[k])
        for k, m in enumerate(moves):
            copies[k] = pltpu.make_async_remote_copy(
                src_ref=m.src,
                dst_ref=m.dst,
                send_sem=send_sem.at[k],
                recv_sem=recv_sem.at[k],
                device_id=device(m.step),
                device_id_type=MESH,
            )
        for k, m in enumerate(moves):
            if m.after is None:
                copies[k].start()
        for k in range(len(locals_)):
            copies[("local", k)].start()
        for k, m in enumerate(moves):
            if m.after is not None:
                if m.after not in arrived:
                    arrived.add(m.after)
                    if isinstance(m.after, tuple):
                        copies[m.after].wait()
                    else:
                        copies[m.after].wait_recv()
                copies[k].start()
        for k in range(len(locals_)):
            if ("local", k) not in arrived:
                copies[("local", k)].wait()
        for k in range(len(moves)):
            if k not in arrived:
                copies[k].wait_recv()
        for k in range(len(moves)):
            copies[k].wait_send()

    count = []

    def trace_counts():
        class Probe:
            def __getattr__(self, name):
                return self

            def __getitem__(self, index):
                return self

        locals_, moves = build((0, 0, 0), [Probe() for _ in ins], [Probe() for _ in outs])
        count.extend((len(locals_), len(moves)))

    trace_counts()
    return pl.pallas_call(
        kernel,
        name=name,
        out_shape=tuple(jax.ShapeDtypeStruct(s, d) for s, d in outs),
        in_specs=[pl.BlockSpec(memory_space=pl.ANY)] * len(ins),
        out_specs=tuple(pl.BlockSpec(memory_space=pl.ANY) for _ in outs),
        scratch_shapes=[
            pltpu.SemaphoreType.DMA((max(1, count[1]),)),
            pltpu.SemaphoreType.DMA((max(1, count[1]),)),
            pltpu.SemaphoreType.DMA((max(1, count[0]),)),
        ],
        compiler_params=pltpu.CompilerParams(collective_id=cid, has_side_effects=True),
        cost_estimate=pl.CostEstimate(
            flops=0, bytes_accessed=int(micros * 3.0e6), transcendentals=0
        ),
    )(*ins)


def mask_of(kt, key_place, query_place, query_low):
    return (key_place <= query_place) & (key_place >= query_low)


def key_places(sorted_rows, kt, place_ref):
    if sorted_rows:
        return lax.broadcasted_iota(jnp.int32, (TILE, TILE), 0) + kt * TILE
    return place_ref[pl.ds(pl.multiple_of(kt * TILE, TILE), TILE), :]


def attend_kernel(
    sorted_rows, bounds, meta_ref, place_ref, q_ref, rows_ref, kvt_ref, out_ref, lse_ref
):
    step = pl.program_id(0)
    queries = q_ref[...]
    place, low = meta_ref[0:1, :], meta_ref[1:2, :]

    def body(kt, carry):
        peak, total, acc = carry
        at = pl.ds(pl.multiple_of(kt * TILE, TILE), TILE)
        scores = dot_f32(rows_ref[at, :], queries)
        allowed = mask_of(kt, key_places(sorted_rows, kt, place_ref), place, low)
        scores = jnp.where(allowed, scores, NEG)
        new_peak = jnp.maximum(peak, jnp.max(scores, axis=0, keepdims=True))
        weights = jnp.exp(scores - new_peak)
        fade = jnp.exp(peak - new_peak)
        total = total * fade + jnp.sum(weights, axis=0, keepdims=True)
        acc = acc * fade + dot_f32(kvt_ref[HEAD_DIM:, at], weights.astype(BF))
        return new_peak, total, acc

    start = (
        jnp.full((1, TILE), NEG, F32),
        jnp.zeros((1, TILE), F32),
        jnp.zeros((HEAD_DIM, TILE), F32),
    )
    peak, total, acc = lax.fori_loop(bounds[step, 0], bounds[step, 1], body, start)
    out_ref[...] = acc / total
    lse_ref[...] = peak + jnp.log(total)


def attend_back_kernel(
    sorted_rows,
    tiles,
    bounds,
    meta_ref,
    place_ref,
    q_ref,
    do_ref,
    out_ref,
    lse_ref,
    rows_ref,
    kvt_ref,
    dq_ref,
    dkv_ref,
    acc_ref,
):
    step = pl.program_id(0)

    @pl.when(step == 0)
    def _():
        acc_ref[...] = jnp.zeros_like(acc_ref)

    queries, flows = q_ref[...], do_ref[...]
    place, low = meta_ref[0:1, :], meta_ref[1:2, :]
    log_total = lse_ref[...]
    delta = jnp.sum(flows[HEAD_DIM:, :].astype(F32) * out_ref[...], axis=0, keepdims=True)

    def body(kt, dq):
        at = pl.ds(pl.multiple_of(kt * TILE, TILE), TILE)
        rows = rows_ref[at, :]
        scores = dot_f32(rows, queries)
        allowed = mask_of(kt, key_places(sorted_rows, kt, place_ref), place, low)
        chances = jnp.exp(jnp.where(allowed, scores - log_total, NEG))
        flow = dot_f32(rows, flows)
        score_grad = (chances * (flow - delta)).astype(BF)
        dq = dq + dot_f32(kvt_ref[:HEAD_DIM, at], score_grad)
        acc_ref[:HEAD_DIM, at] += contract_cols(queries[:HEAD_DIM, :], score_grad)
        acc_ref[HEAD_DIM:, at] += contract_cols(flows[HEAD_DIM:, :], chances.astype(BF))
        return dq

    dq = lax.fori_loop(
        bounds[step, 0], bounds[step, 1], body, jnp.zeros((HEAD_DIM, TILE), F32)
    )
    dq_ref[...] = (dq * SCALE).astype(BF)

    @pl.when(step == tiles - 1)
    def _():
        dkv_ref[...] = acc_ref[...].astype(BF)


def attention_specs(length, query_length):
    def whole(shape):
        return pl.BlockSpec(shape, lambda i: (0, 0))

    def tile(rows):
        return pl.BlockSpec((rows, TILE), lambda i: (0, i))

    return whole, tile


def attend(sorted_rows, bounds, meta, place_col, q_pad, kv_rows, kv_t):
    length, query_length = kv_rows.shape[0], q_pad.shape[1]
    whole, tile = attention_specs(length, query_length)
    return pl.pallas_call(
        functools.partial(attend_kernel, sorted_rows),
        name="attend",
        grid=(query_length // TILE,),
        in_specs=[
            pl.BlockSpec(memory_space=pltpu.SMEM),
            tile(8),
            whole(place_col.shape),
            tile(2 * HEAD_DIM),
            whole((length, 2 * HEAD_DIM)),
            whole((2 * HEAD_DIM, length)),
        ],
        out_specs=(tile(HEAD_DIM), tile(1)),
        out_shape=(
            jax.ShapeDtypeStruct((HEAD_DIM, query_length), F32),
            jax.ShapeDtypeStruct((1, query_length), F32),
        ),
        compiler_params=pltpu.CompilerParams(vmem_limit_bytes=40 * 2**20),
    )(bounds, meta, place_col, q_pad, kv_rows, kv_t)


def attend_back(sorted_rows, bounds, meta, place_col, q_pad, do_pad, out, lse, kv_rows, kv_t):
    length, query_length = kv_rows.shape[0], q_pad.shape[1]
    whole, tile = attention_specs(length, query_length)
    return pl.pallas_call(
        functools.partial(attend_back_kernel, sorted_rows, query_length // TILE),
        name="attend_back",
        grid=(query_length // TILE,),
        in_specs=[
            pl.BlockSpec(memory_space=pltpu.SMEM),
            tile(8),
            whole(place_col.shape),
            tile(2 * HEAD_DIM),
            tile(2 * HEAD_DIM),
            tile(HEAD_DIM),
            tile(1),
            whole((length, 2 * HEAD_DIM)),
            whole((2 * HEAD_DIM, length)),
        ],
        out_specs=(tile(HEAD_DIM), whole((2 * HEAD_DIM, length))),
        out_shape=(
            jax.ShapeDtypeStruct((HEAD_DIM, query_length), BF),
            jax.ShapeDtypeStruct((2 * HEAD_DIM, length), BF),
        ),
        scratch_shapes=[pltpu.VMEM((2 * HEAD_DIM, length), F32)],
        compiler_params=pltpu.CompilerParams(vmem_limit_bytes=40 * 2**20),
    )(bounds, meta, place_col, q_pad, do_pad, out, lse, kv_rows, kv_t)


def gelu_and_slope(x):
    k = math.sqrt(2.0 / math.pi)
    square = x * x
    bent = jnp.tanh(k * (x + 0.044715 * (square * x)))
    half = 0.5 * (1.0 + bent)
    slope = half + (0.5 * k) * x * (1.0 - bent * bent) * (1.0 + (3 * 0.044715) * square)
    return x * half, slope


def span(i, size):
    return pl.ds(pl.multiple_of(i * size, size), size)


def feed_kernel(sizes, copies_count, *refs):
    two, groups, team = sizes
    (send_s, send_g, eup_h, edown_h, second_h, dgrad_h, upw_h, downw_h, sel_h, cot_h, mix_h) = refs[:11]
    (layer_o, grad_o, sums_o, eug_o, edg_o, down_o, up_o) = refs[11:18]
    (
        arr_s, arr_g, eup, edown, second, dgrad, upw, downw, sel, cot, mix,
        slope, active, hgrad, acc, give, got_s, got_g, ret_s, ret_g, back_s, back_g,
        low, ugrad, dense, spart, lay, spa, sums, lay_r, spa_r, sums_r,
        wide, tallb, term_give, term_got, send_sem, recv_sem, load_sem, out_sem,
    ) = refs[18:]
    c = lax.axis_index("dp")
    i = lax.axis_index("ctx")
    g, t = lax.div(i, team), lax.rem(i, team)
    width = second.shape[1]
    rows = lay.shape[1]
    hid, ehid = upw.shape[1], eup.shape[1]
    core = lax.rem(c + 1, two)

    def device(step):
        dc, dg, dt = step
        return (
            lax.rem(c + dc, two),
            lax.rem(g + dg, groups) * team + lax.rem(t + dt, team),
        )

    index = [0]

    def remote(src, dst, step):
        k = index[0]
        index[0] += 1
        assert k < copies_count
        return pltpu.make_async_remote_copy(
            src_ref=src,
            dst_ref=dst,
            send_sem=send_sem.at[k],
            recv_sem=recv_sem.at[k],
            device_id=device(step),
            device_id_type=MESH,
        )

    group_steps = [(0, k, 0) for k in range(1, groups)]
    team_steps = [(0, 0, k) for k in range(1, team)]
    swap = (1, 0, 0)
    loads = []
    for k, (src, dst) in enumerate(
        [
            (second_h, second), (upw_h, upw), (dgrad_h, dgrad), (downw_h, downw),
            (eup_h, eup), (edown_h, edown), (sel_h, sel), (cot_h, cot), (mix_h, mix),
            (send_s.at[g], arr_s.at[c, g]), (send_g.at[g], arr_g.at[c, g]),
        ]
    ):
        load = pltpu.make_async_copy(src, dst, load_sem.at[k])
        load.start()
        loads.append(load)

    barrier = pltpu.get_barrier_semaphore()
    greet = group_steps + team_steps + [swap]
    for step in greet:
        pl.semaphore_signal(barrier, inc=1, device_id=device(step), device_id_type=MESH)
    pl.semaphore_wait(barrier, len(greet))

    every = []

    def launch(copy):
        copy.start()
        every.append(copy)
        return copy

    def to_groups(src, dst):
        return [
            launch(remote(src.at[lax.rem(g + s[1], groups)], dst.at[g], s)) for s in group_steps
        ]

    def source(s):
        return lax.rem(g + groups - s[1], groups)

    out_s = [
        launch(remote(send_s.at[lax.rem(g + s[1], groups)], arr_s.at[c, g], s))
        for s in group_steps
    ]
    swap_s = [launch(remote(send_s.at[g], arr_s.at[c, g], swap))]
    out_g = [
        launch(remote(send_g.at[lax.rem(g + s[1], groups)], arr_g.at[c, g], s))
        for s in group_steps
    ]
    swap_g = [launch(remote(send_g.at[g], arr_g.at[c, g], swap))]

    for load in loads[:4]:
        load.wait()

    def dense_in(h, carry):
        at = span(h, TILE)
        value, bend = gelu_and_slope(dot_f32(second[...], upw[:, at]))
        low[:, at] = value.astype(BF)
        ugrad[:, at] = (bend * contract_cols(dgrad[...], downw[at, :])).astype(BF)
        return carry

    lax.fori_loop(0, hid // TILE, dense_in, 0)

    def dense_out(n, carry):
        at = span(n, TILE)
        dense[:, at] = dot_f32(low[...], downw[:, at])
        spart[:, at] = contract_cols(ugrad[...], upw[at, :])
        return carry

    lax.fori_loop(0, width // TILE, dense_out, 0)

    for load in loads[4:]:
        load.wait()
    for copy, s in zip(out_s, group_steps):
        copy.wait_recv()
        swap_s.append(launch(remote(arr_s.at[c, source(s)], arr_s.at[c, source(s)], swap)))
    for copy in swap_s:
        copy.wait_recv()
    entries = 2 * groups * arr_s.shape[2]

    def expert_in(h, carry):
        at = span(h, TILE)
        value, bend = gelu_and_slope(dot_f32(arr_s[...].reshape(entries, width), eup[:, at]))
        active[:, at] = value.astype(BF)
        slope[:, at] = bend
        return carry

    lax.fori_loop(0, ehid // TILE, expert_in, 0)

    def expert_out(n, carry):
        at = span(n, TILE)
        acc[:, :, at] = dot_f32(active[...], edown[:, at]).reshape(2, entries // 2, TILE)
        return carry

    lax.fori_loop(0, width // TILE, expert_out, 0)
    give[0] = acc[core].astype(BF)
    other_s = launch(remote(give.at[0], got_s, swap))

    for copy, s in zip(out_g, group_steps):
        copy.wait_recv()
        swap_g.append(launch(remote(arr_g.at[c, source(s)], arr_g.at[c, source(s)], swap)))
    other_s.wait_recv()
    ret_s[...] = (acc[c] + got_s[...].astype(F32)).astype(BF).reshape(ret_s.shape)
    home_s = to_groups(ret_s, back_s)
    back_s[g] = ret_s[g]
    for copy in swap_g:
        copy.wait_recv()

    def expert_back(h, carry):
        at = span(h, TILE)
        pull = contract_cols(arr_g[...].reshape(entries, width), edown[at, :])
        hgrad[:, at] = (slope[:, at] * pull).astype(BF)
        return carry

    lax.fori_loop(0, ehid // TILE, expert_back, 0)

    def expert_back_out(n, carry):
        at = span(n, TILE)
        acc[:, :, at] = contract_cols(hgrad[...], eup[at, :]).reshape(2, entries // 2, TILE)
        return carry

    lax.fori_loop(0, width // TILE, expert_back_out, 0)
    give[1] = acc[core].astype(BF)
    other_g = launch(remote(give.at[1], got_g, swap))
    other_g.wait_recv()
    ret_g[...] = (acc[c] + got_g[...].astype(F32)).astype(BF).reshape(ret_g.shape)
    home_g = to_groups(ret_g, back_g)
    back_g[g] = ret_g[g]

    for copy in home_s:
        copy.wait_recv()
    slots = groups * back_s.shape[1]
    lane = lax.broadcasted_iota(jnp.int32, (rows, 128), 1)

    def join_layer(r, carry):
        at = span(r, rows)
        found = dot_f32(sel[at, :], back_s[...].reshape(slots, width))
        own = dense[at, :]
        flow = cot[at, :].astype(F32)
        mixes = mix[at, :]
        lay[r] = (mixes[:, 0:1] * own + mixes[:, 1:2] * found).astype(BF)
        plain = jnp.sum(flow * own, axis=1, keepdims=True)
        routed = jnp.sum(flow * found, axis=1, keepdims=True)
        sums[r] = jnp.where(lane == 0, plain, jnp.where(lane == 1, routed, 0.0))
        return carry

    lax.fori_loop(0, team, join_layer, 0)

    def to_team(src, dst):
        made = [launch(remote(src.at[lax.rem(t + s[2], team)], dst.at[t], s)) for s in team_steps]
        dst[t] = src[t]
        return made

    team_copies = to_team(lay, lay_r) + to_team(sums, sums_r)

    def down_grad(n, carry):
        slot = lax.rem(n, 2)
        at = span(n, tallb.shape[1])
        out = pltpu.make_async_copy(tallb.at[slot], edg_o.at[at, :], out_sem.at[slot])

        @pl.when(n >= 2)
        def _():
            out.wait()

        tallb[slot] = contract_rows(active[:, at], arr_g[...].reshape(entries, width))
        out.start()
        return carry

    def up_grad(n, carry):
        slot = lax.rem(n, 2)
        at = span(n, wide.shape[1])
        out = pltpu.make_async_copy(wide.at[slot], eug_o.at[at, :], out_sem.at[2 + slot])

        @pl.when(n >= 2)
        def _():
            out.wait()

        left = arr_s[:, :, :, at].reshape(entries, wide.shape[1])
        wide[slot] = contract_rows(left, hgrad[...])
        out.start()
        return carry

    lax.fori_loop(0, ehid // tallb.shape[1], down_grad, 0)
    for copy in home_g:
        copy.wait_recv()

    def join_grad(r, carry):
        at = span(r, rows)
        found = dot_f32(sel[at, :], back_g[...].reshape(slots, width))
        spa[r] = (spart[at, :] + found).astype(BF)
        return carry

    lax.fori_loop(0, team, join_grad, 0)
    team_copies += to_team(spa, spa_r)

    half = hid // 2
    term_tile = 128

    def down_term(base, n):
        at = pl.ds(pl.multiple_of(base + n * term_tile, term_tile), term_tile)
        return contract_rows(low[:, at], dgrad[...])

    def up_term(base, n):
        at = pl.ds(pl.multiple_of(base + n * term_tile, term_tile), term_tile)
        return contract_rows(second[:, at], ugrad[...])

    terms = []
    for k, (term, size) in enumerate(((down_term, half), (up_term, width // 2))):

        def giving(n, carry, k=k, term=term, size=size):
            term_give[k, span(n, term_tile), :] = term(core * size, n).astype(BF)
            return carry

        lax.fori_loop(0, size // term_tile, giving, 0)
        terms.append(launch(remote(term_give.at[k], term_got.at[k], swap)))
    lax.fori_loop(0, width // wide.shape[1], up_grad, 0)
    for k, (term, size, out) in enumerate(
        ((down_term, half, down_o), (up_term, width // 2, up_o))
    ):
        terms[k].wait_recv()

        def keeping(n, carry, k=k, term=term, size=size, out=out):
            at = span(n, term_tile)
            out[at, :] = (term(c * size, n) + term_got[k, at, :].astype(F32)).astype(BF)
            return carry

        lax.fori_loop(0, size // term_tile, keeping, 0)

    for copy in team_copies:
        copy.wait_recv()
    layer_o[...] = jnp.sum(lay_r[...].astype(F32), axis=0)
    grad_o[...] = jnp.sum(spa_r[...].astype(F32), axis=0)
    sums_o[...] = jnp.sum(sums_r[...], axis=0)
    for k, (buf, out) in enumerate(((tallb, edg_o), (tallb, edg_o), (wide, eug_o), (wide, eug_o))):
        at = pl.ds(0, buf.shape[1])
        pltpu.make_async_copy(buf.at[k % 2], out.at[at, :], out_sem.at[k]).wait()
    for copy in every:
        copy.wait_send()


def feed_forward(sizes, rows, send_s, send_g, eup, edown, second, dgrad, upw, downw, sel, cot, mix):
    two, groups, team = sizes
    slots = send_s.shape[1]
    width = second.shape[1]
    hid, ehid = upw.shape[1], eup.shape[1]
    entries = 2 * groups * slots
    count = 2 * (groups - 1) * 2 + 2 * groups + 2 + 3 * (team - 1) + 2
    anywhere = pl.BlockSpec(memory_space=pl.ANY)
    inside = pl.BlockSpec(memory_space=pltpu.VMEM)
    team_rows = team * rows
    return pl.pallas_call(
        functools.partial(feed_kernel, sizes, count),
        name="feed_forward",
        out_shape=(
            jax.ShapeDtypeStruct((rows, width), F32),
            jax.ShapeDtypeStruct((rows, width), F32),
            jax.ShapeDtypeStruct((rows, 128), F32),
            jax.ShapeDtypeStruct((width, ehid), F32),
            jax.ShapeDtypeStruct((ehid, width), F32),
            jax.ShapeDtypeStruct((hid // 2, width), BF),
            jax.ShapeDtypeStruct((width // 2, hid), BF),
        ),
        in_specs=[anywhere] * 11,
        out_specs=(inside, inside, inside, anywhere, anywhere, inside, inside),
        scratch_shapes=[
            pltpu.VMEM((two, groups, slots, width), BF),
            pltpu.VMEM((two, groups, slots, width), BF),
            pltpu.VMEM(eup.shape, BF),
            pltpu.VMEM(edown.shape, BF),
            pltpu.VMEM(second.shape, BF),
            pltpu.VMEM(dgrad.shape, BF),
            pltpu.VMEM(upw.shape, BF),
            pltpu.VMEM(downw.shape, BF),
            pltpu.VMEM(sel.shape, BF),
            pltpu.VMEM(cot.shape, BF),
            pltpu.VMEM(mix.shape, F32),
            pltpu.VMEM((entries, ehid), F32),
            pltpu.VMEM((entries, ehid), BF),
            pltpu.VMEM((entries, ehid), BF),
            pltpu.VMEM((2, entries // 2, width), F32),
            pltpu.VMEM((2, entries // 2, width), BF),
            pltpu.VMEM((entries // 2, width), BF),
            pltpu.VMEM((entries // 2, width), BF),
            pltpu.VMEM((groups, slots, width), BF),
            pltpu.VMEM((groups, slots, width), BF),
            pltpu.VMEM((groups, slots, width), BF),
            pltpu.VMEM((groups, slots, width), BF),
            pltpu.VMEM((team_rows, hid), BF),
            pltpu.VMEM((team_rows, hid), BF),
            pltpu.VMEM((team_rows, width), F32),
            pltpu.VMEM((team_rows, width), F32),
            pltpu.VMEM((team, rows, width), BF),
            pltpu.VMEM((team, rows, width), BF),
            pltpu.VMEM((team, rows, 128), F32),
            pltpu.VMEM((team, rows, width), BF),
            pltpu.VMEM((team, rows, width), BF),
            pltpu.VMEM((team, rows, 128), F32),
            pltpu.VMEM((2, 128, ehid), F32),
            pltpu.VMEM((2, 256, width), F32),
            pltpu.VMEM((2, hid // 2, width), BF),
            pltpu.VMEM((2, hid // 2, width), BF),
            pltpu.SemaphoreType.DMA((count,)),
            pltpu.SemaphoreType.DMA((count,)),
            pltpu.SemaphoreType.DMA((11,)),
            pltpu.SemaphoreType.DMA((4,)),
        ],
        compiler_params=pltpu.CompilerParams(
            collective_id=5, has_side_effects=True, vmem_limit_bytes=60 * 2**20
        ),
        cost_estimate=pl.CostEstimate(
            flops=0, bytes_accessed=240_000_000, transcendentals=0
        ),
    )(send_s, send_g, eup, edown, second, dgrad, upw, downw, sel, cot, mix)


def tall(chunk):
    rows, cols = chunk.shape[-2:]
    factor = 1
    while (rows * factor) % 16:
        factor *= 2
    return chunk.reshape(chunk.shape[:-2] + (rows * factor, cols // factor))


def per_device(
    tokens,
    cotangent,
    block_order,
    doc_lengths,
    routes,
    w_qkv,
    w_out,
    w_up,
    w_down,
    router,
    norm_gains,
    norm_biases,
    expert_up,
    expert_down,
):
    rows, width = tokens.shape[1], tokens.shape[2]
    ctx_count = lax.axis_size("ctx")
    two = lax.axis_size("dp")
    team = math.gcd(4, ctx_count)
    groups = ctx_count // team
    sizes = (two, groups, team)
    team_heads = HEADS // team
    reps = groups // team_heads
    length = rows * ctx_count
    group_rows = rows * team
    experts = ctx_count * expert_up.shape[0]
    capacity = max(2, 2 * rows // experts)
    block_rows = length // block_order.shape[0]
    hidden = w_up.shape[1]
    hidden_dev = w_down.shape[0]
    wr = w_qkv.shape[0]
    qkv_cols = 3 * width // team
    up_cols = hidden // team
    core = lax.axis_index("dp")
    ctx = lax.axis_index("ctx")
    group, member = lax.div(ctx, team), lax.rem(ctx, team)
    team_steps = [(0, 0, k) for k in range(1, team)]
    group_steps = [(0, k, 0) for k in range(1, groups)]
    by_group = [[g * team + t for g in range(groups)] for t in range(team)]
    by_team = [[g * team + t for t in range(team)] for g in range(groups)]
    swap = [(d, (d + 1) % two) for d in range(two)]

    small_flat = jnp.concatenate(
        [router.reshape(-1), norm_gains.reshape(-1), norm_biases.reshape(-1)]
    )
    small_size = -(-small_flat.shape[0] // 2048) * 2048
    small = jnp.pad(small_flat, (0, small_size - small_flat.shape[0])).astype(BF)
    small = small.reshape(-1, 128)

    heads_first = (
        w_qkv.reshape(wr, 3, team, team_heads, HEAD_DIM)
        .transpose(2, 0, 3, 1, 4)
        .reshape(team, wr, qkv_cols)
        .astype(BF)
    )
    up_first = (
        w_up.reshape(wr, two * groups, team, hidden_dev)
        .transpose(2, 0, 1, 3)
        .reshape(team, wr, up_cols)
        .astype(BF)
    )
    heads_first, up_first = tall(heads_first), tall(up_first)
    route_row = jnp.broadcast_to(routes[0, :, 0][None, :], (8, rows))

    def first(coords, ins, outs):
        c, g, t = coords
        moves, local = [], []
        for s in team_steps:
            to = lax.rem(t + s[2], team)
            moves.append(Move(s, ins[0], outs[0].at[t]))
            moves.append(Move(s, ins[1].at[to], outs[1].at[t]))
            moves.append(Move(s, ins[3], outs[3].at[t]))
            moves.append(Move(s, ins[4], outs[4].at[t]))
            moves.append(Move(s, ins[2].at[to], outs[2].at[t]))
        local.append((ins[0], outs[0].at[t]))
        local.append((ins[1].at[t], outs[1].at[t]))
        local.append((ins[2].at[t], outs[2].at[t]))
        local.append((ins[3], outs[3].at[t]))
        local.append((ins[4], outs[4].at[t]))
        return local, moves

    token_rows, qkv_part, up_part, small_part, route_all = exchange(
        "first",
        1,
        sizes,
        (tokens[0], heads_first, up_first, small, route_row),
        [
            ((team, rows, width), BF),
            (heads_first.shape, BF),
            (up_first.shape, BF),
            ((team,) + small.shape, BF),
            ((team, 8, rows), jnp.int32),
        ],
        first,
    )

    def second_build(coords, ins, outs):
        c, g, t = coords
        moves, local = [], []
        for k, s in enumerate(group_steps):
            moves.append(Move(s, ins[0], outs[0].at[c, g]))
            moves.append(Move(s, ins[1], outs[1].at[c, g]))
        for s in team_steps:
            moves.append(Move(s, ins[2], outs[2].at[t]))
        local.append((ins[0], outs[0].at[c, g]))
        local.append((ins[1], outs[1].at[c, g]))
        local.append((ins[2], outs[2].at[t]))
        other = (1, 0, 0)
        for n in range(2):
            moves.append(Move(other, outs[n].at[c, g], outs[n].at[c, g], after=("local", n)))
        for k, s in enumerate(group_steps):
            source = lax.rem(g + groups - s[1], groups)
            for n in range(2):
                moves.append(
                    Move(other, outs[n].at[c, source], outs[n].at[c, source], after=2 * k + n)
                )
        return local, moves

    qkv_all, small_all, cot_rows = exchange(
        "second",
        2,
        sizes,
        (qkv_part, small_part, cotangent[0]),
        [
            ((two, groups) + qkv_part.shape, BF),
            ((two, groups) + small_part.shape, BF),
            ((team, rows, width), BF),
        ],
        second_build,
    )
    qkv_weight = qkv_all.reshape(width, qkv_cols)
    small_rows = small_all.reshape(two * ctx_count, -1)
    router_cols = router.shape[1]
    router_weight = small_rows[:, : wr * router_cols].reshape(width, router_cols)
    vectors = small_rows[:, wr * router_cols : small_flat.shape[0]].reshape(
        two * ctx_count, 4, wr
    )
    vectors = vectors.transpose(1, 0, 2).reshape(4, width).astype(F32)
    gains, shifts = vectors[:2], vectors[2:]

    ff_part = jnp.concatenate(
        [up_part.reshape(team * wr, up_cols), w_down.astype(BF).reshape(team * wr, -1)], axis=1
    )
    ff_half = lax.all_gather(ff_part, "ctx", axis=0, tiled=False, axis_index_groups=by_group)
    out_half = lax.all_gather(w_out.astype(BF), "ctx", axis=0, tiled=True)

    def both(half):
        other = lax.ppermute(half, "dp", swap)
        return jnp.where(core == 0, jnp.stack([half, other]), jnp.stack([other, half]))

    out_weight = both(out_half).reshape(width, width)
    up_weight = both(ff_half[:, :, :up_cols]).reshape(width, up_cols)
    down_weight = both(ff_half[:, :, up_cols:]).reshape(up_cols, width)

    doc_id = jnp.arange(doc_lengths.shape[1], dtype=jnp.int32)
    doc_ends = jnp.sum(
        jnp.where(doc_id[:, None] <= doc_id[None, :], doc_lengths[0][:, None], 0), axis=0
    )
    all_rows = jnp.arange(length, dtype=jnp.int32)
    marks = (all_rows // block_rows)[:, None] == jnp.arange(
        block_order.shape[0], dtype=jnp.int32
    )[None, :]
    anchor = jnp.sum(jnp.where(marks, block_order[None, :], 0), axis=1)
    all_place = anchor * block_rows + all_rows % block_rows

    def low_of(place):
        return jnp.max(
            jnp.where(doc_ends[None, :] <= place[:, None], doc_ends[None, :], 0), axis=1
        )

    sorted_rows = reps == 1
    query_length = length // reps
    tiles = query_length // TILE
    if sorted_rows:
        query_place = all_rows
        order = (all_place[:, None] == all_rows[None, :]).astype(BF)
        lows = low_of(all_rows)
        start = lows[::TILE] // TILE
        bounds = jnp.stack([start, jnp.arange(1, tiles + 1, dtype=jnp.int32)], axis=1)
    else:
        part = lax.rem(group, reps)
        query_place = lax.dynamic_slice(all_place, (part * query_length,), (query_length,))
        lows = low_of(query_place)
        bounds = jnp.broadcast_to(
            jnp.array([[0, length // TILE]], dtype=jnp.int32), (tiles, 2)
        )
    meta = jnp.concatenate(
        [query_place[None], lows[None], jnp.zeros((6, query_length), jnp.int32)], axis=0
    )
    place_col = all_place[:, None] if not sorted_rows else jnp.zeros((8, 128), jnp.int32)

    def core_half(term):
        halves = term.reshape((two, term.shape[0] // two) + term.shape[1:])
        keep = lax.dynamic_index_in_dim(halves, core, 0, keepdims=False)
        give = lax.dynamic_index_in_dim(halves, 1 - core, 0, keepdims=False)
        return keep + lax.ppermute(give.astype(BF), "dp", swap).astype(F32)

    def over_groups(term):
        return lax.psum_scatter(
            term,
            "ctx",
            scatter_dimension=0,
            tiled=True,
            axis_index_groups=by_group,
        )

    token_rows = token_rows.reshape(group_rows, width)
    inputs = token_rows.astype(F32)
    normed_low = layer_norm(inputs, gains[0], shifts[0]).astype(BF)
    mixed_t = lax.dot_general(
        qkv_weight, normed_low, (((0,), (1,)), ((), ())), preferred_element_type=F32
    ).astype(BF)
    mixed_t = mixed_t.reshape(team_heads, 3 * HEAD_DIM, group_rows)

    def spread_heads(coords, ins, outs):
        c, g, t = coords
        moves = [
            Move(s, ins[0].at[lax.div(lax.rem(g + s[1], groups), reps)], outs[0].at[g])
            for s in group_steps
        ]
        return [(ins[0].at[lax.div(g, reps)], outs[0].at[g])], moves

    [head_parts] = exchange(
        "heads",
        3,
        sizes,
        (mixed_t,),
        [((groups, 3 * HEAD_DIM, group_rows), BF)],
        spread_heads,
    )
    head_t = head_parts.transpose(1, 0, 2).reshape(3 * HEAD_DIM, length)
    zeros = jnp.zeros((HEAD_DIM, query_length), BF)
    if sorted_rows:
        sorted_t = dot_f32(head_t, order).astype(BF)
        kv_rows = lax.dot_general(
            order, head_t[HEAD_DIM:], (((0,), (1,)), ((), ())), preferred_element_type=F32
        ).astype(BF)
        kv_t = sorted_t[HEAD_DIM:]
        q_t = sorted_t[:HEAD_DIM]
    else:
        kv_t = head_t[HEAD_DIM:]
        kv_rows = kv_t.T
        q_t = lax.dynamic_slice(
            head_t[:HEAD_DIM], (0, part * query_length), (HEAD_DIM, query_length)
        )
    q_pad = jnp.concatenate([q_t * jnp.asarray(SCALE, BF), zeros], axis=0)
    attention_t, log_total = attend(sorted_rows, bounds, meta, place_col, q_pad, kv_rows, kv_t)
    low_t = attention_t.astype(BF)
    if sorted_rows:
        low_t = contract_cols(low_t, order).astype(BF)
    else:
        low_t = lax.dynamic_update_slice(
            jnp.zeros((HEAD_DIM, length), BF), low_t, (0, part * query_length)
        )
    low_t = low_t.reshape(HEAD_DIM, groups, group_rows).transpose(1, 0, 2)

    def gather_heads(coords, ins, outs):
        c, g, t = coords
        moves = [
            Move(s, ins[0].at[lax.rem(g + s[1], groups)], outs[0].at[t, g]) for s in group_steps
        ]
        local = [(ins[0].at[g], outs[0].at[t, g])]
        for s in team_steps:
            moves.append(Move(s, outs[0].at[t, g], outs[0].at[t, g], after=("local", 0)))
        for k, s in enumerate(group_steps):
            source = lax.rem(g + groups - s[1], groups)
            for e in team_steps:
                moves.append(Move(e, outs[0].at[t, source], outs[0].at[t, source], after=k))
        return local, moves

    [attended] = exchange(
        "attended",
        4,
        sizes,
        (low_t,),
        [((team, groups, HEAD_DIM, group_rows), BF)],
        gather_heads,
    )
    if reps > 1:
        attended = lax.dynamic_index_in_dim(
            attended.reshape(team, team_heads, reps, HEAD_DIM, group_rows),
            lax.div(group, groups // reps),
            2,
            keepdims=False,
        )
    attended_t = attended.reshape(width, group_rows)

    middle = inputs + contract_rows(attended_t, out_weight)
    second_low = layer_norm(middle, gains[1], shifts[1]).astype(BF)
    router_logits = dot_f32(second_low, router_weight)
    route = route_all[:, 0, :]
    earlier = jnp.arange(rows)[None, :] < jnp.arange(rows)[:, None]
    same = (route[:, :, None] == route[:, None, :]) & earlier[None]
    rank = jnp.sum(same.astype(jnp.int32), axis=2)
    route_flat = route.reshape(group_rows)
    route_hot = (route_flat[:, None] == jnp.arange(experts, dtype=jnp.int32)[None, :]).astype(F32)
    gate, mix_dense, mix_expert = router_heads(router_logits, route_hot, experts)
    scaled_gate = mix_expert * gate
    out_grad = cot_rows.reshape(group_rows, width).astype(F32)
    dense_grad = (out_grad * mix_dense[:, None]).astype(BF)
    expert_grad = (out_grad * scaled_gate[:, None]).astype(BF)
    slots = team * capacity
    slot = (jnp.arange(team, dtype=jnp.int32)[:, None] * capacity + rank).reshape(group_rows)
    target = jnp.where(
        route_flat % team == member, (route_flat // team) * slots + slot, groups * slots
    )
    select = (
        jnp.arange(groups * slots, dtype=jnp.int32)[:, None] == target[None, :]
    ).astype(BF)
    send_s = dot_f32(select, second_low).astype(BF).reshape(groups, slots, width)
    send_g = dot_f32(select, expert_grad).astype(BF).reshape(groups, slots, width)
    mixes = jnp.pad(jnp.stack([mix_dense, scaled_gate], axis=1), ((0, 0), (0, 126)))
    layer_sum, second_sum, sums_own, expert_up_grad, expert_down_grad, down_half, up_half = (
        feed_forward(
            sizes,
            rows,
            send_s,
            send_g,
            expert_up[0],
            expert_down[0],
            second_low,
            dense_grad,
            up_weight,
            down_weight,
            select.T,
            cot_rows.reshape(group_rows, width),
            mixes,
        )
    )
    down_sum = over_groups(down_half).astype(F32)
    up_sum = over_groups(up_half).reshape(team, wr, up_cols)

    def own(array):
        return lax.dynamic_slice_in_dim(array, member * rows, rows, axis=0)

    middle_own, logits_own, hot_own, second_own = (
        own(middle),
        own(router_logits),
        own(route_hot),
        own(second_low),
    )
    out_grad_own = cotangent[0].astype(F32)
    layer_out = middle_own + layer_sum
    (gate_own, mix_dense_own, mix_expert_own), router_pull = jax.vjp(
        lambda values: router_heads(values, hot_own, experts), logits_own
    )
    logit_grad = router_pull(
        (sums_own[:, 1] * mix_expert_own, sums_own[:, 0], sums_own[:, 1] * gate_own)
    )[0].astype(BF)
    router_term = contract_rows(second_own, logit_grad)
    second_grad = second_sum + contract_cols(logit_grad, router_weight)
    middle_part, gain_second, bias_second = jax.vjp(layer_norm, middle_own, gains[1], shifts[1])[1](
        second_grad
    )
    middle_grad = out_grad_own + middle_part
    branch_grad = middle_grad.astype(BF)
    attended_own = lax.dynamic_slice_in_dim(attended_t, member * rows, rows, axis=1)
    out_term = dot_f32(attended_own, branch_grad)
    flow_t = contract_cols(out_weight, branch_grad).astype(BF)
    flow_t = flow_t.reshape(team, team_heads, HEAD_DIM, rows)

    def spread_flow(coords, ins, outs):
        c, g, t = coords
        moves = []
        for dg in range(groups):
            for dt in range(team):
                if dg or dt:
                    to_g, to_t = lax.rem(g + dg, groups), lax.rem(t + dt, team)
                    moves.append(
                        Move((0, dg, dt), ins[0].at[to_t, lax.div(to_g, reps)], outs[0].at[g, t])
                    )
        return [(ins[0].at[t, lax.div(g, reps)], outs[0].at[g, t])], moves

    [flow_parts] = exchange(
        "flow", 8, sizes, (flow_t,), [((groups, team, HEAD_DIM, rows), BF)], spread_flow
    )
    flow_all = flow_parts.transpose(2, 0, 1, 3).reshape(HEAD_DIM, length)
    if sorted_rows:
        flow_all = dot_f32(flow_all, order).astype(BF)
    else:
        flow_all = lax.dynamic_slice(
            flow_all, (0, part * query_length), (HEAD_DIM, query_length)
        )
    do_pad = jnp.concatenate([zeros, flow_all], axis=0)
    query_grad, pair_grad = attend_back(
        sorted_rows,
        bounds,
        meta,
        place_col,
        q_pad,
        do_pad,
        attention_t,
        log_total,
        kv_rows,
        kv_t,
    )
    if not sorted_rows:
        query_grad = lax.dynamic_update_slice(
            jnp.zeros((HEAD_DIM, length), BF), query_grad, (0, part * query_length)
        )
    grad_t = jnp.concatenate([query_grad, pair_grad], axis=0)
    if sorted_rows:
        grad_t = contract_cols(grad_t, order).astype(BF)
    grad_t = grad_t.reshape(3 * HEAD_DIM, groups, group_rows).transpose(1, 0, 2)
    out_parts = tall(
        core_half(out_term)
        .astype(BF)
        .reshape(groups, team, wr, width)
        .transpose(1, 0, 2, 3)
        .reshape(team, groups * wr, width)
    )

    def mixed_build(coords, ins, outs):
        c, g, t = coords
        moves = [
            Move(s, ins[0].at[lax.rem(g + s[1], groups)], outs[0].at[g]) for s in group_steps
        ]
        moves += [
            Move(s, ins[1].at[lax.rem(t + s[2], team)], outs[1].at[t]) for s in team_steps
        ]
        return [(ins[0].at[g], outs[0].at[g]), (ins[1].at[t], outs[1].at[t])], moves

    grad_parts, out_parts = exchange(
        "mixed",
        9,
        sizes,
        (grad_t, out_parts),
        [(grad_t.shape, BF), (out_parts.shape, BF)],
        mixed_build,
    )
    out_parts = tall(
        jnp.sum(out_parts.astype(F32), axis=0).astype(BF).reshape(groups, wr, width)
    )
    if reps > 1:
        grad_parts = jnp.sum(
            grad_parts.reshape(team_heads, reps, 3 * HEAD_DIM, group_rows).astype(F32), axis=1
        ).astype(BF)
    mixed_grad_t = grad_parts.reshape(qkv_cols, group_rows)
    normed_part = (
        lax.dot_general(
            mixed_grad_t, qkv_weight, (((0,), (1,)), ((), ())), preferred_element_type=F32
        )
        .astype(BF)
        .reshape(team, rows, width)
    )
    qkv_term = lax.dot_general(
        normed_low, mixed_grad_t, (((0,), (1,)), ((), ())), preferred_element_type=F32
    )
    qkv_parts = core_half(qkv_term).astype(BF).reshape(groups, team * wr, qkv_cols)

    def normed_build(coords, ins, outs):
        c, g, t = coords
        moves, local = [], [(ins[2].at[t], outs[2].at[t])]
        for n in range(2):
            for s in group_steps:
                moves.append(Move(s, ins[n].at[lax.rem(g + s[1], groups)], outs[n].at[g]))
            local.append((ins[n].at[g], outs[n].at[g]))
        for s in team_steps:
            moves.append(Move(s, ins[2].at[lax.rem(t + s[2], team)], outs[2].at[t]))
        return local, moves

    qkv_parts, out_parts, normed_own = exchange(
        "normed",
        10,
        sizes,
        (qkv_parts, out_parts, normed_part),
        [(qkv_parts.shape, BF), (out_parts.shape, BF), (normed_part.shape, BF)],
        normed_build,
    )
    qkv_sum = (
        jnp.sum(qkv_parts.astype(F32), axis=0).astype(BF).reshape(team, wr, qkv_cols)
    )
    out_sum = jnp.sum(out_parts.astype(F32), axis=0).reshape(wr, width)
    normed_grad = jnp.sum(normed_own.astype(F32), axis=0)
    input_part_grad, gain_first, bias_first = jax.vjp(
        layer_norm, tokens[0].astype(F32), gains[0], shifts[0]
    )[1](normed_grad)
    input_grad = middle_grad + input_part_grad

    small_term = jnp.concatenate(
        [
            router_term,
            gain_first[:, None],
            gain_second[:, None],
            bias_first[:, None],
            bias_second[:, None],
        ],
        axis=1,
    )
    small_cols = wr * small_term.shape[1]
    small_pad = -(-small_cols // 1024) * 1024
    small_parts = jnp.pad(
        small_term.reshape(two * ctx_count, small_cols), ((0, 0), (0, small_pad - small_cols))
    ).reshape(two * ctx_count, small_pad // 128, 128)

    def owners_build(coords, ins, outs):
        c, g, t = coords
        moves, local = [], []
        for n in range(2):
            for s in team_steps:
                moves.append(Move(s, ins[n].at[lax.rem(t + s[2], team)], outs[n].at[t]))
            local.append((ins[n].at[t], outs[n].at[t]))
        me = c * ctx_count + g * team + t
        for dc in range(two):
            for dg in range(groups):
                for dt in range(team):
                    if dc or dg or dt:
                        to = (
                            lax.rem(c + dc, two) * ctx_count
                            + lax.rem(g + dg, groups) * team
                            + lax.rem(t + dt, team)
                        )
                        moves.append(Move((dc, dg, dt), ins[2].at[to], outs[2].at[me]))
        local.append((ins[2].at[me], outs[2].at[me]))
        return local, moves

    up_own, qkv_own, small_own = exchange(
        "owners",
        11,
        sizes,
        (tall(up_sum), tall(qkv_sum), small_parts),
        [
            (tall(up_sum).shape, BF),
            (tall(qkv_sum).shape, BF),
            (small_parts.shape, F32),
        ],
        owners_build,
    )
    small_sum = (
        jnp.sum(small_own, axis=0).reshape(-1)[:small_cols].reshape(wr, small_term.shape[1])
    )
    up_own = (
        up_own.reshape(team, wr, two * groups, hidden_dev)
        .transpose(1, 2, 0, 3)
        .reshape(wr, hidden)
        .astype(F32)
    )
    qkv_own = (
        qkv_own.reshape(team, wr, team_heads, 3, HEAD_DIM)
        .transpose(1, 3, 0, 2, 4)
        .reshape(wr, 3 * width)
        .astype(F32)
    )
    vector_sums = small_sum[:, router_cols:].T
    return (
        layer_out[None].astype(BF),
        input_grad[None].astype(BF),
        qkv_own,
        out_sum,
        up_own,
        down_sum,
        small_sum[:, :router_cols],
        vector_sums[:2],
        vector_sums[2:],
        expert_up_grad[None],
        expert_down_grad[None],
    )


def solution(mesh):
    in_specs = (
        P("dp", "ctx", None),
        P("dp", "ctx", None),
        P(),
        P("dp", None),
        P("dp", "ctx", None),
        P(("dp", "ctx"), None),
        P(("dp", "ctx"), None),
        P(("dp", "ctx"), None),
        P(("dp", "ctx"), None),
        P(("dp", "ctx"), None),
        P(None, ("dp", "ctx")),
        P(None, ("dp", "ctx")),
        P("ctx", None, "dp"),
        P("ctx", "dp", None),
    )
    out_specs = (
        P("dp", "ctx", None),
        P("dp", "ctx", None),
        P(("dp", "ctx"), None),
        P(("dp", "ctx"), None),
        P(("dp", "ctx"), None),
        P(("dp", "ctx"), None),
        P(("dp", "ctx"), None),
        P(None, ("dp", "ctx")),
        P(None, ("dp", "ctx")),
        P("ctx", None, "dp"),
        P("ctx", "dp", None),
    )
    return jax.shard_map(
        per_device, mesh=mesh, in_specs=in_specs, out_specs=out_specs, check_vma=False
    )
```

```python
import functools
import math

import jax
import jax.numpy as jnp
from jax import lax
from jax.experimental import pallas as pl
from jax.experimental.pallas import tpu as pltpu
from jax.sharding import PartitionSpec as P

HEADS = 16
HEAD_DIM = 64

EPS = 1e-05
NEG = -1e30
SCALE = 0.125
TILE = 256
BF = jnp.bfloat16
F32 = jnp.float32
MESH = pl.DeviceIdType.MESH


def layer_norm(values, gain, shift):
    center = values - jnp.mean(values, axis=-1, keepdims=True)
    spread = jnp.mean(center * center, axis=-1, keepdims=True)
    return center * lax.rsqrt(spread + EPS) * gain + shift


def gelu_tanh(values):
    return jax.nn.gelu(values, approximate=True)


def router_heads(router_logits, route_hot, experts):
    chances = jax.nn.softmax(router_logits[:, :experts], axis=-1)
    gate = jnp.sum(chances * route_hot, axis=-1)
    mixing = jax.nn.softmax(router_logits[:, experts:], axis=-1)
    return (gate, mixing[:, 0], mixing[:, 1])


def dot_f32(left, right):
    return jnp.dot(left, right, preferred_element_type=F32)


def contract_rows(left, right):
    return lax.dot_general(left, right, (((0,), (0,)), ((), ())), preferred_element_type=F32)


def contract_cols(left, right):
    return lax.dot_general(left, right, (((1,), (1,)), ((), ())), preferred_element_type=F32)


def span(i, size):
    return pl.ds(pl.multiple_of(i * size, size), size)


class Move:
    def __init__(self, step, src, dst, after=None):
        self.step, self.src, self.dst, self.after = step, src, dst, after


def exchange(name, cid, sizes, ins, outs, build, micros=20):
    two, groups, team = sizes

    def kernel(*refs):
        in_refs, out_refs = refs[: len(ins)], refs[len(ins) : len(ins) + len(outs)]
        send_sem, recv_sem, local_sem = refs[len(ins) + len(outs) :]
        c = lax.axis_index("dp")
        i = lax.axis_index("ctx")
        g, t = lax.div(i, team), lax.rem(i, team)

        def device(step):
            dc, dg, dt = step
            return (
                lax.rem(c + dc, two),
                lax.rem(g + dg, groups) * team + lax.rem(t + dt, team),
            )

        locals_, moves = build((c, g, t), in_refs, out_refs)
        steps = sorted({m.step for m in moves})
        greet = sorted(
            set(steps) | {((-a) % two, (-b) % groups, (-d) % team) for a, b, d in steps}
        )
        barrier = pltpu.get_barrier_semaphore()
        for step in greet:
            pl.semaphore_signal(barrier, inc=1, device_id=device(step), device_id_type=MESH)
        pl.semaphore_wait(barrier, len(greet))

        copies = {}
        arrived = set()
        for k, (src, dst) in enumerate(locals_):
            copies[("local", k)] = pltpu.make_async_copy(src, dst, local_sem.at[k])
        for k, m in enumerate(moves):
            copies[k] = pltpu.make_async_remote_copy(
                src_ref=m.src,
                dst_ref=m.dst,
                send_sem=send_sem.at[k],
                recv_sem=recv_sem.at[k],
                device_id=device(m.step),
                device_id_type=MESH,
            )
        for k, m in enumerate(moves):
            if m.after is None:
                copies[k].start()
        for k in range(len(locals_)):
            copies[("local", k)].start()
        for k, m in enumerate(moves):
            if m.after is not None:
                if m.after not in arrived:
                    arrived.add(m.after)
                    if isinstance(m.after, tuple):
                        copies[m.after].wait()
                    else:
                        copies[m.after].wait_recv()
                copies[k].start()
        for k in range(len(locals_)):
            if ("local", k) not in arrived:
                copies[("local", k)].wait()
        for k in range(len(moves)):
            if k not in arrived:
                copies[k].wait_recv()
        for k in range(len(moves)):
            copies[k].wait_send()

    count = []

    def trace_counts():
        class Probe:
            def __getattr__(self, name):
                return self

            def __getitem__(self, index):
                return self

        locals_, moves = build((0, 0, 0), [Probe() for _ in ins], [Probe() for _ in outs])
        count.extend((len(locals_), len(moves)))

    trace_counts()
    return pl.pallas_call(
        kernel,
        name=name,
        out_shape=tuple(jax.ShapeDtypeStruct(s, d) for s, d in outs),
        in_specs=[pl.BlockSpec(memory_space=pl.ANY)] * len(ins),
        out_specs=tuple(pl.BlockSpec(memory_space=pl.ANY) for _ in outs),
        scratch_shapes=[
            pltpu.SemaphoreType.DMA((max(1, count[1]),)),
            pltpu.SemaphoreType.DMA((max(1, count[1]),)),
            pltpu.SemaphoreType.DMA((max(1, count[0]),)),
        ],
        compiler_params=pltpu.CompilerParams(collective_id=cid, has_side_effects=True),
        cost_estimate=pl.CostEstimate(
            flops=0, bytes_accessed=int(micros * 3.0e6), transcendentals=0
        ),
    )(*ins)


def mask_of(kt, key_place, query_place, query_low):
    return (key_place <= query_place) & (key_place >= query_low)


def key_places(sorted_rows, kt, place_ref):
    if sorted_rows:
        return lax.broadcasted_iota(jnp.int32, (TILE, TILE), 0) + kt * TILE
    return place_ref[pl.ds(pl.multiple_of(kt * TILE, TILE), TILE), :]


def attend_kernel(
    sorted_rows, bounds, meta_ref, place_ref, q_ref, rows_ref, kvt_ref, out_ref, lse_ref
):
    step = pl.program_id(0)
    queries = q_ref[...]
    place, low = meta_ref[0:1, :], meta_ref[1:2, :]

    def body(kt, carry):
        peak, total, acc = carry
        at = pl.ds(pl.multiple_of(kt * TILE, TILE), TILE)
        scores = dot_f32(rows_ref[at, :], queries)
        allowed = mask_of(kt, key_places(sorted_rows, kt, place_ref), place, low)
        scores = jnp.where(allowed, scores, NEG)
        new_peak = jnp.maximum(peak, jnp.max(scores, axis=0, keepdims=True))
        weights = jnp.exp(scores - new_peak)
        fade = jnp.exp(peak - new_peak)
        total = total * fade + jnp.sum(weights, axis=0, keepdims=True)
        acc = acc * fade + dot_f32(kvt_ref[HEAD_DIM:, at], weights.astype(BF))
        return new_peak, total, acc

    start = (
        jnp.full((1, TILE), NEG, F32),
        jnp.zeros((1, TILE), F32),
        jnp.zeros((HEAD_DIM, TILE), F32),
    )
    peak, total, acc = lax.fori_loop(bounds[step, 0], bounds[step, 1], body, start)
    out_ref[...] = acc / total
    lse_ref[...] = peak + jnp.log(total)


def attend_back_kernel(
    sorted_rows,
    tiles,
    bounds,
    meta_ref,
    place_ref,
    q_ref,
    do_ref,
    out_ref,
    lse_ref,
    rows_ref,
    kvt_ref,
    dq_ref,
    dkv_ref,
    acc_ref,
):
    step = pl.program_id(0)

    @pl.when(step == 0)
    def _():
        acc_ref[...] = jnp.zeros_like(acc_ref)

    queries, flows = q_ref[...], do_ref[...]
    place, low = meta_ref[0:1, :], meta_ref[1:2, :]
    log_total = lse_ref[...]
    delta = jnp.sum(flows[HEAD_DIM:, :].astype(F32) * out_ref[...], axis=0, keepdims=True)

    def body(kt, dq):
        at = pl.ds(pl.multiple_of(kt * TILE, TILE), TILE)
        rows = rows_ref[at, :]
        scores = dot_f32(rows, queries)
        allowed = mask_of(kt, key_places(sorted_rows, kt, place_ref), place, low)
        chances = jnp.exp(jnp.where(allowed, scores - log_total, NEG))
        flow = dot_f32(rows, flows)
        score_grad = (chances * (flow - delta)).astype(BF)
        dq = dq + dot_f32(kvt_ref[:HEAD_DIM, at], score_grad)
        acc_ref[:HEAD_DIM, at] += contract_cols(queries[:HEAD_DIM, :], score_grad)
        acc_ref[HEAD_DIM:, at] += contract_cols(flows[HEAD_DIM:, :], chances.astype(BF))
        return dq

    dq = lax.fori_loop(
        bounds[step, 0], bounds[step, 1], body, jnp.zeros((HEAD_DIM, TILE), F32)
    )
    dq_ref[...] = (dq * SCALE).astype(BF)

    @pl.when(step == tiles - 1)
    def _():
        dkv_ref[...] = acc_ref[...].astype(BF)


def attention_specs(length, query_length):
    def whole(shape):
        return pl.BlockSpec(shape, lambda i: (0, 0))

    def tile(rows):
        return pl.BlockSpec((rows, TILE), lambda i: (0, i))

    return whole, tile


def attend(sorted_rows, bounds, meta, place_col, q_pad, kv_rows, kv_t):
    length, query_length = kv_rows.shape[0], q_pad.shape[1]
    whole, tile = attention_specs(length, query_length)
    return pl.pallas_call(
        functools.partial(attend_kernel, sorted_rows),
        name="attend",
        grid=(query_length // TILE,),
        in_specs=[
            pl.BlockSpec(memory_space=pltpu.SMEM),
            tile(8),
            whole(place_col.shape),
            tile(2 * HEAD_DIM),
            whole((length, 2 * HEAD_DIM)),
            whole((2 * HEAD_DIM, length)),
        ],
        out_specs=(tile(HEAD_DIM), tile(1)),
        out_shape=(
            jax.ShapeDtypeStruct((HEAD_DIM, query_length), F32),
            jax.ShapeDtypeStruct((1, query_length), F32),
        ),
        compiler_params=pltpu.CompilerParams(vmem_limit_bytes=40 * 2**20),
    )(bounds, meta, place_col, q_pad, kv_rows, kv_t)


def attend_back(sorted_rows, bounds, meta, place_col, q_pad, do_pad, out, lse, kv_rows, kv_t):
    length, query_length = kv_rows.shape[0], q_pad.shape[1]
    whole, tile = attention_specs(length, query_length)
    return pl.pallas_call(
        functools.partial(attend_back_kernel, sorted_rows, query_length // TILE),
        name="attend_back",
        grid=(query_length // TILE,),
        in_specs=[
            pl.BlockSpec(memory_space=pltpu.SMEM),
            tile(8),
            whole(place_col.shape),
            tile(2 * HEAD_DIM),
            tile(2 * HEAD_DIM),
            tile(HEAD_DIM),
            tile(1),
            whole((length, 2 * HEAD_DIM)),
            whole((2 * HEAD_DIM, length)),
        ],
        out_specs=(tile(HEAD_DIM), whole((2 * HEAD_DIM, length))),
        out_shape=(
            jax.ShapeDtypeStruct((HEAD_DIM, query_length), BF),
            jax.ShapeDtypeStruct((2 * HEAD_DIM, length), BF),
        ),
        scratch_shapes=[pltpu.VMEM((2 * HEAD_DIM, length), F32)],
        compiler_params=pltpu.CompilerParams(vmem_limit_bytes=40 * 2**20),
    )(bounds, meta, place_col, q_pad, do_pad, out, lse, kv_rows, kv_t)


BLOCK = 64


def pick_pair(load, table, d):
    first, second = table[2 * d], table[2 * d + 1]
    left = load(lax.div(first, 2))
    right = load(lax.div(second, 2))
    lane = lax.broadcasted_iota(jnp.int32, left.shape, 1)
    left = jnp.where(lax.rem(first, 2) == 0, left, pltpu.roll(left, BLOCK, 1))
    right = jnp.where(lax.rem(second, 2) == 1, right, pltpu.roll(right, BLOCK, 1))
    return jnp.where(lane < BLOCK, left, right)


def column_block(ref, k, per):
    return ref[lax.div(k, per), :, span(lax.rem(k, per), 128)].astype(F32)


def sorted_attend_kernel(
    bounds, inverse, order, meta_ref, parts_ref,
    low_ref, out_ref, lse_ref, q_ref, kvt_ref, rows_ref,
):
    step = pl.program_id(0)
    length = q_ref.shape[1]
    per = parts_ref.shape[2] // 128

    @pl.when(step == 0)
    def _():
        def place(d, carry):
            tile = pick_pair(lambda k: column_block(parts_ref, k, per), inverse, d)
            at = span(d, 128)
            q_ref[:HEAD_DIM, at] = (tile[:HEAD_DIM] * SCALE).astype(BF)
            q_ref[HEAD_DIM:, at] = jnp.zeros((HEAD_DIM, 128), BF)
            kvt_ref[:, at] = tile[HEAD_DIM:].astype(BF)
            rows_ref[at, :] = tile[HEAD_DIM:].T.astype(BF)
            return carry

        lax.fori_loop(0, length // 128, place, 0)

    here = span(step, TILE)
    queries = q_ref[:, here]
    place, low = meta_ref[0:1, :], meta_ref[1:2, :]

    def body(kt, carry):
        peak, total, acc = carry
        at = span(kt, TILE)
        scores = dot_f32(rows_ref[at, :], queries)
        allowed = mask_of(kt, key_places(True, kt, None), place, low)
        scores = jnp.where(allowed, scores, NEG)
        new_peak = jnp.maximum(peak, jnp.max(scores, axis=0, keepdims=True))
        weights = jnp.exp(scores - new_peak)
        fade = jnp.exp(peak - new_peak)
        total = total * fade + jnp.sum(weights, axis=0, keepdims=True)
        acc = acc * fade + dot_f32(kvt_ref[HEAD_DIM:, at], weights.astype(BF))
        return new_peak, total, acc

    start = (
        jnp.full((1, TILE), NEG, F32),
        jnp.zeros((1, TILE), F32),
        jnp.zeros((HEAD_DIM, TILE), F32),
    )
    peak, total, acc = lax.fori_loop(bounds[step, 0], bounds[step, 1], body, start)
    out_ref[:, here] = acc / total
    lse_ref[:, here] = peak + jnp.log(total)

    @pl.when(step == length // TILE - 1)
    def _():
        def home(d, carry):
            tile = pick_pair(lambda k: out_ref[:, span(k, 128)], order, d)
            low_ref[lax.div(d, per), :, span(lax.rem(d, per), 128)] = tile.astype(BF)
            return carry

        lax.fori_loop(0, length // 128, home, 0)


def sorted_back_kernel(
    bounds, inverse, order, meta_ref, flow_ref, out_ref, lse_ref, q_ref, kvt_ref, rows_ref,
    grad_ref, do_ref, dq_ref, acc_ref,
):
    step = pl.program_id(0)
    length = q_ref.shape[1]
    per = grad_ref.shape[3] // 128

    @pl.when(step == 0)
    def _():
        acc_ref[...] = jnp.zeros_like(acc_ref)

        def place(d, carry):
            tile = pick_pair(lambda k: flow_ref[k].astype(F32), inverse, d)
            at = span(d, 128)
            do_ref[:HEAD_DIM, at] = jnp.zeros((HEAD_DIM, 128), BF)
            do_ref[HEAD_DIM:, at] = tile.astype(BF)
            return carry

        lax.fori_loop(0, length // 128, place, 0)

    here = span(step, TILE)
    queries, flows = q_ref[:, here], do_ref[:, here]
    place, low = meta_ref[0:1, :], meta_ref[1:2, :]
    log_total = lse_ref[:, here]
    delta = jnp.sum(flows[HEAD_DIM:, :].astype(F32) * out_ref[:, here], axis=0, keepdims=True)

    def body(kt, dq):
        at = span(kt, TILE)
        rows = rows_ref[at, :]
        scores = dot_f32(rows, queries)
        allowed = mask_of(kt, key_places(True, kt, None), place, low)
        chances = jnp.exp(jnp.where(allowed, scores - log_total, NEG))
        flow = dot_f32(rows, flows)
        score_grad = (chances * (flow - delta)).astype(BF)
        dq = dq + dot_f32(kvt_ref[:HEAD_DIM, at], score_grad)
        acc_ref[:HEAD_DIM, at] += contract_cols(queries[:HEAD_DIM, :], score_grad)
        acc_ref[HEAD_DIM:, at] += contract_cols(flows[HEAD_DIM:, :], chances.astype(BF))
        return dq

    dq = lax.fori_loop(
        bounds[step, 0], bounds[step, 1], body, jnp.zeros((HEAD_DIM, TILE), F32)
    )
    dq_ref[:, here] = dq * SCALE

    @pl.when(step == length // TILE - 1)
    def _():
        def home(d, carry):
            at = span(lax.rem(d, per), 128)
            tile = pick_pair(lambda k: dq_ref[:, span(k, 128)], order, d)
            grad_ref[lax.div(d, per), 0, :, at] = tile.astype(BF)
            tile = pick_pair(lambda k: acc_ref[:, span(k, 128)], order, d).astype(BF)
            grad_ref[lax.div(d, per), 1, :, at] = tile[:HEAD_DIM]
            grad_ref[lax.div(d, per), 2, :, at] = tile[HEAD_DIM:]
            return carry

        lax.fori_loop(0, length // 128, home, 0)


def fixed(shape):
    return pl.BlockSpec(shape, lambda i: (0,) * len(shape))


def sorted_attend(bounds, inverse, order, meta, parts):
    groups, _, columns = parts.shape
    length = groups * columns
    shapes = (
        ((groups, HEAD_DIM, columns), BF),
        ((HEAD_DIM, length), F32),
        ((1, length), F32),
        ((2 * HEAD_DIM, length), BF),
        ((2 * HEAD_DIM, length), BF),
        ((length, 2 * HEAD_DIM), BF),
    )
    return pl.pallas_call(
        sorted_attend_kernel,
        name="attend",
        grid=(length // TILE,),
        in_specs=[pl.BlockSpec(memory_space=pltpu.SMEM)] * 3
        + [pl.BlockSpec((8, TILE), lambda i: (0, i)), fixed(parts.shape)],
        out_specs=tuple(fixed(s) for s, _ in shapes),
        out_shape=tuple(jax.ShapeDtypeStruct(s, d) for s, d in shapes),
        compiler_params=pltpu.CompilerParams(vmem_limit_bytes=40 * 2**20),
    )(bounds, inverse, order, meta, parts)


def sorted_back(bounds, inverse, order, meta, flow, out, lse, q_pad, kv_t, kv_rows, groups):
    length = out.shape[1]
    grad = (groups, 3, HEAD_DIM, length // groups)
    return pl.pallas_call(
        sorted_back_kernel,
        name="attend_back",
        grid=(length // TILE,),
        in_specs=[pl.BlockSpec(memory_space=pltpu.SMEM)] * 3
        + [pl.BlockSpec((8, TILE), lambda i: (0, i))]
        + [fixed(a.shape) for a in (flow, out, lse, q_pad, kv_t, kv_rows)],
        out_specs=fixed(grad),
        out_shape=jax.ShapeDtypeStruct(grad, BF),
        scratch_shapes=[
            pltpu.VMEM((2 * HEAD_DIM, length), BF),
            pltpu.VMEM((HEAD_DIM, length), F32),
            pltpu.VMEM((2 * HEAD_DIM, length), F32),
        ],
        compiler_params=pltpu.CompilerParams(vmem_limit_bytes=40 * 2**20),
    )(bounds, inverse, order, meta, flow, out, lse, q_pad, kv_t, kv_rows)


def normalize(values):
    center = values - jnp.mean(values, axis=-1, keepdims=True)
    spread = jnp.mean(center * center, axis=-1, keepdims=True)
    scale = lax.rsqrt(spread + EPS)
    return center * scale, scale


def mid_kernel(
    experts, team, member, att, wo, x, vec, rw, route, cot,
    second, dgrad, send_s, send_g, sel, mixes, middle_own, prob_own, hot_own, second_own, att_own,
    egrad,
):
    rows = middle_own.shape[0]
    slots = send_s.shape[1]
    groups = send_s.shape[0]
    capacity = slots // team
    lane = lax.broadcasted_iota(jnp.int32, (rows, 128), 1)
    row = lax.broadcasted_iota(jnp.int32, (rows, rows), 0)
    col = lax.broadcasted_iota(jnp.int32, (rows, rows), 1)
    me = member[0]

    def block(b, carry):
        at = span(b, rows)
        part = att[:, at]
        middle = x[at, :].astype(F32) + contract_rows(part, wo[...])
        hat, _ = normalize(middle)
        low = (hat * vec[1:2, :] + vec[3:4, :]).astype(BF)
        second[at, :] = low
        logits = dot_f32(low, rw[...])
        is_expert = lane < experts
        is_mix = (lane >= experts) & (lane < experts + 2)
        pe = jnp.where(is_expert, logits, NEG)
        pe = jnp.exp(pe - jnp.max(pe, axis=1, keepdims=True))
        pe = pe / jnp.sum(pe, axis=1, keepdims=True)
        pm = jnp.where(is_mix, logits, NEG)
        pm = jnp.exp(pm - jnp.max(pm, axis=1, keepdims=True))
        pm = pm / jnp.sum(pm, axis=1, keepdims=True)
        route_row = jnp.broadcast_to(route[b][0:1, :], (rows, rows))
        route_col = jnp.sum(jnp.where(row == col, route_row, 0), axis=1, keepdims=True)
        hot = lane == route_col
        gate = jnp.sum(jnp.where(hot, pe, 0.0), axis=1, keepdims=True)
        mix0 = jnp.sum(jnp.where(lane == experts, pm, 0.0), axis=1, keepdims=True)
        mix1 = jnp.sum(jnp.where(lane == experts + 1, pm, 0.0), axis=1, keepdims=True)
        scaled = mix1 * gate
        flow = cot[at, :].astype(F32)
        dgrad[at, :] = (flow * mix0).astype(BF)
        egrad[at, :] = (flow * scaled).astype(BF)
        mixes[at, :] = jnp.where(lane == 0, mix0, jnp.where(lane == 1, scaled, 0.0))
        same = (route_row == route_col) & (col < row)
        rank = jnp.sum(jnp.where(same, 1, 0), axis=1, keepdims=True)
        group = lax.div(route_col, team)
        mine = lax.rem(route_col, team) == me
        target = jnp.where(mine, group * slots + b * capacity + rank, groups * slots)
        slot = lax.broadcasted_iota(jnp.int32, (rows, groups * slots), 1)
        sel[at, :] = jnp.where(slot == target, 1.0, 0.0).astype(BF)

        @pl.when(b == me)
        def _():
            middle_own[...] = middle
            prob_own[...] = jnp.where(is_expert, pe, jnp.where(is_mix, pm, 0.0))
            hot_own[...] = jnp.where(hot, 1.0, 0.0)
            second_own[...] = low
            att_own[...] = part

        return carry

    lax.fori_loop(0, team, block, 0)
    send_s[...] = contract_rows(sel[...], second[...]).astype(BF).reshape(send_s.shape)
    send_g[...] = contract_rows(sel[...], egrad[...]).astype(BF).reshape(send_g.shape)


def between(experts, sizes, slots, member, att, wo, x, vec, rw, route, cot):
    two, groups, team = sizes
    group_rows, width = x.shape
    rows = group_rows // team
    shapes = (
        ((group_rows, width), BF),
        ((group_rows, width), BF),
        ((groups, slots, width), BF),
        ((groups, slots, width), BF),
        ((group_rows, groups * slots), BF),
        ((group_rows, 128), F32),
        ((rows, width), F32),
        ((rows, 128), F32),
        ((rows, 128), F32),
        ((rows, width), BF),
        ((width, rows), BF),
    )
    inside = pl.BlockSpec(memory_space=pltpu.VMEM)
    return pl.pallas_call(
        functools.partial(mid_kernel, experts, team),
        name="between",
        in_specs=[pl.BlockSpec(memory_space=pltpu.SMEM)] + [inside] * 7,
        out_specs=tuple(inside for _ in shapes),
        out_shape=tuple(jax.ShapeDtypeStruct(s, d) for s, d in shapes),
        scratch_shapes=[pltpu.VMEM((group_rows, width), BF)],
        compiler_params=pltpu.CompilerParams(vmem_limit_bytes=48 * 2**20),
    )(member, att, wo, x, vec, rw, route, cot)


def turn_kernel(
    experts, layer_sum, second_sum, sums, middle, prob, hot, second, att, cot, rw, wo, vec,
    layer, middle_grad, flow_t, out_term, small_t,
):
    rows = middle.shape[0]
    lane = lax.broadcasted_iota(jnp.int32, (rows, 128), 1)
    layer[...] = (middle[...] + layer_sum[...]).astype(BF)
    chances, chosen = prob[...], hot[...]
    s0, s1 = sums[:, 0:1], sums[:, 1:2]
    mix1 = jnp.sum(jnp.where(lane == experts + 1, chances, 0.0), axis=1, keepdims=True)
    gate = jnp.sum(chances * chosen, axis=1, keepdims=True)
    pull_gate = s1 * mix1
    pulls = jnp.where(lane == experts, s0, jnp.where(lane == experts + 1, s1 * gate, 0.0))
    mean_pull = jnp.sum(chances * pulls, axis=1, keepdims=True)
    logit_grad = chances * jnp.where(
        lane < experts, pull_gate * (chosen - gate), pulls - mean_pull
    )
    logit_grad = jnp.where(lane < experts + 2, logit_grad, 0.0).astype(BF)
    second_grad = second_sum[...] + contract_cols(logit_grad, rw[...])
    hat, scale = normalize(middle[...])
    pull = second_grad * vec[1:2, :]
    part = scale * (
        pull
        - jnp.mean(pull, axis=-1, keepdims=True)
        - hat * jnp.mean(pull * hat, axis=-1, keepdims=True)
    )
    grad = cot[...].astype(F32) + part
    middle_grad[...] = grad
    branch = grad.astype(BF)
    width = wo.shape[0]

    def tile(n, carry):
        at = span(n, TILE)
        flow_t[at, :] = contract_cols(wo[at, :], branch).astype(BF)
        out_term[at, :] = dot_f32(att[at, :], branch).astype(BF)
        return carry

    lax.fori_loop(0, width // TILE, tile, 0)
    used = small_t.shape[0]
    routed = contract_rows(logit_grad, second[...])[:used, :]
    which = lax.broadcasted_iota(jnp.int32, routed.shape, 0)
    gain = jnp.sum(second_grad * hat, axis=0, keepdims=True)
    bias = jnp.sum(second_grad, axis=0, keepdims=True)
    small_t[...] = jnp.where(
        which == experts + 3, gain, jnp.where(which == experts + 5, bias, routed)
    )


def turn(experts, layer_sum, second_sum, sums, middle, prob, hot, second, att, cot, rw, wo, vec):
    rows, width = middle.shape
    used = -(-(experts + 6) // 8) * 8
    shapes = (
        ((rows, width), BF),
        ((rows, width), F32),
        ((width, rows), BF),
        ((width, width), BF),
        ((used, width), F32),
    )
    inside = pl.BlockSpec(memory_space=pltpu.VMEM)
    return pl.pallas_call(
        functools.partial(turn_kernel, experts),
        name="turn",
        in_specs=[inside] * 12,
        out_specs=tuple(inside for _ in shapes),
        out_shape=tuple(jax.ShapeDtypeStruct(s, d) for s, d in shapes),
        compiler_params=pltpu.CompilerParams(vmem_limit_bytes=40 * 2**20),
    )(layer_sum, second_sum, sums, middle, prob, hot, second, att, cot, rw, wo, vec)


def row_sum_kernel(left, right, out):
    out[0] = contract_rows(left[...], right[...])


def row_sum(left, right, tile):
    many, high = left.shape
    wide = right.shape[1]
    return pl.pallas_call(
        row_sum_kernel,
        name="row_sum",
        grid=(high // tile,),
        in_specs=[pl.BlockSpec((many, tile), lambda i: (0, i)), fixed(right.shape)],
        out_specs=pl.BlockSpec((1, tile, wide), lambda i: (0, i, 0)),
        out_shape=jax.ShapeDtypeStruct((1, high, wide), F32),
        compiler_params=pltpu.CompilerParams(vmem_limit_bytes=40 * 2**20),
        cost_estimate=pl.CostEstimate(
            flops=2 * many * high * wide, bytes_accessed=4 * high * wide, transcendentals=0
        ),
    )(left, right)


def gelu_and_slope(x):
    k = math.sqrt(2.0 / math.pi)
    square = x * x
    bent = jnp.tanh(k * (x + 0.044715 * (square * x)))
    half = 0.5 * (1.0 + bent)
    slope = half + (0.5 * k) * x * (1.0 - bent * bent) * (1.0 + (3 * 0.044715) * square)
    return x * half, slope


def feed_kernel(sizes, copies_count, *refs):
    two, groups, team = sizes
    (send_s, send_g, eup_h, edown_h, second_h, dgrad_h, ff_h, sel_h, cot_h, mix_h) = refs[:10]
    (layer_o, grad_o, sums_o, active_o, hgrad_o, arr_s_o, arr_g_o, ffg_o) = refs[10:18]
    (
        arr_s, arr_g, eup, edown, second, dgrad, upw, downw, sel, cot, mix,
        slope, active, hgrad, acc, give, got_s, got_g, ret_s, ret_g, back_s, back_g,
        low, ugrad, dense, spart, lay, spa, sums, lay_r, spa_r, sums_r,
        term_give, term_got, send_sem, recv_sem, load_sem, out_sem,
    ) = refs[18:]
    c = lax.axis_index("dp")
    i = lax.axis_index("ctx")
    g, t = lax.div(i, team), lax.rem(i, team)
    width = second.shape[1]
    rows = lay.shape[1]
    hid, ehid = upw.shape[1], eup.shape[1]
    core = lax.rem(c + 1, two)

    def device(step):
        dc, dg, dt = step
        return (
            lax.rem(c + dc, two),
            lax.rem(g + dg, groups) * team + lax.rem(t + dt, team),
        )

    index = [0]

    def remote(src, dst, step):
        k = index[0]
        index[0] += 1
        assert k < copies_count
        return pltpu.make_async_remote_copy(
            src_ref=src,
            dst_ref=dst,
            send_sem=send_sem.at[k],
            recv_sem=recv_sem.at[k],
            device_id=device(step),
            device_id_type=MESH,
        )

    group_steps = [(0, k, 0) for k in range(1, groups)]
    team_steps = [(0, 0, k) for k in range(1, team)]
    swap = (1, 0, 0)
    deep = ff_h.shape[2]

    def block_of(core, k):
        return pl.ds(pl.multiple_of((core * groups + k) * deep, deep), deep)

    loads = []
    for k, (src, dst) in enumerate(
        [
            (second_h, second), (dgrad_h, dgrad), (eup_h, eup), (edown_h, edown), (sel_h, sel), (cot_h, cot), (mix_h, mix),
            (send_s.at[g], arr_s.at[c, g]), (send_g.at[g], arr_g.at[c, g]),
        ]
        + [
            (ff_h.at[k, n], weight.at[block_of(c, k), :])
            for k in range(groups)
            for n, weight in enumerate((upw, downw))
        ]
    ):
        load = pltpu.make_async_copy(src, dst, load_sem.at[k])
        load.start()
        loads.append(load)

    barrier = pltpu.get_barrier_semaphore()
    greet = group_steps + team_steps + [swap]
    for step in greet:
        pl.semaphore_signal(barrier, inc=1, device_id=device(step), device_id_type=MESH)
    pl.semaphore_wait(barrier, len(greet))

    every = []

    def launch(copy):
        copy.start()
        every.append(copy)
        return copy

    def to_groups(src, dst):
        return [
            launch(remote(src.at[lax.rem(g + s[1], groups)], dst.at[g], s)) for s in group_steps
        ]

    def source(s):
        return lax.rem(g + groups - s[1], groups)

    swap_w = [
        launch(remote(ff_h.at[k, n], weight.at[block_of(c, k), :], swap))
        for k in range(groups)
        for n, weight in enumerate((upw, downw))
    ]
    out_s = [
        launch(remote(send_s.at[lax.rem(g + s[1], groups)], arr_s.at[c, g], s))
        for s in group_steps
    ]
    swap_s = [launch(remote(send_s.at[g], arr_s.at[c, g], swap))]
    out_g = [
        launch(remote(send_g.at[lax.rem(g + s[1], groups)], arr_g.at[c, g], s))
        for s in group_steps
    ]
    swap_g = [launch(remote(send_g.at[g], arr_g.at[c, g], swap))]

    for load in loads[:2] + loads[9:]:
        load.wait()
    for copy in swap_w:
        copy.wait_recv()

    def dense_in(h, carry):
        at = span(h, TILE)
        value, bend = gelu_and_slope(dot_f32(second[...], upw[:, at]))
        low[:, at] = value.astype(BF)
        ugrad[:, at] = (bend * contract_cols(dgrad[...], downw[at, :])).astype(BF)
        return carry

    lax.fori_loop(0, hid // TILE, dense_in, 0)

    def dense_out(n, carry):
        at = span(n, TILE)
        dense[:, at] = dot_f32(low[...], downw[:, at])
        spart[:, at] = contract_cols(ugrad[...], upw[at, :])
        return carry

    lax.fori_loop(0, width // TILE, dense_out, 0)

    for load in loads[2:9]:
        load.wait()
    for copy, s in zip(out_s, group_steps):
        copy.wait_recv()
        swap_s.append(launch(remote(arr_s.at[c, source(s)], arr_s.at[c, source(s)], swap)))
    for copy in swap_s:
        copy.wait_recv()
    entries = 2 * groups * arr_s.shape[2]

    def expert_in(h, carry):
        at = span(h, TILE)
        value, bend = gelu_and_slope(dot_f32(arr_s[...].reshape(entries, width), eup[:, at]))
        active[:, at] = value.astype(BF)
        slope[:, at] = bend
        return carry

    lax.fori_loop(0, ehid // TILE, expert_in, 0)
    keeps = [
        pltpu.make_async_copy(active, active_o, out_sem.at[0]),
        pltpu.make_async_copy(arr_s, arr_s_o, out_sem.at[1]),
    ]
    for copy in keeps:
        copy.start()

    def expert_out(n, carry):
        at = span(n, TILE)
        acc[:, :, at] = dot_f32(active[...], edown[:, at]).reshape(2, entries // 2, TILE)
        return carry

    lax.fori_loop(0, width // TILE, expert_out, 0)
    give[0] = acc[core].astype(BF)
    other_s = launch(remote(give.at[0], got_s, swap))

    for copy, s in zip(out_g, group_steps):
        copy.wait_recv()
        swap_g.append(launch(remote(arr_g.at[c, source(s)], arr_g.at[c, source(s)], swap)))
    other_s.wait_recv()
    ret_s[...] = (acc[c] + got_s[...].astype(F32)).astype(BF).reshape(ret_s.shape)
    home_s = to_groups(ret_s, back_s)
    back_s[g] = ret_s[g]
    for copy in swap_g:
        copy.wait_recv()

    def expert_back(h, carry):
        at = span(h, TILE)
        pull = contract_cols(arr_g[...].reshape(entries, width), edown[at, :])
        hgrad[:, at] = (slope[:, at] * pull).astype(BF)
        return carry

    lax.fori_loop(0, ehid // TILE, expert_back, 0)
    keeps += [
        pltpu.make_async_copy(hgrad, hgrad_o, out_sem.at[2]),
        pltpu.make_async_copy(arr_g, arr_g_o, out_sem.at[3]),
    ]
    for copy in keeps[2:]:
        copy.start()

    def expert_back_out(n, carry):
        at = span(n, TILE)
        acc[:, :, at] = contract_cols(hgrad[...], eup[at, :]).reshape(2, entries // 2, TILE)
        return carry

    lax.fori_loop(0, width // TILE, expert_back_out, 0)
    give[1] = acc[core].astype(BF)
    other_g = launch(remote(give.at[1], got_g, swap))
    other_g.wait_recv()
    ret_g[...] = (acc[c] + got_g[...].astype(F32)).astype(BF).reshape(ret_g.shape)
    home_g = to_groups(ret_g, back_g)
    back_g[g] = ret_g[g]

    for copy in home_s:
        copy.wait_recv()
    slots = groups * back_s.shape[1]
    lane = lax.broadcasted_iota(jnp.int32, (rows, 128), 1)

    def join_layer(r, carry):
        at = span(r, rows)
        found = dot_f32(sel[at, :], back_s[...].reshape(slots, width))
        own = dense[at, :]
        flow = cot[at, :].astype(F32)
        mixes = mix[at, :]
        lay[r] = (mixes[:, 0:1] * own + mixes[:, 1:2] * found).astype(BF)
        plain = jnp.sum(flow * own, axis=1, keepdims=True)
        routed = jnp.sum(flow * found, axis=1, keepdims=True)
        sums[r] = jnp.where(lane == 0, plain, jnp.where(lane == 1, routed, 0.0))
        return carry

    lax.fori_loop(0, team, join_layer, 0)

    def to_team(src, dst):
        made = [launch(remote(src.at[lax.rem(t + s[2], team)], dst.at[t], s)) for s in team_steps]
        dst[t] = src[t]
        return made

    team_copies = to_team(lay, lay_r) + to_team(sums, sums_r)

    for copy in home_g:
        copy.wait_recv()

    def join_grad(r, carry):
        at = span(r, rows)
        found = dot_f32(sel[at, :], back_g[...].reshape(slots, width))
        spa[r] = (spart[at, :] + found).astype(BF)
        return carry

    lax.fori_loop(0, team, join_grad, 0)
    team_copies += to_team(spa, spa_r)

    half = hid // 2
    term_tile = 128

    def down_term(base, n):
        at = pl.ds(pl.multiple_of(base + n * term_tile, term_tile), term_tile)
        return contract_rows(low[:, at], dgrad[...])

    def up_term(base, n):
        at = pl.ds(pl.multiple_of(base + n * term_tile, term_tile), term_tile)
        return contract_rows(second[:, at], ugrad[...])

    terms = []
    for k, (term, size) in enumerate(((down_term, half), (up_term, width // 2))):

        def giving(n, carry, k=k, term=term, size=size):
            term_give[k, span(n, term_tile), :] = term(core * size, n).astype(BF)
            return carry

        lax.fori_loop(0, size // term_tile, giving, 0)
        terms.append(launch(remote(term_give.at[k], term_got.at[k], swap)))
    for k, (term, size) in enumerate(((down_term, half), (up_term, width // 2))):
        terms[k].wait_recv()

        def keeping(n, carry, k=k, term=term, size=size):
            at = span(n, term_tile)
            total = term(c * size, n) + term_got[k, at, :].astype(F32)
            ffg_o[at, k * width : (k + 1) * width] = total.astype(BF)
            return carry

        lax.fori_loop(0, size // term_tile, keeping, 0)

    for copy in team_copies:
        copy.wait_recv()
    layer_o[...] = jnp.sum(lay_r[...].astype(F32), axis=0)
    grad_o[...] = jnp.sum(spa_r[...].astype(F32), axis=0)
    sums_o[...] = jnp.sum(sums_r[...], axis=0)
    for copy in keeps:
        copy.wait()
    for copy in every:
        copy.wait_send()


def feed_forward(sizes, rows, send_s, send_g, eup, edown, second, dgrad, ff, sel, cot, mix):
    two, groups, team = sizes
    slots = send_s.shape[1]
    width = second.shape[1]
    hid, ehid = second.shape[1] * ff.shape[3] // width, eup.shape[1]
    entries = 2 * groups * slots
    count = 2 * (groups - 1) * 2 + 2 * groups + 2 + 3 * (team - 1) + 2 + 2 * groups
    arrived = (two, groups, slots, width)
    anywhere = pl.BlockSpec(memory_space=pl.ANY)
    inside = pl.BlockSpec(memory_space=pltpu.VMEM)
    team_rows = team * rows
    return pl.pallas_call(
        functools.partial(feed_kernel, sizes, count),
        name="feed_forward",
        out_shape=(
            jax.ShapeDtypeStruct((rows, width), F32),
            jax.ShapeDtypeStruct((rows, width), F32),
            jax.ShapeDtypeStruct((rows, 128), F32),
            jax.ShapeDtypeStruct((entries, ehid), BF),
            jax.ShapeDtypeStruct((entries, ehid), BF),
            jax.ShapeDtypeStruct(arrived, BF),
            jax.ShapeDtypeStruct(arrived, BF),
            jax.ShapeDtypeStruct((hid // 2, 2 * width), BF),
        ),
        in_specs=[anywhere] * 10,
        out_specs=(inside, inside, inside, anywhere, anywhere, anywhere, anywhere, inside),
        scratch_shapes=[
            pltpu.VMEM((two, groups, slots, width), BF),
            pltpu.VMEM((two, groups, slots, width), BF),
            pltpu.VMEM(eup.shape, BF),
            pltpu.VMEM(edown.shape, BF),
            pltpu.VMEM(second.shape, BF),
            pltpu.VMEM(dgrad.shape, BF),
            pltpu.VMEM((width, hid), BF),
            pltpu.VMEM((hid, width), BF),
            pltpu.VMEM(sel.shape, BF),
            pltpu.VMEM(cot.shape, BF),
            pltpu.VMEM(mix.shape, F32),
            pltpu.VMEM((entries, ehid), F32),
            pltpu.VMEM((entries, ehid), BF),
            pltpu.VMEM((entries, ehid), BF),
            pltpu.VMEM((2, entries // 2, width), F32),
            pltpu.VMEM((2, entries // 2, width), BF),
            pltpu.VMEM((entries // 2, width), BF),
            pltpu.VMEM((entries // 2, width), BF),
            pltpu.VMEM((groups, slots, width), BF),
            pltpu.VMEM((groups, slots, width), BF),
            pltpu.VMEM((groups, slots, width), BF),
            pltpu.VMEM((groups, slots, width), BF),
            pltpu.VMEM((team_rows, hid), BF),
            pltpu.VMEM((team_rows, hid), BF),
            pltpu.VMEM((team_rows, width), F32),
            pltpu.VMEM((team_rows, width), F32),
            pltpu.VMEM((team, rows, width), BF),
            pltpu.VMEM((team, rows, width), BF),
            pltpu.VMEM((team, rows, 128), F32),
            pltpu.VMEM((team, rows, width), BF),
            pltpu.VMEM((team, rows, width), BF),
            pltpu.VMEM((team, rows, 128), F32),
            pltpu.VMEM((2, hid // 2, width), BF),
            pltpu.VMEM((2, hid // 2, width), BF),
            pltpu.SemaphoreType.DMA((count,)),
            pltpu.SemaphoreType.DMA((count,)),
            pltpu.SemaphoreType.DMA((9 + 2 * groups,)),
            pltpu.SemaphoreType.DMA((4,)),
        ],
        compiler_params=pltpu.CompilerParams(
            collective_id=5, has_side_effects=True, vmem_limit_bytes=60 * 2**20
        ),
        cost_estimate=pl.CostEstimate(
            flops=0, bytes_accessed=240_000_000, transcendentals=0
        ),
    )(send_s, send_g, eup, edown, second, dgrad, ff, sel, cot, mix)


def tall(chunk):
    rows, cols = chunk.shape[-2:]
    factor = 1
    while (rows * factor) % 16:
        factor *= 2
    return chunk.reshape(chunk.shape[:-2] + (rows * factor, cols // factor))


def per_device(
    tokens,
    cotangent,
    block_order,
    doc_lengths,
    routes,
    w_qkv,
    w_out,
    w_up,
    w_down,
    router,
    norm_gains,
    norm_biases,
    expert_up,
    expert_down,
):
    rows, width = tokens.shape[1], tokens.shape[2]
    ctx_count = lax.axis_size("ctx")
    two = lax.axis_size("dp")
    team = math.gcd(4, ctx_count)
    groups = ctx_count // team
    sizes = (two, groups, team)
    team_heads = HEADS // team
    reps = groups // team_heads
    length = rows * ctx_count
    group_rows = rows * team
    experts = ctx_count * expert_up.shape[0]
    capacity = max(2, 2 * rows // experts)
    block_rows = length // block_order.shape[0]
    hidden = w_up.shape[1]
    hidden_dev = w_down.shape[0]
    wr = w_qkv.shape[0]
    qkv_cols = 3 * width // team
    up_cols = hidden // team
    core = lax.axis_index("dp")
    ctx = lax.axis_index("ctx")
    group, member = lax.div(ctx, team), lax.rem(ctx, team)
    team_steps = [(0, 0, k) for k in range(1, team)]
    group_steps = [(0, k, 0) for k in range(1, groups)]
    by_group = [[g * team + t for g in range(groups)] for t in range(team)]
    by_team = [[g * team + t for t in range(team)] for g in range(groups)]
    swap = [(d, (d + 1) % two) for d in range(two)]

    small_flat = jnp.concatenate(
        [router.reshape(-1), norm_gains.reshape(-1), norm_biases.reshape(-1)]
    )
    small_size = -(-small_flat.shape[0] // 2048) * 2048
    small = jnp.pad(small_flat, (0, small_size - small_flat.shape[0])).astype(BF)
    small = small.reshape(-1, 128)

    qkv_first = tall(
        w_qkv.astype(BF).reshape(wr, 3, team, width // team).transpose(2, 0, 1, 3).reshape(
            team, wr, qkv_cols
        )
    )
    up_first = tall(
        w_up.reshape(wr, two * groups, team, hidden_dev)
        .transpose(2, 0, 1, 3)
        .reshape(team, wr, up_cols)
        .astype(BF)
    )
    down_first = tall(w_down.astype(BF).reshape(team, wr, width))
    out_first = tall(w_out.astype(BF))
    route_row = jnp.broadcast_to(routes[0, :, 0][None, :], (8, rows))

    def first(coords, ins, outs):
        c, g, t = coords
        moves, local = [], []
        for s in team_steps:
            to = lax.rem(t + s[2], team)
            moves.append(Move(s, ins[0], outs[0].at[t]))
            moves.append(Move(s, ins[1].at[to], outs[1].at[t]))
            moves.append(Move(s, ins[3], outs[3].at[t]))
            moves.append(Move(s, ins[4], outs[4].at[t]))
            moves.append(Move(s, ins[2].at[to], outs[2].at[0, t]))
        for s in group_steps:
            moves.append(Move(s, ins[5], outs[5].at[g]))
        local.append((ins[0], outs[0].at[t]))
        local.append((ins[1].at[t], outs[1].at[t]))
        local.append((ins[2].at[t], outs[2].at[0, t]))
        local.append((ins[3], outs[3].at[t]))
        local.append((ins[4], outs[4].at[t]))
        local.append((ins[5], outs[5].at[g]))
        local.append((ins[6], outs[2].at[1]))
        return local, moves

    token_rows, qkv_part, ff_part, small_part, route_all, out_part = exchange(
        "first",
        1,
        sizes,
        (tokens[0], qkv_first, up_first, small, route_row, out_first, down_first),
        [
            ((team, rows, width), BF),
            (qkv_first.shape, BF),
            ((2,) + up_first.shape, BF),
            ((team,) + small.shape, BF),
            ((team, 8, rows), jnp.int32),
            ((groups,) + out_first.shape, BF),
        ],
        first,
    )

    def second_build(coords, ins, outs):
        c, g, t = coords
        moves, local = [], []
        for k, s in enumerate(group_steps):
            moves.append(Move(s, ins[0], outs[0].at[c, g]))
            moves.append(Move(s, ins[1], outs[1].at[c, g]))
        for s in team_steps:
            moves.append(Move(s, ins[2], outs[2].at[t]))
        local.append((ins[0], outs[0].at[c, g]))
        local.append((ins[1], outs[1].at[c, g]))
        local.append((ins[2], outs[2].at[t]))
        other = (1, 0, 0)
        for n in range(2):
            moves.append(Move(other, ins[n], outs[n].at[c, g]))
        for k, s in enumerate(group_steps):
            source = lax.rem(g + groups - s[1], groups)
            for n in range(2):
                moves.append(
                    Move(other, outs[n].at[c, source], outs[n].at[c, source], after=2 * k + n)
                )
        return local, moves

    qkv_all, small_all, cot_rows = exchange(
        "second",
        2,
        sizes,
        (qkv_part, small_part, cotangent[0]),
        [
            ((two, groups) + qkv_part.shape, BF),
            ((two, groups) + small_part.shape, BF),
            ((team, rows, width), BF),
        ],
        second_build,
    )
    qkv_weight = qkv_all.reshape(width, qkv_cols)
    small_rows = small_all.reshape(two * ctx_count, -1)
    router_cols = router.shape[1]
    router_weight = jnp.pad(
        small_rows[:, : wr * router_cols].reshape(width, router_cols),
        ((0, 0), (0, 128 - router_cols)),
    )
    vectors = small_rows[:, wr * router_cols : small_flat.shape[0]].reshape(
        two * ctx_count, 4, wr
    )
    vectors = vectors.transpose(1, 0, 2).reshape(4, width).astype(F32)
    vectors = jnp.pad(vectors, ((0, 4), (0, 0)))

    ff_half = lax.all_gather(
        ff_part.reshape(2, team * wr, width),
        "ctx",
        axis=0,
        tiled=False,
        axis_index_groups=by_group,
    )

    def core_half(term):
        halves = term.reshape((two, term.shape[0] // two) + term.shape[1:])
        keep = lax.dynamic_index_in_dim(halves, core, 0, keepdims=False)
        give = lax.dynamic_index_in_dim(halves, 1 - core, 0, keepdims=False)
        return keep + lax.ppermute(give.astype(BF), "dp", swap).astype(F32)

    def over_groups(term):
        return lax.psum_scatter(
            term, "ctx", scatter_dimension=0, tiled=True, axis_index_groups=by_group
        )

    doc_id = jnp.arange(doc_lengths.shape[1], dtype=jnp.int32)
    doc_ends = jnp.sum(
        jnp.where(doc_id[:, None] <= doc_id[None, :], doc_lengths[0][:, None], 0), axis=0
    )
    all_rows = jnp.arange(length, dtype=jnp.int32)
    marks = (all_rows // block_rows)[:, None] == jnp.arange(
        block_order.shape[0], dtype=jnp.int32
    )[None, :]
    anchor = jnp.sum(jnp.where(marks, block_order[None, :], 0), axis=1)
    all_place = anchor * block_rows + all_rows % block_rows

    def low_of(place):
        return jnp.max(
            jnp.where(doc_ends[None, :] <= place[:, None], doc_ends[None, :], 0), axis=1
        )

    sorted_rows = reps == 1 and block_rows == BLOCK
    query_length = length // reps
    tiles = query_length // TILE
    part = lax.rem(group, reps)
    if sorted_rows:
        query_place = all_rows
        lows = low_of(all_rows)
        bounds = jnp.stack(
            [lows[::TILE] // TILE, jnp.arange(1, tiles + 1, dtype=jnp.int32)], axis=1
        )
        number = jnp.arange(block_order.shape[0], dtype=jnp.int32)
        inverse = jnp.sum(
            jnp.where(block_order[None, :] == number[:, None], number[None, :], 0), axis=1
        )
    else:
        query_place = lax.dynamic_slice(all_place, (part * query_length,), (query_length,))
        lows = low_of(query_place)
        bounds = jnp.broadcast_to(
            jnp.array([[0, length // TILE]], dtype=jnp.int32), (tiles, 2)
        )
    meta = jnp.concatenate(
        [query_place[None], lows[None], jnp.zeros((6, query_length), jnp.int32)], axis=0
    )

    token_rows = token_rows.reshape(group_rows, width)
    inputs = token_rows.astype(F32)
    normed_low = layer_norm(inputs, vectors[0], vectors[2]).astype(BF)
    mixed_t = lax.dot_general(
        qkv_weight, normed_low, (((0,), (1,)), ((), ())), preferred_element_type=F32
    ).astype(BF)
    mixed_t = mixed_t.reshape(3, team_heads, HEAD_DIM, group_rows)

    def spread_heads(coords, ins, outs):
        c, g, t = coords
        moves = [
            Move(s, ins[0].at[:, lax.div(lax.rem(g + s[1], groups), reps)], outs[0].at[g])
            for s in group_steps
        ]
        local = [(ins[0].at[:, lax.div(g, reps)], outs[0].at[g])]
        other = (1, 0, 0)
        moves.append(Move(other, ins[1], outs[1].at[c, :, t]))
        local.append((ins[1], outs[1].at[c, :, t]))
        first_team = len(moves)
        for s in team_steps:
            moves.append(Move(s, ins[1], outs[1].at[c, :, t]))
        for k, s in enumerate(team_steps):
            source = lax.rem(t + team - s[2], team)
            view = outs[1].at[c, :, source]
            moves.append(Move(other, view, view, after=first_team + k))
        return local, moves

    head_parts, out_weight = exchange(
        "heads",
        3,
        sizes,
        (mixed_t, out_part),
        [
            ((groups, 3, HEAD_DIM, group_rows), BF),
            ((two, groups, team) + out_first.shape, BF),
        ],
        spread_heads,
    )
    out_weight = out_weight.reshape(width, width)
    head_parts = head_parts.reshape(groups, 3 * HEAD_DIM, group_rows)
    if sorted_rows:
        low_t, attention_t, log_total, q_pad, kv_t, kv_rows = sorted_attend(
            bounds, inverse, block_order, meta, head_parts
        )
    else:
        place_col = all_place[:, None]
        head_t = head_parts.transpose(1, 0, 2).reshape(3 * HEAD_DIM, length)
        zeros = jnp.zeros((HEAD_DIM, query_length), BF)
        kv_t = head_t[HEAD_DIM:]
        kv_rows = kv_t.T
        q_t = lax.dynamic_slice(
            head_t[:HEAD_DIM], (0, part * query_length), (HEAD_DIM, query_length)
        )
        q_pad = jnp.concatenate([q_t * jnp.asarray(SCALE, BF), zeros], axis=0)
        attention_t, log_total = attend(False, bounds, meta, place_col, q_pad, kv_rows, kv_t)
        low_t = lax.dynamic_update_slice(
            jnp.zeros((HEAD_DIM, length), BF),
            attention_t.astype(BF),
            (0, part * query_length),
        )
        low_t = low_t.reshape(HEAD_DIM, groups, group_rows).transpose(1, 0, 2)

    def gather_heads(coords, ins, outs):
        c, g, t = coords
        moves = [
            Move(s, ins[0].at[lax.rem(g + s[1], groups)], outs[0].at[t, g]) for s in group_steps
        ]
        local = [(ins[0].at[g], outs[0].at[t, g])]
        for s in team_steps:
            moves.append(Move(s, ins[0].at[g], outs[0].at[t, g]))
        for k, s in enumerate(group_steps):
            source = lax.rem(g + groups - s[1], groups)
            for e in team_steps:
                moves.append(Move(e, outs[0].at[t, source], outs[0].at[t, source], after=k))
        return local, moves

    [attended] = exchange(
        "attended",
        4,
        sizes,
        (low_t,),
        [((team, groups, HEAD_DIM, group_rows), BF)],
        gather_heads,
    )
    if reps > 1:
        attended = lax.dynamic_index_in_dim(
            attended.reshape(team, team_heads, reps, HEAD_DIM, group_rows),
            lax.div(group, groups // reps),
            2,
            keepdims=False,
        )
    attended_t = attended.reshape(width, group_rows)

    slots = team * capacity
    (
        second_low,
        dense_grad,
        send_s,
        send_g,
        select,
        mixes,
        middle_own,
        prob_own,
        hot_own,
        second_own,
        attended_own,
    ) = between(
        experts,
        sizes,
        slots,
        member[None],
        attended_t,
        out_weight,
        token_rows,
        vectors,
        router_weight,
        route_all,
        cot_rows.reshape(group_rows, width),
    )
    (
        layer_sum,
        second_sum,
        sums_own,
        expert_active,
        hidden_grad,
        arrived_in,
        arrived_grad,
        ff_terms,
    ) = feed_forward(
        sizes,
        rows,
        send_s,
        send_g,
        expert_up[0],
        expert_down[0],
        second_low,
        dense_grad,
        ff_half,
        select,
        cot_rows.reshape(group_rows, width),
        mixes,
    )
    ff_sum = over_groups(ff_terms)
    down_sum = ff_sum[:, :width].astype(F32)
    up_sum = ff_sum[:, width:].reshape(team, wr, up_cols)
    entries = two * groups * slots
    expert_down_grad = row_sum(expert_active, arrived_grad.reshape(entries, width), TILE)
    expert_up_grad = row_sum(arrived_in.reshape(entries, width), hidden_grad, 128)

    layer_out, middle_grad, flow_t, out_term, small_t = turn(
        experts,
        layer_sum,
        second_sum,
        sums_own,
        middle_own,
        prob_own,
        hot_own,
        second_own,
        attended_own,
        cotangent[0],
        router_weight,
        out_weight,
        vectors,
    )
    flow_t = flow_t.reshape(team, team_heads, HEAD_DIM, rows)
    out_halves = out_term.reshape(two, groups, team, wr, width)

    def spread_flow(coords, ins, outs):
        c, g, t = coords
        moves = []
        for dg in range(groups):
            for dt in range(team):
                if dg or dt:
                    to_g, to_t = lax.rem(g + dg, groups), lax.rem(t + dt, team)
                    moves.append(
                        Move((0, dg, dt), ins[0].at[to_t, lax.div(to_g, reps)], outs[0].at[g, t])
                    )
        moves.append(Move((1, 0, 0), ins[1].at[lax.rem(c + 1, two)], outs[1]))
        return [(ins[0].at[t, lax.div(g, reps)], outs[0].at[g, t])], moves

    flow_parts, out_got = exchange(
        "flow",
        8,
        sizes,
        (flow_t, out_halves),
        [((groups, team, HEAD_DIM, rows), BF), (out_halves.shape[1:], BF)],
        spread_flow,
    )
    if sorted_rows:
        grad_parts = sorted_back(
            bounds,
            inverse,
            block_order,
            meta,
            flow_parts.reshape(ctx_count, HEAD_DIM, rows),
            attention_t,
            log_total,
            q_pad,
            kv_t,
            kv_rows,
            groups,
        )
    else:
        flow_all = flow_parts.transpose(2, 0, 1, 3).reshape(HEAD_DIM, length)
        flow_all = lax.dynamic_slice(
            flow_all, (0, part * query_length), (HEAD_DIM, query_length)
        )
        do_pad = jnp.concatenate([zeros, flow_all], axis=0)
        query_grad, pair_grad = attend_back(
            False,
            bounds,
            meta,
            place_col,
            q_pad,
            do_pad,
            attention_t,
            log_total,
            kv_rows,
            kv_t,
        )
        query_grad = lax.dynamic_update_slice(
            jnp.zeros((HEAD_DIM, length), BF), query_grad, (0, part * query_length)
        )
        grad_parts = jnp.concatenate([query_grad, pair_grad], axis=0)
        grad_parts = grad_parts.reshape(3, HEAD_DIM, groups, group_rows).transpose(2, 0, 1, 3)
    out_keep = lax.dynamic_index_in_dim(out_halves, core, 0, keepdims=False)
    out_parts = tall(
        (out_keep.astype(F32) + out_got.astype(F32))
        .astype(BF)
        .transpose(1, 0, 2, 3)
        .reshape(team, groups * wr, width)
    )

    def mixed_build(coords, ins, outs):
        c, g, t = coords
        moves = [
            Move(s, ins[0].at[lax.rem(g + s[1], groups)], outs[0].at[:, g])
            for s in group_steps
        ]
        moves += [
            Move(s, ins[1].at[lax.rem(t + s[2], team)], outs[1].at[t]) for s in team_steps
        ]
        return [(ins[0].at[g], outs[0].at[:, g]), (ins[1].at[t], outs[1].at[t])], moves

    grad_parts, out_parts = exchange(
        "mixed",
        9,
        sizes,
        (grad_parts, out_parts),
        [((3, groups, HEAD_DIM, group_rows), BF), (out_parts.shape, BF)],
        mixed_build,
    )
    out_parts = tall(
        jnp.sum(out_parts.astype(F32), axis=0).astype(BF).reshape(groups, wr, width)
    )
    if reps > 1:
        grad_parts = jnp.sum(
            grad_parts.reshape(3, team_heads, reps, HEAD_DIM, group_rows).astype(F32), axis=2
        ).astype(BF)
    mixed_grad_t = grad_parts.reshape(qkv_cols, group_rows)
    normed_part = (
        lax.dot_general(
            mixed_grad_t, qkv_weight, (((0,), (1,)), ((), ())), preferred_element_type=F32
        )
        .astype(BF)
        .reshape(team, rows, width)
    )
    qkv_term = lax.dot_general(
        normed_low, mixed_grad_t, (((0,), (1,)), ((), ())), preferred_element_type=F32
    )
    qkv_parts = core_half(qkv_term).astype(BF).reshape(groups, team * wr, qkv_cols)

    def normed_build(coords, ins, outs):
        c, g, t = coords
        moves, local = [], [(ins[2].at[t], outs[2].at[t])]
        for n in range(2):
            for s in group_steps:
                moves.append(Move(s, ins[n].at[lax.rem(g + s[1], groups)], outs[n].at[g]))
            local.append((ins[n].at[g], outs[n].at[g]))
        for s in team_steps:
            moves.append(Move(s, ins[2].at[lax.rem(t + s[2], team)], outs[2].at[t]))
        return local, moves

    qkv_parts, out_parts, normed_own = exchange(
        "normed",
        10,
        sizes,
        (qkv_parts, out_parts, normed_part),
        [(qkv_parts.shape, BF), (out_parts.shape, BF), (normed_part.shape, BF)],
        normed_build,
    )
    qkv_sum = (
        jnp.sum(qkv_parts.astype(F32), axis=0).astype(BF).reshape(team, wr, qkv_cols)
    )
    out_sum = jnp.sum(out_parts.astype(F32), axis=0).reshape(wr, width)
    normed_grad = jnp.sum(normed_own.astype(F32), axis=0)
    input_part_grad, gain_first, bias_first = jax.vjp(
        layer_norm, tokens[0].astype(F32), vectors[0], vectors[2]
    )[1](normed_grad)
    input_grad = middle_grad + input_part_grad

    small_used = small_t.shape[0]
    small_row = jnp.arange(small_used, dtype=jnp.int32)[:, None]
    small_t = jnp.where(
        small_row == experts + 2,
        gain_first[None],
        jnp.where(small_row == experts + 4, bias_first[None], small_t),
    )
    small_cols = small_used * wr
    small_pad = -(-small_cols // 1024) * 1024
    small_parts = jnp.pad(
        small_t.reshape(small_used, two * ctx_count, wr)
        .transpose(1, 0, 2)
        .reshape(two * ctx_count, small_cols),
        ((0, 0), (0, small_pad - small_cols)),
    ).reshape(two * ctx_count, small_pad // 128, 128)

    def owners_build(coords, ins, outs):
        c, g, t = coords
        moves, local = [], []
        for n in range(2):
            for s in team_steps:
                moves.append(Move(s, ins[n].at[lax.rem(t + s[2], team)], outs[n].at[t]))
            local.append((ins[n].at[t], outs[n].at[t]))
        me = c * ctx_count + g * team + t
        for dc in range(two):
            for dg in range(groups):
                for dt in range(team):
                    if dc or dg or dt:
                        to = (
                            lax.rem(c + dc, two) * ctx_count
                            + lax.rem(g + dg, groups) * team
                            + lax.rem(t + dt, team)
                        )
                        moves.append(Move((dc, dg, dt), ins[2].at[to], outs[2].at[me]))
        local.append((ins[2].at[me], outs[2].at[me]))
        return local, moves

    up_own, qkv_own, small_own = exchange(
        "owners",
        11,
        sizes,
        (tall(up_sum), tall(qkv_sum), small_parts),
        [
            (tall(up_sum).shape, BF),
            (tall(qkv_sum).shape, BF),
            (small_parts.shape, F32),
        ],
        owners_build,
    )
    small_sum = jnp.sum(small_own, axis=0).reshape(-1)[:small_cols].reshape(small_used, wr)
    up_own = (
        up_own.reshape(team, wr, two * groups, hidden_dev)
        .transpose(1, 2, 0, 3)
        .reshape(wr, hidden)
        .astype(F32)
    )
    qkv_own = (
        qkv_own.reshape(team, wr, 3, width // team)
        .transpose(1, 2, 0, 3)
        .reshape(wr, 3 * width)
        .astype(F32)
    )
    return (
        layer_out[None],
        input_grad[None].astype(BF),
        qkv_own,
        out_sum,
        up_own,
        down_sum,
        small_sum[:router_cols].T,
        small_sum[router_cols : router_cols + 2],
        small_sum[router_cols + 2 : router_cols + 4],
        expert_up_grad,
        expert_down_grad,
    )


def solution(mesh):
    in_specs = (
        P("dp", "ctx", None),
        P("dp", "ctx", None),
        P(),
        P("dp", None),
        P("dp", "ctx", None),
        P(("dp", "ctx"), None),
        P(("dp", "ctx"), None),
        P(("dp", "ctx"), None),
        P(("dp", "ctx"), None),
        P(("dp", "ctx"), None),
        P(None, ("dp", "ctx")),
        P(None, ("dp", "ctx")),
        P("ctx", None, "dp"),
        P("ctx", "dp", None),
    )
    out_specs = (
        P("dp", "ctx", None),
        P("dp", "ctx", None),
        P(("dp", "ctx"), None),
        P(("dp", "ctx"), None),
        P(("dp", "ctx"), None),
        P(("dp", "ctx"), None),
        P(("dp", "ctx"), None),
        P(None, ("dp", "ctx")),
        P(None, ("dp", "ctx")),
        P("ctx", None, "dp"),
        P("ctx", "dp", None),
    )
    return jax.shard_map(
        per_device, mesh=mesh, in_specs=in_specs, out_specs=out_specs, check_vma=False
    )
```

```python
import functools
import math

import jax
import jax.numpy as jnp
from jax import lax
from jax.experimental import pallas as pl
from jax.experimental.pallas import tpu as pltpu
from jax.sharding import PartitionSpec as P

HEADS = 16
HEAD_DIM = 64

EPS = 1e-05
NEG = -1e30
SCALE = 0.125
TILE = 256
BF = jnp.bfloat16
F32 = jnp.float32
MESH = pl.DeviceIdType.MESH


def layer_norm(values, gain, shift):
    center = values - jnp.mean(values, axis=-1, keepdims=True)
    spread = jnp.mean(center * center, axis=-1, keepdims=True)
    return center * lax.rsqrt(spread + EPS) * gain + shift


def gelu_tanh(values):
    return jax.nn.gelu(values, approximate=True)


def router_heads(router_logits, route_hot, experts):
    chances = jax.nn.softmax(router_logits[:, :experts], axis=-1)
    gate = jnp.sum(chances * route_hot, axis=-1)
    mixing = jax.nn.softmax(router_logits[:, experts:], axis=-1)
    return (gate, mixing[:, 0], mixing[:, 1])


def dot_f32(left, right):
    return jnp.dot(left, right, preferred_element_type=F32)


def contract_rows(left, right):
    return lax.dot_general(left, right, (((0,), (0,)), ((), ())), preferred_element_type=F32)


def contract_cols(left, right):
    return lax.dot_general(left, right, (((1,), (1,)), ((), ())), preferred_element_type=F32)


def span(i, size):
    return pl.ds(pl.multiple_of(i * size, size), size)


class Move:
    def __init__(self, step, src, dst, after=None):
        self.step, self.src, self.dst, self.after = step, src, dst, after


def exchange(name, cid, sizes, ins, outs, build, micros=20):
    two, groups, team = sizes

    def kernel(*refs):
        in_refs, out_refs = refs[: len(ins)], refs[len(ins) : len(ins) + len(outs)]
        send_sem, recv_sem, local_sem = refs[len(ins) + len(outs) :]
        c = lax.axis_index("dp")
        i = lax.axis_index("ctx")
        g, t = lax.div(i, team), lax.rem(i, team)

        def device(step):
            dc, dg, dt = step
            return (
                lax.rem(c + dc, two),
                lax.rem(g + dg, groups) * team + lax.rem(t + dt, team),
            )

        locals_, moves = build((c, g, t), in_refs, out_refs)
        steps = sorted({m.step for m in moves})
        greet = sorted(
            set(steps) | {((-a) % two, (-b) % groups, (-d) % team) for a, b, d in steps}
        )
        barrier = pltpu.get_barrier_semaphore()
        for step in greet:
            pl.semaphore_signal(barrier, inc=1, device_id=device(step), device_id_type=MESH)
        pl.semaphore_wait(barrier, len(greet))

        copies = {}
        arrived = set()
        for k, (src, dst) in enumerate(locals_):
            copies[("local", k)] = pltpu.make_async_copy(src, dst, local_sem.at[k])
        for k, m in enumerate(moves):
            copies[k] = pltpu.make_async_remote_copy(
                src_ref=m.src,
                dst_ref=m.dst,
                send_sem=send_sem.at[k],
                recv_sem=recv_sem.at[k],
                device_id=device(m.step),
                device_id_type=MESH,
            )
        for k, m in enumerate(moves):
            if m.after is None:
                copies[k].start()
        for k in range(len(locals_)):
            copies[("local", k)].start()
        for k, m in enumerate(moves):
            if m.after is not None:
                if m.after not in arrived:
                    arrived.add(m.after)
                    if isinstance(m.after, tuple):
                        copies[m.after].wait()
                    else:
                        copies[m.after].wait_recv()
                copies[k].start()
        for k in range(len(locals_)):
            if ("local", k) not in arrived:
                copies[("local", k)].wait()
        for k in range(len(moves)):
            if k not in arrived:
                copies[k].wait_recv()
        for k in range(len(moves)):
            copies[k].wait_send()

    count = []

    def trace_counts():
        class Probe:
            def __getattr__(self, name):
                return self

            def __getitem__(self, index):
                return self

        locals_, moves = build((0, 0, 0), [Probe() for _ in ins], [Probe() for _ in outs])
        count.extend((len(locals_), len(moves)))

    trace_counts()
    return pl.pallas_call(
        kernel,
        name=name,
        out_shape=tuple(jax.ShapeDtypeStruct(s, d) for s, d in outs),
        in_specs=[pl.BlockSpec(memory_space=pl.ANY)] * len(ins),
        out_specs=tuple(pl.BlockSpec(memory_space=pl.ANY) for _ in outs),
        scratch_shapes=[
            pltpu.SemaphoreType.DMA((max(1, count[1]),)),
            pltpu.SemaphoreType.DMA((max(1, count[1]),)),
            pltpu.SemaphoreType.DMA((max(1, count[0]),)),
        ],
        compiler_params=pltpu.CompilerParams(collective_id=cid, has_side_effects=True),
        cost_estimate=pl.CostEstimate(
            flops=0, bytes_accessed=int(micros * 3.0e6), transcendentals=0
        ),
    )(*ins)


def mask_of(kt, key_place, query_place, query_low):
    return (key_place <= query_place) & (key_place >= query_low)


def key_places(sorted_rows, kt, place_ref):
    if sorted_rows:
        return lax.broadcasted_iota(jnp.int32, (TILE, TILE), 0) + kt * TILE
    return place_ref[pl.ds(pl.multiple_of(kt * TILE, TILE), TILE), :]


def attend_kernel(
    sorted_rows, bounds, meta_ref, place_ref, q_ref, rows_ref, kvt_ref, out_ref, lse_ref
):
    step = pl.program_id(0)
    queries = q_ref[...]
    place, low = meta_ref[0:1, :], meta_ref[1:2, :]

    def body(kt, carry):
        peak, total, acc = carry
        at = pl.ds(pl.multiple_of(kt * TILE, TILE), TILE)
        scores = dot_f32(rows_ref[at, :], queries)
        allowed = mask_of(kt, key_places(sorted_rows, kt, place_ref), place, low)
        scores = jnp.where(allowed, scores, NEG)
        new_peak = jnp.maximum(peak, jnp.max(scores, axis=0, keepdims=True))
        weights = jnp.exp(scores - new_peak)
        fade = jnp.exp(peak - new_peak)
        total = total * fade + jnp.sum(weights, axis=0, keepdims=True)
        acc = acc * fade + dot_f32(kvt_ref[HEAD_DIM:, at], weights.astype(BF))
        return new_peak, total, acc

    start = (
        jnp.full((1, TILE), NEG, F32),
        jnp.zeros((1, TILE), F32),
        jnp.zeros((HEAD_DIM, TILE), F32),
    )
    peak, total, acc = lax.fori_loop(bounds[step, 0], bounds[step, 1], body, start)
    out_ref[...] = acc / total
    lse_ref[...] = peak + jnp.log(total)


def attend_back_kernel(
    sorted_rows,
    tiles,
    bounds,
    meta_ref,
    place_ref,
    q_ref,
    do_ref,
    out_ref,
    lse_ref,
    rows_ref,
    kvt_ref,
    dq_ref,
    dkv_ref,
    acc_ref,
):
    step = pl.program_id(0)

    @pl.when(step == 0)
    def _():
        acc_ref[...] = jnp.zeros_like(acc_ref)

    queries, flows = q_ref[...], do_ref[...]
    place, low = meta_ref[0:1, :], meta_ref[1:2, :]
    log_total = lse_ref[...]
    delta = jnp.sum(flows[HEAD_DIM:, :].astype(F32) * out_ref[...], axis=0, keepdims=True)

    def body(kt, dq):
        at = pl.ds(pl.multiple_of(kt * TILE, TILE), TILE)
        rows = rows_ref[at, :]
        scores = dot_f32(rows, queries)
        allowed = mask_of(kt, key_places(sorted_rows, kt, place_ref), place, low)
        chances = jnp.exp(jnp.where(allowed, scores - log_total, NEG))
        flow = dot_f32(rows, flows)
        score_grad = (chances * (flow - delta)).astype(BF)
        dq = dq + dot_f32(kvt_ref[:HEAD_DIM, at], score_grad)
        acc_ref[:HEAD_DIM, at] += contract_cols(queries[:HEAD_DIM, :], score_grad)
        acc_ref[HEAD_DIM:, at] += contract_cols(flows[HEAD_DIM:, :], chances.astype(BF))
        return dq

    dq = lax.fori_loop(
        bounds[step, 0], bounds[step, 1], body, jnp.zeros((HEAD_DIM, TILE), F32)
    )
    dq_ref[...] = (dq * SCALE).astype(BF)

    @pl.when(step == tiles - 1)
    def _():
        dkv_ref[...] = acc_ref[...].astype(BF)


def attention_specs(length, query_length):
    def whole(shape):
        return pl.BlockSpec(shape, lambda i: (0, 0))

    def tile(rows):
        return pl.BlockSpec((rows, TILE), lambda i: (0, i))

    return whole, tile


def attend(sorted_rows, bounds, meta, place_col, q_pad, kv_rows, kv_t):
    length, query_length = kv_rows.shape[0], q_pad.shape[1]
    whole, tile = attention_specs(length, query_length)
    return pl.pallas_call(
        functools.partial(attend_kernel, sorted_rows),
        name="attend",
        grid=(query_length // TILE,),
        in_specs=[
            pl.BlockSpec(memory_space=pltpu.SMEM),
            tile(8),
            whole(place_col.shape),
            tile(2 * HEAD_DIM),
            whole((length, 2 * HEAD_DIM)),
            whole((2 * HEAD_DIM, length)),
        ],
        out_specs=(tile(HEAD_DIM), tile(1)),
        out_shape=(
            jax.ShapeDtypeStruct((HEAD_DIM, query_length), F32),
            jax.ShapeDtypeStruct((1, query_length), F32),
        ),
        compiler_params=pltpu.CompilerParams(vmem_limit_bytes=40 * 2**20),
    )(bounds, meta, place_col, q_pad, kv_rows, kv_t)


def attend_back(sorted_rows, bounds, meta, place_col, q_pad, do_pad, out, lse, kv_rows, kv_t):
    length, query_length = kv_rows.shape[0], q_pad.shape[1]
    whole, tile = attention_specs(length, query_length)
    return pl.pallas_call(
        functools.partial(attend_back_kernel, sorted_rows, query_length // TILE),
        name="attend_back",
        grid=(query_length // TILE,),
        in_specs=[
            pl.BlockSpec(memory_space=pltpu.SMEM),
            tile(8),
            whole(place_col.shape),
            tile(2 * HEAD_DIM),
            tile(2 * HEAD_DIM),
            tile(HEAD_DIM),
            tile(1),
            whole((length, 2 * HEAD_DIM)),
            whole((2 * HEAD_DIM, length)),
        ],
        out_specs=(tile(HEAD_DIM), whole((2 * HEAD_DIM, length))),
        out_shape=(
            jax.ShapeDtypeStruct((HEAD_DIM, query_length), BF),
            jax.ShapeDtypeStruct((2 * HEAD_DIM, length), BF),
        ),
        scratch_shapes=[pltpu.VMEM((2 * HEAD_DIM, length), F32)],
        compiler_params=pltpu.CompilerParams(vmem_limit_bytes=40 * 2**20),
    )(bounds, meta, place_col, q_pad, do_pad, out, lse, kv_rows, kv_t)


BLOCK = 64


def pick_pair(load, table, d):
    first, second = table[2 * d], table[2 * d + 1]
    left = load(lax.div(first, 2))
    right = load(lax.div(second, 2))
    lane = lax.broadcasted_iota(jnp.int32, left.shape, 1)
    left = jnp.where(lax.rem(first, 2) == 0, left, pltpu.roll(left, BLOCK, 1))
    right = jnp.where(lax.rem(second, 2) == 1, right, pltpu.roll(right, BLOCK, 1))
    return jnp.where(lane < BLOCK, left, right)


def column_block(ref, k, per):
    return ref[lax.div(k, per), :, span(lax.rem(k, per), 128)].astype(F32)


def sorted_attend_kernel(
    bounds, inverse, order, meta_ref, parts_ref,
    low_ref, out_ref, lse_ref, q_ref, kvt_ref, rows_ref,
):
    step = pl.program_id(0)
    length = q_ref.shape[1]
    per = parts_ref.shape[2] // 128

    @pl.when(step == 0)
    def _():
        def place(d, carry):
            tile = pick_pair(lambda k: column_block(parts_ref, k, per), inverse, d)
            at = span(d, 128)
            q_ref[:HEAD_DIM, at] = (tile[:HEAD_DIM] * SCALE).astype(BF)
            q_ref[HEAD_DIM:, at] = jnp.zeros((HEAD_DIM, 128), BF)
            kvt_ref[:, at] = tile[HEAD_DIM:].astype(BF)
            rows_ref[at, :] = tile[HEAD_DIM:].T.astype(BF)
            return carry

        lax.fori_loop(0, length // 128, place, 0)

    here = span(step, TILE)
    queries = q_ref[:, here]
    place, low = meta_ref[0:1, :], meta_ref[1:2, :]

    def body(kt, carry):
        peak, total, acc = carry
        at = span(kt, TILE)
        scores = dot_f32(rows_ref[at, :], queries)
        allowed = mask_of(kt, key_places(True, kt, None), place, low)
        scores = jnp.where(allowed, scores, NEG)
        new_peak = jnp.maximum(peak, jnp.max(scores, axis=0, keepdims=True))
        weights = jnp.exp(scores - new_peak)
        fade = jnp.exp(peak - new_peak)
        total = total * fade + jnp.sum(weights, axis=0, keepdims=True)
        acc = acc * fade + dot_f32(kvt_ref[HEAD_DIM:, at], weights.astype(BF))
        return new_peak, total, acc

    start = (
        jnp.full((1, TILE), NEG, F32),
        jnp.zeros((1, TILE), F32),
        jnp.zeros((HEAD_DIM, TILE), F32),
    )
    peak, total, acc = lax.fori_loop(bounds[step, 0], bounds[step, 1], body, start)
    out_ref[:, here] = acc / total
    lse_ref[:, here] = peak + jnp.log(total)

    @pl.when(step == length // TILE - 1)
    def _():
        def home(d, carry):
            tile = pick_pair(lambda k: out_ref[:, span(k, 128)], order, d)
            low_ref[lax.div(d, per), :, span(lax.rem(d, per), 128)] = tile.astype(BF)
            return carry

        lax.fori_loop(0, length // 128, home, 0)


def sorted_back_kernel(
    bounds, inverse, order, meta_ref, flow_ref, out_ref, lse_ref, q_ref, kvt_ref, rows_ref,
    grad_ref, do_ref, dq_ref, acc_ref,
):
    step = pl.program_id(0)
    length = q_ref.shape[1]
    per = grad_ref.shape[3] // 128

    @pl.when(step == 0)
    def _():
        acc_ref[...] = jnp.zeros_like(acc_ref)

        def place(d, carry):
            tile = pick_pair(lambda k: flow_ref[k].astype(F32), inverse, d)
            at = span(d, 128)
            do_ref[:HEAD_DIM, at] = jnp.zeros((HEAD_DIM, 128), BF)
            do_ref[HEAD_DIM:, at] = tile.astype(BF)
            return carry

        lax.fori_loop(0, length // 128, place, 0)

    here = span(step, TILE)
    queries, flows = q_ref[:, here], do_ref[:, here]
    place, low = meta_ref[0:1, :], meta_ref[1:2, :]
    log_total = lse_ref[:, here]
    delta = jnp.sum(flows[HEAD_DIM:, :].astype(F32) * out_ref[:, here], axis=0, keepdims=True)

    def body(kt, dq):
        at = span(kt, TILE)
        rows = rows_ref[at, :]
        scores = dot_f32(rows, queries)
        allowed = mask_of(kt, key_places(True, kt, None), place, low)
        chances = jnp.exp(jnp.where(allowed, scores - log_total, NEG))
        flow = dot_f32(rows, flows)
        score_grad = (chances * (flow - delta)).astype(BF)
        dq = dq + dot_f32(kvt_ref[:HEAD_DIM, at], score_grad)
        acc_ref[:HEAD_DIM, at] += contract_cols(queries[:HEAD_DIM, :], score_grad)
        acc_ref[HEAD_DIM:, at] += contract_cols(flows[HEAD_DIM:, :], chances.astype(BF))
        return dq

    dq = lax.fori_loop(
        bounds[step, 0], bounds[step, 1], body, jnp.zeros((HEAD_DIM, TILE), F32)
    )
    dq_ref[:, here] = dq * SCALE

    @pl.when(step == length // TILE - 1)
    def _():
        def home(d, carry):
            at = span(lax.rem(d, per), 128)
            tile = pick_pair(lambda k: dq_ref[:, span(k, 128)], order, d)
            grad_ref[lax.div(d, per), 0, :, at] = tile.astype(BF)
            tile = pick_pair(lambda k: acc_ref[:, span(k, 128)], order, d).astype(BF)
            grad_ref[lax.div(d, per), 1, :, at] = tile[:HEAD_DIM]
            grad_ref[lax.div(d, per), 2, :, at] = tile[HEAD_DIM:]
            return carry

        lax.fori_loop(0, length // 128, home, 0)


def fixed(shape):
    return pl.BlockSpec(shape, lambda i: (0,) * len(shape))


def sorted_attend(bounds, inverse, order, meta, parts):
    groups, _, columns = parts.shape
    length = groups * columns
    shapes = (
        ((groups, HEAD_DIM, columns), BF),
        ((HEAD_DIM, length), F32),
        ((1, length), F32),
        ((2 * HEAD_DIM, length), BF),
        ((2 * HEAD_DIM, length), BF),
        ((length, 2 * HEAD_DIM), BF),
    )
    return pl.pallas_call(
        sorted_attend_kernel,
        name="attend",
        grid=(length // TILE,),
        in_specs=[pl.BlockSpec(memory_space=pltpu.SMEM)] * 3
        + [pl.BlockSpec((8, TILE), lambda i: (0, i)), fixed(parts.shape)],
        out_specs=tuple(fixed(s) for s, _ in shapes),
        out_shape=tuple(jax.ShapeDtypeStruct(s, d) for s, d in shapes),
        compiler_params=pltpu.CompilerParams(vmem_limit_bytes=40 * 2**20),
    )(bounds, inverse, order, meta, parts)


def sorted_back(bounds, inverse, order, meta, flow, out, lse, q_pad, kv_t, kv_rows, groups):
    length = out.shape[1]
    grad = (groups, 3, HEAD_DIM, length // groups)
    return pl.pallas_call(
        sorted_back_kernel,
        name="attend_back",
        grid=(length // TILE,),
        in_specs=[pl.BlockSpec(memory_space=pltpu.SMEM)] * 3
        + [pl.BlockSpec((8, TILE), lambda i: (0, i))]
        + [fixed(a.shape) for a in (flow, out, lse, q_pad, kv_t, kv_rows)],
        out_specs=fixed(grad),
        out_shape=jax.ShapeDtypeStruct(grad, BF),
        scratch_shapes=[
            pltpu.VMEM((2 * HEAD_DIM, length), BF),
            pltpu.VMEM((HEAD_DIM, length), F32),
            pltpu.VMEM((2 * HEAD_DIM, length), F32),
        ],
        compiler_params=pltpu.CompilerParams(vmem_limit_bytes=40 * 2**20),
    )(bounds, inverse, order, meta, flow, out, lse, q_pad, kv_t, kv_rows)


def normalize(values):
    center = values - jnp.mean(values, axis=-1, keepdims=True)
    spread = jnp.mean(center * center, axis=-1, keepdims=True)
    scale = lax.rsqrt(spread + EPS)
    return center * scale, scale


def mid_kernel(
    experts, team, member, att, wo, x, vec, rw, route, cot,
    second, dgrad, send_s, send_g, sel, mixes, middle_own, prob_own, hot_own, second_own, att_own,
    egrad,
):
    rows = middle_own.shape[0]
    slots = send_s.shape[1]
    groups = send_s.shape[0]
    capacity = slots // team
    lane = lax.broadcasted_iota(jnp.int32, (rows, 128), 1)
    row = lax.broadcasted_iota(jnp.int32, (rows, rows), 0)
    col = lax.broadcasted_iota(jnp.int32, (rows, rows), 1)
    me = member[0]

    def block(b, carry):
        at = span(b, rows)
        part = att[:, at]
        middle = x[at, :].astype(F32) + contract_rows(part, wo[...])
        hat, _ = normalize(middle)
        low = (hat * vec[5:6, :] + vec[7:8, :]).astype(BF)
        second[at, :] = low
        logits = dot_f32(low, rw[...])
        is_expert = lane < experts
        is_mix = (lane >= experts) & (lane < experts + 2)
        pe = jnp.where(is_expert, logits, NEG)
        pe = jnp.exp(pe - jnp.max(pe, axis=1, keepdims=True))
        pe = pe / jnp.sum(pe, axis=1, keepdims=True)
        pm = jnp.where(is_mix, logits, NEG)
        pm = jnp.exp(pm - jnp.max(pm, axis=1, keepdims=True))
        pm = pm / jnp.sum(pm, axis=1, keepdims=True)
        route_row = jnp.broadcast_to(route[b][0:1, :], (rows, rows))
        route_col = jnp.sum(jnp.where(row == col, route_row, 0), axis=1, keepdims=True)
        hot = lane == route_col
        gate = jnp.sum(jnp.where(hot, pe, 0.0), axis=1, keepdims=True)
        mix0 = jnp.sum(jnp.where(lane == experts, pm, 0.0), axis=1, keepdims=True)
        mix1 = jnp.sum(jnp.where(lane == experts + 1, pm, 0.0), axis=1, keepdims=True)
        scaled = mix1 * gate
        flow = cot[at, :].astype(F32)
        dgrad[at, :] = (flow * mix0).astype(BF)
        egrad[at, :] = (flow * scaled).astype(BF)
        mixes[at, :] = jnp.where(lane == 0, mix0, jnp.where(lane == 1, scaled, 0.0))
        same = (route_row == route_col) & (col < row)
        rank = jnp.sum(jnp.where(same, 1, 0), axis=1, keepdims=True)
        group = lax.div(route_col, team)
        mine = lax.rem(route_col, team) == me
        target = jnp.where(mine, group * slots + b * capacity + rank, groups * slots)
        slot = lax.broadcasted_iota(jnp.int32, (rows, groups * slots), 1)
        sel[at, :] = jnp.where(slot == target, 1.0, 0.0).astype(BF)

        @pl.when(b == me)
        def _():
            middle_own[...] = middle
            prob_own[...] = jnp.where(is_expert, pe, jnp.where(is_mix, pm, 0.0))
            hot_own[...] = jnp.where(hot, 1.0, 0.0)
            second_own[...] = low
            att_own[...] = part

        return carry

    lax.fori_loop(0, team, block, 0)
    send_s[...] = contract_rows(sel[...], second[...]).astype(BF).reshape(send_s.shape)
    send_g[...] = contract_rows(sel[...], egrad[...]).astype(BF).reshape(send_g.shape)


def between(experts, sizes, slots, member, att, wo, x, vec, rw, route, cot):
    two, groups, team = sizes
    group_rows, width = x.shape
    rows = group_rows // team
    shapes = (
        ((group_rows, width), BF),
        ((group_rows, width), BF),
        ((groups, slots, width), BF),
        ((groups, slots, width), BF),
        ((group_rows, groups * slots), BF),
        ((group_rows, 128), F32),
        ((rows, width), F32),
        ((rows, 128), F32),
        ((rows, 128), F32),
        ((rows, width), BF),
        ((width, rows), BF),
    )
    inside = pl.BlockSpec(memory_space=pltpu.VMEM)
    return pl.pallas_call(
        functools.partial(mid_kernel, experts, team),
        name="between",
        in_specs=[pl.BlockSpec(memory_space=pltpu.SMEM)] + [inside] * 7,
        out_specs=tuple(inside for _ in shapes),
        out_shape=tuple(jax.ShapeDtypeStruct(s, d) for s, d in shapes),
        scratch_shapes=[pltpu.VMEM((group_rows, width), BF)],
        compiler_params=pltpu.CompilerParams(vmem_limit_bytes=48 * 2**20),
    )(member, att, wo, x, vec, rw, route, cot)


def turn_kernel(
    experts, layer_sum, second_sum, sums, middle, prob, hot, second, att, cot, rw, wo, vec,
    layer, middle_grad, flow_t, out_term, small_t,
):
    rows = middle.shape[0]
    lane = lax.broadcasted_iota(jnp.int32, (rows, 128), 1)
    layer[...] = (middle[...] + layer_sum[...]).astype(BF)
    chances, chosen = prob[...], hot[...]
    s0, s1 = sums[:, 0:1], sums[:, 1:2]
    mix1 = jnp.sum(jnp.where(lane == experts + 1, chances, 0.0), axis=1, keepdims=True)
    gate = jnp.sum(chances * chosen, axis=1, keepdims=True)
    pull_gate = s1 * mix1
    pulls = jnp.where(lane == experts, s0, jnp.where(lane == experts + 1, s1 * gate, 0.0))
    mean_pull = jnp.sum(chances * pulls, axis=1, keepdims=True)
    logit_grad = chances * jnp.where(
        lane < experts, pull_gate * (chosen - gate), pulls - mean_pull
    )
    logit_grad = jnp.where(lane < experts + 2, logit_grad, 0.0).astype(BF)
    second_grad = second_sum[...] + contract_cols(logit_grad, rw[...])
    hat, scale = normalize(middle[...])
    pull = second_grad * vec[5:6, :]
    part = scale * (
        pull
        - jnp.mean(pull, axis=-1, keepdims=True)
        - hat * jnp.mean(pull * hat, axis=-1, keepdims=True)
    )
    grad = cot[...].astype(F32) + part
    middle_grad[...] = grad
    branch = grad.astype(BF)
    width = wo.shape[0]

    def tile(n, carry):
        at = span(n, TILE)
        flow_t[at, :] = contract_cols(wo[at, :], branch).astype(BF)
        out_term[at, :] = dot_f32(att[at, :], branch).astype(BF)
        return carry

    lax.fori_loop(0, width // TILE, tile, 0)
    used = small_t.shape[0]
    routed = contract_rows(logit_grad, second[...])[:used, :]
    which = lax.broadcasted_iota(jnp.int32, routed.shape, 0)
    gain = jnp.sum(second_grad * hat, axis=0, keepdims=True)
    bias = jnp.sum(second_grad, axis=0, keepdims=True)
    small_t[...] = jnp.where(
        which == experts + 3, gain, jnp.where(which == experts + 5, bias, routed)
    )


def turn(experts, layer_sum, second_sum, sums, middle, prob, hot, second, att, cot, rw, wo, vec):
    rows, width = middle.shape
    used = -(-(experts + 6) // 8) * 8
    shapes = (
        ((rows, width), BF),
        ((rows, width), F32),
        ((width, rows), BF),
        ((width, width), BF),
        ((used, width), F32),
    )
    inside = pl.BlockSpec(memory_space=pltpu.VMEM)
    return pl.pallas_call(
        functools.partial(turn_kernel, experts),
        name="turn",
        in_specs=[inside] * 12,
        out_specs=tuple(inside for _ in shapes),
        out_shape=tuple(jax.ShapeDtypeStruct(s, d) for s, d in shapes),
        compiler_params=pltpu.CompilerParams(vmem_limit_bytes=40 * 2**20),
    )(layer_sum, second_sum, sums, middle, prob, hot, second, att, cot, rw, wo, vec)


def row_sum_kernel(left, right, out):
    out[0] = contract_rows(left[...], right[...])


def row_sum(left, right, tile):
    many, high = left.shape
    wide = right.shape[1]
    return pl.pallas_call(
        row_sum_kernel,
        name="row_sum",
        grid=(high // tile,),
        in_specs=[pl.BlockSpec((many, tile), lambda i: (0, i)), fixed(right.shape)],
        out_specs=pl.BlockSpec((1, tile, wide), lambda i: (0, i, 0)),
        out_shape=jax.ShapeDtypeStruct((1, high, wide), F32),
        compiler_params=pltpu.CompilerParams(vmem_limit_bytes=40 * 2**20),
        cost_estimate=pl.CostEstimate(
            flops=2 * many * high * wide, bytes_accessed=4 * high * wide, transcendentals=0
        ),
    )(left, right)


class Net:
    def __init__(self, sizes, send_sem, recv_sem):
        self.two, self.groups, self.team = sizes
        self.send_sem, self.recv_sem = send_sem, recv_sem
        self.c = lax.axis_index("dp")
        i = lax.axis_index("ctx")
        self.g, self.t = lax.div(i, self.team), lax.rem(i, self.team)
        self.group_steps = [(0, k, 0) for k in range(1, self.groups)]
        self.team_steps = [(0, 0, k) for k in range(1, self.team)]
        self.swap = (1, 0, 0)
        self.started = []

    def device(self, step):
        dc, dg, dt = step
        return (
            lax.rem(self.c + dc, self.two),
            lax.rem(self.g + dg, self.groups) * self.team + lax.rem(self.t + dt, self.team),
        )

    def greet(self):
        barrier = pltpu.get_barrier_semaphore()
        steps = self.group_steps + self.team_steps + [self.swap]
        for step in steps:
            pl.semaphore_signal(barrier, inc=1, device_id=self.device(step), device_id_type=MESH)
        pl.semaphore_wait(barrier, len(steps))

    def send(self, src, dst, step):
        k = len(self.started)
        copy = pltpu.make_async_remote_copy(
            src_ref=src,
            dst_ref=dst,
            send_sem=self.send_sem.at[k],
            recv_sem=self.recv_sem.at[k],
            device_id=self.device(step),
            device_id_type=MESH,
        )
        copy.start()
        self.started.append(copy)
        return copy

    def group_to(self, step):
        return lax.rem(self.g + step[1], self.groups)

    def group_from(self, step):
        return lax.rem(self.g + self.groups - step[1], self.groups)

    def team_to(self, step):
        return lax.rem(self.t + step[2], self.team)

    def team_from(self, step):
        return lax.rem(self.t + self.team - step[2], self.team)

    def close(self):
        for copy in self.started:
            copy.wait_send()


def arrive(copies):
    for copy in copies:
        copy.wait_recv()


class Local:
    def __init__(self, sem):
        self.sem, self.count, self.open = sem, 0, []

    def copy(self, src, dst):
        made = pltpu.make_async_copy(src, dst, self.sem.at[self.count])
        made.start()
        self.count += 1
        self.open.append(made)
        return made

    def wait(self, *copies):
        for made in copies or tuple(self.open):
            made.wait()
            self.open = [other for other in self.open if other is not made]


def start_kernel(sizes, *refs):
    tokens, cot, own, up, down, out, route = refs[:7]
    token_o, cot_o, heads_o, normed_o, weight_o, vec_o, out_o, ff_o, route_o = refs[7:16]
    stage, weights, tokens_v, normed, mixed, heads, out_v, send_sem, recv_sem, local_sem = refs[16:]
    net, local = Net(sizes, send_sem, recv_sem), Local(local_sem)
    c, g, t = net.c, net.g, net.t
    two, groups, team = sizes
    rows, width = tokens.shape
    used = own.shape[2] - 128
    own_stage = local.copy(own.at[t], stage.at[t])
    own_tokens = local.copy(tokens, tokens_v.at[t])
    own_out = local.copy(out, out_v.at[g])
    local.copy(cot, cot_o.at[t])
    local.copy(up.at[t], ff_o.at[0, t])
    local.copy(down, ff_o.at[1])
    local.copy(route, route_o.at[t])
    net.greet()
    staged = [net.send(own.at[net.team_to(s)], stage.at[t], s) for s in net.team_steps]
    told = [net.send(tokens, tokens_v.at[t], s) for s in net.team_steps]
    later = [net.send(route, route_o.at[t], s) for s in net.team_steps]
    later += [net.send(up.at[net.team_to(s)], ff_o.at[0, t], s) for s in net.team_steps]
    local.wait(own_stage)
    arrive(staged)
    spread = [net.send(stage, weights.at[c, g], s) for s in net.group_steps]
    swapped = [net.send(stage, weights.at[c, g], net.swap)]
    mine = local.copy(stage, weights.at[c, g])
    spread_out = [net.send(out, out_v.at[g], s) for s in net.group_steps]
    later += [net.send(cot, cot_o.at[t], s) for s in net.team_steps]
    local.wait(own_tokens)
    arrive(told)
    local.copy(tokens_v, token_o)
    local.wait(mine)
    for copy, s in zip(spread, net.group_steps):
        copy.wait_recv()
        view = weights.at[c, net.group_from(s)]
        swapped.append(net.send(view, view, net.swap))
    arrive(swapped)
    local.copy(weights, weight_o)

    small = weights[:, :, :, :, used:].reshape(width, 128).astype(F32).T
    vec_o[...] = small[120:, :]

    def norm(b, carry):
        hat, _ = normalize(tokens_v[b].astype(F32))
        normed[b] = (hat * vec_o[4:5, :] + vec_o[6:7, :]).astype(BF)
        return carry

    lax.fori_loop(0, team, norm, 0)
    local.copy(normed, normed_o)
    group_rows = rows * team
    per = used // 3 // 128
    pair = 128 // HEAD_DIM
    for n in range(used // 128):
        columns = weights[:, :, :, :, n * 128 : (n + 1) * 128].reshape(width, 128)
        made = dot_f32(normed[...].reshape(group_rows, width), columns).T.astype(BF)
        at = (n % per) * pair
        mixed[n // per, at : at + pair] = made.reshape(pair, HEAD_DIM, group_rows)
    given = [net.send(mixed.at[:, net.group_to(s)], heads.at[g], s) for s in net.group_steps]
    local.wait(local.copy(mixed.at[:, g], heads.at[g]))

    local.wait(own_out)
    arrive(spread_out)
    local.copy(out_v, out_o.at[c, :, t])
    swapped = [net.send(out_v, out_o.at[c, :, t], net.swap)]
    outed = [net.send(out_v, out_o.at[c, :, t], s) for s in net.team_steps]
    for copy, s in zip(outed, net.team_steps):
        copy.wait_recv()
        view = out_o.at[c, :, net.team_from(s)]
        swapped.append(net.send(view, view, net.swap))
    arrive(given)
    local.copy(heads, heads_o)
    arrive(swapped + later)
    local.wait()
    net.close()


def start(sizes, tokens, cot, own, up, down, out, route):
    two, groups, team = sizes
    rows, width = tokens.shape
    wr, cols = own.shape[1], own.shape[2]
    used = cols - 128
    head = (3, groups, HEAD_DIM, team * rows)
    shapes = (
        ((team, rows, width), BF),
        ((team, rows, width), BF),
        ((groups, 3, HEAD_DIM, team * rows), BF),
        ((team, rows, width), BF),
        ((two, groups, team, wr, cols), BF),
        ((8, width), F32),
        ((two, groups, team, wr, width), BF),
        ((2,) + up.shape, BF),
        ((team,) + route.shape, jnp.int32),
    )
    anywhere = pl.BlockSpec(memory_space=pl.ANY)
    inside = pl.BlockSpec(memory_space=pltpu.VMEM)
    count = 6 * (team - 1) + 4 * (groups - 1) + 2 + (team - 1)
    return pl.pallas_call(
        functools.partial(start_kernel, sizes),
        name="start",
        out_shape=tuple(jax.ShapeDtypeStruct(s, d) for s, d in shapes),
        in_specs=[anywhere] * 7,
        out_specs=tuple(inside if n == 5 else anywhere for n in range(9)),
        scratch_shapes=[
            pltpu.VMEM((team, wr, cols), BF),
            pltpu.VMEM((two, groups, team, wr, cols), BF),
            pltpu.VMEM((team, rows, width), BF),
            pltpu.VMEM((team, rows, width), BF),
            pltpu.VMEM(head, BF),
            pltpu.VMEM((groups, 3, HEAD_DIM, team * rows), BF),
            pltpu.VMEM((groups, wr, width), BF),
            pltpu.SemaphoreType.DMA((count,)),
            pltpu.SemaphoreType.DMA((count,)),
            pltpu.SemaphoreType.DMA((14,)),
        ],
        compiler_params=pltpu.CompilerParams(
            collective_id=12, has_side_effects=True, vmem_limit_bytes=32 * 2**20
        ),
        cost_estimate=pl.CostEstimate(flops=0, bytes_accessed=150_000_000, transcendentals=0),
    )(tokens, cot, own, up, down, out, route)


def end_kernel(sizes, experts, *refs):
    groups = sizes[1]
    parts, refs = refs[:groups], refs[groups:]
    weight, normed, tokens, vec, middle_grad, small, up, out = refs[:8]
    grad_o, qkv_o, up_o, out_o, small_o = refs[8:13]
    (
        mixed, turned, weights, normed_v, give, got, zsend, zrecv, npart, nrecv, qsend, qrecv,
        out_r, small_a, small_b, small_c, send_sem, recv_sem, local_sem,
    ) = refs[13:]
    net, local = Net(sizes, send_sem, recv_sem), Local(local_sem)
    c, g, t = net.c, net.g, net.t
    team = sizes[2]
    rows, width = tokens.shape
    group_rows, used = turned.shape
    for k, part in enumerate(parts):
        local.copy(part, mixed.at[:, net.group_from((0, k, 0))])
    local.copy(normed, normed_v)
    local.copy(weight, weights)
    local.copy(up.at[t], up_o.at[t])
    local.copy(out.at[g], out_r.at[g])
    net.greet()
    later = [net.send(up.at[net.team_to(s)], up_o.at[t], s) for s in net.team_steps]
    local.wait()
    per = used // 3 // 128
    pair = 128 // HEAD_DIM
    for n in range(used // 128):
        at = (n % per) * pair
        block = mixed[n // per, at : at + pair].reshape(128, group_rows)
        turned[:, n * 128 : (n + 1) * 128] = block.astype(F32).T.astype(BF)

    half = width // 2
    tile = 128

    def term(core, n):
        at = pl.ds(pl.multiple_of(core * half + n * tile, tile), tile)
        left = normed_v[:, :, at].reshape(group_rows, tile)
        return contract_rows(left, turned[...])

    def giving(n, carry):
        give[span(n, tile), :] = term(lax.rem(c + 1, 2), n).astype(BF)
        return carry

    lax.fori_loop(0, half // tile, giving, 0)
    crossed = net.send(give, got, net.swap)

    def part_of(r, carry):
        columns = weights[:, :, :, :, :used].reshape(width, used)
        npart[r] = contract_cols(turned[span(r, rows), :], columns).astype(BF)
        return carry

    lax.fori_loop(0, team, part_of, 0)
    owned = [net.send(npart.at[net.team_to(s)], nrecv.at[t], s) for s in net.team_steps]
    nrecv[t] = npart[t]
    crossed.wait_recv()

    def keeping(n, carry):
        at = span(n, tile)
        zsend[at, :] = (term(c, n) + got[at, :].astype(F32)).astype(BF)
        return carry

    lax.fori_loop(0, half // tile, keeping, 0)
    deep = half // groups
    summed = [
        net.send(zsend.at[span(net.group_to(s), deep), :], zrecv.at[g], s)
        for s in net.group_steps
    ]
    outed = [net.send(out.at[net.group_to(s)], out_r.at[g], s) for s in net.group_steps]
    zrecv[g] = zsend[span(g, deep), :]

    arrive(owned)
    flow = jnp.sum(nrecv[...].astype(F32), axis=0)
    hat, scale = normalize(tokens[...].astype(F32))
    pull = flow * vec[4:5, :]
    pulled = scale * (
        pull
        - jnp.mean(pull, axis=-1, keepdims=True)
        - hat * jnp.mean(pull * hat, axis=-1, keepdims=True)
    )
    grad_o[...] = (middle_grad[...] + pulled).astype(BF)

    gain = jnp.sum(flow * hat, axis=0, keepdims=True)
    bias = jnp.sum(flow, axis=0, keepdims=True)
    which = lax.broadcasted_iota(jnp.int32, small.shape, 0)
    mine = jnp.where(
        which == experts + 2, gain, jnp.where(which == experts + 4, bias, small[...])
    )
    small_a[c] = mine
    crossing = net.send(small_a.at[c], small_a.at[c], net.swap)
    crossing.wait_recv()
    small_c[...] = small_a[0] + small_a[1]

    def columns_of(k):
        return span(c * groups + k, 128)

    moved = [
        net.send(small_c.at[:, columns_of(net.group_to(s))], small_b.at[g], s)
        for s in net.group_steps
    ]
    small_b[g] = small_c[:, columns_of(g)]
    arrive(moved)
    small_o[t] = jnp.sum(small_b[...], axis=0)
    later += [net.send(small_o.at[t], small_o.at[t], s) for s in net.team_steps]

    arrive(summed)
    qsend[...] = jnp.sum(zrecv[...].astype(F32), axis=0).astype(BF).reshape(qsend.shape)
    later += [net.send(qsend.at[net.team_to(s)], qrecv.at[t], s) for s in net.team_steps]
    qrecv[t] = qsend[t]
    arrive(outed)
    out_o[...] = jnp.sum(out_r[...].astype(F32), axis=0)
    arrive(later)
    qkv_o[...] = qrecv[...]
    net.close()


def end(sizes, experts, parts, weight, normed, tokens, vec, middle_grad, small, up, out):
    two, groups, team = sizes
    rows, width = tokens.shape
    wr = out.shape[1]
    used = 3 * groups * HEAD_DIM
    group_rows = parts[0].shape[2]
    half = width // 2
    shapes = (
        ((rows, width), BF),
        ((team, wr, used), BF),
        ((team, wr, width), BF),
        ((wr, width), F32),
        ((team, small.shape[0], 128), F32),
    )
    anywhere = pl.BlockSpec(memory_space=pl.ANY)
    inside = pl.BlockSpec(memory_space=pltpu.VMEM)
    count = 5 * (team - 1) + 3 * (groups - 1) + 2
    return pl.pallas_call(
        functools.partial(end_kernel, sizes, experts),
        name="end",
        out_shape=tuple(jax.ShapeDtypeStruct(s, d) for s, d in shapes),
        in_specs=[anywhere] * (groups + 2) + [inside] * 4 + [anywhere] * 2,
        out_specs=tuple(inside for _ in shapes),
        scratch_shapes=[
            pltpu.VMEM((3, groups, HEAD_DIM, group_rows), BF),
            pltpu.VMEM((group_rows, used), BF),
            pltpu.VMEM(weight.shape, BF),
            pltpu.VMEM(normed.shape, BF),
            pltpu.VMEM((half, used), BF),
            pltpu.VMEM((half, used), BF),
            pltpu.VMEM((half, used), BF),
            pltpu.VMEM((groups, half // groups, used), BF),
            pltpu.VMEM((team, rows, width), BF),
            pltpu.VMEM((team, rows, width), BF),
            pltpu.VMEM((team, wr, used), BF),
            pltpu.VMEM((team, wr, used), BF),
            pltpu.VMEM((groups, wr, width), BF),
            pltpu.VMEM((2,) + small.shape, F32),
            pltpu.VMEM((groups, small.shape[0], 128), F32),
            pltpu.VMEM(small.shape, F32),
            pltpu.SemaphoreType.DMA((count,)),
            pltpu.SemaphoreType.DMA((count,)),
            pltpu.SemaphoreType.DMA((groups + 4,)),
        ],
        compiler_params=pltpu.CompilerParams(
            collective_id=13, has_side_effects=True, vmem_limit_bytes=32 * 2**20
        ),
        cost_estimate=pl.CostEstimate(flops=0, bytes_accessed=120_000_000, transcendentals=0),
    )(*parts, weight, normed, tokens, vec, middle_grad, small, up, out)


def gelu_and_slope(x):
    k = math.sqrt(2.0 / math.pi)
    square = x * x
    bent = jnp.tanh(k * (x + 0.044715 * (square * x)))
    half = 0.5 * (1.0 + bent)
    slope = half + (0.5 * k) * x * (1.0 - bent * bent) * (1.0 + (3 * 0.044715) * square)
    return x * half, slope


def feed_kernel(sizes, copies_count, *refs):
    two, groups, team = sizes
    (send_s, send_g, eup_h, edown_h, second_h, dgrad_h, ff_h, sel_h, cot_h, mix_h) = refs[:10]
    (layer_o, grad_o, sums_o, active_o, hgrad_o, arr_s_o, arr_g_o, ffg_o) = refs[10:18]
    (
        arr_s, arr_g, eup, edown, second, dgrad, upw, downw, sel, cot, mix,
        slope, active, hgrad, acc, give, got_s, got_g, ret_s, ret_g, back_s, back_g,
        low, ugrad, dense, spart, lay, spa, sums, lay_r, spa_r, sums_r,
        term_give, term_got, send_sem, recv_sem, load_sem, out_sem,
    ) = refs[18:]
    c = lax.axis_index("dp")
    i = lax.axis_index("ctx")
    g, t = lax.div(i, team), lax.rem(i, team)
    width = second.shape[1]
    rows = lay.shape[1]
    hid, ehid = upw.shape[1], eup.shape[1]
    core = lax.rem(c + 1, two)

    def device(step):
        dc, dg, dt = step
        return (
            lax.rem(c + dc, two),
            lax.rem(g + dg, groups) * team + lax.rem(t + dt, team),
        )

    index = [0]

    def remote(src, dst, step):
        k = index[0]
        index[0] += 1
        assert k < copies_count
        return pltpu.make_async_remote_copy(
            src_ref=src,
            dst_ref=dst,
            send_sem=send_sem.at[k],
            recv_sem=recv_sem.at[k],
            device_id=device(step),
            device_id_type=MESH,
        )

    group_steps = [(0, k, 0) for k in range(1, groups)]
    team_steps = [(0, 0, k) for k in range(1, team)]
    swap = (1, 0, 0)
    deep = ff_h.shape[2]

    def block_of(core, k):
        return pl.ds(pl.multiple_of((core * groups + k) * deep, deep), deep)

    loads = []
    for k, (src, dst) in enumerate(
        [
            (second_h, second), (dgrad_h, dgrad), (eup_h, eup), (edown_h, edown), (sel_h, sel), (cot_h, cot), (mix_h, mix),
            (send_s.at[g], arr_s.at[c, g]), (send_g.at[g], arr_g.at[c, g]),
        ]
        + [
            (ff_h.at[k, n], weight.at[block_of(c, k), :])
            for k in range(groups)
            for n, weight in enumerate((upw, downw))
        ]
    ):
        load = pltpu.make_async_copy(src, dst, load_sem.at[k])
        load.start()
        loads.append(load)

    barrier = pltpu.get_barrier_semaphore()
    greet = group_steps + team_steps + [swap]
    for step in greet:
        pl.semaphore_signal(barrier, inc=1, device_id=device(step), device_id_type=MESH)
    pl.semaphore_wait(barrier, len(greet))

    every = []

    def launch(copy):
        copy.start()
        every.append(copy)
        return copy

    def to_groups(src, dst):
        return [
            launch(remote(src.at[lax.rem(g + s[1], groups)], dst.at[g], s)) for s in group_steps
        ]

    def source(s):
        return lax.rem(g + groups - s[1], groups)

    swap_w = [
        launch(remote(ff_h.at[k, n], weight.at[block_of(c, k), :], swap))
        for k in range(groups)
        for n, weight in enumerate((upw, downw))
    ]
    out_s = [
        launch(remote(send_s.at[lax.rem(g + s[1], groups)], arr_s.at[c, g], s))
        for s in group_steps
    ]
    swap_s = [launch(remote(send_s.at[g], arr_s.at[c, g], swap))]
    out_g = [
        launch(remote(send_g.at[lax.rem(g + s[1], groups)], arr_g.at[c, g], s))
        for s in group_steps
    ]
    swap_g = [launch(remote(send_g.at[g], arr_g.at[c, g], swap))]

    for load in loads[:2] + loads[9:]:
        load.wait()
    for copy in swap_w:
        copy.wait_recv()

    def dense_in(h, carry):
        at = span(h, TILE)
        value, bend = gelu_and_slope(dot_f32(second[...], upw[:, at]))
        low[:, at] = value.astype(BF)
        ugrad[:, at] = (bend * contract_cols(dgrad[...], downw[at, :])).astype(BF)
        return carry

    lax.fori_loop(0, hid // TILE, dense_in, 0)

    def dense_out(n, carry):
        at = span(n, TILE)
        dense[:, at] = dot_f32(low[...], downw[:, at])
        spart[:, at] = contract_cols(ugrad[...], upw[at, :])
        return carry

    lax.fori_loop(0, width // TILE, dense_out, 0)

    for load in loads[2:9]:
        load.wait()
    for copy, s in zip(out_s, group_steps):
        copy.wait_recv()
        swap_s.append(launch(remote(arr_s.at[c, source(s)], arr_s.at[c, source(s)], swap)))
    for copy in swap_s:
        copy.wait_recv()
    entries = 2 * groups * arr_s.shape[2]

    def expert_in(h, carry):
        at = span(h, TILE)
        value, bend = gelu_and_slope(dot_f32(arr_s[...].reshape(entries, width), eup[:, at]))
        active[:, at] = value.astype(BF)
        slope[:, at] = bend
        return carry

    lax.fori_loop(0, ehid // TILE, expert_in, 0)
    keeps = [
        pltpu.make_async_copy(active, active_o, out_sem.at[0]),
        pltpu.make_async_copy(arr_s, arr_s_o, out_sem.at[1]),
    ]
    for copy in keeps:
        copy.start()

    def expert_out(n, carry):
        at = span(n, TILE)
        acc[:, :, at] = dot_f32(active[...], edown[:, at]).reshape(2, entries // 2, TILE)
        return carry

    lax.fori_loop(0, width // TILE, expert_out, 0)
    give[0] = acc[core].astype(BF)
    other_s = launch(remote(give.at[0], got_s, swap))

    for copy, s in zip(out_g, group_steps):
        copy.wait_recv()
        swap_g.append(launch(remote(arr_g.at[c, source(s)], arr_g.at[c, source(s)], swap)))
    other_s.wait_recv()
    ret_s[...] = (acc[c] + got_s[...].astype(F32)).astype(BF).reshape(ret_s.shape)
    home_s = to_groups(ret_s, back_s)
    back_s[g] = ret_s[g]
    for copy in swap_g:
        copy.wait_recv()

    def expert_back(h, carry):
        at = span(h, TILE)
        pull = contract_cols(arr_g[...].reshape(entries, width), edown[at, :])
        hgrad[:, at] = (slope[:, at] * pull).astype(BF)
        return carry

    lax.fori_loop(0, ehid // TILE, expert_back, 0)
    keeps += [
        pltpu.make_async_copy(hgrad, hgrad_o, out_sem.at[2]),
        pltpu.make_async_copy(arr_g, arr_g_o, out_sem.at[3]),
    ]
    for copy in keeps[2:]:
        copy.start()

    def expert_back_out(n, carry):
        at = span(n, TILE)
        acc[:, :, at] = contract_cols(hgrad[...], eup[at, :]).reshape(2, entries // 2, TILE)
        return carry

    lax.fori_loop(0, width // TILE, expert_back_out, 0)
    give[1] = acc[core].astype(BF)
    other_g = launch(remote(give.at[1], got_g, swap))
    other_g.wait_recv()
    ret_g[...] = (acc[c] + got_g[...].astype(F32)).astype(BF).reshape(ret_g.shape)
    home_g = to_groups(ret_g, back_g)
    back_g[g] = ret_g[g]

    for copy in home_s:
        copy.wait_recv()
    slots = groups * back_s.shape[1]
    lane = lax.broadcasted_iota(jnp.int32, (rows, 128), 1)

    def join_layer(r, carry):
        at = span(r, rows)
        found = dot_f32(sel[at, :], back_s[...].reshape(slots, width))
        own = dense[at, :]
        flow = cot[at, :].astype(F32)
        mixes = mix[at, :]
        lay[r] = (mixes[:, 0:1] * own + mixes[:, 1:2] * found).astype(BF)
        plain = jnp.sum(flow * own, axis=1, keepdims=True)
        routed = jnp.sum(flow * found, axis=1, keepdims=True)
        sums[r] = jnp.where(lane == 0, plain, jnp.where(lane == 1, routed, 0.0))
        return carry

    lax.fori_loop(0, team, join_layer, 0)

    def to_team(src, dst):
        made = [launch(remote(src.at[lax.rem(t + s[2], team)], dst.at[t], s)) for s in team_steps]
        dst[t] = src[t]
        return made

    team_copies = to_team(lay, lay_r) + to_team(sums, sums_r)

    for copy in home_g:
        copy.wait_recv()

    def join_grad(r, carry):
        at = span(r, rows)
        found = dot_f32(sel[at, :], back_g[...].reshape(slots, width))
        spa[r] = (spart[at, :] + found).astype(BF)
        return carry

    lax.fori_loop(0, team, join_grad, 0)
    team_copies += to_team(spa, spa_r)

    half = hid // 2
    term_tile = 128

    def down_term(base, n):
        at = pl.ds(pl.multiple_of(base + n * term_tile, term_tile), term_tile)
        return contract_rows(low[:, at], dgrad[...])

    def up_term(base, n):
        at = pl.ds(pl.multiple_of(base + n * term_tile, term_tile), term_tile)
        return contract_rows(second[:, at], ugrad[...])

    terms = []
    for k, (term, size) in enumerate(((down_term, half), (up_term, width // 2))):

        def giving(n, carry, k=k, term=term, size=size):
            term_give[k, span(n, term_tile), :] = term(core * size, n).astype(BF)
            return carry

        lax.fori_loop(0, size // term_tile, giving, 0)
        terms.append(launch(remote(term_give.at[k], term_got.at[k], swap)))
    for k, (term, size) in enumerate(((down_term, half), (up_term, width // 2))):
        terms[k].wait_recv()

        def keeping(n, carry, k=k, term=term, size=size):
            at = span(n, term_tile)
            total = term(c * size, n) + term_got[k, at, :].astype(F32)
            ffg_o[at, k * width : (k + 1) * width] = total.astype(BF)
            return carry

        lax.fori_loop(0, size // term_tile, keeping, 0)

    for copy in team_copies:
        copy.wait_recv()
    layer_o[...] = jnp.sum(lay_r[...].astype(F32), axis=0)
    grad_o[...] = jnp.sum(spa_r[...].astype(F32), axis=0)
    sums_o[...] = jnp.sum(sums_r[...], axis=0)
    for copy in keeps:
        copy.wait()
    for copy in every:
        copy.wait_send()


def feed_forward(sizes, rows, send_s, send_g, eup, edown, second, dgrad, ff, sel, cot, mix):
    two, groups, team = sizes
    slots = send_s.shape[1]
    width = second.shape[1]
    hid, ehid = second.shape[1] * ff.shape[3] // width, eup.shape[1]
    entries = 2 * groups * slots
    count = 2 * (groups - 1) * 2 + 2 * groups + 2 + 3 * (team - 1) + 2 + 2 * groups
    arrived = (two, groups, slots, width)
    anywhere = pl.BlockSpec(memory_space=pl.ANY)
    inside = pl.BlockSpec(memory_space=pltpu.VMEM)
    team_rows = team * rows
    return pl.pallas_call(
        functools.partial(feed_kernel, sizes, count),
        name="feed_forward",
        out_shape=(
            jax.ShapeDtypeStruct((rows, width), F32),
            jax.ShapeDtypeStruct((rows, width), F32),
            jax.ShapeDtypeStruct((rows, 128), F32),
            jax.ShapeDtypeStruct((entries, ehid), BF),
            jax.ShapeDtypeStruct((entries, ehid), BF),
            jax.ShapeDtypeStruct(arrived, BF),
            jax.ShapeDtypeStruct(arrived, BF),
            jax.ShapeDtypeStruct((hid // 2, 2 * width), BF),
        ),
        in_specs=[anywhere] * 10,
        out_specs=(inside, inside, inside, anywhere, anywhere, anywhere, anywhere, inside),
        scratch_shapes=[
            pltpu.VMEM((two, groups, slots, width), BF),
            pltpu.VMEM((two, groups, slots, width), BF),
            pltpu.VMEM(eup.shape, BF),
            pltpu.VMEM(edown.shape, BF),
            pltpu.VMEM(second.shape, BF),
            pltpu.VMEM(dgrad.shape, BF),
            pltpu.VMEM((width, hid), BF),
            pltpu.VMEM((hid, width), BF),
            pltpu.VMEM(sel.shape, BF),
            pltpu.VMEM(cot.shape, BF),
            pltpu.VMEM(mix.shape, F32),
            pltpu.VMEM((entries, ehid), F32),
            pltpu.VMEM((entries, ehid), BF),
            pltpu.VMEM((entries, ehid), BF),
            pltpu.VMEM((2, entries // 2, width), F32),
            pltpu.VMEM((2, entries // 2, width), BF),
            pltpu.VMEM((entries // 2, width), BF),
            pltpu.VMEM((entries // 2, width), BF),
            pltpu.VMEM((groups, slots, width), BF),
            pltpu.VMEM((groups, slots, width), BF),
            pltpu.VMEM((groups, slots, width), BF),
            pltpu.VMEM((groups, slots, width), BF),
            pltpu.VMEM((team_rows, hid), BF),
            pltpu.VMEM((team_rows, hid), BF),
            pltpu.VMEM((team_rows, width), F32),
            pltpu.VMEM((team_rows, width), F32),
            pltpu.VMEM((team, rows, width), BF),
            pltpu.VMEM((team, rows, width), BF),
            pltpu.VMEM((team, rows, 128), F32),
            pltpu.VMEM((team, rows, width), BF),
            pltpu.VMEM((team, rows, width), BF),
            pltpu.VMEM((team, rows, 128), F32),
            pltpu.VMEM((2, hid // 2, width), BF),
            pltpu.VMEM((2, hid // 2, width), BF),
            pltpu.SemaphoreType.DMA((count,)),
            pltpu.SemaphoreType.DMA((count,)),
            pltpu.SemaphoreType.DMA((9 + 2 * groups,)),
            pltpu.SemaphoreType.DMA((4,)),
        ],
        compiler_params=pltpu.CompilerParams(
            collective_id=5, has_side_effects=True, vmem_limit_bytes=60 * 2**20
        ),
        cost_estimate=pl.CostEstimate(
            flops=0, bytes_accessed=240_000_000, transcendentals=0
        ),
    )(send_s, send_g, eup, edown, second, dgrad, ff, sel, cot, mix)


def tall(chunk):
    rows, cols = chunk.shape[-2:]
    factor = 1
    while (rows * factor) % 16:
        factor *= 2
    return chunk.reshape(chunk.shape[:-2] + (rows * factor, cols // factor))


def per_device_general(
    tokens,
    cotangent,
    block_order,
    doc_lengths,
    routes,
    w_qkv,
    w_out,
    w_up,
    w_down,
    router,
    norm_gains,
    norm_biases,
    expert_up,
    expert_down,
):
    rows, width = tokens.shape[1], tokens.shape[2]
    ctx_count = lax.axis_size("ctx")
    two = lax.axis_size("dp")
    team = math.gcd(4, ctx_count)
    groups = ctx_count // team
    sizes = (two, groups, team)
    team_heads = HEADS // team
    reps = groups // team_heads
    length = rows * ctx_count
    group_rows = rows * team
    experts = ctx_count * expert_up.shape[0]
    capacity = max(2, 2 * rows // experts)
    block_rows = length // block_order.shape[0]
    hidden = w_up.shape[1]
    hidden_dev = w_down.shape[0]
    wr = w_qkv.shape[0]
    qkv_cols = 3 * width // team
    up_cols = hidden // team
    core = lax.axis_index("dp")
    ctx = lax.axis_index("ctx")
    group, member = lax.div(ctx, team), lax.rem(ctx, team)
    team_steps = [(0, 0, k) for k in range(1, team)]
    group_steps = [(0, k, 0) for k in range(1, groups)]
    by_group = [[g * team + t for g in range(groups)] for t in range(team)]
    by_team = [[g * team + t for t in range(team)] for g in range(groups)]
    swap = [(d, (d + 1) % two) for d in range(two)]

    small_flat = jnp.concatenate(
        [router.reshape(-1), norm_gains.reshape(-1), norm_biases.reshape(-1)]
    )
    small_size = -(-small_flat.shape[0] // 2048) * 2048
    small = jnp.pad(small_flat, (0, small_size - small_flat.shape[0])).astype(BF)
    small = small.reshape(-1, 128)

    qkv_first = tall(
        w_qkv.astype(BF).reshape(wr, 3, team, width // team).transpose(2, 0, 1, 3).reshape(
            team, wr, qkv_cols
        )
    )
    up_first = tall(
        w_up.reshape(wr, two * groups, team, hidden_dev)
        .transpose(2, 0, 1, 3)
        .reshape(team, wr, up_cols)
        .astype(BF)
    )
    down_first = tall(w_down.astype(BF).reshape(team, wr, width))
    out_first = tall(w_out.astype(BF))
    route_row = jnp.broadcast_to(routes[0, :, 0][None, :], (8, rows))

    def first(coords, ins, outs):
        c, g, t = coords
        moves, local = [], []
        for s in team_steps:
            to = lax.rem(t + s[2], team)
            moves.append(Move(s, ins[0], outs[0].at[t]))
            moves.append(Move(s, ins[1].at[to], outs[1].at[t]))
            moves.append(Move(s, ins[3], outs[3].at[t]))
            moves.append(Move(s, ins[4], outs[4].at[t]))
            moves.append(Move(s, ins[2].at[to], outs[2].at[0, t]))
        for s in group_steps:
            moves.append(Move(s, ins[5], outs[5].at[g]))
        local.append((ins[0], outs[0].at[t]))
        local.append((ins[1].at[t], outs[1].at[t]))
        local.append((ins[2].at[t], outs[2].at[0, t]))
        local.append((ins[3], outs[3].at[t]))
        local.append((ins[4], outs[4].at[t]))
        local.append((ins[5], outs[5].at[g]))
        local.append((ins[6], outs[2].at[1]))
        return local, moves

    token_rows, qkv_part, ff_part, small_part, route_all, out_part = exchange(
        "first",
        1,
        sizes,
        (tokens[0], qkv_first, up_first, small, route_row, out_first, down_first),
        [
            ((team, rows, width), BF),
            (qkv_first.shape, BF),
            ((2,) + up_first.shape, BF),
            ((team,) + small.shape, BF),
            ((team, 8, rows), jnp.int32),
            ((groups,) + out_first.shape, BF),
        ],
        first,
    )

    def second_build(coords, ins, outs):
        c, g, t = coords
        moves, local = [], []
        for k, s in enumerate(group_steps):
            moves.append(Move(s, ins[0], outs[0].at[c, g]))
            moves.append(Move(s, ins[1], outs[1].at[c, g]))
        for s in team_steps:
            moves.append(Move(s, ins[2], outs[2].at[t]))
        local.append((ins[0], outs[0].at[c, g]))
        local.append((ins[1], outs[1].at[c, g]))
        local.append((ins[2], outs[2].at[t]))
        other = (1, 0, 0)
        for n in range(2):
            moves.append(Move(other, ins[n], outs[n].at[c, g]))
        for k, s in enumerate(group_steps):
            source = lax.rem(g + groups - s[1], groups)
            for n in range(2):
                moves.append(
                    Move(other, outs[n].at[c, source], outs[n].at[c, source], after=2 * k + n)
                )
        return local, moves

    qkv_all, small_all, cot_rows = exchange(
        "second",
        2,
        sizes,
        (qkv_part, small_part, cotangent[0]),
        [
            ((two, groups) + qkv_part.shape, BF),
            ((two, groups) + small_part.shape, BF),
            ((team, rows, width), BF),
        ],
        second_build,
    )
    qkv_weight = qkv_all.reshape(width, qkv_cols)
    small_rows = small_all.reshape(two * ctx_count, -1)
    router_cols = router.shape[1]
    router_weight = jnp.pad(
        small_rows[:, : wr * router_cols].reshape(width, router_cols),
        ((0, 0), (0, 128 - router_cols)),
    )
    vectors = small_rows[:, wr * router_cols : small_flat.shape[0]].reshape(
        two * ctx_count, 4, wr
    )
    vectors = vectors.transpose(1, 0, 2).reshape(4, width).astype(F32)
    vectors = jnp.pad(vectors, ((4, 0), (0, 0)))

    ff_half = lax.all_gather(
        ff_part.reshape(2, team * wr, width),
        "ctx",
        axis=0,
        tiled=False,
        axis_index_groups=by_group,
    )

    def core_half(term):
        halves = term.reshape((two, term.shape[0] // two) + term.shape[1:])
        keep = lax.dynamic_index_in_dim(halves, core, 0, keepdims=False)
        give = lax.dynamic_index_in_dim(halves, 1 - core, 0, keepdims=False)
        return keep + lax.ppermute(give.astype(BF), "dp", swap).astype(F32)

    def over_groups(term):
        return lax.psum_scatter(
            term, "ctx", scatter_dimension=0, tiled=True, axis_index_groups=by_group
        )

    doc_id = jnp.arange(doc_lengths.shape[1], dtype=jnp.int32)
    doc_ends = jnp.sum(
        jnp.where(doc_id[:, None] <= doc_id[None, :], doc_lengths[0][:, None], 0), axis=0
    )
    all_rows = jnp.arange(length, dtype=jnp.int32)
    marks = (all_rows // block_rows)[:, None] == jnp.arange(
        block_order.shape[0], dtype=jnp.int32
    )[None, :]
    anchor = jnp.sum(jnp.where(marks, block_order[None, :], 0), axis=1)
    all_place = anchor * block_rows + all_rows % block_rows

    def low_of(place):
        return jnp.max(
            jnp.where(doc_ends[None, :] <= place[:, None], doc_ends[None, :], 0), axis=1
        )

    sorted_rows = reps == 1 and block_rows == BLOCK
    query_length = length // reps
    tiles = query_length // TILE
    part = lax.rem(group, reps)
    if sorted_rows:
        query_place = all_rows
        lows = low_of(all_rows)
        bounds = jnp.stack(
            [lows[::TILE] // TILE, jnp.arange(1, tiles + 1, dtype=jnp.int32)], axis=1
        )
        number = jnp.arange(block_order.shape[0], dtype=jnp.int32)
        inverse = jnp.sum(
            jnp.where(block_order[None, :] == number[:, None], number[None, :], 0), axis=1
        )
    else:
        query_place = lax.dynamic_slice(all_place, (part * query_length,), (query_length,))
        lows = low_of(query_place)
        bounds = jnp.broadcast_to(
            jnp.array([[0, length // TILE]], dtype=jnp.int32), (tiles, 2)
        )
    meta = jnp.concatenate(
        [query_place[None], lows[None], jnp.zeros((6, query_length), jnp.int32)], axis=0
    )

    token_rows = token_rows.reshape(group_rows, width)
    inputs = token_rows.astype(F32)
    normed_low = layer_norm(inputs, vectors[4], vectors[6]).astype(BF)
    mixed_t = lax.dot_general(
        qkv_weight, normed_low, (((0,), (1,)), ((), ())), preferred_element_type=F32
    ).astype(BF)
    mixed_t = mixed_t.reshape(3, team_heads, HEAD_DIM, group_rows)

    def spread_heads(coords, ins, outs):
        c, g, t = coords
        moves = [
            Move(s, ins[0].at[:, lax.div(lax.rem(g + s[1], groups), reps)], outs[0].at[g])
            for s in group_steps
        ]
        local = [(ins[0].at[:, lax.div(g, reps)], outs[0].at[g])]
        other = (1, 0, 0)
        moves.append(Move(other, ins[1], outs[1].at[c, :, t]))
        local.append((ins[1], outs[1].at[c, :, t]))
        first_team = len(moves)
        for s in team_steps:
            moves.append(Move(s, ins[1], outs[1].at[c, :, t]))
        for k, s in enumerate(team_steps):
            source = lax.rem(t + team - s[2], team)
            view = outs[1].at[c, :, source]
            moves.append(Move(other, view, view, after=first_team + k))
        return local, moves

    head_parts, out_weight = exchange(
        "heads",
        3,
        sizes,
        (mixed_t, out_part),
        [
            ((groups, 3, HEAD_DIM, group_rows), BF),
            ((two, groups, team) + out_first.shape, BF),
        ],
        spread_heads,
    )
    out_weight = out_weight.reshape(width, width)
    head_parts = head_parts.reshape(groups, 3 * HEAD_DIM, group_rows)
    if sorted_rows:
        low_t, attention_t, log_total, q_pad, kv_t, kv_rows = sorted_attend(
            bounds, inverse, block_order, meta, head_parts
        )
    else:
        place_col = all_place[:, None]
        head_t = head_parts.transpose(1, 0, 2).reshape(3 * HEAD_DIM, length)
        zeros = jnp.zeros((HEAD_DIM, query_length), BF)
        kv_t = head_t[HEAD_DIM:]
        kv_rows = kv_t.T
        q_t = lax.dynamic_slice(
            head_t[:HEAD_DIM], (0, part * query_length), (HEAD_DIM, query_length)
        )
        q_pad = jnp.concatenate([q_t * jnp.asarray(SCALE, BF), zeros], axis=0)
        attention_t, log_total = attend(False, bounds, meta, place_col, q_pad, kv_rows, kv_t)
        low_t = lax.dynamic_update_slice(
            jnp.zeros((HEAD_DIM, length), BF),
            attention_t.astype(BF),
            (0, part * query_length),
        )
        low_t = low_t.reshape(HEAD_DIM, groups, group_rows).transpose(1, 0, 2)

    def gather_heads(coords, ins, outs):
        c, g, t = coords
        moves = [
            Move(s, ins[0].at[lax.rem(g + s[1], groups)], outs[0].at[t, g]) for s in group_steps
        ]
        local = [(ins[0].at[g], outs[0].at[t, g])]
        for s in team_steps:
            moves.append(Move(s, ins[0].at[g], outs[0].at[t, g]))
        for k, s in enumerate(group_steps):
            source = lax.rem(g + groups - s[1], groups)
            for e in team_steps:
                moves.append(Move(e, outs[0].at[t, source], outs[0].at[t, source], after=k))
        return local, moves

    [attended] = exchange(
        "attended",
        4,
        sizes,
        (low_t,),
        [((team, groups, HEAD_DIM, group_rows), BF)],
        gather_heads,
    )
    if reps > 1:
        attended = lax.dynamic_index_in_dim(
            attended.reshape(team, team_heads, reps, HEAD_DIM, group_rows),
            lax.div(group, groups // reps),
            2,
            keepdims=False,
        )
    attended_t = attended.reshape(width, group_rows)

    slots = team * capacity
    (
        second_low,
        dense_grad,
        send_s,
        send_g,
        select,
        mixes,
        middle_own,
        prob_own,
        hot_own,
        second_own,
        attended_own,
    ) = between(
        experts,
        sizes,
        slots,
        member[None],
        attended_t,
        out_weight,
        token_rows,
        vectors,
        router_weight,
        route_all,
        cot_rows.reshape(group_rows, width),
    )
    (
        layer_sum,
        second_sum,
        sums_own,
        expert_active,
        hidden_grad,
        arrived_in,
        arrived_grad,
        ff_terms,
    ) = feed_forward(
        sizes,
        rows,
        send_s,
        send_g,
        expert_up[0],
        expert_down[0],
        second_low,
        dense_grad,
        ff_half,
        select,
        cot_rows.reshape(group_rows, width),
        mixes,
    )
    ff_sum = over_groups(ff_terms)
    down_sum = ff_sum[:, :width].astype(F32)
    up_sum = ff_sum[:, width:].reshape(team, wr, up_cols)
    entries = two * groups * slots
    expert_down_grad = row_sum(expert_active, arrived_grad.reshape(entries, width), TILE)
    expert_up_grad = row_sum(arrived_in.reshape(entries, width), hidden_grad, 128)

    layer_out, middle_grad, flow_t, out_term, small_t = turn(
        experts,
        layer_sum,
        second_sum,
        sums_own,
        middle_own,
        prob_own,
        hot_own,
        second_own,
        attended_own,
        cotangent[0],
        router_weight,
        out_weight,
        vectors,
    )
    flow_t = flow_t.reshape(team, team_heads, HEAD_DIM, rows)
    out_halves = out_term.reshape(two, groups, team, wr, width)

    def spread_flow(coords, ins, outs):
        c, g, t = coords
        moves = []
        for dg in range(groups):
            for dt in range(team):
                if dg or dt:
                    to_g, to_t = lax.rem(g + dg, groups), lax.rem(t + dt, team)
                    moves.append(
                        Move((0, dg, dt), ins[0].at[to_t, lax.div(to_g, reps)], outs[0].at[g, t])
                    )
        moves.append(Move((1, 0, 0), ins[1].at[lax.rem(c + 1, two)], outs[1]))
        return [(ins[0].at[t, lax.div(g, reps)], outs[0].at[g, t])], moves

    flow_parts, out_got = exchange(
        "flow",
        8,
        sizes,
        (flow_t, out_halves),
        [((groups, team, HEAD_DIM, rows), BF), (out_halves.shape[1:], BF)],
        spread_flow,
    )
    if sorted_rows:
        grad_parts = sorted_back(
            bounds,
            inverse,
            block_order,
            meta,
            flow_parts.reshape(ctx_count, HEAD_DIM, rows),
            attention_t,
            log_total,
            q_pad,
            kv_t,
            kv_rows,
            groups,
        )
    else:
        flow_all = flow_parts.transpose(2, 0, 1, 3).reshape(HEAD_DIM, length)
        flow_all = lax.dynamic_slice(
            flow_all, (0, part * query_length), (HEAD_DIM, query_length)
        )
        do_pad = jnp.concatenate([zeros, flow_all], axis=0)
        query_grad, pair_grad = attend_back(
            False,
            bounds,
            meta,
            place_col,
            q_pad,
            do_pad,
            attention_t,
            log_total,
            kv_rows,
            kv_t,
        )
        query_grad = lax.dynamic_update_slice(
            jnp.zeros((HEAD_DIM, length), BF), query_grad, (0, part * query_length)
        )
        grad_parts = jnp.concatenate([query_grad, pair_grad], axis=0)
        grad_parts = grad_parts.reshape(3, HEAD_DIM, groups, group_rows).transpose(2, 0, 1, 3)
    out_keep = lax.dynamic_index_in_dim(out_halves, core, 0, keepdims=False)
    out_parts = tall(
        (out_keep.astype(F32) + out_got.astype(F32))
        .astype(BF)
        .transpose(1, 0, 2, 3)
        .reshape(team, groups * wr, width)
    )

    def mixed_build(coords, ins, outs):
        c, g, t = coords
        moves = [
            Move(s, ins[0].at[lax.rem(g + s[1], groups)], outs[0].at[:, g])
            for s in group_steps
        ]
        moves += [
            Move(s, ins[1].at[lax.rem(t + s[2], team)], outs[1].at[t]) for s in team_steps
        ]
        return [(ins[0].at[g], outs[0].at[:, g]), (ins[1].at[t], outs[1].at[t])], moves

    grad_parts, out_parts = exchange(
        "mixed",
        9,
        sizes,
        (grad_parts, out_parts),
        [((3, groups, HEAD_DIM, group_rows), BF), (out_parts.shape, BF)],
        mixed_build,
    )
    out_parts = tall(
        jnp.sum(out_parts.astype(F32), axis=0).astype(BF).reshape(groups, wr, width)
    )
    if reps > 1:
        grad_parts = jnp.sum(
            grad_parts.reshape(3, team_heads, reps, HEAD_DIM, group_rows).astype(F32), axis=2
        ).astype(BF)
    mixed_grad_t = grad_parts.reshape(qkv_cols, group_rows)
    normed_part = (
        lax.dot_general(
            mixed_grad_t, qkv_weight, (((0,), (1,)), ((), ())), preferred_element_type=F32
        )
        .astype(BF)
        .reshape(team, rows, width)
    )
    qkv_term = lax.dot_general(
        normed_low, mixed_grad_t, (((0,), (1,)), ((), ())), preferred_element_type=F32
    )
    qkv_parts = core_half(qkv_term).astype(BF).reshape(groups, team * wr, qkv_cols)

    def normed_build(coords, ins, outs):
        c, g, t = coords
        moves, local = [], [(ins[2].at[t], outs[2].at[t])]
        for n in range(2):
            for s in group_steps:
                moves.append(Move(s, ins[n].at[lax.rem(g + s[1], groups)], outs[n].at[g]))
            local.append((ins[n].at[g], outs[n].at[g]))
        for s in team_steps:
            moves.append(Move(s, ins[2].at[lax.rem(t + s[2], team)], outs[2].at[t]))
        return local, moves

    qkv_parts, out_parts, normed_own = exchange(
        "normed",
        10,
        sizes,
        (qkv_parts, out_parts, normed_part),
        [(qkv_parts.shape, BF), (out_parts.shape, BF), (normed_part.shape, BF)],
        normed_build,
    )
    qkv_sum = (
        jnp.sum(qkv_parts.astype(F32), axis=0).astype(BF).reshape(team, wr, qkv_cols)
    )
    out_sum = jnp.sum(out_parts.astype(F32), axis=0).reshape(wr, width)
    normed_grad = jnp.sum(normed_own.astype(F32), axis=0)
    input_part_grad, gain_first, bias_first = jax.vjp(
        layer_norm, tokens[0].astype(F32), vectors[4], vectors[6]
    )[1](normed_grad)
    input_grad = middle_grad + input_part_grad

    small_used = small_t.shape[0]
    small_row = jnp.arange(small_used, dtype=jnp.int32)[:, None]
    small_t = jnp.where(
        small_row == experts + 2,
        gain_first[None],
        jnp.where(small_row == experts + 4, bias_first[None], small_t),
    )
    small_cols = small_used * wr
    small_pad = -(-small_cols // 1024) * 1024
    small_parts = jnp.pad(
        small_t.reshape(small_used, two * ctx_count, wr)
        .transpose(1, 0, 2)
        .reshape(two * ctx_count, small_cols),
        ((0, 0), (0, small_pad - small_cols)),
    ).reshape(two * ctx_count, small_pad // 128, 128)

    def owners_build(coords, ins, outs):
        c, g, t = coords
        moves, local = [], []
        for n in range(2):
            for s in team_steps:
                moves.append(Move(s, ins[n].at[lax.rem(t + s[2], team)], outs[n].at[t]))
            local.append((ins[n].at[t], outs[n].at[t]))
        me = c * ctx_count + g * team + t
        for dc in range(two):
            for dg in range(groups):
                for dt in range(team):
                    if dc or dg or dt:
                        to = (
                            lax.rem(c + dc, two) * ctx_count
                            + lax.rem(g + dg, groups) * team
                            + lax.rem(t + dt, team)
                        )
                        moves.append(Move((dc, dg, dt), ins[2].at[to], outs[2].at[me]))
        local.append((ins[2].at[me], outs[2].at[me]))
        return local, moves

    up_own, qkv_own, small_own = exchange(
        "owners",
        11,
        sizes,
        (tall(up_sum), tall(qkv_sum), small_parts),
        [
            (tall(up_sum).shape, BF),
            (tall(qkv_sum).shape, BF),
            (small_parts.shape, F32),
        ],
        owners_build,
    )
    small_sum = jnp.sum(small_own, axis=0).reshape(-1)[:small_cols].reshape(small_used, wr)
    up_own = (
        up_own.reshape(team, wr, two * groups, hidden_dev)
        .transpose(1, 2, 0, 3)
        .reshape(wr, hidden)
        .astype(F32)
    )
    qkv_own = (
        qkv_own.reshape(team, wr, 3, width // team)
        .transpose(1, 2, 0, 3)
        .reshape(wr, 3 * width)
        .astype(F32)
    )
    return (
        layer_out[None],
        input_grad[None].astype(BF),
        qkv_own,
        out_sum,
        up_own,
        down_sum,
        small_sum[:router_cols].T,
        small_sum[router_cols : router_cols + 2],
        small_sum[router_cols + 2 : router_cols + 4],
        expert_up_grad,
        expert_down_grad,
    )


def where_rows(block_order, doc_lengths, rows, block_rows):
    doc_id = jnp.arange(doc_lengths.shape[1], dtype=jnp.int32)
    doc_ends = jnp.sum(
        jnp.where(doc_id[:, None] <= doc_id[None, :], doc_lengths[0][:, None], 0), axis=0
    )
    lows = jnp.max(jnp.where(doc_ends[None, :] <= rows[:, None], doc_ends[None, :], 0), axis=1)
    tiles = rows.shape[0] // TILE
    bounds = jnp.stack([lows[::TILE] // TILE, jnp.arange(1, tiles + 1, dtype=jnp.int32)], axis=1)
    number = jnp.arange(block_order.shape[0], dtype=jnp.int32)
    inverse = jnp.sum(
        jnp.where(block_order[None, :] == number[:, None], number[None, :], 0), axis=1
    )
    meta = jnp.concatenate(
        [rows[None], lows[None], jnp.zeros((6, rows.shape[0]), jnp.int32)], axis=0
    )
    return bounds, inverse, meta


def per_device(
    tokens,
    cotangent,
    block_order,
    doc_lengths,
    routes,
    w_qkv,
    w_out,
    w_up,
    w_down,
    router,
    norm_gains,
    norm_biases,
    expert_up,
    expert_down,
):
    rows, width = tokens.shape[1], tokens.shape[2]
    ctx_count = lax.axis_size("ctx")
    two = lax.axis_size("dp")
    team = math.gcd(4, ctx_count)
    groups = ctx_count // team
    sizes = (two, groups, team)
    length = rows * ctx_count
    wr = w_qkv.shape[0]
    experts = ctx_count * expert_up.shape[0]
    if groups * team != HEADS or length // block_order.shape[0] != BLOCK or team * wr != 128:
        return per_device_general(
            tokens, cotangent, block_order, doc_lengths, routes, w_qkv, w_out, w_up, w_down,
            router, norm_gains, norm_biases, expert_up, expert_down,
        )
    group_rows = rows * team
    capacity = max(2, 2 * rows // experts)
    slots = team * capacity
    hidden = w_up.shape[1]
    hidden_dev = w_down.shape[0]
    qkv_cols = 3 * width // team
    up_cols = hidden // team
    ctx = lax.axis_index("ctx")
    core = lax.axis_index("dp")
    group, member = lax.div(ctx, team), lax.rem(ctx, team)
    by_group = [[g * team + t for g in range(groups)] for t in range(team)]
    team_steps = [(0, 0, k) for k in range(1, team)]

    router_cols = router.shape[1]
    small = jnp.concatenate(
        [router, jnp.zeros((wr, 124 - router_cols), F32), norm_gains.T, norm_biases.T], axis=1
    )
    own = jnp.concatenate(
        [
            w_qkv.reshape(wr, 3, team, width // team)
            .transpose(2, 0, 1, 3)
            .reshape(team, wr, qkv_cols),
            jnp.broadcast_to(small[None], (team, wr, 128)),
        ],
        axis=2,
    ).astype(BF)
    up_first = (
        w_up.reshape(wr, two * groups, team, hidden_dev)
        .transpose(2, 0, 1, 3)
        .reshape(team, wr, up_cols)
        .astype(BF)
    )
    route_row = jnp.broadcast_to(routes[0, :, 0][None, :], (8, rows))
    (
        token_rows,
        cot_rows,
        head_parts,
        normed,
        weights,
        vectors,
        out_weight,
        ff_part,
        route_all,
    ) = start(
        sizes,
        tokens[0],
        cotangent[0],
        own,
        up_first,
        w_down.astype(BF).reshape(team, wr, width),
        w_out.astype(BF),
        route_row,
    )
    router_weight = weights[:, :, :, :, qkv_cols:].reshape(width, 128)
    out_weight = out_weight.reshape(width, width)
    token_rows = token_rows.reshape(group_rows, width)
    cot_rows = cot_rows.reshape(group_rows, width)

    ff_half = lax.all_gather(
        ff_part.reshape(2, team * wr, width),
        "ctx",
        axis=0,
        tiled=False,
        axis_index_groups=by_group,
    )
    bounds, inverse, meta = where_rows(
        block_order, doc_lengths, jnp.arange(length, dtype=jnp.int32), BLOCK
    )
    low_t, attention_t, log_total, q_pad, kv_t, kv_rows = sorted_attend(
        bounds, inverse, block_order, meta, head_parts.reshape(groups, 3 * HEAD_DIM, group_rows)
    )

    def gather_heads(coords, ins, outs):
        c, g, t = coords
        steps = [(0, k, 0) for k in range(1, groups)]
        moves = [Move(s, ins[0].at[lax.rem(g + s[1], groups)], outs[0].at[t, g]) for s in steps]
        local = [(ins[0].at[g], outs[0].at[t, g])]
        for s in team_steps:
            moves.append(Move(s, ins[0].at[g], outs[0].at[t, g]))
        for k, s in enumerate(steps):
            source = lax.rem(g + groups - s[1], groups)
            for e in team_steps:
                moves.append(Move(e, outs[0].at[t, source], outs[0].at[t, source], after=k))
        return local, moves

    [attended] = exchange(
        "attended",
        4,
        sizes,
        (low_t,),
        [((team, groups, HEAD_DIM, group_rows), BF)],
        gather_heads,
    )
    (
        second_low,
        dense_grad,
        send_s,
        send_g,
        select,
        mixes,
        middle_own,
        prob_own,
        hot_own,
        second_own,
        attended_own,
    ) = between(
        experts,
        sizes,
        slots,
        member[None],
        attended.reshape(width, group_rows),
        out_weight,
        token_rows,
        vectors,
        router_weight,
        route_all,
        cot_rows,
    )
    (
        layer_sum,
        second_sum,
        sums_own,
        expert_active,
        hidden_grad,
        arrived_in,
        arrived_grad,
        ff_terms,
    ) = feed_forward(
        sizes,
        rows,
        send_s,
        send_g,
        expert_up[0],
        expert_down[0],
        second_low,
        dense_grad,
        ff_half,
        select,
        cot_rows,
        mixes,
    )
    ff_sum = lax.psum_scatter(
        ff_terms, "ctx", scatter_dimension=0, tiled=True, axis_index_groups=by_group
    )
    down_sum = ff_sum[:, :width].astype(F32)
    up_sum = ff_sum[:, width:].reshape(team, wr, up_cols)

    layer_out, middle_grad, flow_t, out_term, small_t = turn(
        experts,
        layer_sum,
        second_sum,
        sums_own,
        middle_own,
        prob_own,
        hot_own,
        second_own,
        attended_own,
        cotangent[0],
        router_weight,
        out_weight,
        vectors,
    )
    flow_t = flow_t.reshape(team, groups, HEAD_DIM, rows)
    out_halves = out_term.reshape(two, groups, team, wr, width)

    def spread_flow(coords, ins, outs):
        c, g, t = coords
        moves = []
        for dg in range(groups):
            for dt in range(team):
                if dg or dt:
                    to_g, to_t = lax.rem(g + dg, groups), lax.rem(t + dt, team)
                    moves.append(Move((0, dg, dt), ins[0].at[to_t, to_g], outs[0].at[g, t]))
        moves.append(Move((1, 0, 0), ins[1].at[lax.rem(c + 1, two)], outs[1]))
        return [(ins[0].at[t, g], outs[0].at[g, t])], moves

    flow_parts, out_got = exchange(
        "flow",
        8,
        sizes,
        (flow_t, out_halves),
        [((groups, team, HEAD_DIM, rows), BF), (out_halves.shape[1:], BF)],
        spread_flow,
    )
    out_keep = lax.dynamic_index_in_dim(out_halves, core, 0, keepdims=False)
    out_parts = (out_keep.astype(F32) + out_got.astype(F32)).astype(BF).transpose(1, 0, 2, 3)
    grad_parts = sorted_back(
        bounds,
        inverse,
        block_order,
        meta,
        flow_parts.reshape(ctx_count, HEAD_DIM, rows),
        attention_t,
        log_total,
        q_pad,
        kv_t,
        kv_rows,
        groups,
    )

    def moved(array, axis, step, base, count, pairs):
        chunk = lax.dynamic_index_in_dim(
            array, lax.rem(base + step, count), axis, keepdims=False
        )
        return lax.ppermute(chunk, "ctx", pairs)

    group_pairs = [
        [(g * team + t, (g + k) % groups * team + t) for g in range(groups) for t in range(team)]
        for k in range(groups)
    ]
    team_pairs = [
        [(g * team + t, g * team + (t + k) % team) for g in range(groups) for t in range(team)]
        for k in range(team)
    ]
    pieces = [lax.dynamic_index_in_dim(grad_parts, group, 0, keepdims=False)]
    pieces += [moved(grad_parts, 0, k, group, groups, group_pairs[k]) for k in range(1, groups)]
    out_sum = lax.dynamic_index_in_dim(out_parts, member, 0, keepdims=False).astype(F32)
    for k in range(1, team):
        out_sum = out_sum + moved(out_parts, 0, k, member, team, team_pairs[k]).astype(F32)
    entries = two * groups * slots
    expert_down_grad = row_sum(expert_active, arrived_grad.reshape(entries, width), TILE)
    expert_up_grad = row_sum(arrived_in.reshape(entries, width), hidden_grad, 128)
    input_grad, qkv_own, up_own, out_own, small_own = end(
        sizes,
        experts,
        pieces,
        weights,
        normed,
        tokens[0],
        vectors,
        middle_grad,
        small_t,
        up_sum,
        out_sum.astype(BF),
    )
    up_own = (
        up_own.reshape(team, wr, two * groups, hidden_dev)
        .transpose(1, 2, 0, 3)
        .reshape(wr, hidden)
        .astype(F32)
    )
    qkv_own = (
        qkv_own.reshape(team, wr, 3, width // team)
        .transpose(1, 2, 0, 3)
        .reshape(wr, 3 * width)
        .astype(F32)
    )
    small_sum = lax.dynamic_slice_in_dim(jnp.sum(small_own, axis=0), member * wr, wr, axis=1)
    return (
        layer_out[None],
        input_grad[None],
        qkv_own,
        out_own,
        up_own,
        down_sum,
        small_sum[:router_cols].T,
        small_sum[router_cols : router_cols + 2],
        small_sum[router_cols + 2 : router_cols + 4],
        expert_up_grad,
        expert_down_grad,
    )


def solution(mesh):
    in_specs = (
        P("dp", "ctx", None),
        P("dp", "ctx", None),
        P(),
        P("dp", None),
        P("dp", "ctx", None),
        P(("dp", "ctx"), None),
        P(("dp", "ctx"), None),
        P(("dp", "ctx"), None),
        P(("dp", "ctx"), None),
        P(("dp", "ctx"), None),
        P(None, ("dp", "ctx")),
        P(None, ("dp", "ctx")),
        P("ctx", None, "dp"),
        P("ctx", "dp", None),
    )
    out_specs = (
        P("dp", "ctx", None),
        P("dp", "ctx", None),
        P(("dp", "ctx"), None),
        P(("dp", "ctx"), None),
        P(("dp", "ctx"), None),
        P(("dp", "ctx"), None),
        P(("dp", "ctx"), None),
        P(None, ("dp", "ctx")),
        P(None, ("dp", "ctx")),
        P("ctx", None, "dp"),
        P("ctx", "dp", None),
    )
    return jax.shard_map(
        per_device, mesh=mesh, in_specs=in_specs, out_specs=out_specs, check_vma=False
    )
```

```python
import functools
import math

import jax
import jax.numpy as jnp
from jax import lax
from jax.experimental import pallas as pl
from jax.experimental.pallas import tpu as pltpu
from jax.sharding import PartitionSpec as P

HEADS = 16
HEAD_DIM = 64

EPS = 1e-05
NEG = -1e30
SCALE = 0.125
TILE = 256
BF = jnp.bfloat16
F32 = jnp.float32
MESH = pl.DeviceIdType.MESH


def layer_norm(values, gain, shift):
    center = values - jnp.mean(values, axis=-1, keepdims=True)
    spread = jnp.mean(center * center, axis=-1, keepdims=True)
    return center * lax.rsqrt(spread + EPS) * gain + shift


def gelu_tanh(values):
    return jax.nn.gelu(values, approximate=True)


def router_heads(router_logits, route_hot, experts):
    chances = jax.nn.softmax(router_logits[:, :experts], axis=-1)
    gate = jnp.sum(chances * route_hot, axis=-1)
    mixing = jax.nn.softmax(router_logits[:, experts:], axis=-1)
    return (gate, mixing[:, 0], mixing[:, 1])


def dot_f32(left, right):
    return jnp.dot(left, right, preferred_element_type=F32)


def contract_rows(left, right):
    return lax.dot_general(left, right, (((0,), (0,)), ((), ())), preferred_element_type=F32)


def contract_cols(left, right):
    return lax.dot_general(left, right, (((1,), (1,)), ((), ())), preferred_element_type=F32)


def span(i, size):
    return pl.ds(pl.multiple_of(i * size, size), size)


class Move:
    def __init__(self, step, src, dst, after=None):
        self.step, self.src, self.dst, self.after = step, src, dst, after


def exchange(name, cid, sizes, ins, outs, build, micros=20):
    two, groups, team = sizes

    def kernel(*refs):
        in_refs, out_refs = refs[: len(ins)], refs[len(ins) : len(ins) + len(outs)]
        send_sem, recv_sem, local_sem = refs[len(ins) + len(outs) :]
        c = lax.axis_index("dp")
        i = lax.axis_index("ctx")
        g, t = lax.div(i, team), lax.rem(i, team)

        def device(step):
            dc, dg, dt = step
            return (
                lax.rem(c + dc, two),
                lax.rem(g + dg, groups) * team + lax.rem(t + dt, team),
            )

        locals_, moves = build((c, g, t), in_refs, out_refs)
        steps = sorted({m.step for m in moves})
        greet = sorted(
            set(steps) | {((-a) % two, (-b) % groups, (-d) % team) for a, b, d in steps}
        )
        barrier = pltpu.get_barrier_semaphore()
        for step in greet:
            pl.semaphore_signal(barrier, inc=1, device_id=device(step), device_id_type=MESH)
        pl.semaphore_wait(barrier, len(greet))

        copies = {}
        arrived = set()
        for k, (src, dst) in enumerate(locals_):
            copies[("local", k)] = pltpu.make_async_copy(src, dst, local_sem.at[k])
        for k, m in enumerate(moves):
            copies[k] = pltpu.make_async_remote_copy(
                src_ref=m.src,
                dst_ref=m.dst,
                send_sem=send_sem.at[k],
                recv_sem=recv_sem.at[k],
                device_id=device(m.step),
                device_id_type=MESH,
            )
        for k, m in enumerate(moves):
            if m.after is None:
                copies[k].start()
        for k in range(len(locals_)):
            copies[("local", k)].start()
        for k, m in enumerate(moves):
            if m.after is not None:
                if m.after not in arrived:
                    arrived.add(m.after)
                    if isinstance(m.after, tuple):
                        copies[m.after].wait()
                    else:
                        copies[m.after].wait_recv()
                copies[k].start()
        for k in range(len(locals_)):
            if ("local", k) not in arrived:
                copies[("local", k)].wait()
        for k in range(len(moves)):
            if k not in arrived:
                copies[k].wait_recv()
        for k in range(len(moves)):
            copies[k].wait_send()

    count = []

    def trace_counts():
        class Probe:
            def __getattr__(self, name):
                return self

            def __getitem__(self, index):
                return self

        locals_, moves = build((0, 0, 0), [Probe() for _ in ins], [Probe() for _ in outs])
        count.extend((len(locals_), len(moves)))

    trace_counts()
    return pl.pallas_call(
        kernel,
        name=name,
        out_shape=tuple(jax.ShapeDtypeStruct(s, d) for s, d in outs),
        in_specs=[pl.BlockSpec(memory_space=pl.ANY)] * len(ins),
        out_specs=tuple(pl.BlockSpec(memory_space=pl.ANY) for _ in outs),
        scratch_shapes=[
            pltpu.SemaphoreType.DMA((max(1, count[1]),)),
            pltpu.SemaphoreType.DMA((max(1, count[1]),)),
            pltpu.SemaphoreType.DMA((max(1, count[0]),)),
        ],
        compiler_params=pltpu.CompilerParams(collective_id=cid, has_side_effects=True),
        cost_estimate=pl.CostEstimate(
            flops=0, bytes_accessed=int(micros * 3.0e6), transcendentals=0
        ),
    )(*ins)


def mask_of(kt, key_place, query_place, query_low):
    return (key_place <= query_place) & (key_place >= query_low)


def key_places(sorted_rows, kt, place_ref):
    if sorted_rows:
        return lax.broadcasted_iota(jnp.int32, (TILE, TILE), 0) + kt * TILE
    return place_ref[pl.ds(pl.multiple_of(kt * TILE, TILE), TILE), :]


def attend_kernel(
    sorted_rows, bounds, meta_ref, place_ref, q_ref, rows_ref, kvt_ref, out_ref, lse_ref
):
    step = pl.program_id(0)
    queries = q_ref[...]
    place, low = meta_ref[0:1, :], meta_ref[1:2, :]

    def body(kt, carry):
        peak, total, acc = carry
        at = pl.ds(pl.multiple_of(kt * TILE, TILE), TILE)
        scores = dot_f32(rows_ref[at, :], queries)
        allowed = mask_of(kt, key_places(sorted_rows, kt, place_ref), place, low)
        scores = jnp.where(allowed, scores, NEG)
        new_peak = jnp.maximum(peak, jnp.max(scores, axis=0, keepdims=True))
        weights = jnp.exp(scores - new_peak)
        fade = jnp.exp(peak - new_peak)
        total = total * fade + jnp.sum(weights, axis=0, keepdims=True)
        acc = acc * fade + dot_f32(kvt_ref[HEAD_DIM:, at], weights.astype(BF))
        return new_peak, total, acc

    start = (
        jnp.full((1, TILE), NEG, F32),
        jnp.zeros((1, TILE), F32),
        jnp.zeros((HEAD_DIM, TILE), F32),
    )
    peak, total, acc = lax.fori_loop(bounds[step, 0], bounds[step, 1], body, start)
    out_ref[...] = acc / total
    lse_ref[...] = peak + jnp.log(total)


def attend_back_kernel(
    sorted_rows,
    tiles,
    bounds,
    meta_ref,
    place_ref,
    q_ref,
    do_ref,
    out_ref,
    lse_ref,
    rows_ref,
    kvt_ref,
    dq_ref,
    dkv_ref,
    acc_ref,
):
    step = pl.program_id(0)

    @pl.when(step == 0)
    def _():
        acc_ref[...] = jnp.zeros_like(acc_ref)

    queries, flows = q_ref[...], do_ref[...]
    place, low = meta_ref[0:1, :], meta_ref[1:2, :]
    log_total = lse_ref[...]
    delta = jnp.sum(flows[HEAD_DIM:, :].astype(F32) * out_ref[...], axis=0, keepdims=True)

    def body(kt, dq):
        at = pl.ds(pl.multiple_of(kt * TILE, TILE), TILE)
        rows = rows_ref[at, :]
        scores = dot_f32(rows, queries)
        allowed = mask_of(kt, key_places(sorted_rows, kt, place_ref), place, low)
        chances = jnp.exp(jnp.where(allowed, scores - log_total, NEG))
        flow = dot_f32(rows, flows)
        score_grad = (chances * (flow - delta)).astype(BF)
        dq = dq + dot_f32(kvt_ref[:HEAD_DIM, at], score_grad)
        acc_ref[:HEAD_DIM, at] += contract_cols(queries[:HEAD_DIM, :], score_grad)
        acc_ref[HEAD_DIM:, at] += contract_cols(flows[HEAD_DIM:, :], chances.astype(BF))
        return dq

    dq = lax.fori_loop(
        bounds[step, 0], bounds[step, 1], body, jnp.zeros((HEAD_DIM, TILE), F32)
    )
    dq_ref[...] = (dq * SCALE).astype(BF)

    @pl.when(step == tiles - 1)
    def _():
        dkv_ref[...] = acc_ref[...].astype(BF)


def attention_specs(length, query_length):
    def whole(shape):
        return pl.BlockSpec(shape, lambda i: (0, 0))

    def tile(rows):
        return pl.BlockSpec((rows, TILE), lambda i: (0, i))

    return whole, tile


def attend(sorted_rows, bounds, meta, place_col, q_pad, kv_rows, kv_t):
    length, query_length = kv_rows.shape[0], q_pad.shape[1]
    whole, tile = attention_specs(length, query_length)
    return pl.pallas_call(
        functools.partial(attend_kernel, sorted_rows),
        name="attend",
        grid=(query_length // TILE,),
        in_specs=[
            pl.BlockSpec(memory_space=pltpu.SMEM),
            tile(8),
            whole(place_col.shape),
            tile(2 * HEAD_DIM),
            whole((length, 2 * HEAD_DIM)),
            whole((2 * HEAD_DIM, length)),
        ],
        out_specs=(tile(HEAD_DIM), tile(1)),
        out_shape=(
            jax.ShapeDtypeStruct((HEAD_DIM, query_length), F32),
            jax.ShapeDtypeStruct((1, query_length), F32),
        ),
        compiler_params=pltpu.CompilerParams(vmem_limit_bytes=40 * 2**20),
    )(bounds, meta, place_col, q_pad, kv_rows, kv_t)


def attend_back(sorted_rows, bounds, meta, place_col, q_pad, do_pad, out, lse, kv_rows, kv_t):
    length, query_length = kv_rows.shape[0], q_pad.shape[1]
    whole, tile = attention_specs(length, query_length)
    return pl.pallas_call(
        functools.partial(attend_back_kernel, sorted_rows, query_length // TILE),
        name="attend_back",
        grid=(query_length // TILE,),
        in_specs=[
            pl.BlockSpec(memory_space=pltpu.SMEM),
            tile(8),
            whole(place_col.shape),
            tile(2 * HEAD_DIM),
            tile(2 * HEAD_DIM),
            tile(HEAD_DIM),
            tile(1),
            whole((length, 2 * HEAD_DIM)),
            whole((2 * HEAD_DIM, length)),
        ],
        out_specs=(tile(HEAD_DIM), whole((2 * HEAD_DIM, length))),
        out_shape=(
            jax.ShapeDtypeStruct((HEAD_DIM, query_length), BF),
            jax.ShapeDtypeStruct((2 * HEAD_DIM, length), BF),
        ),
        scratch_shapes=[pltpu.VMEM((2 * HEAD_DIM, length), F32)],
        compiler_params=pltpu.CompilerParams(vmem_limit_bytes=40 * 2**20),
    )(bounds, meta, place_col, q_pad, do_pad, out, lse, kv_rows, kv_t)


BLOCK = 64


def pick_pair(load, table, d):
    first, second = table[2 * d], table[2 * d + 1]
    left = load(lax.div(first, 2))
    right = load(lax.div(second, 2))
    lane = lax.broadcasted_iota(jnp.int32, left.shape, 1)
    left = jnp.where(lax.rem(first, 2) == 0, left, pltpu.roll(left, BLOCK, 1))
    right = jnp.where(lax.rem(second, 2) == 1, right, pltpu.roll(right, BLOCK, 1))
    return jnp.where(lane < BLOCK, left, right)


def column_block(ref, k, per):
    return ref[lax.div(k, per), :, span(lax.rem(k, per), 128)].astype(F32)


def fill_inverse(order, inverse, count):
    def put(n, carry):
        inverse[order[n]] = n
        return carry

    lax.fori_loop(0, count, put, 0)


def query_lows(lengths, step):
    place = lax.broadcasted_iota(jnp.int32, (1, TILE), 1) + step * TILE
    low = jnp.zeros((1, TILE), jnp.int32)
    first, end = 0, 0
    for n in range(lengths.shape[0]):
        end = end + lengths[n]
        low = jnp.where(end <= place, end, low)
        first = jnp.where(end <= step * TILE, end, first)
    return place, low, lax.div(first, TILE)


def sorted_attend_kernel(
    lengths, order, parts_ref, low_ref, out_ref, lse_ref, q_ref, kvt_ref, rows_ref, inverse
):
    step = pl.program_id(0)
    length = q_ref.shape[1]
    per = parts_ref.shape[2] // 128

    @pl.when(step == 0)
    def _():
        fill_inverse(order, inverse, length // BLOCK)

        def place(d, carry):
            tile = pick_pair(lambda k: column_block(parts_ref, k, per), inverse, d)
            at = span(d, 128)
            q_ref[:HEAD_DIM, at] = (tile[:HEAD_DIM] * SCALE).astype(BF)
            q_ref[HEAD_DIM:, at] = jnp.zeros((HEAD_DIM, 128), BF)
            kvt_ref[:, at] = tile[HEAD_DIM:].astype(BF)
            rows_ref[at, :] = tile[HEAD_DIM:].T.astype(BF)
            return carry

        lax.fori_loop(0, length // 128, place, 0)

    here = span(step, TILE)
    queries = q_ref[:, here]
    place, low, first = query_lows(lengths, step)

    def body(kt, carry):
        peak, total, acc = carry
        at = span(kt, TILE)
        scores = dot_f32(rows_ref[at, :], queries)
        allowed = mask_of(kt, key_places(True, kt, None), place, low)
        scores = jnp.where(allowed, scores, NEG)
        new_peak = jnp.maximum(peak, jnp.max(scores, axis=0, keepdims=True))
        weights = jnp.exp(scores - new_peak)
        fade = jnp.exp(peak - new_peak)
        total = total * fade + jnp.sum(weights, axis=0, keepdims=True)
        acc = acc * fade + dot_f32(kvt_ref[HEAD_DIM:, at], weights.astype(BF))
        return new_peak, total, acc

    start = (
        jnp.full((1, TILE), NEG, F32),
        jnp.zeros((1, TILE), F32),
        jnp.zeros((HEAD_DIM, TILE), F32),
    )
    peak, total, acc = lax.fori_loop(first, step + 1, body, start)
    out_ref[:, here] = acc / total
    lse_ref[:, here] = peak + jnp.log(total)

    @pl.when(step == length // TILE - 1)
    def _():
        def home(d, carry):
            tile = pick_pair(lambda k: out_ref[:, span(k, 128)], order, d)
            low_ref[lax.div(d, per), :, span(lax.rem(d, per), 128)] = tile.astype(BF)
            return carry

        lax.fori_loop(0, length // 128, home, 0)


def sorted_back_kernel(
    lengths, order, flow_ref, out_ref, lse_ref, q_ref, kvt_ref, rows_ref,
    grad_ref, do_ref, dq_ref, acc_ref, inverse,
):
    step = pl.program_id(0)
    length = q_ref.shape[1]
    per = grad_ref.shape[3] // 128

    @pl.when(step == 0)
    def _():
        acc_ref[...] = jnp.zeros_like(acc_ref)
        fill_inverse(order, inverse, length // BLOCK)

        def place(d, carry):
            tile = pick_pair(lambda k: flow_ref[k].astype(F32), inverse, d)
            at = span(d, 128)
            do_ref[:HEAD_DIM, at] = jnp.zeros((HEAD_DIM, 128), BF)
            do_ref[HEAD_DIM:, at] = tile.astype(BF)
            return carry

        lax.fori_loop(0, length // 128, place, 0)

    here = span(step, TILE)
    queries, flows = q_ref[:, here], do_ref[:, here]
    place, low, first = query_lows(lengths, step)
    log_total = lse_ref[:, here]
    delta = jnp.sum(flows[HEAD_DIM:, :].astype(F32) * out_ref[:, here], axis=0, keepdims=True)

    def body(kt, dq):
        at = span(kt, TILE)
        rows = rows_ref[at, :]
        scores = dot_f32(rows, queries)
        allowed = mask_of(kt, key_places(True, kt, None), place, low)
        chances = jnp.exp(jnp.where(allowed, scores - log_total, NEG))
        flow = dot_f32(rows, flows)
        score_grad = (chances * (flow - delta)).astype(BF)
        dq = dq + dot_f32(kvt_ref[:HEAD_DIM, at], score_grad)
        acc_ref[:HEAD_DIM, at] += contract_cols(queries[:HEAD_DIM, :], score_grad)
        acc_ref[HEAD_DIM:, at] += contract_cols(flows[HEAD_DIM:, :], chances.astype(BF))
        return dq

    dq = lax.fori_loop(
        first, step + 1, body, jnp.zeros((HEAD_DIM, TILE), F32)
    )
    dq_ref[:, here] = dq * SCALE

    @pl.when(step == length // TILE - 1)
    def _():
        def home(d, carry):
            at = span(lax.rem(d, per), 128)
            tile = pick_pair(lambda k: dq_ref[:, span(k, 128)], order, d)
            grad_ref[lax.div(d, per), 0, :, at] = tile.astype(BF)
            tile = pick_pair(lambda k: acc_ref[:, span(k, 128)], order, d).astype(BF)
            grad_ref[lax.div(d, per), 1, :, at] = tile[:HEAD_DIM]
            grad_ref[lax.div(d, per), 2, :, at] = tile[HEAD_DIM:]
            return carry

        lax.fori_loop(0, length // 128, home, 0)


def fixed(shape):
    return pl.BlockSpec(shape, lambda i: (0,) * len(shape))


def sorted_attend(lengths, order, parts):
    groups, _, columns = parts.shape
    length = groups * columns
    shapes = (
        ((groups, HEAD_DIM, columns), BF),
        ((HEAD_DIM, length), F32),
        ((1, length), F32),
        ((2 * HEAD_DIM, length), BF),
        ((2 * HEAD_DIM, length), BF),
        ((length, 2 * HEAD_DIM), BF),
    )
    return pl.pallas_call(
        sorted_attend_kernel,
        name="attend",
        grid=(length // TILE,),
        in_specs=[pl.BlockSpec(memory_space=pltpu.SMEM)] * 2 + [fixed(parts.shape)],
        out_specs=tuple(fixed(s) for s, _ in shapes),
        out_shape=tuple(jax.ShapeDtypeStruct(s, d) for s, d in shapes),
        scratch_shapes=[pltpu.SMEM((length // BLOCK,), jnp.int32)],
        compiler_params=pltpu.CompilerParams(vmem_limit_bytes=60 * 2**20),
        cost_estimate=pl.CostEstimate(
            flops=0, bytes_accessed=42_000_000, transcendentals=0
        ),
    )(lengths, order, parts)


def sorted_back(lengths, order, flow, out, lse, q_pad, kv_t, kv_rows, groups):
    length = out.shape[1]
    grad = (groups, 3, HEAD_DIM, length // groups)
    return pl.pallas_call(
        sorted_back_kernel,
        name="attend_back",
        grid=(length // TILE,),
        in_specs=[pl.BlockSpec(memory_space=pltpu.SMEM)] * 2
        + [fixed(a.shape) for a in (flow, out, lse, q_pad, kv_t, kv_rows)],
        out_specs=fixed(grad),
        out_shape=jax.ShapeDtypeStruct(grad, BF),
        scratch_shapes=[
            pltpu.VMEM((2 * HEAD_DIM, length), BF),
            pltpu.VMEM((HEAD_DIM, length), F32),
            pltpu.VMEM((2 * HEAD_DIM, length), F32),
            pltpu.SMEM((length // BLOCK,), jnp.int32),
        ],
        compiler_params=pltpu.CompilerParams(vmem_limit_bytes=40 * 2**20),
        cost_estimate=pl.CostEstimate(
            flops=0, bytes_accessed=42_000_000, transcendentals=0
        ),
    )(lengths, order, flow, out, lse, q_pad, kv_t, kv_rows)


def normalize(values):
    center = values - jnp.mean(values, axis=-1, keepdims=True)
    spread = jnp.mean(center * center, axis=-1, keepdims=True)
    scale = lax.rsqrt(spread + EPS)
    return center * scale, scale


def mid_kernel(
    experts, team, member, att, wo, x, vec, rw, route, cot,
    second, dgrad, send_s, send_g, sel, mixes, middle_own, prob_own, hot_own, second_own, att_own,
    egrad,
):
    rows = middle_own.shape[0]
    slots = send_s.shape[1]
    groups = send_s.shape[0]
    capacity = slots // team
    lane = lax.broadcasted_iota(jnp.int32, (rows, 128), 1)
    row = lax.broadcasted_iota(jnp.int32, (rows, rows), 0)
    col = lax.broadcasted_iota(jnp.int32, (rows, rows), 1)
    me = member[0]

    def block(b, carry):
        at = span(b, rows)
        part = att[:, at]
        middle = x[at, :].astype(F32) + contract_rows(part, wo[...])
        hat, _ = normalize(middle)
        low = (hat * vec[5:6, :] + vec[7:8, :]).astype(BF)
        second[at, :] = low
        logits = dot_f32(low, rw[...])
        is_expert = lane < experts
        is_mix = (lane >= experts) & (lane < experts + 2)
        pe = jnp.where(is_expert, logits, NEG)
        pe = jnp.exp(pe - jnp.max(pe, axis=1, keepdims=True))
        pe = pe / jnp.sum(pe, axis=1, keepdims=True)
        pm = jnp.where(is_mix, logits, NEG)
        pm = jnp.exp(pm - jnp.max(pm, axis=1, keepdims=True))
        pm = pm / jnp.sum(pm, axis=1, keepdims=True)
        route_row = jnp.broadcast_to(route[b][0:1, :], (rows, rows))
        route_col = jnp.sum(jnp.where(row == col, route_row, 0), axis=1, keepdims=True)
        hot = lane == route_col
        gate = jnp.sum(jnp.where(hot, pe, 0.0), axis=1, keepdims=True)
        mix0 = jnp.sum(jnp.where(lane == experts, pm, 0.0), axis=1, keepdims=True)
        mix1 = jnp.sum(jnp.where(lane == experts + 1, pm, 0.0), axis=1, keepdims=True)
        scaled = mix1 * gate
        flow = cot[at, :].astype(F32)
        dgrad[at, :] = (flow * mix0).astype(BF)
        egrad[at, :] = (flow * scaled).astype(BF)
        mixes[at, :] = jnp.where(lane == 0, mix0, jnp.where(lane == 1, scaled, 0.0))
        same = (route_row == route_col) & (col < row)
        rank = jnp.sum(jnp.where(same, 1, 0), axis=1, keepdims=True)
        group = lax.div(route_col, team)
        mine = lax.rem(route_col, team) == me
        target = jnp.where(mine, group * slots + b * capacity + rank, groups * slots)
        slot = lax.broadcasted_iota(jnp.int32, (rows, groups * slots), 1)
        sel[at, :] = jnp.where(slot == target, 1.0, 0.0).astype(BF)

        @pl.when(b == me)
        def _():
            middle_own[...] = middle
            prob_own[...] = jnp.where(is_expert, pe, jnp.where(is_mix, pm, 0.0))
            hot_own[...] = jnp.where(hot, 1.0, 0.0)
            second_own[...] = low
            att_own[...] = part

        return carry

    lax.fori_loop(0, team, block, 0)
    send_s[...] = contract_rows(sel[...], second[...]).astype(BF).reshape(send_s.shape)
    send_g[...] = contract_rows(sel[...], egrad[...]).astype(BF).reshape(send_g.shape)


def between(experts, sizes, slots, member, att, wo, x, vec, rw, route, cot):
    two, groups, team = sizes
    group_rows, width = x.shape
    rows = group_rows // team
    shapes = (
        ((group_rows, width), BF),
        ((group_rows, width), BF),
        ((groups, slots, width), BF),
        ((groups, slots, width), BF),
        ((group_rows, groups * slots), BF),
        ((group_rows, 128), F32),
        ((rows, width), F32),
        ((rows, 128), F32),
        ((rows, 128), F32),
        ((rows, width), BF),
        ((width, rows), BF),
    )
    inside = pl.BlockSpec(memory_space=pltpu.VMEM)
    return pl.pallas_call(
        functools.partial(mid_kernel, experts, team),
        name="between",
        in_specs=[pl.BlockSpec(memory_space=pltpu.SMEM)] + [inside] * 7,
        out_specs=tuple(inside for _ in shapes),
        out_shape=tuple(jax.ShapeDtypeStruct(s, d) for s, d in shapes),
        scratch_shapes=[pltpu.VMEM((group_rows, width), BF)],
        compiler_params=pltpu.CompilerParams(vmem_limit_bytes=60 * 2**20),
    )(member, att, wo, x, vec, rw, route, cot)


def turn_kernel(
    experts, layer_sum, second_sum, sums, middle, prob, hot, second, att, cot, rw, wo, vec,
    layer, middle_grad, flow_t, out_term, small_t,
):
    rows = middle.shape[0]
    lane = lax.broadcasted_iota(jnp.int32, (rows, 128), 1)
    layer[...] = (middle[...] + layer_sum[...]).astype(BF)
    chances, chosen = prob[...], hot[...]
    s0, s1 = sums[:, 0:1], sums[:, 1:2]
    mix1 = jnp.sum(jnp.where(lane == experts + 1, chances, 0.0), axis=1, keepdims=True)
    gate = jnp.sum(chances * chosen, axis=1, keepdims=True)
    pull_gate = s1 * mix1
    pulls = jnp.where(lane == experts, s0, jnp.where(lane == experts + 1, s1 * gate, 0.0))
    mean_pull = jnp.sum(chances * pulls, axis=1, keepdims=True)
    logit_grad = chances * jnp.where(
        lane < experts, pull_gate * (chosen - gate), pulls - mean_pull
    )
    logit_grad = jnp.where(lane < experts + 2, logit_grad, 0.0).astype(BF)
    second_grad = second_sum[...] + contract_cols(logit_grad, rw[...])
    hat, scale = normalize(middle[...])
    pull = second_grad * vec[5:6, :]
    part = scale * (
        pull
        - jnp.mean(pull, axis=-1, keepdims=True)
        - hat * jnp.mean(pull * hat, axis=-1, keepdims=True)
    )
    grad = cot[...].astype(F32) + part
    middle_grad[...] = grad
    branch = grad.astype(BF)
    width = wo.shape[0]

    def tile(n, carry):
        at = span(n, TILE)
        flow_t[at, :] = contract_cols(wo[at, :], branch).astype(BF)
        out_term[at, :] = dot_f32(att[at, :], branch).astype(BF)
        return carry

    lax.fori_loop(0, width // TILE, tile, 0)
    used = small_t.shape[0]
    routed = contract_rows(logit_grad, second[...])[:used, :]
    which = lax.broadcasted_iota(jnp.int32, routed.shape, 0)
    gain = jnp.sum(second_grad * hat, axis=0, keepdims=True)
    bias = jnp.sum(second_grad, axis=0, keepdims=True)
    small_t[...] = jnp.where(
        which == experts + 3, gain, jnp.where(which == experts + 5, bias, routed)
    )


def turn(experts, layer_sum, second_sum, sums, middle, prob, hot, second, att, cot, rw, wo, vec):
    rows, width = middle.shape
    used = -(-(experts + 6) // 8) * 8
    shapes = (
        ((rows, width), BF),
        ((rows, width), F32),
        ((width, rows), BF),
        ((width, width), BF),
        ((used, width), F32),
    )
    inside = pl.BlockSpec(memory_space=pltpu.VMEM)
    return pl.pallas_call(
        functools.partial(turn_kernel, experts),
        name="turn",
        in_specs=[inside] * 12,
        out_specs=tuple(inside for _ in shapes),
        out_shape=tuple(jax.ShapeDtypeStruct(s, d) for s, d in shapes),
        compiler_params=pltpu.CompilerParams(vmem_limit_bytes=40 * 2**20),
    )(layer_sum, second_sum, sums, middle, prob, hot, second, att, cot, rw, wo, vec)


def row_sum_kernel(left, right, out):
    out[0] = contract_rows(left[...], right[...])


def row_sum(left, right, tile):
    many, high = left.shape
    wide = right.shape[1]
    return pl.pallas_call(
        row_sum_kernel,
        name="row_sum",
        grid=(high // tile,),
        in_specs=[pl.BlockSpec((many, tile), lambda i: (0, i)), fixed(right.shape)],
        out_specs=pl.BlockSpec((1, tile, wide), lambda i: (0, i, 0)),
        out_shape=jax.ShapeDtypeStruct((1, high, wide), F32),
        compiler_params=pltpu.CompilerParams(vmem_limit_bytes=40 * 2**20),
        cost_estimate=pl.CostEstimate(
            flops=2 * many * high * wide, bytes_accessed=4 * high * wide, transcendentals=0
        ),
    )(left, right)


class Net:
    def __init__(self, sizes, send_sem, recv_sem):
        self.two, self.groups, self.team = sizes
        self.send_sem, self.recv_sem = send_sem, recv_sem
        self.c = lax.axis_index("dp")
        i = lax.axis_index("ctx")
        self.g, self.t = lax.div(i, self.team), lax.rem(i, self.team)
        self.group_steps = [(0, k, 0) for k in range(1, self.groups)]
        self.team_steps = [(0, 0, k) for k in range(1, self.team)]
        self.swap = (1, 0, 0)
        self.started = []

    def device(self, step):
        dc, dg, dt = step
        return (
            lax.rem(self.c + dc, self.two),
            lax.rem(self.g + dg, self.groups) * self.team + lax.rem(self.t + dt, self.team),
        )

    def greet(self):
        barrier = pltpu.get_barrier_semaphore()
        steps = self.group_steps + self.team_steps + [self.swap]
        for step in steps:
            pl.semaphore_signal(barrier, inc=1, device_id=self.device(step), device_id_type=MESH)
        pl.semaphore_wait(barrier, len(steps))

    def send(self, src, dst, step):
        k = len(self.started)
        copy = pltpu.make_async_remote_copy(
            src_ref=src,
            dst_ref=dst,
            send_sem=self.send_sem.at[k],
            recv_sem=self.recv_sem.at[k],
            device_id=self.device(step),
            device_id_type=MESH,
        )
        copy.start()
        self.started.append(copy)
        return copy

    def group_to(self, step):
        return lax.rem(self.g + step[1], self.groups)

    def group_from(self, step):
        return lax.rem(self.g + self.groups - step[1], self.groups)

    def team_to(self, step):
        return lax.rem(self.t + step[2], self.team)

    def team_from(self, step):
        return lax.rem(self.t + self.team - step[2], self.team)

    def close(self):
        for copy in self.started:
            copy.wait_send()


def arrive(copies):
    for copy in copies:
        copy.wait_recv()


class Local:
    def __init__(self, sem):
        self.sem, self.count, self.open = sem, 0, []

    def copy(self, src, dst):
        made = pltpu.make_async_copy(src, dst, self.sem.at[self.count])
        made.start()
        self.count += 1
        self.open.append(made)
        return made

    def wait(self, *copies):
        for made in copies or tuple(self.open):
            made.wait()
            self.open = [other for other in self.open if other is not made]


def start_kernel(sizes, *refs):
    tokens, cot, w_qkv, w_up, w_down, w_out, router, gains, biases, routes = refs[:10]
    token_o, cot_o, heads_o, normed_o, weight_o, vec_o, out_o, ff_o, route_o = refs[10:19]
    (
        own, up, down, route, square, stage, weights, tokens_v, normed, mixed, heads, out_v,
        send_sem, recv_sem, local_sem,
    ) = refs[19:]
    net, local = Net(sizes, send_sem, recv_sem), Local(local_sem)
    c, g, t = net.c, net.g, net.t
    two, groups, team = sizes
    rows, width = tokens.shape
    used = own.shape[2] - 128
    wr = own.shape[1]
    own_tokens = local.copy(tokens, tokens_v.at[t])
    local.copy(cot, cot_o.at[t])

    square[...] = jnp.zeros_like(square)
    square[: router.shape[0], :wr] = router[...]
    square[124:126, :wr] = gains[...]
    square[126:128, :wr] = biases[...]
    small = square[...].T[:wr, :].astype(BF)
    third = used // 3
    for n in range(team):
        for k in range(3):
            at = k * width + n * third
            own[n, :, k * third : (k + 1) * third] = w_qkv[:, at : at + third].astype(BF)
        own[n, :, used:] = small
    stage[t] = own[t]
    net.greet()
    staged = [net.send(own.at[net.team_to(s)], stage.at[t], s) for s in net.team_steps]
    told = [net.send(tokens, tokens_v.at[t], s) for s in net.team_steps]
    out_v[g] = w_out[...].astype(BF)
    spread_out = [net.send(out_v.at[g], out_v.at[g], s) for s in net.group_steps]
    deep = w_down.shape[0]
    for n in range(team):
        for k in range(two * groups):
            at = (k * team + n) * deep
            up[n, :, k * deep : (k + 1) * deep] = w_up[:, at : at + deep].astype(BF)
    down[...] = w_down[...].astype(BF).reshape(down.shape)
    route[...] = jnp.broadcast_to(routes[...], route.shape)
    local.copy(up.at[t], ff_o.at[0, t])
    local.copy(down, ff_o.at[1])
    local.copy(route, route_o.at[t])
    later = [net.send(route, route_o.at[t], s) for s in net.team_steps]
    later += [net.send(up.at[net.team_to(s)], ff_o.at[0, t], s) for s in net.team_steps]
    arrive(staged)
    spread = [net.send(stage, weights.at[c, g], s) for s in net.group_steps]
    swapped = [net.send(stage, weights.at[c, g], net.swap)]
    mine = local.copy(stage, weights.at[c, g])
    later += [net.send(cot, cot_o.at[t], s) for s in net.team_steps]
    local.wait(own_tokens)
    arrive(told)
    local.copy(tokens_v, token_o)
    local.wait(mine)
    for copy, s in zip(spread, net.group_steps):
        copy.wait_recv()
        view = weights.at[c, net.group_from(s)]
        swapped.append(net.send(view, view, net.swap))
    arrive(swapped)
    local.copy(weights, weight_o)

    small = weights[:, :, :, :, used:].reshape(width, 128).astype(F32).T
    vec_o[...] = small[120:, :]

    def norm(b, carry):
        hat, _ = normalize(tokens_v[b].astype(F32))
        normed[b] = (hat * vec_o[4:5, :] + vec_o[6:7, :]).astype(BF)
        return carry

    lax.fori_loop(0, team, norm, 0)
    local.copy(normed, normed_o)
    group_rows = rows * team
    per = used // 3 // 128
    pair = 128 // HEAD_DIM
    for n in range(used // 128):
        columns = weights[:, :, :, :, n * 128 : (n + 1) * 128].reshape(width, 128)
        made = dot_f32(normed[...].reshape(group_rows, width), columns).T.astype(BF)
        at = (n % per) * pair
        mixed[n // per, at : at + pair] = made.reshape(pair, HEAD_DIM, group_rows)
    given = [net.send(mixed.at[:, net.group_to(s)], heads.at[g], s) for s in net.group_steps]
    local.wait(local.copy(mixed.at[:, g], heads.at[g]))

    arrive(spread_out)
    local.copy(out_v, out_o.at[c, :, t])
    swapped = [net.send(out_v, out_o.at[c, :, t], net.swap)]
    outed = [net.send(out_v, out_o.at[c, :, t], s) for s in net.team_steps]
    for copy, s in zip(outed, net.team_steps):
        copy.wait_recv()
        view = out_o.at[c, :, net.team_from(s)]
        swapped.append(net.send(view, view, net.swap))
    arrive(given)
    local.copy(heads, heads_o)
    arrive(swapped + later)
    local.wait()
    net.close()


def start(sizes, tokens, cot, w_qkv, w_up, w_down, w_out, router, gains, biases, routes):
    two, groups, team = sizes
    rows, width = tokens.shape
    wr = w_qkv.shape[0]
    used = 3 * width // team
    cols = used + 128
    head = (3, groups, HEAD_DIM, team * rows)
    up = (team, wr, width)
    shapes = (
        ((team, rows, width), BF),
        ((team, rows, width), BF),
        ((groups, 3, HEAD_DIM, team * rows), BF),
        ((team, rows, width), BF),
        ((two, groups, team, wr, cols), BF),
        ((8, width), F32),
        ((two, groups, team, wr, width), BF),
        ((2,) + up, BF),
        ((team, 8, rows), jnp.int32),
    )
    anywhere = pl.BlockSpec(memory_space=pl.ANY)
    inside = pl.BlockSpec(memory_space=pltpu.VMEM)
    count = 6 * (team - 1) + 4 * (groups - 1) + 2 + (team - 1)
    return pl.pallas_call(
        functools.partial(start_kernel, sizes),
        name="start",
        out_shape=tuple(jax.ShapeDtypeStruct(s, d) for s, d in shapes),
        in_specs=[anywhere] * 2 + [inside] * 8,
        out_specs=tuple(inside if n == 5 else anywhere for n in range(9)),
        scratch_shapes=[
            pltpu.VMEM((team, wr, cols), BF),
            pltpu.VMEM(up, BF),
            pltpu.VMEM(up, BF),
            pltpu.VMEM((8, rows), jnp.int32),
            pltpu.VMEM((128, 128), F32),
            pltpu.VMEM((team, wr, cols), BF),
            pltpu.VMEM((two, groups, team, wr, cols), BF),
            pltpu.VMEM((team, rows, width), BF),
            pltpu.VMEM((team, rows, width), BF),
            pltpu.VMEM(head, BF),
            pltpu.VMEM((groups, 3, HEAD_DIM, team * rows), BF),
            pltpu.VMEM((groups, wr, width), BF),
            pltpu.SemaphoreType.DMA((count,)),
            pltpu.SemaphoreType.DMA((count,)),
            pltpu.SemaphoreType.DMA((14,)),
        ],
        compiler_params=pltpu.CompilerParams(
            collective_id=12, has_side_effects=True, vmem_limit_bytes=60 * 2**20
        ),
        cost_estimate=pl.CostEstimate(flops=0, bytes_accessed=150_000_000, transcendentals=0),
    )(tokens, cot, w_qkv, w_up, w_down, w_out, router, gains, biases, routes)


def end_kernel(sizes, experts, *refs):
    groups = sizes[1]
    parts, refs = refs[:groups], refs[groups:]
    weight, normed, tokens, vec, middle_grad, small, up, out = refs[:8]
    grad_o, qkv_o, up_o, out_o, small_o = refs[8:13]
    (
        up_r, small_d, mixed, turned, weights, normed_v, give, got, zsend, zrecv, npart, nrecv, qsend, qrecv,
        out_r, small_a, small_b, small_c, send_sem, recv_sem, local_sem,
    ) = refs[13:]
    net, local = Net(sizes, send_sem, recv_sem), Local(local_sem)
    c, g, t = net.c, net.g, net.t
    team = sizes[2]
    rows, width = tokens.shape
    group_rows, used = turned.shape
    for k, part in enumerate(parts):
        local.copy(part, mixed.at[:, net.group_from((0, k, 0))])
    local.copy(normed, normed_v)
    local.copy(weight, weights)
    local.copy(up.at[t], up_r.at[t])
    local.copy(out.at[g], out_r.at[g])
    net.greet()
    outed = [net.send(out.at[net.group_to(s)], out_r.at[g], s) for s in net.group_steps]
    later = [net.send(up.at[net.team_to(s)], up_r.at[t], s) for s in net.team_steps]
    local.wait()
    per = used // 3 // 128
    pair = 128 // HEAD_DIM
    for n in range(used // 128):
        at = (n % per) * pair
        block = mixed[n // per, at : at + pair].reshape(128, group_rows)
        turned[:, n * 128 : (n + 1) * 128] = block.astype(F32).T.astype(BF)

    half = width // 2
    tile = 128

    def term(core, n):
        at = pl.ds(pl.multiple_of(core * half + n * tile, tile), tile)
        left = normed_v[:, :, at].reshape(group_rows, tile)
        return contract_rows(left, turned[...])

    def giving(n, carry):
        give[span(n, tile), :] = term(lax.rem(c + 1, 2), n).astype(BF)
        return carry

    lax.fori_loop(0, half // tile, giving, 0)
    crossed = net.send(give, got, net.swap)

    def part_of(r, carry):
        columns = weights[:, :, :, :, :used].reshape(width, used)
        npart[r] = contract_cols(turned[span(r, rows), :], columns).astype(BF)
        return carry

    lax.fori_loop(0, team, part_of, 0)
    owned = [net.send(npart.at[net.team_to(s)], nrecv.at[t], s) for s in net.team_steps]
    nrecv[t] = npart[t]
    crossed.wait_recv()

    def keeping(n, carry):
        at = span(n, tile)
        zsend[at, :] = (term(c, n) + got[at, :].astype(F32)).astype(BF)
        return carry

    lax.fori_loop(0, half // tile, keeping, 0)
    deep = half // groups
    summed = [
        net.send(zsend.at[span(net.group_to(s), deep), :], zrecv.at[g], s)
        for s in net.group_steps
    ]
    zrecv[g] = zsend[span(g, deep), :]

    arrive(owned)
    flow = jnp.sum(nrecv[...].astype(F32), axis=0)
    hat, scale = normalize(tokens[...].astype(F32))
    pull = flow * vec[4:5, :]
    pulled = scale * (
        pull
        - jnp.mean(pull, axis=-1, keepdims=True)
        - hat * jnp.mean(pull * hat, axis=-1, keepdims=True)
    )
    grad_o[...] = (middle_grad[...] + pulled).astype(BF)

    gain = jnp.sum(flow * hat, axis=0, keepdims=True)
    bias = jnp.sum(flow, axis=0, keepdims=True)
    which = lax.broadcasted_iota(jnp.int32, small.shape, 0)
    mine = jnp.where(
        which == experts + 2, gain, jnp.where(which == experts + 4, bias, small[...])
    )
    small_a[c] = mine
    crossing = net.send(small_a.at[c], small_a.at[c], net.swap)
    crossing.wait_recv()
    small_c[...] = small_a[0] + small_a[1]

    def columns_of(k):
        return span(c * groups + k, 128)

    moved = [
        net.send(small_c.at[:, columns_of(net.group_to(s))], small_b.at[g], s)
        for s in net.group_steps
    ]
    small_b[g] = small_c[:, columns_of(g)]
    arrive(moved)
    small_d[t] = jnp.sum(small_b[...], axis=0)
    later += [net.send(small_d.at[t], small_d.at[t], s) for s in net.team_steps]

    arrive(summed)
    qsend[...] = jnp.sum(zrecv[...].astype(F32), axis=0).astype(BF).reshape(qsend.shape)
    later += [net.send(qsend.at[net.team_to(s)], qrecv.at[t], s) for s in net.team_steps]
    qrecv[t] = qsend[t]
    arrive(outed)
    out_o[...] = jnp.sum(out_r[...].astype(F32), axis=0)
    arrive(later)
    small_o[...] = jnp.sum(small_d[...], axis=0)
    third = used // 3
    deep = up_o.shape[1] // (2 * groups * team)
    for n in range(team):
        for k in range(3):
            at = k * width + n * third
            qkv_o[:, at : at + third] = qrecv[n, :, k * third : (k + 1) * third].astype(F32)
        for k in range(2 * groups):
            at = (k * team + n) * deep
            up_o[:, at : at + deep] = up_r[n, :, k * deep : (k + 1) * deep].astype(F32)
    net.close()


def end(sizes, experts, parts, weight, normed, tokens, vec, middle_grad, small, up, out):
    two, groups, team = sizes
    rows, width = tokens.shape
    wr = out.shape[1]
    used = 3 * groups * HEAD_DIM
    group_rows = parts[0].shape[2]
    half = width // 2
    shapes = (
        ((rows, width), BF),
        ((wr, 3 * width), F32),
        ((wr, team * width), F32),
        ((wr, width), F32),
        ((small.shape[0], 128), F32),
    )
    anywhere = pl.BlockSpec(memory_space=pl.ANY)
    inside = pl.BlockSpec(memory_space=pltpu.VMEM)
    count = 5 * (team - 1) + 3 * (groups - 1) + 2
    return pl.pallas_call(
        functools.partial(end_kernel, sizes, experts),
        name="end",
        out_shape=tuple(jax.ShapeDtypeStruct(s, d) for s, d in shapes),
        in_specs=[anywhere] * (groups + 2) + [inside] * 4 + [anywhere] * 2,
        out_specs=tuple(inside for _ in shapes),
        scratch_shapes=[
            pltpu.VMEM((team, wr, width), BF),
            pltpu.VMEM((team, small.shape[0], 128), F32),
            pltpu.VMEM((3, groups, HEAD_DIM, group_rows), BF),
            pltpu.VMEM((group_rows, used), BF),
            pltpu.VMEM(weight.shape, BF),
            pltpu.VMEM(normed.shape, BF),
            pltpu.VMEM((half, used), BF),
            pltpu.VMEM((half, used), BF),
            pltpu.VMEM((half, used), BF),
            pltpu.VMEM((groups, half // groups, used), BF),
            pltpu.VMEM((team, rows, width), BF),
            pltpu.VMEM((team, rows, width), BF),
            pltpu.VMEM((team, wr, used), BF),
            pltpu.VMEM((team, wr, used), BF),
            pltpu.VMEM((groups, wr, width), BF),
            pltpu.VMEM((2,) + small.shape, F32),
            pltpu.VMEM((groups, small.shape[0], 128), F32),
            pltpu.VMEM(small.shape, F32),
            pltpu.SemaphoreType.DMA((count,)),
            pltpu.SemaphoreType.DMA((count,)),
            pltpu.SemaphoreType.DMA((groups + 4,)),
        ],
        compiler_params=pltpu.CompilerParams(
            collective_id=13, has_side_effects=True, vmem_limit_bytes=60 * 2**20
        ),
        cost_estimate=pl.CostEstimate(flops=0, bytes_accessed=120_000_000, transcendentals=0),
    )(*parts, weight, normed, tokens, vec, middle_grad, small, up, out)


def gelu_and_slope(x):
    k = math.sqrt(2.0 / math.pi)
    square = x * x
    bent = jnp.tanh(k * (x + 0.044715 * (square * x)))
    half = 0.5 * (1.0 + bent)
    slope = half + (0.5 * k) * x * (1.0 - bent * bent) * (1.0 + (3 * 0.044715) * square)
    return x * half, slope


def feed_kernel(sizes, copies_count, *refs):
    two, groups, team = sizes
    (send_s, send_g, eup_h, edown_h, second_h, dgrad_h, ff_h, sel_h, cot_h, mix_h) = refs[:10]
    (layer_o, grad_o, sums_o, active_o, hgrad_o, arr_s_o, arr_g_o, ffg_o) = refs[10:18]
    (
        arr_s, arr_g, eup, edown, second, dgrad, upw, downw, sel, cot, mix,
        slope, active, hgrad, acc, give, got_s, got_g, ret_s, ret_g, back_s, back_g,
        low, ugrad, dense, spart, lay, spa, sums, lay_r, spa_r, sums_r,
        term_give, term_got, send_sem, recv_sem, load_sem, out_sem,
    ) = refs[18:]
    c = lax.axis_index("dp")
    i = lax.axis_index("ctx")
    g, t = lax.div(i, team), lax.rem(i, team)
    width = second.shape[1]
    rows = lay.shape[1]
    hid, ehid = upw.shape[1], eup.shape[1]
    core = lax.rem(c + 1, two)

    def device(step):
        dc, dg, dt = step
        return (
            lax.rem(c + dc, two),
            lax.rem(g + dg, groups) * team + lax.rem(t + dt, team),
        )

    index = [0]

    def remote(src, dst, step):
        k = index[0]
        index[0] += 1
        assert k < copies_count
        return pltpu.make_async_remote_copy(
            src_ref=src,
            dst_ref=dst,
            send_sem=send_sem.at[k],
            recv_sem=recv_sem.at[k],
            device_id=device(step),
            device_id_type=MESH,
        )

    group_steps = [(0, k, 0) for k in range(1, groups)]
    team_steps = [(0, 0, k) for k in range(1, team)]
    swap = (1, 0, 0)
    deep = ff_h.shape[2]

    def block_of(core, k):
        return pl.ds(pl.multiple_of((core * groups + k) * deep, deep), deep)

    loads = []
    for k, (src, dst) in enumerate(
        [
            (second_h, second), (dgrad_h, dgrad), (eup_h, eup), (edown_h, edown), (sel_h, sel), (cot_h, cot), (mix_h, mix),
            (send_s.at[g], arr_s.at[c, g]), (send_g.at[g], arr_g.at[c, g]),
        ]
        + [
            (ff_h.at[k, n], weight.at[block_of(c, k), :])
            for k in range(groups)
            for n, weight in enumerate((upw, downw))
        ]
    ):
        load = pltpu.make_async_copy(src, dst, load_sem.at[k])
        load.start()
        loads.append(load)

    barrier = pltpu.get_barrier_semaphore()
    greet = group_steps + team_steps + [swap]
    for step in greet:
        pl.semaphore_signal(barrier, inc=1, device_id=device(step), device_id_type=MESH)
    pl.semaphore_wait(barrier, len(greet))

    every = []

    def launch(copy):
        copy.start()
        every.append(copy)
        return copy

    def to_groups(src, dst):
        return [
            launch(remote(src.at[lax.rem(g + s[1], groups)], dst.at[g], s)) for s in group_steps
        ]

    def source(s):
        return lax.rem(g + groups - s[1], groups)

    swap_w = [
        launch(remote(ff_h.at[k, n], weight.at[block_of(c, k), :], swap))
        for k in range(groups)
        for n, weight in enumerate((upw, downw))
    ]
    out_s = [
        launch(remote(send_s.at[lax.rem(g + s[1], groups)], arr_s.at[c, g], s))
        for s in group_steps
    ]
    swap_s = [launch(remote(send_s.at[g], arr_s.at[c, g], swap))]
    out_g = [
        launch(remote(send_g.at[lax.rem(g + s[1], groups)], arr_g.at[c, g], s))
        for s in group_steps
    ]
    swap_g = [launch(remote(send_g.at[g], arr_g.at[c, g], swap))]

    for load in loads[:2] + loads[9:]:
        load.wait()
    for copy in swap_w:
        copy.wait_recv()

    def dense_in(h, carry):
        at = span(h, TILE)
        value, bend = gelu_and_slope(dot_f32(second[...], upw[:, at]))
        low[:, at] = value.astype(BF)
        ugrad[:, at] = (bend * contract_cols(dgrad[...], downw[at, :])).astype(BF)
        return carry

    lax.fori_loop(0, hid // TILE, dense_in, 0)

    def dense_out(n, carry):
        at = span(n, TILE)
        dense[:, at] = dot_f32(low[...], downw[:, at])
        spart[:, at] = contract_cols(ugrad[...], upw[at, :])
        return carry

    lax.fori_loop(0, width // TILE, dense_out, 0)

    for load in loads[2:9]:
        load.wait()
    for copy, s in zip(out_s, group_steps):
        copy.wait_recv()
        swap_s.append(launch(remote(arr_s.at[c, source(s)], arr_s.at[c, source(s)], swap)))
    for copy in swap_s:
        copy.wait_recv()
    entries = 2 * groups * arr_s.shape[2]

    def expert_in(h, carry):
        at = span(h, TILE)
        value, bend = gelu_and_slope(dot_f32(arr_s[...].reshape(entries, width), eup[:, at]))
        active[:, at] = value.astype(BF)
        slope[:, at] = bend
        return carry

    lax.fori_loop(0, ehid // TILE, expert_in, 0)
    keeps = [
        pltpu.make_async_copy(active, active_o, out_sem.at[0]),
        pltpu.make_async_copy(arr_s, arr_s_o, out_sem.at[1]),
    ]
    for copy in keeps:
        copy.start()

    def expert_out(n, carry):
        at = span(n, TILE)
        acc[:, :, at] = dot_f32(active[...], edown[:, at]).reshape(2, entries // 2, TILE)
        return carry

    lax.fori_loop(0, width // TILE, expert_out, 0)
    give[0] = acc[core].astype(BF)
    other_s = launch(remote(give.at[0], got_s, swap))

    for copy, s in zip(out_g, group_steps):
        copy.wait_recv()
        swap_g.append(launch(remote(arr_g.at[c, source(s)], arr_g.at[c, source(s)], swap)))
    other_s.wait_recv()
    ret_s[...] = (acc[c] + got_s[...].astype(F32)).astype(BF).reshape(ret_s.shape)
    home_s = to_groups(ret_s, back_s)
    back_s[g] = ret_s[g]
    for copy in swap_g:
        copy.wait_recv()

    def expert_back(h, carry):
        at = span(h, TILE)
        pull = contract_cols(arr_g[...].reshape(entries, width), edown[at, :])
        hgrad[:, at] = (slope[:, at] * pull).astype(BF)
        return carry

    lax.fori_loop(0, ehid // TILE, expert_back, 0)
    keeps += [
        pltpu.make_async_copy(hgrad, hgrad_o, out_sem.at[2]),
        pltpu.make_async_copy(arr_g, arr_g_o, out_sem.at[3]),
    ]
    for copy in keeps[2:]:
        copy.start()

    def expert_back_out(n, carry):
        at = span(n, TILE)
        acc[:, :, at] = contract_cols(hgrad[...], eup[at, :]).reshape(2, entries // 2, TILE)
        return carry

    lax.fori_loop(0, width // TILE, expert_back_out, 0)
    give[1] = acc[core].astype(BF)
    other_g = launch(remote(give.at[1], got_g, swap))
    other_g.wait_recv()
    ret_g[...] = (acc[c] + got_g[...].astype(F32)).astype(BF).reshape(ret_g.shape)
    home_g = to_groups(ret_g, back_g)
    back_g[g] = ret_g[g]

    for copy in home_s:
        copy.wait_recv()
    slots = groups * back_s.shape[1]
    lane = lax.broadcasted_iota(jnp.int32, (rows, 128), 1)

    def join_layer(r, carry):
        at = span(r, rows)
        found = dot_f32(sel[at, :], back_s[...].reshape(slots, width))
        own = dense[at, :]
        flow = cot[at, :].astype(F32)
        mixes = mix[at, :]
        lay[r] = (mixes[:, 0:1] * own + mixes[:, 1:2] * found).astype(BF)
        plain = jnp.sum(flow * own, axis=1, keepdims=True)
        routed = jnp.sum(flow * found, axis=1, keepdims=True)
        sums[r] = jnp.where(lane == 0, plain, jnp.where(lane == 1, routed, 0.0))
        return carry

    lax.fori_loop(0, team, join_layer, 0)

    def to_team(src, dst):
        made = [launch(remote(src.at[lax.rem(t + s[2], team)], dst.at[t], s)) for s in team_steps]
        dst[t] = src[t]
        return made

    team_copies = to_team(lay, lay_r) + to_team(sums, sums_r)

    for copy in home_g:
        copy.wait_recv()

    def join_grad(r, carry):
        at = span(r, rows)
        found = dot_f32(sel[at, :], back_g[...].reshape(slots, width))
        spa[r] = (spart[at, :] + found).astype(BF)
        return carry

    lax.fori_loop(0, team, join_grad, 0)
    team_copies += to_team(spa, spa_r)

    half = hid // 2
    term_tile = 128

    def down_term(base, n):
        at = pl.ds(pl.multiple_of(base + n * term_tile, term_tile), term_tile)
        return contract_rows(low[:, at], dgrad[...])

    def up_term(base, n):
        at = pl.ds(pl.multiple_of(base + n * term_tile, term_tile), term_tile)
        return contract_rows(second[:, at], ugrad[...])

    terms = []
    for k, (term, size) in enumerate(((down_term, half), (up_term, width // 2))):

        def giving(n, carry, k=k, term=term, size=size):
            term_give[k, span(n, term_tile), :] = term(core * size, n).astype(BF)
            return carry

        lax.fori_loop(0, size // term_tile, giving, 0)
        terms.append(launch(remote(term_give.at[k], term_got.at[k], swap)))
    for k, (term, size) in enumerate(((down_term, half), (up_term, width // 2))):
        terms[k].wait_recv()

        def keeping(n, carry, k=k, term=term, size=size):
            at = span(n, term_tile)
            total = term(c * size, n) + term_got[k, at, :].astype(F32)
            ffg_o[at, k * width : (k + 1) * width] = total.astype(BF)
            return carry

        lax.fori_loop(0, size // term_tile, keeping, 0)

    for copy in team_copies:
        copy.wait_recv()
    layer_o[...] = jnp.sum(lay_r[...].astype(F32), axis=0)
    grad_o[...] = jnp.sum(spa_r[...].astype(F32), axis=0)
    sums_o[...] = jnp.sum(sums_r[...], axis=0)
    for copy in keeps:
        copy.wait()
    for copy in every:
        copy.wait_send()


def feed_forward(sizes, rows, send_s, send_g, eup, edown, second, dgrad, ff, sel, cot, mix):
    two, groups, team = sizes
    slots = send_s.shape[1]
    width = second.shape[1]
    hid, ehid = second.shape[1] * ff.shape[3] // width, eup.shape[1]
    entries = 2 * groups * slots
    count = 2 * (groups - 1) * 2 + 2 * groups + 2 + 3 * (team - 1) + 2 + 2 * groups
    arrived = (two, groups, slots, width)
    anywhere = pl.BlockSpec(memory_space=pl.ANY)
    inside = pl.BlockSpec(memory_space=pltpu.VMEM)
    team_rows = team * rows
    return pl.pallas_call(
        functools.partial(feed_kernel, sizes, count),
        name="feed_forward",
        out_shape=(
            jax.ShapeDtypeStruct((rows, width), F32),
            jax.ShapeDtypeStruct((rows, width), F32),
            jax.ShapeDtypeStruct((rows, 128), F32),
            jax.ShapeDtypeStruct((entries, ehid), BF),
            jax.ShapeDtypeStruct((entries, ehid), BF),
            jax.ShapeDtypeStruct(arrived, BF),
            jax.ShapeDtypeStruct(arrived, BF),
            jax.ShapeDtypeStruct((hid // 2, 2 * width), BF),
        ),
        in_specs=[anywhere] * 10,
        out_specs=(inside, inside, inside, anywhere, anywhere, anywhere, anywhere, inside),
        scratch_shapes=[
            pltpu.VMEM((two, groups, slots, width), BF),
            pltpu.VMEM((two, groups, slots, width), BF),
            pltpu.VMEM(eup.shape, BF),
            pltpu.VMEM(edown.shape, BF),
            pltpu.VMEM(second.shape, BF),
            pltpu.VMEM(dgrad.shape, BF),
            pltpu.VMEM((width, hid), BF),
            pltpu.VMEM((hid, width), BF),
            pltpu.VMEM(sel.shape, BF),
            pltpu.VMEM(cot.shape, BF),
            pltpu.VMEM(mix.shape, F32),
            pltpu.VMEM((entries, ehid), F32),
            pltpu.VMEM((entries, ehid), BF),
            pltpu.VMEM((entries, ehid), BF),
            pltpu.VMEM((2, entries // 2, width), F32),
            pltpu.VMEM((2, entries // 2, width), BF),
            pltpu.VMEM((entries // 2, width), BF),
            pltpu.VMEM((entries // 2, width), BF),
            pltpu.VMEM((groups, slots, width), BF),
            pltpu.VMEM((groups, slots, width), BF),
            pltpu.VMEM((groups, slots, width), BF),
            pltpu.VMEM((groups, slots, width), BF),
            pltpu.VMEM((team_rows, hid), BF),
            pltpu.VMEM((team_rows, hid), BF),
            pltpu.VMEM((team_rows, width), F32),
            pltpu.VMEM((team_rows, width), F32),
            pltpu.VMEM((team, rows, width), BF),
            pltpu.VMEM((team, rows, width), BF),
            pltpu.VMEM((team, rows, 128), F32),
            pltpu.VMEM((team, rows, width), BF),
            pltpu.VMEM((team, rows, width), BF),
            pltpu.VMEM((team, rows, 128), F32),
            pltpu.VMEM((2, hid // 2, width), BF),
            pltpu.VMEM((2, hid // 2, width), BF),
            pltpu.SemaphoreType.DMA((count,)),
            pltpu.SemaphoreType.DMA((count,)),
            pltpu.SemaphoreType.DMA((9 + 2 * groups,)),
            pltpu.SemaphoreType.DMA((4,)),
        ],
        compiler_params=pltpu.CompilerParams(
            collective_id=5, has_side_effects=True, vmem_limit_bytes=60 * 2**20
        ),
        cost_estimate=pl.CostEstimate(
            flops=0, bytes_accessed=240_000_000, transcendentals=0
        ),
    )(send_s, send_g, eup, edown, second, dgrad, ff, sel, cot, mix)


def tall(chunk):
    rows, cols = chunk.shape[-2:]
    factor = 1
    while (rows * factor) % 16:
        factor *= 2
    return chunk.reshape(chunk.shape[:-2] + (rows * factor, cols // factor))


def per_device_general(
    tokens,
    cotangent,
    block_order,
    doc_lengths,
    routes,
    w_qkv,
    w_out,
    w_up,
    w_down,
    router,
    norm_gains,
    norm_biases,
    expert_up,
    expert_down,
):
    rows, width = tokens.shape[1], tokens.shape[2]
    ctx_count = lax.axis_size("ctx")
    two = lax.axis_size("dp")
    team = math.gcd(4, ctx_count)
    groups = ctx_count // team
    sizes = (two, groups, team)
    team_heads = HEADS // team
    reps = groups // team_heads
    length = rows * ctx_count
    group_rows = rows * team
    experts = ctx_count * expert_up.shape[0]
    capacity = max(2, 2 * rows // experts)
    block_rows = length // block_order.shape[0]
    hidden = w_up.shape[1]
    hidden_dev = w_down.shape[0]
    wr = w_qkv.shape[0]
    qkv_cols = 3 * width // team
    up_cols = hidden // team
    core = lax.axis_index("dp")
    ctx = lax.axis_index("ctx")
    group, member = lax.div(ctx, team), lax.rem(ctx, team)
    team_steps = [(0, 0, k) for k in range(1, team)]
    group_steps = [(0, k, 0) for k in range(1, groups)]
    by_group = [[g * team + t for g in range(groups)] for t in range(team)]
    by_team = [[g * team + t for t in range(team)] for g in range(groups)]
    swap = [(d, (d + 1) % two) for d in range(two)]

    small_flat = jnp.concatenate(
        [router.reshape(-1), norm_gains.reshape(-1), norm_biases.reshape(-1)]
    )
    small_size = -(-small_flat.shape[0] // 2048) * 2048
    small = jnp.pad(small_flat, (0, small_size - small_flat.shape[0])).astype(BF)
    small = small.reshape(-1, 128)

    qkv_first = tall(
        w_qkv.astype(BF).reshape(wr, 3, team, width // team).transpose(2, 0, 1, 3).reshape(
            team, wr, qkv_cols
        )
    )
    up_first = tall(
        w_up.reshape(wr, two * groups, team, hidden_dev)
        .transpose(2, 0, 1, 3)
        .reshape(team, wr, up_cols)
        .astype(BF)
    )
    down_first = tall(w_down.astype(BF).reshape(team, wr, width))
    out_first = tall(w_out.astype(BF))
    route_row = jnp.broadcast_to(routes[0, :, 0][None, :], (8, rows))

    def first(coords, ins, outs):
        c, g, t = coords
        moves, local = [], []
        for s in team_steps:
            to = lax.rem(t + s[2], team)
            moves.append(Move(s, ins[0], outs[0].at[t]))
            moves.append(Move(s, ins[1].at[to], outs[1].at[t]))
            moves.append(Move(s, ins[3], outs[3].at[t]))
            moves.append(Move(s, ins[4], outs[4].at[t]))
            moves.append(Move(s, ins[2].at[to], outs[2].at[0, t]))
        for s in group_steps:
            moves.append(Move(s, ins[5], outs[5].at[g]))
        local.append((ins[0], outs[0].at[t]))
        local.append((ins[1].at[t], outs[1].at[t]))
        local.append((ins[2].at[t], outs[2].at[0, t]))
        local.append((ins[3], outs[3].at[t]))
        local.append((ins[4], outs[4].at[t]))
        local.append((ins[5], outs[5].at[g]))
        local.append((ins[6], outs[2].at[1]))
        return local, moves

    token_rows, qkv_part, ff_part, small_part, route_all, out_part = exchange(
        "first",
        1,
        sizes,
        (tokens[0], qkv_first, up_first, small, route_row, out_first, down_first),
        [
            ((team, rows, width), BF),
            (qkv_first.shape, BF),
            ((2,) + up_first.shape, BF),
            ((team,) + small.shape, BF),
            ((team, 8, rows), jnp.int32),
            ((groups,) + out_first.shape, BF),
        ],
        first,
    )

    def second_build(coords, ins, outs):
        c, g, t = coords
        moves, local = [], []
        for k, s in enumerate(group_steps):
            moves.append(Move(s, ins[0], outs[0].at[c, g]))
            moves.append(Move(s, ins[1], outs[1].at[c, g]))
        for s in team_steps:
            moves.append(Move(s, ins[2], outs[2].at[t]))
        local.append((ins[0], outs[0].at[c, g]))
        local.append((ins[1], outs[1].at[c, g]))
        local.append((ins[2], outs[2].at[t]))
        other = (1, 0, 0)
        for n in range(2):
            moves.append(Move(other, ins[n], outs[n].at[c, g]))
        for k, s in enumerate(group_steps):
            source = lax.rem(g + groups - s[1], groups)
            for n in range(2):
                moves.append(
                    Move(other, outs[n].at[c, source], outs[n].at[c, source], after=2 * k + n)
                )
        return local, moves

    qkv_all, small_all, cot_rows = exchange(
        "second",
        2,
        sizes,
        (qkv_part, small_part, cotangent[0]),
        [
            ((two, groups) + qkv_part.shape, BF),
            ((two, groups) + small_part.shape, BF),
            ((team, rows, width), BF),
        ],
        second_build,
    )
    qkv_weight = qkv_all.reshape(width, qkv_cols)
    small_rows = small_all.reshape(two * ctx_count, -1)
    router_cols = router.shape[1]
    router_weight = jnp.pad(
        small_rows[:, : wr * router_cols].reshape(width, router_cols),
        ((0, 0), (0, 128 - router_cols)),
    )
    vectors = small_rows[:, wr * router_cols : small_flat.shape[0]].reshape(
        two * ctx_count, 4, wr
    )
    vectors = vectors.transpose(1, 0, 2).reshape(4, width).astype(F32)
    vectors = jnp.pad(vectors, ((4, 0), (0, 0)))

    ff_half = lax.all_gather(
        ff_part.reshape(2, team * wr, width),
        "ctx",
        axis=0,
        tiled=False,
        axis_index_groups=by_group,
    )

    def core_half(term):
        halves = term.reshape((two, term.shape[0] // two) + term.shape[1:])
        keep = lax.dynamic_index_in_dim(halves, core, 0, keepdims=False)
        give = lax.dynamic_index_in_dim(halves, 1 - core, 0, keepdims=False)
        return keep + lax.ppermute(give.astype(BF), "dp", swap).astype(F32)

    def over_groups(term):
        return lax.psum_scatter(
            term, "ctx", scatter_dimension=0, tiled=True, axis_index_groups=by_group
        )

    doc_id = jnp.arange(doc_lengths.shape[1], dtype=jnp.int32)
    doc_ends = jnp.sum(
        jnp.where(doc_id[:, None] <= doc_id[None, :], doc_lengths[0][:, None], 0), axis=0
    )
    all_rows = jnp.arange(length, dtype=jnp.int32)
    marks = (all_rows // block_rows)[:, None] == jnp.arange(
        block_order.shape[0], dtype=jnp.int32
    )[None, :]
    anchor = jnp.sum(jnp.where(marks, block_order[None, :], 0), axis=1)
    all_place = anchor * block_rows + all_rows % block_rows

    def low_of(place):
        return jnp.max(
            jnp.where(doc_ends[None, :] <= place[:, None], doc_ends[None, :], 0), axis=1
        )

    query_length = length // reps
    tiles = query_length // TILE
    part = lax.rem(group, reps)
    query_place = lax.dynamic_slice(all_place, (part * query_length,), (query_length,))
    lows = low_of(query_place)
    bounds = jnp.broadcast_to(jnp.array([[0, length // TILE]], dtype=jnp.int32), (tiles, 2))
    meta = jnp.concatenate(
        [query_place[None], lows[None], jnp.zeros((6, query_length), jnp.int32)], axis=0
    )

    token_rows = token_rows.reshape(group_rows, width)
    inputs = token_rows.astype(F32)
    normed_low = layer_norm(inputs, vectors[4], vectors[6]).astype(BF)
    mixed_t = lax.dot_general(
        qkv_weight, normed_low, (((0,), (1,)), ((), ())), preferred_element_type=F32
    ).astype(BF)
    mixed_t = mixed_t.reshape(3, team_heads, HEAD_DIM, group_rows)

    def spread_heads(coords, ins, outs):
        c, g, t = coords
        moves = [
            Move(s, ins[0].at[:, lax.div(lax.rem(g + s[1], groups), reps)], outs[0].at[g])
            for s in group_steps
        ]
        local = [(ins[0].at[:, lax.div(g, reps)], outs[0].at[g])]
        other = (1, 0, 0)
        moves.append(Move(other, ins[1], outs[1].at[c, :, t]))
        local.append((ins[1], outs[1].at[c, :, t]))
        first_team = len(moves)
        for s in team_steps:
            moves.append(Move(s, ins[1], outs[1].at[c, :, t]))
        for k, s in enumerate(team_steps):
            source = lax.rem(t + team - s[2], team)
            view = outs[1].at[c, :, source]
            moves.append(Move(other, view, view, after=first_team + k))
        return local, moves

    head_parts, out_weight = exchange(
        "heads",
        3,
        sizes,
        (mixed_t, out_part),
        [
            ((groups, 3, HEAD_DIM, group_rows), BF),
            ((two, groups, team) + out_first.shape, BF),
        ],
        spread_heads,
    )
    out_weight = out_weight.reshape(width, width)
    head_parts = head_parts.reshape(groups, 3 * HEAD_DIM, group_rows)
    place_col = all_place[:, None]
    head_t = head_parts.transpose(1, 0, 2).reshape(3 * HEAD_DIM, length)
    zeros = jnp.zeros((HEAD_DIM, query_length), BF)
    kv_t = head_t[HEAD_DIM:]
    kv_rows = kv_t.T
    q_t = lax.dynamic_slice(
        head_t[:HEAD_DIM], (0, part * query_length), (HEAD_DIM, query_length)
    )
    q_pad = jnp.concatenate([q_t * jnp.asarray(SCALE, BF), zeros], axis=0)
    attention_t, log_total = attend(False, bounds, meta, place_col, q_pad, kv_rows, kv_t)
    low_t = lax.dynamic_update_slice(
        jnp.zeros((HEAD_DIM, length), BF),
        attention_t.astype(BF),
        (0, part * query_length),
    )
    low_t = low_t.reshape(HEAD_DIM, groups, group_rows).transpose(1, 0, 2)

    def gather_heads(coords, ins, outs):
        c, g, t = coords
        moves = [
            Move(s, ins[0].at[lax.rem(g + s[1], groups)], outs[0].at[t, g]) for s in group_steps
        ]
        local = [(ins[0].at[g], outs[0].at[t, g])]
        for s in team_steps:
            moves.append(Move(s, ins[0].at[g], outs[0].at[t, g]))
        for k, s in enumerate(group_steps):
            source = lax.rem(g + groups - s[1], groups)
            for e in team_steps:
                moves.append(Move(e, outs[0].at[t, source], outs[0].at[t, source], after=k))
        return local, moves

    [attended] = exchange(
        "attended",
        4,
        sizes,
        (low_t,),
        [((team, groups, HEAD_DIM, group_rows), BF)],
        gather_heads,
    )
    if reps > 1:
        attended = lax.dynamic_index_in_dim(
            attended.reshape(team, team_heads, reps, HEAD_DIM, group_rows),
            lax.div(group, groups // reps),
            2,
            keepdims=False,
        )
    attended_t = attended.reshape(width, group_rows)

    slots = team * capacity
    (
        second_low,
        dense_grad,
        send_s,
        send_g,
        select,
        mixes,
        middle_own,
        prob_own,
        hot_own,
        second_own,
        attended_own,
    ) = between(
        experts,
        sizes,
        slots,
        member[None],
        attended_t,
        out_weight,
        token_rows,
        vectors,
        router_weight,
        route_all,
        cot_rows.reshape(group_rows, width),
    )
    (
        layer_sum,
        second_sum,
        sums_own,
        expert_active,
        hidden_grad,
        arrived_in,
        arrived_grad,
        ff_terms,
    ) = feed_forward(
        sizes,
        rows,
        send_s,
        send_g,
        expert_up[0],
        expert_down[0],
        second_low,
        dense_grad,
        ff_half,
        select,
        cot_rows.reshape(group_rows, width),
        mixes,
    )
    ff_sum = over_groups(ff_terms)
    down_sum = ff_sum[:, :width].astype(F32)
    up_sum = ff_sum[:, width:].reshape(team, wr, up_cols)
    entries = two * groups * slots
    expert_down_grad = row_sum(expert_active, arrived_grad.reshape(entries, width), TILE)
    expert_up_grad = row_sum(arrived_in.reshape(entries, width), hidden_grad, 128)

    layer_out, middle_grad, flow_t, out_term, small_t = turn(
        experts,
        layer_sum,
        second_sum,
        sums_own,
        middle_own,
        prob_own,
        hot_own,
        second_own,
        attended_own,
        cotangent[0],
        router_weight,
        out_weight,
        vectors,
    )
    flow_t = flow_t.reshape(team, team_heads, HEAD_DIM, rows)
    out_halves = out_term.reshape(two, groups, team, wr, width)

    def spread_flow(coords, ins, outs):
        c, g, t = coords
        moves = []
        for dg in range(groups):
            for dt in range(team):
                if dg or dt:
                    to_g, to_t = lax.rem(g + dg, groups), lax.rem(t + dt, team)
                    moves.append(
                        Move((0, dg, dt), ins[0].at[to_t, lax.div(to_g, reps)], outs[0].at[g, t])
                    )
        moves.append(Move((1, 0, 0), ins[1].at[lax.rem(c + 1, two)], outs[1]))
        return [(ins[0].at[t, lax.div(g, reps)], outs[0].at[g, t])], moves

    flow_parts, out_got = exchange(
        "flow",
        8,
        sizes,
        (flow_t, out_halves),
        [((groups, team, HEAD_DIM, rows), BF), (out_halves.shape[1:], BF)],
        spread_flow,
    )
    flow_all = flow_parts.transpose(2, 0, 1, 3).reshape(HEAD_DIM, length)
    flow_all = lax.dynamic_slice(
        flow_all, (0, part * query_length), (HEAD_DIM, query_length)
    )
    do_pad = jnp.concatenate([zeros, flow_all], axis=0)
    query_grad, pair_grad = attend_back(
        False,
        bounds,
        meta,
        place_col,
        q_pad,
        do_pad,
        attention_t,
        log_total,
        kv_rows,
        kv_t,
    )
    query_grad = lax.dynamic_update_slice(
        jnp.zeros((HEAD_DIM, length), BF), query_grad, (0, part * query_length)
    )
    grad_parts = jnp.concatenate([query_grad, pair_grad], axis=0)
    grad_parts = grad_parts.reshape(3, HEAD_DIM, groups, group_rows).transpose(2, 0, 1, 3)
    out_keep = lax.dynamic_index_in_dim(out_halves, core, 0, keepdims=False)
    out_parts = tall(
        (out_keep.astype(F32) + out_got.astype(F32))
        .astype(BF)
        .transpose(1, 0, 2, 3)
        .reshape(team, groups * wr, width)
    )

    def mixed_build(coords, ins, outs):
        c, g, t = coords
        moves = [
            Move(s, ins[0].at[lax.rem(g + s[1], groups)], outs[0].at[:, g])
            for s in group_steps
        ]
        moves += [
            Move(s, ins[1].at[lax.rem(t + s[2], team)], outs[1].at[t]) for s in team_steps
        ]
        return [(ins[0].at[g], outs[0].at[:, g]), (ins[1].at[t], outs[1].at[t])], moves

    grad_parts, out_parts = exchange(
        "mixed",
        9,
        sizes,
        (grad_parts, out_parts),
        [((3, groups, HEAD_DIM, group_rows), BF), (out_parts.shape, BF)],
        mixed_build,
    )
    out_parts = tall(
        jnp.sum(out_parts.astype(F32), axis=0).astype(BF).reshape(groups, wr, width)
    )
    if reps > 1:
        grad_parts = jnp.sum(
            grad_parts.reshape(3, team_heads, reps, HEAD_DIM, group_rows).astype(F32), axis=2
        ).astype(BF)
    mixed_grad_t = grad_parts.reshape(qkv_cols, group_rows)
    normed_part = (
        lax.dot_general(
            mixed_grad_t, qkv_weight, (((0,), (1,)), ((), ())), preferred_element_type=F32
        )
        .astype(BF)
        .reshape(team, rows, width)
    )
    qkv_term = lax.dot_general(
        normed_low, mixed_grad_t, (((0,), (1,)), ((), ())), preferred_element_type=F32
    )
    qkv_parts = core_half(qkv_term).astype(BF).reshape(groups, team * wr, qkv_cols)

    def normed_build(coords, ins, outs):
        c, g, t = coords
        moves, local = [], [(ins[2].at[t], outs[2].at[t])]
        for n in range(2):
            for s in group_steps:
                moves.append(Move(s, ins[n].at[lax.rem(g + s[1], groups)], outs[n].at[g]))
            local.append((ins[n].at[g], outs[n].at[g]))
        for s in team_steps:
            moves.append(Move(s, ins[2].at[lax.rem(t + s[2], team)], outs[2].at[t]))
        return local, moves

    qkv_parts, out_parts, normed_own = exchange(
        "normed",
        10,
        sizes,
        (qkv_parts, out_parts, normed_part),
        [(qkv_parts.shape, BF), (out_parts.shape, BF), (normed_part.shape, BF)],
        normed_build,
    )
    qkv_sum = (
        jnp.sum(qkv_parts.astype(F32), axis=0).astype(BF).reshape(team, wr, qkv_cols)
    )
    out_sum = jnp.sum(out_parts.astype(F32), axis=0).reshape(wr, width)
    normed_grad = jnp.sum(normed_own.astype(F32), axis=0)
    input_part_grad, gain_first, bias_first = jax.vjp(
        layer_norm, tokens[0].astype(F32), vectors[4], vectors[6]
    )[1](normed_grad)
    input_grad = middle_grad + input_part_grad

    small_used = small_t.shape[0]
    small_row = jnp.arange(small_used, dtype=jnp.int32)[:, None]
    small_t = jnp.where(
        small_row == experts + 2,
        gain_first[None],
        jnp.where(small_row == experts + 4, bias_first[None], small_t),
    )
    small_cols = small_used * wr
    small_pad = -(-small_cols // 1024) * 1024
    small_parts = jnp.pad(
        small_t.reshape(small_used, two * ctx_count, wr)
        .transpose(1, 0, 2)
        .reshape(two * ctx_count, small_cols),
        ((0, 0), (0, small_pad - small_cols)),
    ).reshape(two * ctx_count, small_pad // 128, 128)

    def owners_build(coords, ins, outs):
        c, g, t = coords
        moves, local = [], []
        for n in range(2):
            for s in team_steps:
                moves.append(Move(s, ins[n].at[lax.rem(t + s[2], team)], outs[n].at[t]))
            local.append((ins[n].at[t], outs[n].at[t]))
        me = c * ctx_count + g * team + t
        for dc in range(two):
            for dg in range(groups):
                for dt in range(team):
                    if dc or dg or dt:
                        to = (
                            lax.rem(c + dc, two) * ctx_count
                            + lax.rem(g + dg, groups) * team
                            + lax.rem(t + dt, team)
                        )
                        moves.append(Move((dc, dg, dt), ins[2].at[to], outs[2].at[me]))
        local.append((ins[2].at[me], outs[2].at[me]))
        return local, moves

    up_own, qkv_own, small_own = exchange(
        "owners",
        11,
        sizes,
        (tall(up_sum), tall(qkv_sum), small_parts),
        [
            (tall(up_sum).shape, BF),
            (tall(qkv_sum).shape, BF),
            (small_parts.shape, F32),
        ],
        owners_build,
    )
    small_sum = jnp.sum(small_own, axis=0).reshape(-1)[:small_cols].reshape(small_used, wr)
    up_own = (
        up_own.reshape(team, wr, two * groups, hidden_dev)
        .transpose(1, 2, 0, 3)
        .reshape(wr, hidden)
        .astype(F32)
    )
    qkv_own = (
        qkv_own.reshape(team, wr, 3, width // team)
        .transpose(1, 2, 0, 3)
        .reshape(wr, 3 * width)
        .astype(F32)
    )
    return (
        layer_out[None],
        input_grad[None].astype(BF),
        qkv_own,
        out_sum,
        up_own,
        down_sum,
        small_sum[:router_cols].T,
        small_sum[router_cols : router_cols + 2],
        small_sum[router_cols + 2 : router_cols + 4],
        expert_up_grad,
        expert_down_grad,
    )


def whole_kernel(sizes, experts, copies_count, *refs):
    two, groups, team = sizes
    (send_s, send_g, eup_h, edown_h, second_h, dgrad_h, ff_h, sel_h, cot_h, mix_h) = refs[:10]
    (middle_h, prob_h, hot_h, own_h, att_h, rw_h, wo_h, vec_h) = refs[10:18]
    (
        layer_o, middle_o, small_o, flow_o, out_o, down_o, up_o,
        active_o, hgrad_o, arr_s_o, arr_g_o,
    ) = refs[18:29]
    (
        arr_s, arr_g, eup, edown, second, dgrad, upw, downw, sel, cot, mix,
        slope, active, hgrad, acc, give, got_s, got_g, ret_s, ret_g, back_s, back_g,
        low, ugrad, dense, spart, lay, spa, sums, lay_r, spa_r, sums_r,
        term_give, term_got, ffg, ff_r,
        middle, prob, hot, own, att, rw, wo, vec, flow_t, flow_1,
        send_sem, recv_sem, load_sem, out_sem,
    ) = refs[29:]
    c = lax.axis_index("dp")
    i = lax.axis_index("ctx")
    g, t = lax.div(i, team), lax.rem(i, team)
    width = second.shape[1]
    rows = lay.shape[1]
    hid, ehid = upw.shape[1], eup.shape[1]
    core = lax.rem(c + 1, two)

    def device(step):
        dc, dg, dt = step
        return (
            lax.rem(c + dc, two),
            lax.rem(g + dg, groups) * team + lax.rem(t + dt, team),
        )

    index = [0]

    def remote(src, dst, step):
        k = index[0]
        index[0] += 1
        assert k < copies_count
        return pltpu.make_async_remote_copy(
            src_ref=src,
            dst_ref=dst,
            send_sem=send_sem.at[k],
            recv_sem=recv_sem.at[k],
            device_id=device(step),
            device_id_type=MESH,
        )

    group_steps = [(0, k, 0) for k in range(1, groups)]
    team_steps = [(0, 0, k) for k in range(1, team)]
    swap = (1, 0, 0)
    deep = ff_h.shape[2]

    def block_of(core, k):
        return pl.ds(pl.multiple_of((core * groups + k) * deep, deep), deep)

    loads = []
    for k, (src, dst) in enumerate(
        [
            (second_h, second), (dgrad_h, dgrad), (eup_h, eup), (edown_h, edown), (sel_h, sel), (cot_h, cot), (mix_h, mix),
            (send_s.at[g], arr_s.at[c, g]), (send_g.at[g], arr_g.at[c, g]),
            (middle_h, middle), (prob_h, prob), (hot_h, hot), (own_h, own),
            (att_h, att), (rw_h, rw), (wo_h, wo), (vec_h, vec),
        ]
        + [
            (ff_h.at[k, n], weight.at[block_of(c, k), :])
            for k in range(groups)
            for n, weight in enumerate((upw, downw))
        ]
    ):
        load = pltpu.make_async_copy(src, dst, load_sem.at[k])
        load.start()
        loads.append(load)

    barrier = pltpu.get_barrier_semaphore()
    greet = group_steps + team_steps + [swap]
    for step in greet:
        pl.semaphore_signal(barrier, inc=1, device_id=device(step), device_id_type=MESH)
    pl.semaphore_wait(barrier, len(greet))

    every = []

    def launch(copy):
        copy.start()
        every.append(copy)
        return copy

    def to_groups(src, dst):
        return [
            launch(remote(src.at[lax.rem(g + s[1], groups)], dst.at[g], s)) for s in group_steps
        ]

    def source(s):
        return lax.rem(g + groups - s[1], groups)

    swap_w = [
        launch(remote(ff_h.at[k, n], weight.at[block_of(c, k), :], swap))
        for k in range(groups)
        for n, weight in enumerate((upw, downw))
    ]
    out_s = [
        launch(remote(send_s.at[lax.rem(g + s[1], groups)], arr_s.at[c, g], s))
        for s in group_steps
    ]
    swap_s = [launch(remote(send_s.at[g], arr_s.at[c, g], swap))]
    out_g = [
        launch(remote(send_g.at[lax.rem(g + s[1], groups)], arr_g.at[c, g], s))
        for s in group_steps
    ]
    swap_g = [launch(remote(send_g.at[g], arr_g.at[c, g], swap))]

    for load in loads[:2] + loads[17:]:
        load.wait()
    for copy in swap_w:
        copy.wait_recv()

    def dense_in(h, carry):
        at = span(h, TILE)
        value, bend = gelu_and_slope(dot_f32(second[...], upw[:, at]))
        low[:, at] = value.astype(BF)
        ugrad[:, at] = (bend * contract_cols(dgrad[...], downw[at, :])).astype(BF)
        return carry

    lax.fori_loop(0, hid // TILE, dense_in, 0)

    def dense_out(n, carry):
        at = span(n, TILE)
        dense[:, at] = dot_f32(low[...], downw[:, at])
        spart[:, at] = contract_cols(ugrad[...], upw[at, :])
        return carry

    lax.fori_loop(0, width // TILE, dense_out, 0)

    half = hid // 2
    term_tile = 128

    def down_term(base, n):
        at = pl.ds(pl.multiple_of(base + n * term_tile, term_tile), term_tile)
        return contract_rows(low[:, at], dgrad[...])

    def up_term(base, n):
        at = pl.ds(pl.multiple_of(base + n * term_tile, term_tile), term_tile)
        return contract_rows(second[:, at], ugrad[...])

    terms = []
    for k, (term, size) in enumerate(((down_term, half), (up_term, width // 2))):

        def giving(n, carry, k=k, term=term, size=size):
            term_give[k, span(n, term_tile), :] = term(core * size, n).astype(BF)
            return carry

        lax.fori_loop(0, size // term_tile, giving, 0)
        terms.append(launch(remote(term_give.at[k], term_got.at[k], swap)))
    for k, (term, size) in enumerate(((down_term, half), (up_term, width // 2))):
        terms[k].wait_recv()

        def keeping(n, carry, k=k, term=term, size=size):
            at = span(n, term_tile)
            total = term(c * size, n) + term_got[k, at, :].astype(F32)
            ffg[k, at, :] = total.astype(BF)
            return carry

        lax.fori_loop(0, size // term_tile, keeping, 0)
    up_copy = pltpu.make_async_copy(ffg.at[1], up_o, out_sem.at[4])
    up_copy.start()

    for load in loads[2:17]:
        load.wait()
    for copy, s in zip(out_s, group_steps):
        copy.wait_recv()
        swap_s.append(launch(remote(arr_s.at[c, source(s)], arr_s.at[c, source(s)], swap)))
    for copy in swap_s:
        copy.wait_recv()
    entries = 2 * groups * arr_s.shape[2]

    def expert_in(h, carry):
        at = span(h, TILE)
        value, bend = gelu_and_slope(dot_f32(arr_s[...].reshape(entries, width), eup[:, at]))
        active[:, at] = value.astype(BF)
        slope[:, at] = bend
        return carry

    lax.fori_loop(0, ehid // TILE, expert_in, 0)
    keeps = [
        pltpu.make_async_copy(active, active_o, out_sem.at[0]),
        pltpu.make_async_copy(arr_s, arr_s_o, out_sem.at[1]),
    ]
    for copy in keeps:
        copy.start()

    def expert_out(n, carry):
        at = span(n, TILE)
        acc[:, :, at] = dot_f32(active[...], edown[:, at]).reshape(2, entries // 2, TILE)
        return carry

    lax.fori_loop(0, width // TILE, expert_out, 0)
    give[0] = acc[core].astype(BF)
    other_s = launch(remote(give.at[0], got_s, swap))

    for copy, s in zip(out_g, group_steps):
        copy.wait_recv()
        swap_g.append(launch(remote(arr_g.at[c, source(s)], arr_g.at[c, source(s)], swap)))
    other_s.wait_recv()
    ret_s[...] = (acc[c] + got_s[...].astype(F32)).astype(BF).reshape(ret_s.shape)
    home_s = to_groups(ret_s, back_s)
    back_s[g] = ret_s[g]
    for copy in swap_g:
        copy.wait_recv()

    def expert_back(h, carry):
        at = span(h, TILE)
        pull = contract_cols(arr_g[...].reshape(entries, width), edown[at, :])
        hgrad[:, at] = (slope[:, at] * pull).astype(BF)
        return carry

    lax.fori_loop(0, ehid // TILE, expert_back, 0)
    keeps += [
        pltpu.make_async_copy(hgrad, hgrad_o, out_sem.at[2]),
        pltpu.make_async_copy(arr_g, arr_g_o, out_sem.at[3]),
    ]
    for copy in keeps[2:]:
        copy.start()

    def expert_back_out(n, carry):
        at = span(n, TILE)
        acc[:, :, at] = contract_cols(hgrad[...], eup[at, :]).reshape(2, entries // 2, TILE)
        return carry

    lax.fori_loop(0, width // TILE, expert_back_out, 0)
    give[1] = acc[core].astype(BF)
    other_g = launch(remote(give.at[1], got_g, swap))
    other_g.wait_recv()
    ret_g[...] = (acc[c] + got_g[...].astype(F32)).astype(BF).reshape(ret_g.shape)
    home_g = to_groups(ret_g, back_g)
    back_g[g] = ret_g[g]

    for copy in home_s:
        copy.wait_recv()
    slots = groups * back_s.shape[1]
    lane = lax.broadcasted_iota(jnp.int32, (rows, 128), 1)

    def join_layer(r, carry):
        at = span(r, rows)
        found = dot_f32(sel[at, :], back_s[...].reshape(slots, width))
        own = dense[at, :]
        flow = cot[at, :].astype(F32)
        mixes = mix[at, :]
        lay[r] = (mixes[:, 0:1] * own + mixes[:, 1:2] * found).astype(BF)
        plain = jnp.sum(flow * own, axis=1, keepdims=True)
        routed = jnp.sum(flow * found, axis=1, keepdims=True)
        sums[r] = jnp.where(lane == 0, plain, jnp.where(lane == 1, routed, 0.0))
        return carry

    lax.fori_loop(0, team, join_layer, 0)

    def to_team(src, dst):
        made = [launch(remote(src.at[lax.rem(t + s[2], team)], dst.at[t], s)) for s in team_steps]
        dst[t] = src[t]
        return made

    team_copies = to_team(lay, lay_r) + to_team(sums, sums_r)

    for copy in home_g:
        copy.wait_recv()
    piece = half // groups
    downs = [
        launch(remote(ffg.at[0, span(lax.rem(g + s[1], groups), piece), :], ff_r.at[g], s))
        for s in group_steps
    ]
    ff_r[g] = ffg[0, span(g, piece), :]

    def join_grad(r, carry):
        at = span(r, rows)
        found = dot_f32(sel[at, :], back_g[...].reshape(slots, width))
        spa[r] = (spart[at, :] + found).astype(BF)
        return carry

    lax.fori_loop(0, team, join_grad, 0)
    team_copies += to_team(spa, spa_r)

    for copy in team_copies:
        copy.wait_recv()

    sum_own = jnp.sum(sums_r[...], axis=0)
    layer_o[...] = (middle[...] + jnp.sum(lay_r[...].astype(F32), axis=0)).astype(BF)
    chances, chosen = prob[...], hot[...]
    s0, s1 = sum_own[:, 0:1], sum_own[:, 1:2]
    mix1 = jnp.sum(jnp.where(lane == experts + 1, chances, 0.0), axis=1, keepdims=True)
    gate = jnp.sum(chances * chosen, axis=1, keepdims=True)
    pulls = jnp.where(lane == experts, s0, jnp.where(lane == experts + 1, s1 * gate, 0.0))
    mean_pull = jnp.sum(chances * pulls, axis=1, keepdims=True)
    logit_grad = chances * jnp.where(
        lane < experts, (s1 * mix1) * (chosen - gate), pulls - mean_pull
    )
    logit_grad = jnp.where(lane < experts + 2, logit_grad, 0.0).astype(BF)
    second_grad = jnp.sum(spa_r[...].astype(F32), axis=0) + contract_cols(logit_grad, rw[...])
    hat, scale = normalize(middle[...])
    pull = second_grad * vec[5:6, :]
    moved = scale * (
        pull
        - jnp.mean(pull, axis=-1, keepdims=True)
        - hat * jnp.mean(pull * hat, axis=-1, keepdims=True)
    )
    middle_grad = cot[span(t, rows), :].astype(F32) + moved
    middle_o[...] = middle_grad
    branch = middle_grad.astype(BF)

    for n in range(team):
        at = slice(n * (width // team), (n + 1) * (width // team))
        flow_t[n] = contract_cols(wo[at, :], branch).astype(BF).reshape(flow_t.shape[1:])
    flowed = [
        launch(remote(flow_t.at[lax.rem(t + s[2], team)], flow_1.at[t], s)) for s in team_steps
    ]
    flow_1[t] = flow_t[t]

    def out_term(base, n):
        at = pl.ds(pl.multiple_of(base + n * term_tile, term_tile), term_tile)
        return dot_f32(att[at, :], branch)

    def out_giving(n, carry):
        term_give[0, span(n, term_tile), :] = out_term(core * (width // 2), n).astype(BF)
        return carry

    terms[0].wait_send()
    every[:] = [copy for copy in every if copy is not terms[0]]
    lax.fori_loop(0, width // 2 // term_tile, out_giving, 0)
    out_cross = launch(remote(term_give.at[0], term_got.at[0], swap))
    for copy in flowed:
        copy.wait_recv()
    flowed = [
        launch(remote(flow_1.at[:, lax.rem(g + s[1], groups)], flow_o.at[g], s))
        for s in group_steps
    ]
    own_flow = pltpu.make_async_copy(flow_1.at[:, g], flow_o.at[g], out_sem.at[5])
    own_flow.start()
    out_cross.wait_recv()
    wr = out_o.shape[2]

    def out_keeping(n, carry):
        at = span(n, term_tile)
        total = out_term(c * (width // 2), n) + term_got[0, at, :].astype(F32)
        out_o[:, n] = total.astype(BF).reshape(team, wr, width)
        return carry

    lax.fori_loop(0, groups, out_keeping, 0)

    routed = contract_rows(logit_grad, own[...])[: small_o.shape[0], :]
    which = lax.broadcasted_iota(jnp.int32, routed.shape, 0)
    gain = jnp.sum(second_grad * hat, axis=0, keepdims=True)
    bias = jnp.sum(second_grad, axis=0, keepdims=True)
    small_o[...] = jnp.where(
        which == experts + 3, gain, jnp.where(which == experts + 5, bias, routed)
    )
    for copy in downs:
        copy.wait_recv()
    down_o[...] = jnp.sum(ff_r[...].astype(F32), axis=0)
    for copy in flowed:
        copy.wait_recv()
    for copy in keeps + [up_copy, own_flow]:
        copy.wait()
    for copy in every:
        copy.wait_send()


def whole(
    sizes, rows, experts, wr, send_s, send_g, eup, edown, second, dgrad, ff, sel, cot, mix,
    middle, prob, hot, own, att, rw, wo, vec,
):
    two, groups, team = sizes
    slots = send_s.shape[1]
    width = second.shape[1]
    hid, ehid = ff.shape[3], eup.shape[1]
    entries = 2 * groups * slots
    used = -(-(experts + 6) // 8) * 8
    count = 6 * (groups - 1) + 2 * groups + 5 + 5 * (team - 1) + 2 * groups
    arrived = (two, groups, slots, width)
    anywhere = pl.BlockSpec(memory_space=pl.ANY)
    inside = pl.BlockSpec(memory_space=pltpu.VMEM)
    team_rows = team * rows
    heads = (groups, HEAD_DIM, rows)
    shapes = (
        ((rows, width), BF),
        ((rows, width), F32),
        ((used, width), F32),
        ((groups, team, HEAD_DIM, rows), BF),
        ((team, groups, wr, width), BF),
        ((hid // 2 // groups, width), F32),
        ((width // 2, hid), BF),
        ((entries, ehid), BF),
        ((entries, ehid), BF),
        (arrived, BF),
        (arrived, BF),
    )
    scratch = (
        (arrived, BF), (arrived, BF), (eup.shape, BF), (edown.shape, BF), (second.shape, BF),
        (dgrad.shape, BF), ((width, hid), BF), ((hid, width), BF), (sel.shape, BF),
        (cot.shape, BF), (mix.shape, F32),
        ((entries, ehid), F32), ((entries, ehid), BF), ((entries, ehid), BF),
        ((2, entries // 2, width), F32), ((2, entries // 2, width), BF),
        ((entries // 2, width), BF), ((entries // 2, width), BF),
        ((groups, slots, width), BF), ((groups, slots, width), BF),
        ((groups, slots, width), BF), ((groups, slots, width), BF),
        ((team_rows, hid), BF), ((team_rows, hid), BF), ((team_rows, width), F32),
        ((team_rows, width), F32), ((team, rows, width), BF), ((team, rows, width), BF),
        ((team, rows, 128), F32), ((team, rows, width), BF), ((team, rows, width), BF),
        ((team, rows, 128), F32),
        ((2, hid // 2, width), BF), ((2, hid // 2, width), BF), ((2, hid // 2, width), BF),
        ((groups, hid // 2 // groups, width), BF),
        (middle.shape, F32), (prob.shape, F32), (hot.shape, F32), (own.shape, BF),
        (att.shape, BF), (rw.shape, BF), (wo.shape, BF), (vec.shape, F32),
        ((team,) + heads, BF), ((team,) + heads, BF),
    )
    return pl.pallas_call(
        functools.partial(whole_kernel, sizes, experts, count),
        name="feed_forward",
        out_shape=tuple(jax.ShapeDtypeStruct(s, d) for s, d in shapes),
        in_specs=[anywhere] * 18,
        out_specs=tuple(inside if n in (0, 1, 2, 4, 5) else anywhere for n in range(11)),
        scratch_shapes=[pltpu.VMEM(s, d) for s, d in scratch]
        + [
            pltpu.SemaphoreType.DMA((count,)),
            pltpu.SemaphoreType.DMA((count,)),
            pltpu.SemaphoreType.DMA((17 + 2 * groups,)),
            pltpu.SemaphoreType.DMA((6,)),
        ],
        compiler_params=pltpu.CompilerParams(
            collective_id=14, has_side_effects=True, vmem_limit_bytes=60 * 2**20
        ),
        cost_estimate=pl.CostEstimate(flops=0, bytes_accessed=300_000_000, transcendentals=0),
    )(
        send_s, send_g, eup, edown, second, dgrad, ff, sel, cot, mix,
        middle, prob, hot, own, att, rw, wo, vec,
    )


def deliver_kernel(experts, count, shift, small, *refs):
    ins, outs = refs[:count], refs[count : 2 * count]
    router, vectors = refs[2 * count : 2 * count + 2]
    sem = refs[2 * count + 2]
    copies = [pltpu.make_async_copy(a, b, sem.at[n]) for n, (a, b) in enumerate(zip(ins, outs))]
    for copy in copies:
        copy.start()
    wr = router.shape[1]
    mine = pltpu.roll(small[...], lax.rem(128 - shift[0], 128), 1)[:, :wr]
    router[...] = mine[: experts + 2, :]
    vectors[...] = mine[experts + 2 : experts + 6, :]
    for copy in copies:
        copy.wait()


def deliver(experts, shift, small, arrays):
    wr = arrays[2].shape[0]
    anywhere = pl.BlockSpec(memory_space=pl.ANY)
    inside = pl.BlockSpec(memory_space=pltpu.VMEM)
    count = len(arrays)
    return pl.pallas_call(
        functools.partial(deliver_kernel, experts, count),
        name="deliver",
        in_specs=[pl.BlockSpec(memory_space=pltpu.SMEM), inside] + [anywhere] * count,
        out_specs=tuple([anywhere] * count + [inside] * 2),
        out_shape=tuple(jax.ShapeDtypeStruct(a.shape, a.dtype) for a in arrays)
        + (
            jax.ShapeDtypeStruct((experts + 2, wr), F32),
            jax.ShapeDtypeStruct((4, wr), F32),
        ),
        scratch_shapes=[pltpu.SemaphoreType.DMA((count,))],
        compiler_params=pltpu.CompilerParams(vmem_limit_bytes=60 * 2**20),
    )(shift, small, *arrays)


def per_device(
    tokens,
    cotangent,
    block_order,
    doc_lengths,
    routes,
    w_qkv,
    w_out,
    w_up,
    w_down,
    router,
    norm_gains,
    norm_biases,
    expert_up,
    expert_down,
):
    rows, width = tokens.shape[1], tokens.shape[2]
    ctx_count = lax.axis_size("ctx")
    two = lax.axis_size("dp")
    team = math.gcd(4, ctx_count)
    groups = ctx_count // team
    sizes = (two, groups, team)
    length = rows * ctx_count
    wr = w_qkv.shape[0]
    experts = ctx_count * expert_up.shape[0]
    fits = groups * team == HEADS and team * wr == 128 and w_up.shape[1] == team * width
    if not fits or length // block_order.shape[0] != BLOCK:
        return per_device_general(
            tokens, cotangent, block_order, doc_lengths, routes, w_qkv, w_out, w_up, w_down,
            router, norm_gains, norm_biases, expert_up, expert_down,
        )
    group_rows = rows * team
    capacity = max(2, 2 * rows // experts)
    slots = team * capacity
    hidden = w_up.shape[1]
    hidden_dev = w_down.shape[0]
    qkv_cols = 3 * width // team
    up_cols = hidden // team
    ctx = lax.axis_index("ctx")
    core = lax.axis_index("dp")
    group, member = lax.div(ctx, team), lax.rem(ctx, team)
    by_group = [[g * team + t for g in range(groups)] for t in range(team)]
    team_steps = [(0, 0, k) for k in range(1, team)]

    router_cols = router.shape[1]
    (
        token_rows,
        cot_rows,
        head_parts,
        normed,
        weights,
        vectors,
        out_weight,
        ff_part,
        route_all,
    ) = start(
        sizes,
        tokens[0],
        cotangent[0],
        w_qkv,
        w_up,
        w_down,
        w_out,
        router.T,
        norm_gains,
        norm_biases,
        routes[0].reshape(1, rows),
    )
    router_weight = weights[:, :, :, :, qkv_cols:].reshape(width, 128)
    out_weight = out_weight.reshape(width, width)
    token_rows = token_rows.reshape(group_rows, width)
    cot_rows = cot_rows.reshape(group_rows, width)

    ff_half = lax.all_gather(
        ff_part.reshape(2, team * wr, width),
        "ctx",
        axis=0,
        tiled=False,
        axis_index_groups=by_group,
    )
    low_t, attention_t, log_total, q_pad, kv_t, kv_rows = sorted_attend(
        doc_lengths[0], block_order, head_parts.reshape(groups, 3 * HEAD_DIM, group_rows)
    )

    def gather_heads(coords, ins, outs):
        c, g, t = coords
        steps = [(0, k, 0) for k in range(1, groups)]
        moves = [Move(s, ins[0].at[lax.rem(g + s[1], groups)], outs[0].at[t, g]) for s in steps]
        local = [(ins[0].at[g], outs[0].at[t, g])]
        for s in team_steps:
            moves.append(Move(s, ins[0].at[g], outs[0].at[t, g]))
        for k, s in enumerate(steps):
            source = lax.rem(g + groups - s[1], groups)
            for e in team_steps:
                moves.append(Move(e, outs[0].at[t, source], outs[0].at[t, source], after=k))
        return local, moves

    [attended] = exchange(
        "attended",
        4,
        sizes,
        (low_t,),
        [((team, groups, HEAD_DIM, group_rows), BF)],
        gather_heads,
    )
    (
        second_low,
        dense_grad,
        send_s,
        send_g,
        select,
        mixes,
        middle_own,
        prob_own,
        hot_own,
        second_own,
        attended_own,
    ) = between(
        experts,
        sizes,
        slots,
        member[None],
        attended.reshape(width, group_rows),
        out_weight,
        token_rows,
        vectors,
        router_weight,
        route_all,
        cot_rows,
    )
    (
        layer_out,
        middle_grad,
        small_t,
        flow_parts,
        out_half,
        down_sum,
        up_half,
        expert_active,
        hidden_grad,
        arrived_in,
        arrived_grad,
    ) = whole(
        sizes,
        rows,
        experts,
        wr,
        send_s,
        send_g,
        expert_up[0],
        expert_down[0],
        second_low,
        dense_grad,
        ff_half,
        select,
        cot_rows,
        mixes,
        middle_own,
        prob_own,
        hot_own,
        second_own,
        attended_own,
        router_weight,
        out_weight,
        vectors,
    )

    def pieces_of(array, along):
        count = groups if along == "g" else team
        me = group if along == "g" else member
        found = [lax.dynamic_index_in_dim(array, me, 0, keepdims=False)]
        for step in range(1, count):
            if along == "g":
                pairs = [
                    (g * team + t, (g + step) % groups * team + t)
                    for g in range(groups)
                    for t in range(team)
                ]
            else:
                pairs = [
                    (g * team + t, g * team + (t + step) % team)
                    for g in range(groups)
                    for t in range(team)
                ]
            chunk = lax.dynamic_index_in_dim(array, lax.rem(me + step, count), 0, keepdims=False)
            found.append(lax.ppermute(chunk, "ctx", pairs))
        return found

    up_sum = lax.psum_scatter(
        up_half, "ctx", scatter_dimension=0, tiled=True, axis_index_groups=by_group
    ).reshape(team, wr, up_cols)
    out_pieces = pieces_of(out_half, "t")
    grad_parts = sorted_back(
        doc_lengths[0],
        block_order,
        flow_parts.reshape(ctx_count, HEAD_DIM, rows),
        attention_t,
        log_total,
        q_pad,
        kv_t,
        kv_rows,
        groups,
    )

    grad_parts, expert_active, hidden_grad = lax.optimization_barrier(
        (grad_parts, expert_active, hidden_grad)
    )

    pieces = pieces_of(grad_parts, "g")
    out_sum = sum(piece.astype(F32) for piece in out_pieces).astype(BF)
    entries = two * groups * slots
    expert_down_grad = row_sum(expert_active, arrived_grad.reshape(entries, width), TILE)
    expert_up_grad = row_sum(arrived_in.reshape(entries, width), hidden_grad, 128)
    input_grad, qkv_own, up_own, out_own, small_own = end(
        sizes,
        experts,
        pieces,
        weights,
        normed,
        tokens[0],
        vectors,
        middle_grad,
        small_t,
        up_sum,
        out_sum,
    )
    delivered = deliver(
        experts,
        member[None] * wr,
        small_own,
        (layer_out, input_grad, qkv_own, out_own, up_own, down_sum),
    )
    layer_out, input_grad, qkv_own, out_own, up_own, down_sum, router_own, vectors_own = delivered
    return (
        layer_out[None],
        input_grad[None],
        qkv_own,
        out_own,
        up_own,
        down_sum,
        router_own.T,
        vectors_own[:2],
        vectors_own[2:],
        expert_up_grad,
        expert_down_grad,
    )


def solution(mesh):
    in_specs = (
        P("dp", "ctx", None),
        P("dp", "ctx", None),
        P(),
        P("dp", None),
        P("dp", "ctx", None),
        P(("dp", "ctx"), None),
        P(("dp", "ctx"), None),
        P(("dp", "ctx"), None),
        P(("dp", "ctx"), None),
        P(("dp", "ctx"), None),
        P(None, ("dp", "ctx")),
        P(None, ("dp", "ctx")),
        P("ctx", None, "dp"),
        P("ctx", "dp", None),
    )
    out_specs = (
        P("dp", "ctx", None),
        P("dp", "ctx", None),
        P(("dp", "ctx"), None),
        P(("dp", "ctx"), None),
        P(("dp", "ctx"), None),
        P(("dp", "ctx"), None),
        P(("dp", "ctx"), None),
        P(None, ("dp", "ctx")),
        P(None, ("dp", "ctx")),
        P("ctx", None, "dp"),
        P("ctx", "dp", None),
    )
    return jax.shard_map(
        per_device, mesh=mesh, in_specs=in_specs, out_specs=out_specs, check_vma=False
    )
```

```python
import functools
import math

import jax
import jax.numpy as jnp
from jax import lax
from jax.experimental import pallas as pl
from jax.experimental.pallas import tpu as pltpu
from jax.sharding import PartitionSpec as P

HEADS = 16
HEAD_DIM = 64

EPS = 1e-05
NEG = -1e30
SCALE = 0.125
TILE = 256
BF = jnp.bfloat16
F32 = jnp.float32
MESH = pl.DeviceIdType.MESH


def layer_norm(values, gain, shift):
    center = values - jnp.mean(values, axis=-1, keepdims=True)
    spread = jnp.mean(center * center, axis=-1, keepdims=True)
    return center * lax.rsqrt(spread + EPS) * gain + shift


def gelu_tanh(values):
    return jax.nn.gelu(values, approximate=True)


def router_heads(router_logits, route_hot, experts):
    chances = jax.nn.softmax(router_logits[:, :experts], axis=-1)
    gate = jnp.sum(chances * route_hot, axis=-1)
    mixing = jax.nn.softmax(router_logits[:, experts:], axis=-1)
    return (gate, mixing[:, 0], mixing[:, 1])


def dot_f32(left, right):
    return jnp.dot(left, right, preferred_element_type=F32)


def contract_rows(left, right):
    return lax.dot_general(left, right, (((0,), (0,)), ((), ())), preferred_element_type=F32)


def contract_cols(left, right):
    return lax.dot_general(left, right, (((1,), (1,)), ((), ())), preferred_element_type=F32)


def span(i, size):
    return pl.ds(pl.multiple_of(i * size, size), size)


class Move:
    def __init__(self, step, src, dst, after=None):
        self.step, self.src, self.dst, self.after = step, src, dst, after


def exchange(name, cid, sizes, ins, outs, build, micros=20):
    two, groups, team = sizes

    def kernel(*refs):
        in_refs, out_refs = refs[: len(ins)], refs[len(ins) : len(ins) + len(outs)]
        send_sem, recv_sem, local_sem = refs[len(ins) + len(outs) :]
        c = lax.axis_index("dp")
        i = lax.axis_index("ctx")
        g, t = lax.div(i, team), lax.rem(i, team)

        def device(step):
            dc, dg, dt = step
            return (
                lax.rem(c + dc, two),
                lax.rem(g + dg, groups) * team + lax.rem(t + dt, team),
            )

        locals_, moves = build((c, g, t), in_refs, out_refs)
        steps = sorted({m.step for m in moves})
        greet = sorted(
            set(steps) | {((-a) % two, (-b) % groups, (-d) % team) for a, b, d in steps}
        )
        barrier = pltpu.get_barrier_semaphore()
        for step in greet:
            pl.semaphore_signal(barrier, inc=1, device_id=device(step), device_id_type=MESH)
        pl.semaphore_wait(barrier, len(greet))

        copies = {}
        arrived = set()
        for k, (src, dst) in enumerate(locals_):
            copies[("local", k)] = pltpu.make_async_copy(src, dst, local_sem.at[k])
        for k, m in enumerate(moves):
            copies[k] = pltpu.make_async_remote_copy(
                src_ref=m.src,
                dst_ref=m.dst,
                send_sem=send_sem.at[k],
                recv_sem=recv_sem.at[k],
                device_id=device(m.step),
                device_id_type=MESH,
            )
        for k, m in enumerate(moves):
            if m.after is None:
                copies[k].start()
        for k in range(len(locals_)):
            copies[("local", k)].start()
        for k, m in enumerate(moves):
            if m.after is not None:
                if m.after not in arrived:
                    arrived.add(m.after)
                    if isinstance(m.after, tuple):
                        copies[m.after].wait()
                    else:
                        copies[m.after].wait_recv()
                copies[k].start()
        for k in range(len(locals_)):
            if ("local", k) not in arrived:
                copies[("local", k)].wait()
        for k in range(len(moves)):
            if k not in arrived:
                copies[k].wait_recv()
        for k in range(len(moves)):
            copies[k].wait_send()

    count = []

    def trace_counts():
        class Probe:
            def __getattr__(self, name):
                return self

            def __getitem__(self, index):
                return self

        locals_, moves = build((0, 0, 0), [Probe() for _ in ins], [Probe() for _ in outs])
        count.extend((len(locals_), len(moves)))

    trace_counts()
    return pl.pallas_call(
        kernel,
        name=name,
        out_shape=tuple(jax.ShapeDtypeStruct(s, d) for s, d in outs),
        in_specs=[pl.BlockSpec(memory_space=pl.ANY)] * len(ins),
        out_specs=tuple(pl.BlockSpec(memory_space=pl.ANY) for _ in outs),
        scratch_shapes=[
            pltpu.SemaphoreType.DMA((max(1, count[1]),)),
            pltpu.SemaphoreType.DMA((max(1, count[1]),)),
            pltpu.SemaphoreType.DMA((max(1, count[0]),)),
        ],
        compiler_params=pltpu.CompilerParams(collective_id=cid, has_side_effects=True),
        cost_estimate=pl.CostEstimate(
            flops=0, bytes_accessed=int(micros * 3.0e6), transcendentals=0
        ),
    )(*ins)


def mask_of(kt, key_place, query_place, query_low):
    return (key_place <= query_place) & (key_place >= query_low)


def key_places(sorted_rows, kt, place_ref):
    if sorted_rows:
        return lax.broadcasted_iota(jnp.int32, (TILE, TILE), 0) + kt * TILE
    return place_ref[pl.ds(pl.multiple_of(kt * TILE, TILE), TILE), :]


def attend_kernel(
    sorted_rows, bounds, meta_ref, place_ref, q_ref, rows_ref, kvt_ref, out_ref, lse_ref
):
    step = pl.program_id(0)
    queries = q_ref[...]
    place, low = meta_ref[0:1, :], meta_ref[1:2, :]

    def body(kt, carry):
        peak, total, acc = carry
        at = pl.ds(pl.multiple_of(kt * TILE, TILE), TILE)
        scores = dot_f32(rows_ref[at, :], queries)
        allowed = mask_of(kt, key_places(sorted_rows, kt, place_ref), place, low)
        scores = jnp.where(allowed, scores, NEG)
        new_peak = jnp.maximum(peak, jnp.max(scores, axis=0, keepdims=True))
        weights = jnp.exp(scores - new_peak)
        fade = jnp.exp(peak - new_peak)
        total = total * fade + jnp.sum(weights, axis=0, keepdims=True)
        acc = acc * fade + dot_f32(kvt_ref[HEAD_DIM:, at], weights.astype(BF))
        return new_peak, total, acc

    start = (
        jnp.full((1, TILE), NEG, F32),
        jnp.zeros((1, TILE), F32),
        jnp.zeros((HEAD_DIM, TILE), F32),
    )
    peak, total, acc = lax.fori_loop(bounds[step, 0], bounds[step, 1], body, start)
    out_ref[...] = acc / total
    lse_ref[...] = peak + jnp.log(total)


def attend_back_kernel(
    sorted_rows,
    tiles,
    bounds,
    meta_ref,
    place_ref,
    q_ref,
    do_ref,
    out_ref,
    lse_ref,
    rows_ref,
    kvt_ref,
    dq_ref,
    dkv_ref,
    acc_ref,
):
    step = pl.program_id(0)

    @pl.when(step == 0)
    def _():
        acc_ref[...] = jnp.zeros_like(acc_ref)

    queries, flows = q_ref[...], do_ref[...]
    place, low = meta_ref[0:1, :], meta_ref[1:2, :]
    log_total = lse_ref[...]
    delta = jnp.sum(flows[HEAD_DIM:, :].astype(F32) * out_ref[...], axis=0, keepdims=True)

    def body(kt, dq):
        at = pl.ds(pl.multiple_of(kt * TILE, TILE), TILE)
        rows = rows_ref[at, :]
        scores = dot_f32(rows, queries)
        allowed = mask_of(kt, key_places(sorted_rows, kt, place_ref), place, low)
        chances = jnp.exp(jnp.where(allowed, scores - log_total, NEG))
        flow = dot_f32(rows, flows)
        score_grad = (chances * (flow - delta)).astype(BF)
        dq = dq + dot_f32(kvt_ref[:HEAD_DIM, at], score_grad)
        acc_ref[:HEAD_DIM, at] += contract_cols(queries[:HEAD_DIM, :], score_grad)
        acc_ref[HEAD_DIM:, at] += contract_cols(flows[HEAD_DIM:, :], chances.astype(BF))
        return dq

    dq = lax.fori_loop(
        bounds[step, 0], bounds[step, 1], body, jnp.zeros((HEAD_DIM, TILE), F32)
    )
    dq_ref[...] = (dq * SCALE).astype(BF)

    @pl.when(step == tiles - 1)
    def _():
        dkv_ref[...] = acc_ref[...].astype(BF)


def attention_specs(length, query_length):
    def whole(shape):
        return pl.BlockSpec(shape, lambda i: (0, 0))

    def tile(rows):
        return pl.BlockSpec((rows, TILE), lambda i: (0, i))

    return whole, tile


def attend(sorted_rows, bounds, meta, place_col, q_pad, kv_rows, kv_t):
    length, query_length = kv_rows.shape[0], q_pad.shape[1]
    whole, tile = attention_specs(length, query_length)
    return pl.pallas_call(
        functools.partial(attend_kernel, sorted_rows),
        name="attend",
        grid=(query_length // TILE,),
        in_specs=[
            pl.BlockSpec(memory_space=pltpu.SMEM),
            tile(8),
            whole(place_col.shape),
            tile(2 * HEAD_DIM),
            whole((length, 2 * HEAD_DIM)),
            whole((2 * HEAD_DIM, length)),
        ],
        out_specs=(tile(HEAD_DIM), tile(1)),
        out_shape=(
            jax.ShapeDtypeStruct((HEAD_DIM, query_length), F32),
            jax.ShapeDtypeStruct((1, query_length), F32),
        ),
        compiler_params=pltpu.CompilerParams(vmem_limit_bytes=40 * 2**20),
    )(bounds, meta, place_col, q_pad, kv_rows, kv_t)


def attend_back(sorted_rows, bounds, meta, place_col, q_pad, do_pad, out, lse, kv_rows, kv_t):
    length, query_length = kv_rows.shape[0], q_pad.shape[1]
    whole, tile = attention_specs(length, query_length)
    return pl.pallas_call(
        functools.partial(attend_back_kernel, sorted_rows, query_length // TILE),
        name="attend_back",
        grid=(query_length // TILE,),
        in_specs=[
            pl.BlockSpec(memory_space=pltpu.SMEM),
            tile(8),
            whole(place_col.shape),
            tile(2 * HEAD_DIM),
            tile(2 * HEAD_DIM),
            tile(HEAD_DIM),
            tile(1),
            whole((length, 2 * HEAD_DIM)),
            whole((2 * HEAD_DIM, length)),
        ],
        out_specs=(tile(HEAD_DIM), whole((2 * HEAD_DIM, length))),
        out_shape=(
            jax.ShapeDtypeStruct((HEAD_DIM, query_length), BF),
            jax.ShapeDtypeStruct((2 * HEAD_DIM, length), BF),
        ),
        scratch_shapes=[pltpu.VMEM((2 * HEAD_DIM, length), F32)],
        compiler_params=pltpu.CompilerParams(vmem_limit_bytes=40 * 2**20),
    )(bounds, meta, place_col, q_pad, do_pad, out, lse, kv_rows, kv_t)


BLOCK = 64


def pick_pair(load, table, d):
    first, second = table[2 * d], table[2 * d + 1]
    left = load(lax.div(first, 2))
    right = load(lax.div(second, 2))
    lane = lax.broadcasted_iota(jnp.int32, left.shape, 1)
    left = jnp.where(lax.rem(first, 2) == 0, left, pltpu.roll(left, BLOCK, 1))
    right = jnp.where(lax.rem(second, 2) == 1, right, pltpu.roll(right, BLOCK, 1))
    return jnp.where(lane < BLOCK, left, right)


def column_block(ref, k, per):
    return ref[lax.div(k, per), :, span(lax.rem(k, per), 128)].astype(F32)


def fill_inverse(order, inverse, count):
    def put(n, carry):
        inverse[order[n]] = n
        return carry

    lax.fori_loop(0, count, put, 0)


def query_lows(lengths, step):
    place = lax.broadcasted_iota(jnp.int32, (1, TILE), 1) + step * TILE
    low = jnp.zeros((1, TILE), jnp.int32)
    first, end = 0, 0
    for n in range(lengths.shape[0]):
        end = end + lengths[n]
        low = jnp.where(end <= place, end, low)
        first = jnp.where(end <= step * TILE, end, first)
    return place, low, lax.div(first, TILE)


def sorted_attend_kernel(
    lengths, order, parts_ref, low_ref, out_ref, lse_ref, q_ref, kvt_ref, rows_ref, inverse
):
    step = pl.program_id(0)
    length = q_ref.shape[1]
    per = parts_ref.shape[2] // 128

    @pl.when(step == 0)
    def _():
        fill_inverse(order, inverse, length // BLOCK)

        def place(d, carry):
            tile = pick_pair(lambda k: column_block(parts_ref, k, per), inverse, d)
            at = span(d, 128)
            q_ref[:HEAD_DIM, at] = (tile[:HEAD_DIM] * SCALE).astype(BF)
            q_ref[HEAD_DIM:, at] = jnp.zeros((HEAD_DIM, 128), BF)
            kvt_ref[:, at] = tile[HEAD_DIM:].astype(BF)
            rows_ref[at, :] = tile[HEAD_DIM:].T.astype(BF)
            return carry

        lax.fori_loop(0, length // 128, place, 0)

    here = span(step, TILE)
    queries = q_ref[:, here]
    place, low, first = query_lows(lengths, step)

    def body(kt, carry):
        peak, total, acc = carry
        at = span(kt, TILE)
        scores = dot_f32(rows_ref[at, :], queries)
        allowed = mask_of(kt, key_places(True, kt, None), place, low)
        scores = jnp.where(allowed, scores, NEG)
        new_peak = jnp.maximum(peak, jnp.max(scores, axis=0, keepdims=True))
        weights = jnp.exp(scores - new_peak)
        fade = jnp.exp(peak - new_peak)
        total = total * fade + jnp.sum(weights, axis=0, keepdims=True)
        acc = acc * fade + dot_f32(kvt_ref[HEAD_DIM:, at], weights.astype(BF))
        return new_peak, total, acc

    start = (
        jnp.full((1, TILE), NEG, F32),
        jnp.zeros((1, TILE), F32),
        jnp.zeros((HEAD_DIM, TILE), F32),
    )
    peak, total, acc = lax.fori_loop(first, step + 1, body, start)
    out_ref[:, here] = acc / total
    lse_ref[:, here] = peak + jnp.log(total)

    @pl.when(step == length // TILE - 1)
    def _():
        def home(d, carry):
            tile = pick_pair(lambda k: out_ref[:, span(k, 128)], order, d)
            low_ref[lax.div(d, per), :, span(lax.rem(d, per), 128)] = tile.astype(BF)
            return carry

        lax.fori_loop(0, length // 128, home, 0)


def sorted_back_kernel(
    lengths, order, flow_ref, out_ref, lse_ref, q_ref, kvt_ref, rows_ref,
    grad_ref, do_ref, dq_ref, acc_ref, inverse,
):
    step = pl.program_id(0)
    length = q_ref.shape[1]
    per = grad_ref.shape[3] // 128

    @pl.when(step == 0)
    def _():
        acc_ref[...] = jnp.zeros_like(acc_ref)
        fill_inverse(order, inverse, length // BLOCK)

        def place(d, carry):
            tile = pick_pair(lambda k: flow_ref[k].astype(F32), inverse, d)
            at = span(d, 128)
            do_ref[:HEAD_DIM, at] = jnp.zeros((HEAD_DIM, 128), BF)
            do_ref[HEAD_DIM:, at] = tile.astype(BF)
            return carry

        lax.fori_loop(0, length // 128, place, 0)

    here = span(step, TILE)
    queries, flows = q_ref[:, here], do_ref[:, here]
    place, low, first = query_lows(lengths, step)
    log_total = lse_ref[:, here]
    delta = jnp.sum(flows[HEAD_DIM:, :].astype(F32) * out_ref[:, here], axis=0, keepdims=True)

    def body(kt, dq):
        at = span(kt, TILE)
        rows = rows_ref[at, :]
        scores = dot_f32(rows, queries)
        allowed = mask_of(kt, key_places(True, kt, None), place, low)
        chances = jnp.exp(jnp.where(allowed, scores - log_total, NEG))
        flow = dot_f32(rows, flows)
        score_grad = (chances * (flow - delta)).astype(BF)
        dq = dq + dot_f32(kvt_ref[:HEAD_DIM, at], score_grad)
        acc_ref[:HEAD_DIM, at] += contract_cols(queries[:HEAD_DIM, :], score_grad)
        acc_ref[HEAD_DIM:, at] += contract_cols(flows[HEAD_DIM:, :], chances.astype(BF))
        return dq

    dq = lax.fori_loop(
        first, step + 1, body, jnp.zeros((HEAD_DIM, TILE), F32)
    )
    dq_ref[:, here] = dq * SCALE

    @pl.when(step == length // TILE - 1)
    def _():
        def home(d, carry):
            at = span(lax.rem(d, per), 128)
            tile = pick_pair(lambda k: dq_ref[:, span(k, 128)], order, d)
            grad_ref[lax.div(d, per), 0, :, at] = tile.astype(BF)
            tile = pick_pair(lambda k: acc_ref[:, span(k, 128)], order, d).astype(BF)
            grad_ref[lax.div(d, per), 1, :, at] = tile[:HEAD_DIM]
            grad_ref[lax.div(d, per), 2, :, at] = tile[HEAD_DIM:]
            return carry

        lax.fori_loop(0, length // 128, home, 0)


def fixed(shape):
    return pl.BlockSpec(shape, lambda i: (0,) * len(shape))


def sorted_attend(lengths, order, parts):
    groups, _, columns = parts.shape
    length = groups * columns
    shapes = (
        ((groups, HEAD_DIM, columns), BF),
        ((HEAD_DIM, length), F32),
        ((1, length), F32),
        ((2 * HEAD_DIM, length), BF),
        ((2 * HEAD_DIM, length), BF),
        ((length, 2 * HEAD_DIM), BF),
    )
    return pl.pallas_call(
        sorted_attend_kernel,
        name="attend",
        grid=(length // TILE,),
        in_specs=[pl.BlockSpec(memory_space=pltpu.SMEM)] * 2 + [fixed(parts.shape)],
        out_specs=tuple(fixed(s) for s, _ in shapes),
        out_shape=tuple(jax.ShapeDtypeStruct(s, d) for s, d in shapes),
        scratch_shapes=[pltpu.SMEM((length // BLOCK,), jnp.int32)],
        compiler_params=pltpu.CompilerParams(vmem_limit_bytes=60 * 2**20),
        cost_estimate=pl.CostEstimate(
            flops=0, bytes_accessed=42_000_000, transcendentals=0
        ),
    )(lengths, order, parts)


def sorted_back(lengths, order, flow, out, lse, q_pad, kv_t, kv_rows, groups):
    length = out.shape[1]
    grad = (groups, 3, HEAD_DIM, length // groups)
    return pl.pallas_call(
        sorted_back_kernel,
        name="attend_back",
        grid=(length // TILE,),
        in_specs=[pl.BlockSpec(memory_space=pltpu.SMEM)] * 2
        + [fixed(a.shape) for a in (flow, out, lse, q_pad, kv_t, kv_rows)],
        out_specs=fixed(grad),
        out_shape=jax.ShapeDtypeStruct(grad, BF),
        scratch_shapes=[
            pltpu.VMEM((2 * HEAD_DIM, length), BF),
            pltpu.VMEM((HEAD_DIM, length), F32),
            pltpu.VMEM((2 * HEAD_DIM, length), F32),
            pltpu.SMEM((length // BLOCK,), jnp.int32),
        ],
        compiler_params=pltpu.CompilerParams(vmem_limit_bytes=40 * 2**20),
        cost_estimate=pl.CostEstimate(
            flops=0, bytes_accessed=42_000_000, transcendentals=0
        ),
    )(lengths, order, flow, out, lse, q_pad, kv_t, kv_rows)


def normalize(values):
    center = values - jnp.mean(values, axis=-1, keepdims=True)
    spread = jnp.mean(center * center, axis=-1, keepdims=True)
    scale = lax.rsqrt(spread + EPS)
    return center * scale, scale


def mid_kernel(
    experts, team, member, att, wo, x, vec, rw, route, cot,
    second, dgrad, send_s, send_g, sel, mixes, middle_own, prob_own, hot_own, second_own, att_own,
    egrad,
):
    rows = middle_own.shape[0]
    slots = send_s.shape[1]
    groups = send_s.shape[0]
    capacity = slots // team
    lane = lax.broadcasted_iota(jnp.int32, (rows, 128), 1)
    row = lax.broadcasted_iota(jnp.int32, (rows, rows), 0)
    col = lax.broadcasted_iota(jnp.int32, (rows, rows), 1)
    me = member[0]

    def block(b, carry):
        at = span(b, rows)
        part = att[:, at]
        middle = x[at, :].astype(F32) + contract_rows(part, wo[...])
        hat, _ = normalize(middle)
        low = (hat * vec[5:6, :] + vec[7:8, :]).astype(BF)
        second[at, :] = low
        logits = dot_f32(low, rw[...])
        is_expert = lane < experts
        is_mix = (lane >= experts) & (lane < experts + 2)
        pe = jnp.where(is_expert, logits, NEG)
        pe = jnp.exp(pe - jnp.max(pe, axis=1, keepdims=True))
        pe = pe / jnp.sum(pe, axis=1, keepdims=True)
        pm = jnp.where(is_mix, logits, NEG)
        pm = jnp.exp(pm - jnp.max(pm, axis=1, keepdims=True))
        pm = pm / jnp.sum(pm, axis=1, keepdims=True)
        route_row = jnp.broadcast_to(route[b][0:1, :], (rows, rows))
        route_col = jnp.sum(jnp.where(row == col, route_row, 0), axis=1, keepdims=True)
        hot = lane == route_col
        gate = jnp.sum(jnp.where(hot, pe, 0.0), axis=1, keepdims=True)
        mix0 = jnp.sum(jnp.where(lane == experts, pm, 0.0), axis=1, keepdims=True)
        mix1 = jnp.sum(jnp.where(lane == experts + 1, pm, 0.0), axis=1, keepdims=True)
        scaled = mix1 * gate
        flow = cot[at, :].astype(F32)
        dgrad[at, :] = (flow * mix0).astype(BF)
        egrad[at, :] = (flow * scaled).astype(BF)
        mixes[at, :] = jnp.where(lane == 0, mix0, jnp.where(lane == 1, scaled, 0.0))
        same = (route_row == route_col) & (col < row)
        rank = jnp.sum(jnp.where(same, 1, 0), axis=1, keepdims=True)
        group = lax.div(route_col, team)
        mine = lax.rem(route_col, team) == me
        target = jnp.where(mine, group * slots + b * capacity + rank, groups * slots)
        slot = lax.broadcasted_iota(jnp.int32, (rows, groups * slots), 1)
        sel[at, :] = jnp.where(slot == target, 1.0, 0.0).astype(BF)

        @pl.when(b == me)
        def _():
            middle_own[...] = middle
            prob_own[...] = jnp.where(is_expert, pe, jnp.where(is_mix, pm, 0.0))
            hot_own[...] = jnp.where(hot, 1.0, 0.0)
            second_own[...] = low
            att_own[...] = part

        return carry

    lax.fori_loop(0, team, block, 0)
    send_s[...] = contract_rows(sel[...], second[...]).astype(BF).reshape(send_s.shape)
    send_g[...] = contract_rows(sel[...], egrad[...]).astype(BF).reshape(send_g.shape)


def between(experts, sizes, slots, member, att, wo, x, vec, rw, route, cot):
    two, groups, team = sizes
    group_rows, width = x.shape
    rows = group_rows // team
    shapes = (
        ((group_rows, width), BF),
        ((group_rows, width), BF),
        ((groups, slots, width), BF),
        ((groups, slots, width), BF),
        ((group_rows, groups * slots), BF),
        ((group_rows, 128), F32),
        ((rows, width), F32),
        ((rows, 128), F32),
        ((rows, 128), F32),
        ((rows, width), BF),
        ((width, rows), BF),
    )
    inside = pl.BlockSpec(memory_space=pltpu.VMEM)
    return pl.pallas_call(
        functools.partial(mid_kernel, experts, team),
        name="between",
        in_specs=[pl.BlockSpec(memory_space=pltpu.SMEM)] + [inside] * 7,
        out_specs=tuple(inside for _ in shapes),
        out_shape=tuple(jax.ShapeDtypeStruct(s, d) for s, d in shapes),
        scratch_shapes=[pltpu.VMEM((group_rows, width), BF)],
        compiler_params=pltpu.CompilerParams(vmem_limit_bytes=60 * 2**20),
    )(member, att, wo, x, vec, rw, route, cot)


def turn_kernel(
    experts, layer_sum, second_sum, sums, middle, prob, hot, second, att, cot, rw, wo, vec,
    layer, middle_grad, flow_t, out_term, small_t,
):
    rows = middle.shape[0]
    lane = lax.broadcasted_iota(jnp.int32, (rows, 128), 1)
    layer[...] = (middle[...] + layer_sum[...]).astype(BF)
    chances, chosen = prob[...], hot[...]
    s0, s1 = sums[:, 0:1], sums[:, 1:2]
    mix1 = jnp.sum(jnp.where(lane == experts + 1, chances, 0.0), axis=1, keepdims=True)
    gate = jnp.sum(chances * chosen, axis=1, keepdims=True)
    pull_gate = s1 * mix1
    pulls = jnp.where(lane == experts, s0, jnp.where(lane == experts + 1, s1 * gate, 0.0))
    mean_pull = jnp.sum(chances * pulls, axis=1, keepdims=True)
    logit_grad = chances * jnp.where(
        lane < experts, pull_gate * (chosen - gate), pulls - mean_pull
    )
    logit_grad = jnp.where(lane < experts + 2, logit_grad, 0.0).astype(BF)
    second_grad = second_sum[...] + contract_cols(logit_grad, rw[...])
    hat, scale = normalize(middle[...])
    pull = second_grad * vec[5:6, :]
    part = scale * (
        pull
        - jnp.mean(pull, axis=-1, keepdims=True)
        - hat * jnp.mean(pull * hat, axis=-1, keepdims=True)
    )
    grad = cot[...].astype(F32) + part
    middle_grad[...] = grad
    branch = grad.astype(BF)
    width = wo.shape[0]

    def tile(n, carry):
        at = span(n, TILE)
        flow_t[at, :] = contract_cols(wo[at, :], branch).astype(BF)
        out_term[at, :] = dot_f32(att[at, :], branch).astype(BF)
        return carry

    lax.fori_loop(0, width // TILE, tile, 0)
    used = small_t.shape[0]
    routed = contract_rows(logit_grad, second[...])[:used, :]
    which = lax.broadcasted_iota(jnp.int32, routed.shape, 0)
    gain = jnp.sum(second_grad * hat, axis=0, keepdims=True)
    bias = jnp.sum(second_grad, axis=0, keepdims=True)
    small_t[...] = jnp.where(
        which == experts + 3, gain, jnp.where(which == experts + 5, bias, routed)
    )


def turn(experts, layer_sum, second_sum, sums, middle, prob, hot, second, att, cot, rw, wo, vec):
    rows, width = middle.shape
    used = -(-(experts + 6) // 8) * 8
    shapes = (
        ((rows, width), BF),
        ((rows, width), F32),
        ((width, rows), BF),
        ((width, width), BF),
        ((used, width), F32),
    )
    inside = pl.BlockSpec(memory_space=pltpu.VMEM)
    return pl.pallas_call(
        functools.partial(turn_kernel, experts),
        name="turn",
        in_specs=[inside] * 12,
        out_specs=tuple(inside for _ in shapes),
        out_shape=tuple(jax.ShapeDtypeStruct(s, d) for s, d in shapes),
        compiler_params=pltpu.CompilerParams(vmem_limit_bytes=40 * 2**20),
    )(layer_sum, second_sum, sums, middle, prob, hot, second, att, cot, rw, wo, vec)


def row_sum_kernel(left, right, out):
    out[0] = contract_rows(left[...], right[...])


def row_sum(left, right, tile):
    many, high = left.shape
    wide = right.shape[1]
    return pl.pallas_call(
        row_sum_kernel,
        name="row_sum",
        grid=(high // tile,),
        in_specs=[pl.BlockSpec((many, tile), lambda i: (0, i)), fixed(right.shape)],
        out_specs=pl.BlockSpec((1, tile, wide), lambda i: (0, i, 0)),
        out_shape=jax.ShapeDtypeStruct((1, high, wide), F32),
        compiler_params=pltpu.CompilerParams(vmem_limit_bytes=40 * 2**20),
        cost_estimate=pl.CostEstimate(
            flops=2 * many * high * wide, bytes_accessed=4 * high * wide, transcendentals=0
        ),
    )(left, right)


class Net:
    def __init__(self, sizes, send_sem, recv_sem):
        self.two, self.groups, self.team = sizes
        self.send_sem, self.recv_sem = send_sem, recv_sem
        self.c = lax.axis_index("dp")
        i = lax.axis_index("ctx")
        self.g, self.t = lax.div(i, self.team), lax.rem(i, self.team)
        self.group_steps = [(0, k, 0) for k in range(1, self.groups)]
        self.team_steps = [(0, 0, k) for k in range(1, self.team)]
        self.swap = (1, 0, 0)
        self.started = []

    def device(self, step):
        dc, dg, dt = step
        return (
            lax.rem(self.c + dc, self.two),
            lax.rem(self.g + dg, self.groups) * self.team + lax.rem(self.t + dt, self.team),
        )

    def greet(self):
        barrier = pltpu.get_barrier_semaphore()
        steps = self.group_steps + self.team_steps + [self.swap]
        for step in steps:
            pl.semaphore_signal(barrier, inc=1, device_id=self.device(step), device_id_type=MESH)
        pl.semaphore_wait(barrier, len(steps))

    def send(self, src, dst, step):
        k = len(self.started)
        copy = pltpu.make_async_remote_copy(
            src_ref=src,
            dst_ref=dst,
            send_sem=self.send_sem.at[k],
            recv_sem=self.recv_sem.at[k],
            device_id=self.device(step),
            device_id_type=MESH,
        )
        copy.start()
        self.started.append(copy)
        return copy

    def group_to(self, step):
        return lax.rem(self.g + step[1], self.groups)

    def group_from(self, step):
        return lax.rem(self.g + self.groups - step[1], self.groups)

    def team_to(self, step):
        return lax.rem(self.t + step[2], self.team)

    def team_from(self, step):
        return lax.rem(self.t + self.team - step[2], self.team)

    def close(self):
        for copy in self.started:
            copy.wait_send()


def arrive(copies):
    for copy in copies:
        copy.wait_recv()


class Local:
    def __init__(self, sem):
        self.sem, self.count, self.open = sem, 0, []

    def copy(self, src, dst):
        made = pltpu.make_async_copy(src, dst, self.sem.at[self.count])
        made.start()
        self.count += 1
        self.open.append(made)
        return made

    def wait(self, *copies):
        for made in copies or tuple(self.open):
            made.wait()
            self.open = [other for other in self.open if other is not made]


def start_kernel(sizes, *refs):
    tokens, cot, w_qkv, w_up, w_down, w_out, router, gains, biases, routes = refs[:10]
    token_o, cot_o, heads_o, normed_o, weight_o, vec_o, out_o, ff_o, route_o = refs[10:19]
    (
        own, up, down, route, square, stage, weights, tokens_v, normed, mixed, heads, out_v,
        send_sem, recv_sem, local_sem,
    ) = refs[19:]
    net, local = Net(sizes, send_sem, recv_sem), Local(local_sem)
    c, g, t = net.c, net.g, net.t
    two, groups, team = sizes
    rows, width = tokens.shape
    used = own.shape[2] - 128
    wr = own.shape[1]
    own_tokens = local.copy(tokens, tokens_v.at[t])
    local.copy(cot, cot_o.at[t])

    square[...] = jnp.zeros_like(square)
    square[: router.shape[0], :wr] = router[...]
    square[124:126, :wr] = gains[...]
    square[126:128, :wr] = biases[...]
    small = square[...].T[:wr, :].astype(BF)
    third = used // 3
    for n in range(team):
        for k in range(3):
            at = k * width + n * third
            own[n, :, k * third : (k + 1) * third] = w_qkv[:, at : at + third].astype(BF)
        own[n, :, used:] = small
    stage[t] = own[t]
    net.greet()
    staged = [net.send(own.at[net.team_to(s)], stage.at[t], s) for s in net.team_steps]
    told = [net.send(tokens, tokens_v.at[t], s) for s in net.team_steps]
    out_v[g] = w_out[...].astype(BF)
    spread_out = [net.send(out_v.at[g], out_v.at[g], s) for s in net.group_steps]
    deep = w_down.shape[0]
    for n in range(team):
        for k in range(two * groups):
            at = (k * team + n) * deep
            up[n, :, k * deep : (k + 1) * deep] = w_up[:, at : at + deep].astype(BF)
    down[...] = w_down[...].astype(BF).reshape(down.shape)
    route[...] = jnp.broadcast_to(routes[...], route.shape)
    local.copy(up.at[t], ff_o.at[0, t])
    local.copy(down, ff_o.at[1])
    local.copy(route, route_o.at[t])
    later = [net.send(route, route_o.at[t], s) for s in net.team_steps]
    later += [net.send(up.at[net.team_to(s)], ff_o.at[0, t], s) for s in net.team_steps]
    arrive(staged)
    spread = [net.send(stage, weights.at[c, g], s) for s in net.group_steps]
    swapped = [net.send(stage, weights.at[c, g], net.swap)]
    mine = local.copy(stage, weights.at[c, g])
    later += [net.send(cot, cot_o.at[t], s) for s in net.team_steps]
    local.wait(own_tokens)
    arrive(told)
    local.copy(tokens_v, token_o)
    local.wait(mine)
    for copy, s in zip(spread, net.group_steps):
        copy.wait_recv()
        view = weights.at[c, net.group_from(s)]
        swapped.append(net.send(view, view, net.swap))
    arrive(swapped)
    local.copy(weights, weight_o)

    small = weights[:, :, :, :, used:].reshape(width, 128).astype(F32).T
    vec_o[...] = small[120:, :]

    def norm(b, carry):
        hat, _ = normalize(tokens_v[b].astype(F32))
        normed[b] = (hat * vec_o[4:5, :] + vec_o[6:7, :]).astype(BF)
        return carry

    lax.fori_loop(0, team, norm, 0)
    local.copy(normed, normed_o)
    group_rows = rows * team
    per = used // 3 // 128
    pair = 128 // HEAD_DIM
    for n in range(used // 128):
        columns = weights[:, :, :, :, n * 128 : (n + 1) * 128].reshape(width, 128)
        made = dot_f32(normed[...].reshape(group_rows, width), columns).T.astype(BF)
        at = (n % per) * pair
        mixed[n // per, at : at + pair] = made.reshape(pair, HEAD_DIM, group_rows)
    given = [net.send(mixed.at[:, net.group_to(s)], heads.at[g], s) for s in net.group_steps]
    local.wait(local.copy(mixed.at[:, g], heads.at[g]))

    arrive(spread_out)
    local.copy(out_v, out_o.at[c, :, t])
    swapped = [net.send(out_v, out_o.at[c, :, t], net.swap)]
    outed = [net.send(out_v, out_o.at[c, :, t], s) for s in net.team_steps]
    for copy, s in zip(outed, net.team_steps):
        copy.wait_recv()
        view = out_o.at[c, :, net.team_from(s)]
        swapped.append(net.send(view, view, net.swap))
    arrive(given)
    local.copy(heads, heads_o)
    arrive(swapped + later)
    local.wait()
    net.close()


def start(sizes, tokens, cot, w_qkv, w_up, w_down, w_out, router, gains, biases, routes):
    two, groups, team = sizes
    rows, width = tokens.shape
    wr = w_qkv.shape[0]
    used = 3 * width // team
    cols = used + 128
    head = (3, groups, HEAD_DIM, team * rows)
    up = (team, wr, width)
    shapes = (
        ((team, rows, width), BF),
        ((team, rows, width), BF),
        ((groups, 3, HEAD_DIM, team * rows), BF),
        ((team, rows, width), BF),
        ((two, groups, team, wr, cols), BF),
        ((8, width), F32),
        ((two, groups, team, wr, width), BF),
        ((2,) + up, BF),
        ((team, 8, rows), jnp.int32),
    )
    anywhere = pl.BlockSpec(memory_space=pl.ANY)
    inside = pl.BlockSpec(memory_space=pltpu.VMEM)
    count = 6 * (team - 1) + 4 * (groups - 1) + 2 + (team - 1)
    return pl.pallas_call(
        functools.partial(start_kernel, sizes),
        name="start",
        out_shape=tuple(jax.ShapeDtypeStruct(s, d) for s, d in shapes),
        in_specs=[anywhere] * 2 + [inside] * 8,
        out_specs=tuple(inside if n == 5 else anywhere for n in range(9)),
        scratch_shapes=[
            pltpu.VMEM((team, wr, cols), BF),
            pltpu.VMEM(up, BF),
            pltpu.VMEM(up, BF),
            pltpu.VMEM((8, rows), jnp.int32),
            pltpu.VMEM((128, 128), F32),
            pltpu.VMEM((team, wr, cols), BF),
            pltpu.VMEM((two, groups, team, wr, cols), BF),
            pltpu.VMEM((team, rows, width), BF),
            pltpu.VMEM((team, rows, width), BF),
            pltpu.VMEM(head, BF),
            pltpu.VMEM((groups, 3, HEAD_DIM, team * rows), BF),
            pltpu.VMEM((groups, wr, width), BF),
            pltpu.SemaphoreType.DMA((count,)),
            pltpu.SemaphoreType.DMA((count,)),
            pltpu.SemaphoreType.DMA((14,)),
        ],
        compiler_params=pltpu.CompilerParams(
            collective_id=12, has_side_effects=True, vmem_limit_bytes=60 * 2**20
        ),
        cost_estimate=pl.CostEstimate(flops=0, bytes_accessed=150_000_000, transcendentals=0),
    )(tokens, cot, w_qkv, w_up, w_down, w_out, router, gains, biases, routes)


def end_kernel(sizes, experts, *refs):
    groups = sizes[1]
    parts, refs = refs[:groups], refs[groups:]
    weight, normed, tokens, vec, middle_grad, small, up, out = refs[:8]
    grad_o, qkv_o, up_o, out_o, small_o = refs[8:13]
    (
        up_r, small_d, mixed, turned, weights, normed_v, give, got, zsend, zrecv, npart, nrecv, qsend, qrecv,
        out_r, small_a, small_b, small_c, send_sem, recv_sem, local_sem,
    ) = refs[13:]
    net, local = Net(sizes, send_sem, recv_sem), Local(local_sem)
    c, g, t = net.c, net.g, net.t
    team = sizes[2]
    rows, width = tokens.shape
    group_rows, used = turned.shape
    for k, part in enumerate(parts):
        local.copy(part, mixed.at[:, net.group_from((0, k, 0))])
    local.copy(normed, normed_v)
    local.copy(weight, weights)
    local.copy(up.at[t], up_r.at[t])
    local.copy(out.at[g], out_r.at[g])
    net.greet()
    outed = [net.send(out.at[net.group_to(s)], out_r.at[g], s) for s in net.group_steps]
    later = [net.send(up.at[net.team_to(s)], up_r.at[t], s) for s in net.team_steps]
    local.wait()
    per = used // 3 // 128
    pair = 128 // HEAD_DIM
    for n in range(used // 128):
        at = (n % per) * pair
        block = mixed[n // per, at : at + pair].reshape(128, group_rows)
        turned[:, n * 128 : (n + 1) * 128] = block.astype(F32).T.astype(BF)

    half = width // 2
    tile = 128

    def term(core, n):
        at = pl.ds(pl.multiple_of(core * half + n * tile, tile), tile)
        left = normed_v[:, :, at].reshape(group_rows, tile)
        return contract_rows(left, turned[...])

    def giving(n, carry):
        give[span(n, tile), :] = term(lax.rem(c + 1, 2), n).astype(BF)
        return carry

    lax.fori_loop(0, half // tile, giving, 0)
    crossed = net.send(give, got, net.swap)

    def part_of(r, carry):
        columns = weights[:, :, :, :, :used].reshape(width, used)
        npart[r] = contract_cols(turned[span(r, rows), :], columns).astype(BF)
        return carry

    lax.fori_loop(0, team, part_of, 0)
    owned = [net.send(npart.at[net.team_to(s)], nrecv.at[t], s) for s in net.team_steps]
    nrecv[t] = npart[t]
    crossed.wait_recv()

    def keeping(n, carry):
        at = span(n, tile)
        zsend[at, :] = (term(c, n) + got[at, :].astype(F32)).astype(BF)
        return carry

    lax.fori_loop(0, half // tile, keeping, 0)
    deep = half // groups
    summed = [
        net.send(zsend.at[span(net.group_to(s), deep), :], zrecv.at[g], s)
        for s in net.group_steps
    ]
    zrecv[g] = zsend[span(g, deep), :]

    arrive(owned)
    flow = jnp.sum(nrecv[...].astype(F32), axis=0)
    hat, scale = normalize(tokens[...].astype(F32))
    pull = flow * vec[4:5, :]
    pulled = scale * (
        pull
        - jnp.mean(pull, axis=-1, keepdims=True)
        - hat * jnp.mean(pull * hat, axis=-1, keepdims=True)
    )
    grad_o[...] = (middle_grad[...] + pulled).astype(BF)

    gain = jnp.sum(flow * hat, axis=0, keepdims=True)
    bias = jnp.sum(flow, axis=0, keepdims=True)
    which = lax.broadcasted_iota(jnp.int32, small.shape, 0)
    mine = jnp.where(
        which == experts + 2, gain, jnp.where(which == experts + 4, bias, small[...])
    )
    small_a[c] = mine
    crossing = net.send(small_a.at[c], small_a.at[c], net.swap)
    crossing.wait_recv()
    small_c[...] = small_a[0] + small_a[1]

    def columns_of(k):
        return span(c * groups + k, 128)

    moved = [
        net.send(small_c.at[:, columns_of(net.group_to(s))], small_b.at[g], s)
        for s in net.group_steps
    ]
    small_b[g] = small_c[:, columns_of(g)]
    arrive(moved)
    small_d[t] = jnp.sum(small_b[...], axis=0)
    later += [net.send(small_d.at[t], small_d.at[t], s) for s in net.team_steps]

    arrive(summed)
    qsend[...] = jnp.sum(zrecv[...].astype(F32), axis=0).astype(BF).reshape(qsend.shape)
    later += [net.send(qsend.at[net.team_to(s)], qrecv.at[t], s) for s in net.team_steps]
    qrecv[t] = qsend[t]
    arrive(outed)
    out_o[...] = jnp.sum(out_r[...].astype(F32), axis=0)
    arrive(later)
    small_o[...] = jnp.sum(small_d[...], axis=0)
    third = used // 3
    deep = up_o.shape[1] // (2 * groups * team)
    for n in range(team):
        for k in range(3):
            at = k * width + n * third
            qkv_o[:, at : at + third] = qrecv[n, :, k * third : (k + 1) * third].astype(F32)
        for k in range(2 * groups):
            at = (k * team + n) * deep
            up_o[:, at : at + deep] = up_r[n, :, k * deep : (k + 1) * deep].astype(F32)
    net.close()


def end(sizes, experts, parts, weight, normed, tokens, vec, middle_grad, small, up, out):
    two, groups, team = sizes
    rows, width = tokens.shape
    wr = out.shape[1]
    used = 3 * groups * HEAD_DIM
    group_rows = parts[0].shape[2]
    half = width // 2
    shapes = (
        ((rows, width), BF),
        ((wr, 3 * width), F32),
        ((wr, team * width), F32),
        ((wr, width), F32),
        ((small.shape[0], 128), F32),
    )
    anywhere = pl.BlockSpec(memory_space=pl.ANY)
    inside = pl.BlockSpec(memory_space=pltpu.VMEM)
    count = 5 * (team - 1) + 3 * (groups - 1) + 2
    return pl.pallas_call(
        functools.partial(end_kernel, sizes, experts),
        name="end",
        out_shape=tuple(jax.ShapeDtypeStruct(s, d) for s, d in shapes),
        in_specs=[anywhere] * (groups + 2) + [inside] * 4 + [anywhere] * 2,
        out_specs=tuple(inside for _ in shapes),
        scratch_shapes=[
            pltpu.VMEM((team, wr, width), BF),
            pltpu.VMEM((team, small.shape[0], 128), F32),
            pltpu.VMEM((3, groups, HEAD_DIM, group_rows), BF),
            pltpu.VMEM((group_rows, used), BF),
            pltpu.VMEM(weight.shape, BF),
            pltpu.VMEM(normed.shape, BF),
            pltpu.VMEM((half, used), BF),
            pltpu.VMEM((half, used), BF),
            pltpu.VMEM((half, used), BF),
            pltpu.VMEM((groups, half // groups, used), BF),
            pltpu.VMEM((team, rows, width), BF),
            pltpu.VMEM((team, rows, width), BF),
            pltpu.VMEM((team, wr, used), BF),
            pltpu.VMEM((team, wr, used), BF),
            pltpu.VMEM((groups, wr, width), BF),
            pltpu.VMEM((2,) + small.shape, F32),
            pltpu.VMEM((groups, small.shape[0], 128), F32),
            pltpu.VMEM(small.shape, F32),
            pltpu.SemaphoreType.DMA((count,)),
            pltpu.SemaphoreType.DMA((count,)),
            pltpu.SemaphoreType.DMA((groups + 4,)),
        ],
        compiler_params=pltpu.CompilerParams(
            collective_id=13, has_side_effects=True, vmem_limit_bytes=60 * 2**20
        ),
        cost_estimate=pl.CostEstimate(flops=0, bytes_accessed=120_000_000, transcendentals=0),
    )(*parts, weight, normed, tokens, vec, middle_grad, small, up, out)


def gelu_and_slope(x):
    k = math.sqrt(2.0 / math.pi)
    square = x * x
    bent = jnp.tanh(k * (x + 0.044715 * (square * x)))
    half = 0.5 * (1.0 + bent)
    slope = half + (0.5 * k) * x * (1.0 - bent * bent) * (1.0 + (3 * 0.044715) * square)
    return x * half, slope


def feed_kernel(sizes, copies_count, *refs):
    two, groups, team = sizes
    (send_s, send_g, eup_h, edown_h, second_h, dgrad_h, ff_h, sel_h, cot_h, mix_h) = refs[:10]
    (layer_o, grad_o, sums_o, active_o, hgrad_o, arr_s_o, arr_g_o, ffg_o) = refs[10:18]
    (
        arr_s, arr_g, eup, edown, second, dgrad, upw, downw, sel, cot, mix,
        slope, active, hgrad, acc, give, got_s, got_g, ret_s, ret_g, back_s, back_g,
        low, ugrad, dense, spart, lay, spa, sums, lay_r, spa_r, sums_r,
        term_give, term_got, send_sem, recv_sem, load_sem, out_sem,
    ) = refs[18:]
    c = lax.axis_index("dp")
    i = lax.axis_index("ctx")
    g, t = lax.div(i, team), lax.rem(i, team)
    width = second.shape[1]
    rows = lay.shape[1]
    hid, ehid = upw.shape[1], eup.shape[1]
    core = lax.rem(c + 1, two)

    def device(step):
        dc, dg, dt = step
        return (
            lax.rem(c + dc, two),
            lax.rem(g + dg, groups) * team + lax.rem(t + dt, team),
        )

    index = [0]

    def remote(src, dst, step):
        k = index[0]
        index[0] += 1
        assert k < copies_count
        return pltpu.make_async_remote_copy(
            src_ref=src,
            dst_ref=dst,
            send_sem=send_sem.at[k],
            recv_sem=recv_sem.at[k],
            device_id=device(step),
            device_id_type=MESH,
        )

    group_steps = [(0, k, 0) for k in range(1, groups)]
    team_steps = [(0, 0, k) for k in range(1, team)]
    swap = (1, 0, 0)
    deep = ff_h.shape[2]

    def block_of(core, k):
        return pl.ds(pl.multiple_of((core * groups + k) * deep, deep), deep)

    loads = []
    for k, (src, dst) in enumerate(
        [
            (second_h, second), (dgrad_h, dgrad), (eup_h, eup), (edown_h, edown), (sel_h, sel), (cot_h, cot), (mix_h, mix),
            (send_s.at[g], arr_s.at[c, g]), (send_g.at[g], arr_g.at[c, g]),
        ]
        + [
            (ff_h.at[k, n], weight.at[block_of(c, k), :])
            for k in range(groups)
            for n, weight in enumerate((upw, downw))
        ]
    ):
        load = pltpu.make_async_copy(src, dst, load_sem.at[k])
        load.start()
        loads.append(load)

    barrier = pltpu.get_barrier_semaphore()
    greet = group_steps + team_steps + [swap]
    for step in greet:
        pl.semaphore_signal(barrier, inc=1, device_id=device(step), device_id_type=MESH)
    pl.semaphore_wait(barrier, len(greet))

    every = []

    def launch(copy):
        copy.start()
        every.append(copy)
        return copy

    def to_groups(src, dst):
        return [
            launch(remote(src.at[lax.rem(g + s[1], groups)], dst.at[g], s)) for s in group_steps
        ]

    def source(s):
        return lax.rem(g + groups - s[1], groups)

    swap_w = [
        launch(remote(ff_h.at[k, n], weight.at[block_of(c, k), :], swap))
        for k in range(groups)
        for n, weight in enumerate((upw, downw))
    ]
    out_s = [
        launch(remote(send_s.at[lax.rem(g + s[1], groups)], arr_s.at[c, g], s))
        for s in group_steps
    ]
    swap_s = [launch(remote(send_s.at[g], arr_s.at[c, g], swap))]
    out_g = [
        launch(remote(send_g.at[lax.rem(g + s[1], groups)], arr_g.at[c, g], s))
        for s in group_steps
    ]
    swap_g = [launch(remote(send_g.at[g], arr_g.at[c, g], swap))]

    for load in loads[:2] + loads[9:]:
        load.wait()
    for copy in swap_w:
        copy.wait_recv()

    def dense_in(h, carry):
        at = span(h, TILE)
        value, bend = gelu_and_slope(dot_f32(second[...], upw[:, at]))
        low[:, at] = value.astype(BF)
        ugrad[:, at] = (bend * contract_cols(dgrad[...], downw[at, :])).astype(BF)
        return carry

    lax.fori_loop(0, hid // TILE, dense_in, 0)

    def dense_out(n, carry):
        at = span(n, TILE)
        dense[:, at] = dot_f32(low[...], downw[:, at])
        spart[:, at] = contract_cols(ugrad[...], upw[at, :])
        return carry

    lax.fori_loop(0, width // TILE, dense_out, 0)

    for load in loads[2:9]:
        load.wait()
    for copy, s in zip(out_s, group_steps):
        copy.wait_recv()
        swap_s.append(launch(remote(arr_s.at[c, source(s)], arr_s.at[c, source(s)], swap)))
    for copy in swap_s:
        copy.wait_recv()
    entries = 2 * groups * arr_s.shape[2]

    def expert_in(h, carry):
        at = span(h, TILE)
        value, bend = gelu_and_slope(dot_f32(arr_s[...].reshape(entries, width), eup[:, at]))
        active[:, at] = value.astype(BF)
        slope[:, at] = bend
        return carry

    lax.fori_loop(0, ehid // TILE, expert_in, 0)
    keeps = [
        pltpu.make_async_copy(active, active_o, out_sem.at[0]),
        pltpu.make_async_copy(arr_s, arr_s_o, out_sem.at[1]),
    ]
    for copy in keeps:
        copy.start()

    def expert_out(n, carry):
        at = span(n, TILE)
        acc[:, :, at] = dot_f32(active[...], edown[:, at]).reshape(2, entries // 2, TILE)
        return carry

    lax.fori_loop(0, width // TILE, expert_out, 0)
    give[0] = acc[core].astype(BF)
    other_s = launch(remote(give.at[0], got_s, swap))

    for copy, s in zip(out_g, group_steps):
        copy.wait_recv()
        swap_g.append(launch(remote(arr_g.at[c, source(s)], arr_g.at[c, source(s)], swap)))
    other_s.wait_recv()
    ret_s[...] = (acc[c] + got_s[...].astype(F32)).astype(BF).reshape(ret_s.shape)
    home_s = to_groups(ret_s, back_s)
    back_s[g] = ret_s[g]
    for copy in swap_g:
        copy.wait_recv()

    def expert_back(h, carry):
        at = span(h, TILE)
        pull = contract_cols(arr_g[...].reshape(entries, width), edown[at, :])
        hgrad[:, at] = (slope[:, at] * pull).astype(BF)
        return carry

    lax.fori_loop(0, ehid // TILE, expert_back, 0)
    keeps += [
        pltpu.make_async_copy(hgrad, hgrad_o, out_sem.at[2]),
        pltpu.make_async_copy(arr_g, arr_g_o, out_sem.at[3]),
    ]
    for copy in keeps[2:]:
        copy.start()

    def expert_back_out(n, carry):
        at = span(n, TILE)
        acc[:, :, at] = contract_cols(hgrad[...], eup[at, :]).reshape(2, entries // 2, TILE)
        return carry

    lax.fori_loop(0, width // TILE, expert_back_out, 0)
    give[1] = acc[core].astype(BF)
    other_g = launch(remote(give.at[1], got_g, swap))
    other_g.wait_recv()
    ret_g[...] = (acc[c] + got_g[...].astype(F32)).astype(BF).reshape(ret_g.shape)
    home_g = to_groups(ret_g, back_g)
    back_g[g] = ret_g[g]

    for copy in home_s:
        copy.wait_recv()
    slots = groups * back_s.shape[1]
    lane = lax.broadcasted_iota(jnp.int32, (rows, 128), 1)

    def join_layer(r, carry):
        at = span(r, rows)
        found = dot_f32(sel[at, :], back_s[...].reshape(slots, width))
        own = dense[at, :]
        flow = cot[at, :].astype(F32)
        mixes = mix[at, :]
        lay[r] = (mixes[:, 0:1] * own + mixes[:, 1:2] * found).astype(BF)
        plain = jnp.sum(flow * own, axis=1, keepdims=True)
        routed = jnp.sum(flow * found, axis=1, keepdims=True)
        sums[r] = jnp.where(lane == 0, plain, jnp.where(lane == 1, routed, 0.0))
        return carry

    lax.fori_loop(0, team, join_layer, 0)

    def to_team(src, dst):
        made = [launch(remote(src.at[lax.rem(t + s[2], team)], dst.at[t], s)) for s in team_steps]
        dst[t] = src[t]
        return made

    team_copies = to_team(lay, lay_r) + to_team(sums, sums_r)

    for copy in home_g:
        copy.wait_recv()

    def join_grad(r, carry):
        at = span(r, rows)
        found = dot_f32(sel[at, :], back_g[...].reshape(slots, width))
        spa[r] = (spart[at, :] + found).astype(BF)
        return carry

    lax.fori_loop(0, team, join_grad, 0)
    team_copies += to_team(spa, spa_r)

    half = hid // 2
    term_tile = 128

    def down_term(base, n):
        at = pl.ds(pl.multiple_of(base + n * term_tile, term_tile), term_tile)
        return contract_rows(low[:, at], dgrad[...])

    def up_term(base, n):
        at = pl.ds(pl.multiple_of(base + n * term_tile, term_tile), term_tile)
        return contract_rows(second[:, at], ugrad[...])

    terms = []
    for k, (term, size) in enumerate(((down_term, half), (up_term, width // 2))):

        def giving(n, carry, k=k, term=term, size=size):
            term_give[k, span(n, term_tile), :] = term(core * size, n).astype(BF)
            return carry

        lax.fori_loop(0, size // term_tile, giving, 0)
        terms.append(launch(remote(term_give.at[k], term_got.at[k], swap)))
    for k, (term, size) in enumerate(((down_term, half), (up_term, width // 2))):
        terms[k].wait_recv()

        def keeping(n, carry, k=k, term=term, size=size):
            at = span(n, term_tile)
            total = term(c * size, n) + term_got[k, at, :].astype(F32)
            ffg_o[at, k * width : (k + 1) * width] = total.astype(BF)
            return carry

        lax.fori_loop(0, size // term_tile, keeping, 0)

    for copy in team_copies:
        copy.wait_recv()
    layer_o[...] = jnp.sum(lay_r[...].astype(F32), axis=0)
    grad_o[...] = jnp.sum(spa_r[...].astype(F32), axis=0)
    sums_o[...] = jnp.sum(sums_r[...], axis=0)
    for copy in keeps:
        copy.wait()
    for copy in every:
        copy.wait_send()


def feed_forward(sizes, rows, send_s, send_g, eup, edown, second, dgrad, ff, sel, cot, mix):
    two, groups, team = sizes
    slots = send_s.shape[1]
    width = second.shape[1]
    hid, ehid = second.shape[1] * ff.shape[3] // width, eup.shape[1]
    entries = 2 * groups * slots
    count = 2 * (groups - 1) * 2 + 2 * groups + 2 + 3 * (team - 1) + 2 + 2 * groups
    arrived = (two, groups, slots, width)
    anywhere = pl.BlockSpec(memory_space=pl.ANY)
    inside = pl.BlockSpec(memory_space=pltpu.VMEM)
    team_rows = team * rows
    return pl.pallas_call(
        functools.partial(feed_kernel, sizes, count),
        name="feed_forward",
        out_shape=(
            jax.ShapeDtypeStruct((rows, width), F32),
            jax.ShapeDtypeStruct((rows, width), F32),
            jax.ShapeDtypeStruct((rows, 128), F32),
            jax.ShapeDtypeStruct((entries, ehid), BF),
            jax.ShapeDtypeStruct((entries, ehid), BF),
            jax.ShapeDtypeStruct(arrived, BF),
            jax.ShapeDtypeStruct(arrived, BF),
            jax.ShapeDtypeStruct((hid // 2, 2 * width), BF),
        ),
        in_specs=[anywhere] * 10,
        out_specs=(inside, inside, inside, anywhere, anywhere, anywhere, anywhere, inside),
        scratch_shapes=[
            pltpu.VMEM((two, groups, slots, width), BF),
            pltpu.VMEM((two, groups, slots, width), BF),
            pltpu.VMEM(eup.shape, BF),
            pltpu.VMEM(edown.shape, BF),
            pltpu.VMEM(second.shape, BF),
            pltpu.VMEM(dgrad.shape, BF),
            pltpu.VMEM((width, hid), BF),
            pltpu.VMEM((hid, width), BF),
            pltpu.VMEM(sel.shape, BF),
            pltpu.VMEM(cot.shape, BF),
            pltpu.VMEM(mix.shape, F32),
            pltpu.VMEM((entries, ehid), F32),
            pltpu.VMEM((entries, ehid), BF),
            pltpu.VMEM((entries, ehid), BF),
            pltpu.VMEM((2, entries // 2, width), F32),
            pltpu.VMEM((2, entries // 2, width), BF),
            pltpu.VMEM((entries // 2, width), BF),
            pltpu.VMEM((entries // 2, width), BF),
            pltpu.VMEM((groups, slots, width), BF),
            pltpu.VMEM((groups, slots, width), BF),
            pltpu.VMEM((groups, slots, width), BF),
            pltpu.VMEM((groups, slots, width), BF),
            pltpu.VMEM((team_rows, hid), BF),
            pltpu.VMEM((team_rows, hid), BF),
            pltpu.VMEM((team_rows, width), F32),
            pltpu.VMEM((team_rows, width), F32),
            pltpu.VMEM((team, rows, width), BF),
            pltpu.VMEM((team, rows, width), BF),
            pltpu.VMEM((team, rows, 128), F32),
            pltpu.VMEM((team, rows, width), BF),
            pltpu.VMEM((team, rows, width), BF),
            pltpu.VMEM((team, rows, 128), F32),
            pltpu.VMEM((2, hid // 2, width), BF),
            pltpu.VMEM((2, hid // 2, width), BF),
            pltpu.SemaphoreType.DMA((count,)),
            pltpu.SemaphoreType.DMA((count,)),
            pltpu.SemaphoreType.DMA((9 + 2 * groups,)),
            pltpu.SemaphoreType.DMA((4,)),
        ],
        compiler_params=pltpu.CompilerParams(
            collective_id=5, has_side_effects=True, vmem_limit_bytes=60 * 2**20
        ),
        cost_estimate=pl.CostEstimate(
            flops=0, bytes_accessed=240_000_000, transcendentals=0
        ),
    )(send_s, send_g, eup, edown, second, dgrad, ff, sel, cot, mix)


def tall(chunk):
    rows, cols = chunk.shape[-2:]
    factor = 1
    while (rows * factor) % 16:
        factor *= 2
    return chunk.reshape(chunk.shape[:-2] + (rows * factor, cols // factor))


def per_device_general(
    tokens,
    cotangent,
    block_order,
    doc_lengths,
    routes,
    w_qkv,
    w_out,
    w_up,
    w_down,
    router,
    norm_gains,
    norm_biases,
    expert_up,
    expert_down,
):
    rows, width = tokens.shape[1], tokens.shape[2]
    ctx_count = lax.axis_size("ctx")
    two = lax.axis_size("dp")
    team = math.gcd(4, ctx_count)
    groups = ctx_count // team
    sizes = (two, groups, team)
    team_heads = HEADS // team
    reps = groups // team_heads
    length = rows * ctx_count
    group_rows = rows * team
    experts = ctx_count * expert_up.shape[0]
    capacity = max(2, 2 * rows // experts)
    block_rows = length // block_order.shape[0]
    hidden = w_up.shape[1]
    hidden_dev = w_down.shape[0]
    wr = w_qkv.shape[0]
    qkv_cols = 3 * width // team
    up_cols = hidden // team
    core = lax.axis_index("dp")
    ctx = lax.axis_index("ctx")
    group, member = lax.div(ctx, team), lax.rem(ctx, team)
    team_steps = [(0, 0, k) for k in range(1, team)]
    group_steps = [(0, k, 0) for k in range(1, groups)]
    by_group = [[g * team + t for g in range(groups)] for t in range(team)]
    by_team = [[g * team + t for t in range(team)] for g in range(groups)]
    swap = [(d, (d + 1) % two) for d in range(two)]

    small_flat = jnp.concatenate(
        [router.reshape(-1), norm_gains.reshape(-1), norm_biases.reshape(-1)]
    )
    small_size = -(-small_flat.shape[0] // 2048) * 2048
    small = jnp.pad(small_flat, (0, small_size - small_flat.shape[0])).astype(BF)
    small = small.reshape(-1, 128)

    qkv_first = tall(
        w_qkv.astype(BF).reshape(wr, 3, team, width // team).transpose(2, 0, 1, 3).reshape(
            team, wr, qkv_cols
        )
    )
    up_first = tall(
        w_up.reshape(wr, two * groups, team, hidden_dev)
        .transpose(2, 0, 1, 3)
        .reshape(team, wr, up_cols)
        .astype(BF)
    )
    down_first = tall(w_down.astype(BF).reshape(team, wr, width))
    out_first = tall(w_out.astype(BF))
    route_row = jnp.broadcast_to(routes[0, :, 0][None, :], (8, rows))

    def first(coords, ins, outs):
        c, g, t = coords
        moves, local = [], []
        for s in team_steps:
            to = lax.rem(t + s[2], team)
            moves.append(Move(s, ins[0], outs[0].at[t]))
            moves.append(Move(s, ins[1].at[to], outs[1].at[t]))
            moves.append(Move(s, ins[3], outs[3].at[t]))
            moves.append(Move(s, ins[4], outs[4].at[t]))
            moves.append(Move(s, ins[2].at[to], outs[2].at[0, t]))
        for s in group_steps:
            moves.append(Move(s, ins[5], outs[5].at[g]))
        local.append((ins[0], outs[0].at[t]))
        local.append((ins[1].at[t], outs[1].at[t]))
        local.append((ins[2].at[t], outs[2].at[0, t]))
        local.append((ins[3], outs[3].at[t]))
        local.append((ins[4], outs[4].at[t]))
        local.append((ins[5], outs[5].at[g]))
        local.append((ins[6], outs[2].at[1]))
        return local, moves

    token_rows, qkv_part, ff_part, small_part, route_all, out_part = exchange(
        "first",
        1,
        sizes,
        (tokens[0], qkv_first, up_first, small, route_row, out_first, down_first),
        [
            ((team, rows, width), BF),
            (qkv_first.shape, BF),
            ((2,) + up_first.shape, BF),
            ((team,) + small.shape, BF),
            ((team, 8, rows), jnp.int32),
            ((groups,) + out_first.shape, BF),
        ],
        first,
    )

    def second_build(coords, ins, outs):
        c, g, t = coords
        moves, local = [], []
        for k, s in enumerate(group_steps):
            moves.append(Move(s, ins[0], outs[0].at[c, g]))
            moves.append(Move(s, ins[1], outs[1].at[c, g]))
        for s in team_steps:
            moves.append(Move(s, ins[2], outs[2].at[t]))
        local.append((ins[0], outs[0].at[c, g]))
        local.append((ins[1], outs[1].at[c, g]))
        local.append((ins[2], outs[2].at[t]))
        other = (1, 0, 0)
        for n in range(2):
            moves.append(Move(other, ins[n], outs[n].at[c, g]))
        for k, s in enumerate(group_steps):
            source = lax.rem(g + groups - s[1], groups)
            for n in range(2):
                moves.append(
                    Move(other, outs[n].at[c, source], outs[n].at[c, source], after=2 * k + n)
                )
        return local, moves

    qkv_all, small_all, cot_rows = exchange(
        "second",
        2,
        sizes,
        (qkv_part, small_part, cotangent[0]),
        [
            ((two, groups) + qkv_part.shape, BF),
            ((two, groups) + small_part.shape, BF),
            ((team, rows, width), BF),
        ],
        second_build,
    )
    qkv_weight = qkv_all.reshape(width, qkv_cols)
    small_rows = small_all.reshape(two * ctx_count, -1)
    router_cols = router.shape[1]
    router_weight = jnp.pad(
        small_rows[:, : wr * router_cols].reshape(width, router_cols),
        ((0, 0), (0, 128 - router_cols)),
    )
    vectors = small_rows[:, wr * router_cols : small_flat.shape[0]].reshape(
        two * ctx_count, 4, wr
    )
    vectors = vectors.transpose(1, 0, 2).reshape(4, width).astype(F32)
    vectors = jnp.pad(vectors, ((4, 0), (0, 0)))

    ff_half = lax.all_gather(
        ff_part.reshape(2, team * wr, width),
        "ctx",
        axis=0,
        tiled=False,
        axis_index_groups=by_group,
    )

    def core_half(term):
        halves = term.reshape((two, term.shape[0] // two) + term.shape[1:])
        keep = lax.dynamic_index_in_dim(halves, core, 0, keepdims=False)
        give = lax.dynamic_index_in_dim(halves, 1 - core, 0, keepdims=False)
        return keep + lax.ppermute(give.astype(BF), "dp", swap).astype(F32)

    def over_groups(term):
        return lax.psum_scatter(
            term, "ctx", scatter_dimension=0, tiled=True, axis_index_groups=by_group
        )

    doc_id = jnp.arange(doc_lengths.shape[1], dtype=jnp.int32)
    doc_ends = jnp.sum(
        jnp.where(doc_id[:, None] <= doc_id[None, :], doc_lengths[0][:, None], 0), axis=0
    )
    all_rows = jnp.arange(length, dtype=jnp.int32)
    marks = (all_rows // block_rows)[:, None] == jnp.arange(
        block_order.shape[0], dtype=jnp.int32
    )[None, :]
    anchor = jnp.sum(jnp.where(marks, block_order[None, :], 0), axis=1)
    all_place = anchor * block_rows + all_rows % block_rows

    def low_of(place):
        return jnp.max(
            jnp.where(doc_ends[None, :] <= place[:, None], doc_ends[None, :], 0), axis=1
        )

    query_length = length // reps
    tiles = query_length // TILE
    part = lax.rem(group, reps)
    query_place = lax.dynamic_slice(all_place, (part * query_length,), (query_length,))
    lows = low_of(query_place)
    bounds = jnp.broadcast_to(jnp.array([[0, length // TILE]], dtype=jnp.int32), (tiles, 2))
    meta = jnp.concatenate(
        [query_place[None], lows[None], jnp.zeros((6, query_length), jnp.int32)], axis=0
    )

    token_rows = token_rows.reshape(group_rows, width)
    inputs = token_rows.astype(F32)
    normed_low = layer_norm(inputs, vectors[4], vectors[6]).astype(BF)
    mixed_t = lax.dot_general(
        qkv_weight, normed_low, (((0,), (1,)), ((), ())), preferred_element_type=F32
    ).astype(BF)
    mixed_t = mixed_t.reshape(3, team_heads, HEAD_DIM, group_rows)

    def spread_heads(coords, ins, outs):
        c, g, t = coords
        moves = [
            Move(s, ins[0].at[:, lax.div(lax.rem(g + s[1], groups), reps)], outs[0].at[g])
            for s in group_steps
        ]
        local = [(ins[0].at[:, lax.div(g, reps)], outs[0].at[g])]
        other = (1, 0, 0)
        moves.append(Move(other, ins[1], outs[1].at[c, :, t]))
        local.append((ins[1], outs[1].at[c, :, t]))
        first_team = len(moves)
        for s in team_steps:
            moves.append(Move(s, ins[1], outs[1].at[c, :, t]))
        for k, s in enumerate(team_steps):
            source = lax.rem(t + team - s[2], team)
            view = outs[1].at[c, :, source]
            moves.append(Move(other, view, view, after=first_team + k))
        return local, moves

    head_parts, out_weight = exchange(
        "heads",
        3,
        sizes,
        (mixed_t, out_part),
        [
            ((groups, 3, HEAD_DIM, group_rows), BF),
            ((two, groups, team) + out_first.shape, BF),
        ],
        spread_heads,
    )
    out_weight = out_weight.reshape(width, width)
    head_parts = head_parts.reshape(groups, 3 * HEAD_DIM, group_rows)
    place_col = all_place[:, None]
    head_t = head_parts.transpose(1, 0, 2).reshape(3 * HEAD_DIM, length)
    zeros = jnp.zeros((HEAD_DIM, query_length), BF)
    kv_t = head_t[HEAD_DIM:]
    kv_rows = kv_t.T
    q_t = lax.dynamic_slice(
        head_t[:HEAD_DIM], (0, part * query_length), (HEAD_DIM, query_length)
    )
    q_pad = jnp.concatenate([q_t * jnp.asarray(SCALE, BF), zeros], axis=0)
    attention_t, log_total = attend(False, bounds, meta, place_col, q_pad, kv_rows, kv_t)
    low_t = lax.dynamic_update_slice(
        jnp.zeros((HEAD_DIM, length), BF),
        attention_t.astype(BF),
        (0, part * query_length),
    )
    low_t = low_t.reshape(HEAD_DIM, groups, group_rows).transpose(1, 0, 2)

    def gather_heads(coords, ins, outs):
        c, g, t = coords
        moves = [
            Move(s, ins[0].at[lax.rem(g + s[1], groups)], outs[0].at[t, g]) for s in group_steps
        ]
        local = [(ins[0].at[g], outs[0].at[t, g])]
        for s in team_steps:
            moves.append(Move(s, ins[0].at[g], outs[0].at[t, g]))
        for k, s in enumerate(group_steps):
            source = lax.rem(g + groups - s[1], groups)
            for e in team_steps:
                moves.append(Move(e, outs[0].at[t, source], outs[0].at[t, source], after=k))
        return local, moves

    [attended] = exchange(
        "attended",
        4,
        sizes,
        (low_t,),
        [((team, groups, HEAD_DIM, group_rows), BF)],
        gather_heads,
    )
    if reps > 1:
        attended = lax.dynamic_index_in_dim(
            attended.reshape(team, team_heads, reps, HEAD_DIM, group_rows),
            lax.div(group, groups // reps),
            2,
            keepdims=False,
        )
    attended_t = attended.reshape(width, group_rows)

    slots = team * capacity
    (
        second_low,
        dense_grad,
        send_s,
        send_g,
        select,
        mixes,
        middle_own,
        prob_own,
        hot_own,
        second_own,
        attended_own,
    ) = between(
        experts,
        sizes,
        slots,
        member[None],
        attended_t,
        out_weight,
        token_rows,
        vectors,
        router_weight,
        route_all,
        cot_rows.reshape(group_rows, width),
    )
    (
        layer_sum,
        second_sum,
        sums_own,
        expert_active,
        hidden_grad,
        arrived_in,
        arrived_grad,
        ff_terms,
    ) = feed_forward(
        sizes,
        rows,
        send_s,
        send_g,
        expert_up[0],
        expert_down[0],
        second_low,
        dense_grad,
        ff_half,
        select,
        cot_rows.reshape(group_rows, width),
        mixes,
    )
    ff_sum = over_groups(ff_terms)
    down_sum = ff_sum[:, :width].astype(F32)
    up_sum = ff_sum[:, width:].reshape(team, wr, up_cols)
    entries = two * groups * slots
    expert_down_grad = row_sum(expert_active, arrived_grad.reshape(entries, width), TILE)
    expert_up_grad = row_sum(arrived_in.reshape(entries, width), hidden_grad, 128)

    layer_out, middle_grad, flow_t, out_term, small_t = turn(
        experts,
        layer_sum,
        second_sum,
        sums_own,
        middle_own,
        prob_own,
        hot_own,
        second_own,
        attended_own,
        cotangent[0],
        router_weight,
        out_weight,
        vectors,
    )
    flow_t = flow_t.reshape(team, team_heads, HEAD_DIM, rows)
    out_halves = out_term.reshape(two, groups, team, wr, width)

    def spread_flow(coords, ins, outs):
        c, g, t = coords
        moves = []
        for dg in range(groups):
            for dt in range(team):
                if dg or dt:
                    to_g, to_t = lax.rem(g + dg, groups), lax.rem(t + dt, team)
                    moves.append(
                        Move((0, dg, dt), ins[0].at[to_t, lax.div(to_g, reps)], outs[0].at[g, t])
                    )
        moves.append(Move((1, 0, 0), ins[1].at[lax.rem(c + 1, two)], outs[1]))
        return [(ins[0].at[t, lax.div(g, reps)], outs[0].at[g, t])], moves

    flow_parts, out_got = exchange(
        "flow",
        8,
        sizes,
        (flow_t, out_halves),
        [((groups, team, HEAD_DIM, rows), BF), (out_halves.shape[1:], BF)],
        spread_flow,
    )
    flow_all = flow_parts.transpose(2, 0, 1, 3).reshape(HEAD_DIM, length)
    flow_all = lax.dynamic_slice(
        flow_all, (0, part * query_length), (HEAD_DIM, query_length)
    )
    do_pad = jnp.concatenate([zeros, flow_all], axis=0)
    query_grad, pair_grad = attend_back(
        False,
        bounds,
        meta,
        place_col,
        q_pad,
        do_pad,
        attention_t,
        log_total,
        kv_rows,
        kv_t,
    )
    query_grad = lax.dynamic_update_slice(
        jnp.zeros((HEAD_DIM, length), BF), query_grad, (0, part * query_length)
    )
    grad_parts = jnp.concatenate([query_grad, pair_grad], axis=0)
    grad_parts = grad_parts.reshape(3, HEAD_DIM, groups, group_rows).transpose(2, 0, 1, 3)
    out_keep = lax.dynamic_index_in_dim(out_halves, core, 0, keepdims=False)
    out_parts = tall(
        (out_keep.astype(F32) + out_got.astype(F32))
        .astype(BF)
        .transpose(1, 0, 2, 3)
        .reshape(team, groups * wr, width)
    )

    def mixed_build(coords, ins, outs):
        c, g, t = coords
        moves = [
            Move(s, ins[0].at[lax.rem(g + s[1], groups)], outs[0].at[:, g])
            for s in group_steps
        ]
        moves += [
            Move(s, ins[1].at[lax.rem(t + s[2], team)], outs[1].at[t]) for s in team_steps
        ]
        return [(ins[0].at[g], outs[0].at[:, g]), (ins[1].at[t], outs[1].at[t])], moves

    grad_parts, out_parts = exchange(
        "mixed",
        9,
        sizes,
        (grad_parts, out_parts),
        [((3, groups, HEAD_DIM, group_rows), BF), (out_parts.shape, BF)],
        mixed_build,
    )
    out_parts = tall(
        jnp.sum(out_parts.astype(F32), axis=0).astype(BF).reshape(groups, wr, width)
    )
    if reps > 1:
        grad_parts = jnp.sum(
            grad_parts.reshape(3, team_heads, reps, HEAD_DIM, group_rows).astype(F32), axis=2
        ).astype(BF)
    mixed_grad_t = grad_parts.reshape(qkv_cols, group_rows)
    normed_part = (
        lax.dot_general(
            mixed_grad_t, qkv_weight, (((0,), (1,)), ((), ())), preferred_element_type=F32
        )
        .astype(BF)
        .reshape(team, rows, width)
    )
    qkv_term = lax.dot_general(
        normed_low, mixed_grad_t, (((0,), (1,)), ((), ())), preferred_element_type=F32
    )
    qkv_parts = core_half(qkv_term).astype(BF).reshape(groups, team * wr, qkv_cols)

    def normed_build(coords, ins, outs):
        c, g, t = coords
        moves, local = [], [(ins[2].at[t], outs[2].at[t])]
        for n in range(2):
            for s in group_steps:
                moves.append(Move(s, ins[n].at[lax.rem(g + s[1], groups)], outs[n].at[g]))
            local.append((ins[n].at[g], outs[n].at[g]))
        for s in team_steps:
            moves.append(Move(s, ins[2].at[lax.rem(t + s[2], team)], outs[2].at[t]))
        return local, moves

    qkv_parts, out_parts, normed_own = exchange(
        "normed",
        10,
        sizes,
        (qkv_parts, out_parts, normed_part),
        [(qkv_parts.shape, BF), (out_parts.shape, BF), (normed_part.shape, BF)],
        normed_build,
    )
    qkv_sum = (
        jnp.sum(qkv_parts.astype(F32), axis=0).astype(BF).reshape(team, wr, qkv_cols)
    )
    out_sum = jnp.sum(out_parts.astype(F32), axis=0).reshape(wr, width)
    normed_grad = jnp.sum(normed_own.astype(F32), axis=0)
    input_part_grad, gain_first, bias_first = jax.vjp(
        layer_norm, tokens[0].astype(F32), vectors[4], vectors[6]
    )[1](normed_grad)
    input_grad = middle_grad + input_part_grad

    small_used = small_t.shape[0]
    small_row = jnp.arange(small_used, dtype=jnp.int32)[:, None]
    small_t = jnp.where(
        small_row == experts + 2,
        gain_first[None],
        jnp.where(small_row == experts + 4, bias_first[None], small_t),
    )
    small_cols = small_used * wr
    small_pad = -(-small_cols // 1024) * 1024
    small_parts = jnp.pad(
        small_t.reshape(small_used, two * ctx_count, wr)
        .transpose(1, 0, 2)
        .reshape(two * ctx_count, small_cols),
        ((0, 0), (0, small_pad - small_cols)),
    ).reshape(two * ctx_count, small_pad // 128, 128)

    def owners_build(coords, ins, outs):
        c, g, t = coords
        moves, local = [], []
        for n in range(2):
            for s in team_steps:
                moves.append(Move(s, ins[n].at[lax.rem(t + s[2], team)], outs[n].at[t]))
            local.append((ins[n].at[t], outs[n].at[t]))
        me = c * ctx_count + g * team + t
        for dc in range(two):
            for dg in range(groups):
                for dt in range(team):
                    if dc or dg or dt:
                        to = (
                            lax.rem(c + dc, two) * ctx_count
                            + lax.rem(g + dg, groups) * team
                            + lax.rem(t + dt, team)
                        )
                        moves.append(Move((dc, dg, dt), ins[2].at[to], outs[2].at[me]))
        local.append((ins[2].at[me], outs[2].at[me]))
        return local, moves

    up_own, qkv_own, small_own = exchange(
        "owners",
        11,
        sizes,
        (tall(up_sum), tall(qkv_sum), small_parts),
        [
            (tall(up_sum).shape, BF),
            (tall(qkv_sum).shape, BF),
            (small_parts.shape, F32),
        ],
        owners_build,
    )
    small_sum = jnp.sum(small_own, axis=0).reshape(-1)[:small_cols].reshape(small_used, wr)
    up_own = (
        up_own.reshape(team, wr, two * groups, hidden_dev)
        .transpose(1, 2, 0, 3)
        .reshape(wr, hidden)
        .astype(F32)
    )
    qkv_own = (
        qkv_own.reshape(team, wr, 3, width // team)
        .transpose(1, 2, 0, 3)
        .reshape(wr, 3 * width)
        .astype(F32)
    )
    return (
        layer_out[None],
        input_grad[None].astype(BF),
        qkv_own,
        out_sum,
        up_own,
        down_sum,
        small_sum[:router_cols].T,
        small_sum[router_cols : router_cols + 2],
        small_sum[router_cols + 2 : router_cols + 4],
        expert_up_grad,
        expert_down_grad,
    )


def whole_kernel(sizes, experts, copies_count, *refs):
    two, groups, team = sizes
    (send_s, send_g, eup_h, edown_h, second_h, dgrad_h, ff_h, sel_h, cot_h, mix_h) = refs[:10]
    (middle_h, prob_h, hot_h, own_h, att_h, rw_h, wo_h, vec_h) = refs[10:18]
    (
        layer_o, middle_o, small_o, flow_o, out_o, down_o, up_o,
        active_o, hgrad_o, arr_s_o, arr_g_o,
    ) = refs[18:29]
    (
        arr_s, arr_g, eup, edown, second, dgrad, upw, downw, sel, cot, mix,
        slope, active, hgrad, acc, give, got_s, got_g, ret_s, ret_g, back_s, back_g,
        low, ugrad, dense, spart, lay, spa, sums, lay_r, spa_r, sums_r,
        term_give, term_got, ffg, ff_r,
        middle, prob, hot, own, att, rw, wo, vec, flow_t, flow_1,
        send_sem, recv_sem, load_sem, out_sem,
    ) = refs[29:]
    c = lax.axis_index("dp")
    i = lax.axis_index("ctx")
    g, t = lax.div(i, team), lax.rem(i, team)
    width = second.shape[1]
    rows = lay.shape[1]
    hid, ehid = upw.shape[1], eup.shape[1]
    core = lax.rem(c + 1, two)

    def device(step):
        dc, dg, dt = step
        return (
            lax.rem(c + dc, two),
            lax.rem(g + dg, groups) * team + lax.rem(t + dt, team),
        )

    index = [0]

    def remote(src, dst, step):
        k = index[0]
        index[0] += 1
        assert k < copies_count
        return pltpu.make_async_remote_copy(
            src_ref=src,
            dst_ref=dst,
            send_sem=send_sem.at[k],
            recv_sem=recv_sem.at[k],
            device_id=device(step),
            device_id_type=MESH,
        )

    group_steps = [(0, k, 0) for k in range(1, groups)]
    team_steps = [(0, 0, k) for k in range(1, team)]
    swap = (1, 0, 0)
    deep = ff_h.shape[2]

    def block_of(core, k):
        return pl.ds(pl.multiple_of((core * groups + k) * deep, deep), deep)

    loads = []
    for k, (src, dst) in enumerate(
        [
            (second_h, second), (dgrad_h, dgrad), (eup_h, eup), (edown_h, edown), (sel_h, sel), (cot_h, cot), (mix_h, mix),
            (send_s.at[g], arr_s.at[c, g]), (send_g.at[g], arr_g.at[c, g]),
            (middle_h, middle), (prob_h, prob), (hot_h, hot), (own_h, own),
            (att_h, att), (rw_h, rw), (wo_h, wo), (vec_h, vec),
        ]
        + [
            (ff_h.at[k, n], weight.at[block_of(c, k), :])
            for k in range(groups)
            for n, weight in enumerate((upw, downw))
        ]
    ):
        load = pltpu.make_async_copy(src, dst, load_sem.at[k])
        load.start()
        loads.append(load)

    barrier = pltpu.get_barrier_semaphore()
    greet = group_steps + team_steps + [swap]
    for step in greet:
        pl.semaphore_signal(barrier, inc=1, device_id=device(step), device_id_type=MESH)
    pl.semaphore_wait(barrier, len(greet))

    every = []

    def launch(copy):
        copy.start()
        every.append(copy)
        return copy

    def to_groups(src, dst):
        return [
            launch(remote(src.at[lax.rem(g + s[1], groups)], dst.at[g], s)) for s in group_steps
        ]

    def source(s):
        return lax.rem(g + groups - s[1], groups)

    swap_w = [
        launch(remote(ff_h.at[k, n], weight.at[block_of(c, k), :], swap))
        for k in range(groups)
        for n, weight in enumerate((upw, downw))
    ]
    out_s = [
        launch(remote(send_s.at[lax.rem(g + s[1], groups)], arr_s.at[c, g], s))
        for s in group_steps
    ]
    swap_s = [launch(remote(send_s.at[g], arr_s.at[c, g], swap))]
    out_g = [
        launch(remote(send_g.at[lax.rem(g + s[1], groups)], arr_g.at[c, g], s))
        for s in group_steps
    ]
    swap_g = [launch(remote(send_g.at[g], arr_g.at[c, g], swap))]

    for load in loads[:2] + loads[17:]:
        load.wait()
    for copy in swap_w:
        copy.wait_recv()

    def dense_in(h, carry):
        at = span(h, TILE)
        value, bend = gelu_and_slope(dot_f32(second[...], upw[:, at]))
        low[:, at] = value.astype(BF)
        ugrad[:, at] = (bend * contract_cols(dgrad[...], downw[at, :])).astype(BF)
        return carry

    lax.fori_loop(0, hid // TILE, dense_in, 0)

    def dense_out(n, carry):
        at = span(n, TILE)
        dense[:, at] = dot_f32(low[...], downw[:, at])
        spart[:, at] = contract_cols(ugrad[...], upw[at, :])
        return carry

    lax.fori_loop(0, width // TILE, dense_out, 0)

    half = hid // 2
    term_tile = 128

    def down_term(base, n):
        at = pl.ds(pl.multiple_of(base + n * term_tile, term_tile), term_tile)
        return contract_rows(low[:, at], dgrad[...])

    def up_term(base, n):
        at = pl.ds(pl.multiple_of(base + n * term_tile, term_tile), term_tile)
        return contract_rows(second[:, at], ugrad[...])

    terms = []
    for k, (term, size) in enumerate(((down_term, half), (up_term, width // 2))):

        def giving(n, carry, k=k, term=term, size=size):
            term_give[k, span(n, term_tile), :] = term(core * size, n).astype(BF)
            return carry

        lax.fori_loop(0, size // term_tile, giving, 0)
        terms.append(launch(remote(term_give.at[k], term_got.at[k], swap)))
    for k, (term, size) in enumerate(((down_term, half), (up_term, width // 2))):
        terms[k].wait_recv()

        def keeping(n, carry, k=k, term=term, size=size):
            at = span(n, term_tile)
            total = term(c * size, n) + term_got[k, at, :].astype(F32)
            ffg[k, at, :] = total.astype(BF)
            return carry

        lax.fori_loop(0, size // term_tile, keeping, 0)
    up_copy = pltpu.make_async_copy(ffg.at[1], up_o, out_sem.at[4])
    up_copy.start()

    for load in loads[2:17]:
        load.wait()
    for copy, s in zip(out_s, group_steps):
        copy.wait_recv()
        swap_s.append(launch(remote(arr_s.at[c, source(s)], arr_s.at[c, source(s)], swap)))
    for copy in swap_s:
        copy.wait_recv()
    entries = 2 * groups * arr_s.shape[2]

    def expert_in(h, carry):
        at = span(h, TILE)
        value, bend = gelu_and_slope(dot_f32(arr_s[...].reshape(entries, width), eup[:, at]))
        active[:, at] = value.astype(BF)
        slope[:, at] = bend
        return carry

    lax.fori_loop(0, ehid // TILE, expert_in, 0)
    keeps = [
        pltpu.make_async_copy(active, active_o, out_sem.at[0]),
        pltpu.make_async_copy(arr_s, arr_s_o, out_sem.at[1]),
    ]
    for copy in keeps:
        copy.start()

    def expert_out(n, carry):
        at = span(n, TILE)
        acc[:, :, at] = dot_f32(active[...], edown[:, at]).reshape(2, entries // 2, TILE)
        return carry

    lax.fori_loop(0, width // TILE, expert_out, 0)
    give[0] = acc[core].astype(BF)
    other_s = launch(remote(give.at[0], got_s, swap))

    for copy, s in zip(out_g, group_steps):
        copy.wait_recv()
        swap_g.append(launch(remote(arr_g.at[c, source(s)], arr_g.at[c, source(s)], swap)))
    other_s.wait_recv()
    ret_s[...] = (acc[c] + got_s[...].astype(F32)).astype(BF).reshape(ret_s.shape)
    home_s = to_groups(ret_s, back_s)
    back_s[g] = ret_s[g]
    for copy in swap_g:
        copy.wait_recv()

    def expert_back(h, carry):
        at = span(h, TILE)
        pull = contract_cols(arr_g[...].reshape(entries, width), edown[at, :])
        hgrad[:, at] = (slope[:, at] * pull).astype(BF)
        return carry

    lax.fori_loop(0, ehid // TILE, expert_back, 0)
    keeps += [
        pltpu.make_async_copy(hgrad, hgrad_o, out_sem.at[2]),
        pltpu.make_async_copy(arr_g, arr_g_o, out_sem.at[3]),
    ]
    for copy in keeps[2:]:
        copy.start()

    def expert_back_out(n, carry):
        at = span(n, TILE)
        acc[:, :, at] = contract_cols(hgrad[...], eup[at, :]).reshape(2, entries // 2, TILE)
        return carry

    lax.fori_loop(0, width // TILE, expert_back_out, 0)
    give[1] = acc[core].astype(BF)
    other_g = launch(remote(give.at[1], got_g, swap))
    other_g.wait_recv()
    ret_g[...] = (acc[c] + got_g[...].astype(F32)).astype(BF).reshape(ret_g.shape)
    home_g = to_groups(ret_g, back_g)
    back_g[g] = ret_g[g]

    for copy in home_s:
        copy.wait_recv()
    slots = groups * back_s.shape[1]
    lane = lax.broadcasted_iota(jnp.int32, (rows, 128), 1)

    def join_layer(r, carry):
        at = span(r, rows)
        found = dot_f32(sel[at, :], back_s[...].reshape(slots, width))
        own = dense[at, :]
        flow = cot[at, :].astype(F32)
        mixes = mix[at, :]
        lay[r] = (mixes[:, 0:1] * own + mixes[:, 1:2] * found).astype(BF)
        plain = jnp.sum(flow * own, axis=1, keepdims=True)
        routed = jnp.sum(flow * found, axis=1, keepdims=True)
        sums[r] = jnp.where(lane == 0, plain, jnp.where(lane == 1, routed, 0.0))
        return carry

    lax.fori_loop(0, team, join_layer, 0)

    def to_team(src, dst):
        made = [launch(remote(src.at[lax.rem(t + s[2], team)], dst.at[t], s)) for s in team_steps]
        dst[t] = src[t]
        return made

    team_copies = to_team(lay, lay_r) + to_team(sums, sums_r)

    for copy in home_g:
        copy.wait_recv()
    piece = half // groups
    downs = [
        launch(remote(ffg.at[0, span(lax.rem(g + s[1], groups), piece), :], ff_r.at[g], s))
        for s in group_steps
    ]
    ff_r[g] = ffg[0, span(g, piece), :]

    def join_grad(r, carry):
        at = span(r, rows)
        found = dot_f32(sel[at, :], back_g[...].reshape(slots, width))
        spa[r] = (spart[at, :] + found).astype(BF)
        return carry

    lax.fori_loop(0, team, join_grad, 0)
    team_copies += to_team(spa, spa_r)

    for copy in team_copies:
        copy.wait_recv()

    sum_own = jnp.sum(sums_r[...], axis=0)
    layer_o[...] = (middle[...] + jnp.sum(lay_r[...].astype(F32), axis=0)).astype(BF)
    chances, chosen = prob[...], hot[...]
    s0, s1 = sum_own[:, 0:1], sum_own[:, 1:2]
    mix1 = jnp.sum(jnp.where(lane == experts + 1, chances, 0.0), axis=1, keepdims=True)
    gate = jnp.sum(chances * chosen, axis=1, keepdims=True)
    pulls = jnp.where(lane == experts, s0, jnp.where(lane == experts + 1, s1 * gate, 0.0))
    mean_pull = jnp.sum(chances * pulls, axis=1, keepdims=True)
    logit_grad = chances * jnp.where(
        lane < experts, (s1 * mix1) * (chosen - gate), pulls - mean_pull
    )
    logit_grad = jnp.where(lane < experts + 2, logit_grad, 0.0).astype(BF)
    second_grad = jnp.sum(spa_r[...].astype(F32), axis=0) + contract_cols(logit_grad, rw[...])
    hat, scale = normalize(middle[...])
    pull = second_grad * vec[5:6, :]
    moved = scale * (
        pull
        - jnp.mean(pull, axis=-1, keepdims=True)
        - hat * jnp.mean(pull * hat, axis=-1, keepdims=True)
    )
    middle_grad = cot[span(t, rows), :].astype(F32) + moved
    middle_o[...] = middle_grad
    branch = middle_grad.astype(BF)

    for n in range(team):
        at = slice(n * (width // team), (n + 1) * (width // team))
        flow_t[n] = contract_cols(wo[at, :], branch).astype(BF).reshape(flow_t.shape[1:])
    flowed = [
        launch(remote(flow_t.at[lax.rem(t + s[2], team)], flow_1.at[t], s)) for s in team_steps
    ]
    flow_1[t] = flow_t[t]

    def out_term(base, n):
        at = pl.ds(pl.multiple_of(base + n * term_tile, term_tile), term_tile)
        return dot_f32(att[at, :], branch)

    def out_giving(n, carry):
        term_give[0, span(n, term_tile), :] = out_term(core * (width // 2), n).astype(BF)
        return carry

    terms[0].wait_send()
    every[:] = [copy for copy in every if copy is not terms[0]]
    lax.fori_loop(0, width // 2 // term_tile, out_giving, 0)
    out_cross = launch(remote(term_give.at[0], term_got.at[0], swap))
    for copy in flowed:
        copy.wait_recv()
    flowed = [
        launch(remote(flow_1.at[:, lax.rem(g + s[1], groups)], flow_o.at[g], s))
        for s in group_steps
    ]
    own_flow = pltpu.make_async_copy(flow_1.at[:, g], flow_o.at[g], out_sem.at[5])
    own_flow.start()
    out_cross.wait_recv()
    wr = out_o.shape[2]

    def out_keeping(n, carry):
        at = span(n, term_tile)
        total = out_term(c * (width // 2), n) + term_got[0, at, :].astype(F32)
        out_o[:, n] = total.astype(BF).reshape(team, wr, width)
        return carry

    lax.fori_loop(0, groups, out_keeping, 0)

    routed = contract_rows(logit_grad, own[...])[: small_o.shape[0], :]
    which = lax.broadcasted_iota(jnp.int32, routed.shape, 0)
    gain = jnp.sum(second_grad * hat, axis=0, keepdims=True)
    bias = jnp.sum(second_grad, axis=0, keepdims=True)
    small_o[...] = jnp.where(
        which == experts + 3, gain, jnp.where(which == experts + 5, bias, routed)
    )
    for copy in downs:
        copy.wait_recv()
    down_o[...] = jnp.sum(ff_r[...].astype(F32), axis=0)
    for copy in flowed:
        copy.wait_recv()
    for copy in keeps + [up_copy, own_flow]:
        copy.wait()
    for copy in every:
        copy.wait_send()


def whole(
    sizes, rows, experts, wr, send_s, send_g, eup, edown, second, dgrad, ff, sel, cot, mix,
    middle, prob, hot, own, att, rw, wo, vec,
):
    two, groups, team = sizes
    slots = send_s.shape[1]
    width = second.shape[1]
    hid, ehid = ff.shape[3], eup.shape[1]
    entries = 2 * groups * slots
    used = -(-(experts + 6) // 8) * 8
    count = 6 * (groups - 1) + 2 * groups + 5 + 5 * (team - 1) + 2 * groups
    arrived = (two, groups, slots, width)
    anywhere = pl.BlockSpec(memory_space=pl.ANY)
    inside = pl.BlockSpec(memory_space=pltpu.VMEM)
    team_rows = team * rows
    heads = (groups, HEAD_DIM, rows)
    shapes = (
        ((rows, width), BF),
        ((rows, width), F32),
        ((used, width), F32),
        ((groups, team, HEAD_DIM, rows), BF),
        ((team, groups, wr, width), BF),
        ((hid // 2 // groups, width), F32),
        ((width // 2, hid), BF),
        ((entries, ehid), BF),
        ((entries, ehid), BF),
        (arrived, BF),
        (arrived, BF),
    )
    scratch = (
        (arrived, BF), (arrived, BF), (eup.shape, BF), (edown.shape, BF), (second.shape, BF),
        (dgrad.shape, BF), ((width, hid), BF), ((hid, width), BF), (sel.shape, BF),
        (cot.shape, BF), (mix.shape, F32),
        ((entries, ehid), F32), ((entries, ehid), BF), ((entries, ehid), BF),
        ((2, entries // 2, width), F32), ((2, entries // 2, width), BF),
        ((entries // 2, width), BF), ((entries // 2, width), BF),
        ((groups, slots, width), BF), ((groups, slots, width), BF),
        ((groups, slots, width), BF), ((groups, slots, width), BF),
        ((team_rows, hid), BF), ((team_rows, hid), BF), ((team_rows, width), F32),
        ((team_rows, width), F32), ((team, rows, width), BF), ((team, rows, width), BF),
        ((team, rows, 128), F32), ((team, rows, width), BF), ((team, rows, width), BF),
        ((team, rows, 128), F32),
        ((2, hid // 2, width), BF), ((2, hid // 2, width), BF), ((2, hid // 2, width), BF),
        ((groups, hid // 2 // groups, width), BF),
        (middle.shape, F32), (prob.shape, F32), (hot.shape, F32), (own.shape, BF),
        (att.shape, BF), (rw.shape, BF), (wo.shape, BF), (vec.shape, F32),
        ((team,) + heads, BF), ((team,) + heads, BF),
    )
    return pl.pallas_call(
        functools.partial(whole_kernel, sizes, experts, count),
        name="feed_forward",
        out_shape=tuple(jax.ShapeDtypeStruct(s, d) for s, d in shapes),
        in_specs=[anywhere] * 18,
        out_specs=tuple(inside if n in (0, 1, 2, 4, 5) else anywhere for n in range(11)),
        scratch_shapes=[pltpu.VMEM(s, d) for s, d in scratch]
        + [
            pltpu.SemaphoreType.DMA((count,)),
            pltpu.SemaphoreType.DMA((count,)),
            pltpu.SemaphoreType.DMA((17 + 2 * groups,)),
            pltpu.SemaphoreType.DMA((6,)),
        ],
        compiler_params=pltpu.CompilerParams(
            collective_id=14, has_side_effects=True, vmem_limit_bytes=60 * 2**20
        ),
        cost_estimate=pl.CostEstimate(flops=0, bytes_accessed=300_000_000, transcendentals=0),
    )(
        send_s, send_g, eup, edown, second, dgrad, ff, sel, cot, mix,
        middle, prob, hot, own, att, rw, wo, vec,
    )


def deliver_kernel(experts, count, shift, small, *refs):
    ins, outs = refs[:count], refs[count : 2 * count]
    router, vectors = refs[2 * count : 2 * count + 2]
    sem = refs[2 * count + 2]
    copies = [pltpu.make_async_copy(a, b, sem.at[n]) for n, (a, b) in enumerate(zip(ins, outs))]
    for copy in copies:
        copy.start()
    wr = router.shape[1]
    mine = pltpu.roll(small[...], lax.rem(128 - shift[0], 128), 1)[:, :wr]
    router[...] = mine[: experts + 2, :]
    vectors[...] = mine[experts + 2 : experts + 6, :]
    for copy in copies:
        copy.wait()


def deliver(experts, shift, small, arrays):
    wr = arrays[2].shape[0]
    anywhere = pl.BlockSpec(memory_space=pl.ANY)
    inside = pl.BlockSpec(memory_space=pltpu.VMEM)
    count = len(arrays)
    return pl.pallas_call(
        functools.partial(deliver_kernel, experts, count),
        name="deliver",
        in_specs=[pl.BlockSpec(memory_space=pltpu.SMEM)] + [inside] * (count + 1),
        out_specs=tuple([anywhere] * count + [inside] * 2),
        out_shape=tuple(jax.ShapeDtypeStruct(a.shape, a.dtype) for a in arrays)
        + (
            jax.ShapeDtypeStruct((experts + 2, wr), F32),
            jax.ShapeDtypeStruct((4, wr), F32),
        ),
        scratch_shapes=[pltpu.SemaphoreType.DMA((count,))],
        compiler_params=pltpu.CompilerParams(vmem_limit_bytes=60 * 2**20),
    )(shift, small, *arrays)


def per_device(
    tokens,
    cotangent,
    block_order,
    doc_lengths,
    routes,
    w_qkv,
    w_out,
    w_up,
    w_down,
    router,
    norm_gains,
    norm_biases,
    expert_up,
    expert_down,
):
    rows, width = tokens.shape[1], tokens.shape[2]
    ctx_count = lax.axis_size("ctx")
    two = lax.axis_size("dp")
    team = math.gcd(4, ctx_count)
    groups = ctx_count // team
    sizes = (two, groups, team)
    length = rows * ctx_count
    wr = w_qkv.shape[0]
    experts = ctx_count * expert_up.shape[0]
    fits = groups * team == HEADS and team * wr == 128 and w_up.shape[1] == team * width
    if not fits or length // block_order.shape[0] != BLOCK:
        return per_device_general(
            tokens, cotangent, block_order, doc_lengths, routes, w_qkv, w_out, w_up, w_down,
            router, norm_gains, norm_biases, expert_up, expert_down,
        )
    group_rows = rows * team
    capacity = max(2, 2 * rows // experts)
    slots = team * capacity
    hidden = w_up.shape[1]
    hidden_dev = w_down.shape[0]
    qkv_cols = 3 * width // team
    up_cols = hidden // team
    ctx = lax.axis_index("ctx")
    core = lax.axis_index("dp")
    group, member = lax.div(ctx, team), lax.rem(ctx, team)
    by_group = [[g * team + t for g in range(groups)] for t in range(team)]
    team_steps = [(0, 0, k) for k in range(1, team)]

    router_cols = router.shape[1]
    (
        token_rows,
        cot_rows,
        head_parts,
        normed,
        weights,
        vectors,
        out_weight,
        ff_part,
        route_all,
    ) = start(
        sizes,
        tokens[0],
        cotangent[0],
        w_qkv,
        w_up,
        w_down,
        w_out,
        router.T,
        norm_gains,
        norm_biases,
        routes[0].reshape(1, rows),
    )
    router_weight = weights[:, :, :, :, qkv_cols:].reshape(width, 128)
    out_weight = out_weight.reshape(width, width)
    token_rows = token_rows.reshape(group_rows, width)
    cot_rows = cot_rows.reshape(group_rows, width)

    ff_half = lax.all_gather(
        ff_part.reshape(2, team * wr, width),
        "ctx",
        axis=0,
        tiled=False,
        axis_index_groups=by_group,
    )
    low_t, attention_t, log_total, q_pad, kv_t, kv_rows = sorted_attend(
        doc_lengths[0], block_order, head_parts.reshape(groups, 3 * HEAD_DIM, group_rows)
    )

    def gather_heads(coords, ins, outs):
        c, g, t = coords
        steps = [(0, k, 0) for k in range(1, groups)]
        moves = [Move(s, ins[0].at[lax.rem(g + s[1], groups)], outs[0].at[t, g]) for s in steps]
        local = [(ins[0].at[g], outs[0].at[t, g])]
        for s in team_steps:
            moves.append(Move(s, ins[0].at[g], outs[0].at[t, g]))
        for k, s in enumerate(steps):
            source = lax.rem(g + groups - s[1], groups)
            for e in team_steps:
                moves.append(Move(e, outs[0].at[t, source], outs[0].at[t, source], after=k))
        return local, moves

    [attended] = exchange(
        "attended",
        4,
        sizes,
        (low_t,),
        [((team, groups, HEAD_DIM, group_rows), BF)],
        gather_heads,
    )
    (
        second_low,
        dense_grad,
        send_s,
        send_g,
        select,
        mixes,
        middle_own,
        prob_own,
        hot_own,
        second_own,
        attended_own,
    ) = between(
        experts,
        sizes,
        slots,
        member[None],
        attended.reshape(width, group_rows),
        out_weight,
        token_rows,
        vectors,
        router_weight,
        route_all,
        cot_rows,
    )
    (
        layer_out,
        middle_grad,
        small_t,
        flow_parts,
        out_half,
        down_sum,
        up_half,
        expert_active,
        hidden_grad,
        arrived_in,
        arrived_grad,
    ) = whole(
        sizes,
        rows,
        experts,
        wr,
        send_s,
        send_g,
        expert_up[0],
        expert_down[0],
        second_low,
        dense_grad,
        ff_half,
        select,
        cot_rows,
        mixes,
        middle_own,
        prob_own,
        hot_own,
        second_own,
        attended_own,
        router_weight,
        out_weight,
        vectors,
    )

    def pieces_of(array, along):
        count = groups if along == "g" else team
        me = group if along == "g" else member
        found = [lax.dynamic_index_in_dim(array, me, 0, keepdims=False)]
        for step in range(1, count):
            if along == "g":
                pairs = [
                    (g * team + t, (g + step) % groups * team + t)
                    for g in range(groups)
                    for t in range(team)
                ]
            else:
                pairs = [
                    (g * team + t, g * team + (t + step) % team)
                    for g in range(groups)
                    for t in range(team)
                ]
            chunk = lax.dynamic_index_in_dim(array, lax.rem(me + step, count), 0, keepdims=False)
            found.append(lax.ppermute(chunk, "ctx", pairs))
        return found

    up_sum = lax.psum_scatter(
        up_half, "ctx", scatter_dimension=0, tiled=True, axis_index_groups=by_group
    ).reshape(team, wr, up_cols)
    out_pieces = pieces_of(out_half, "t")
    grad_parts = sorted_back(
        doc_lengths[0],
        block_order,
        flow_parts.reshape(ctx_count, HEAD_DIM, rows),
        attention_t,
        log_total,
        q_pad,
        kv_t,
        kv_rows,
        groups,
    )

    grad_parts, expert_active, hidden_grad = lax.optimization_barrier(
        (grad_parts, expert_active, hidden_grad)
    )

    pieces = pieces_of(grad_parts, "g")
    out_sum = sum(piece.astype(F32) for piece in out_pieces).astype(BF)
    entries = two * groups * slots
    expert_down_grad = row_sum(expert_active, arrived_grad.reshape(entries, width), TILE)
    expert_up_grad = row_sum(arrived_in.reshape(entries, width), hidden_grad, 128)
    input_grad, qkv_own, up_own, out_own, small_own = end(
        sizes,
        experts,
        pieces,
        weights,
        normed,
        tokens[0],
        vectors,
        middle_grad,
        small_t,
        up_sum,
        out_sum,
    )
    delivered = deliver(
        experts,
        member[None] * wr,
        small_own,
        (layer_out, input_grad, qkv_own, out_own, up_own, down_sum),
    )
    layer_out, input_grad, qkv_own, out_own, up_own, down_sum, router_own, vectors_own = delivered
    return (
        layer_out[None],
        input_grad[None],
        qkv_own,
        out_own,
        up_own,
        down_sum,
        router_own.T,
        vectors_own[:2],
        vectors_own[2:],
        expert_up_grad,
        expert_down_grad,
    )


def solution(mesh):
    in_specs = (
        P("dp", "ctx", None),
        P("dp", "ctx", None),
        P(),
        P("dp", None),
        P("dp", "ctx", None),
        P(("dp", "ctx"), None),
        P(("dp", "ctx"), None),
        P(("dp", "ctx"), None),
        P(("dp", "ctx"), None),
        P(("dp", "ctx"), None),
        P(None, ("dp", "ctx")),
        P(None, ("dp", "ctx")),
        P("ctx", None, "dp"),
        P("ctx", "dp", None),
    )
    out_specs = (
        P("dp", "ctx", None),
        P("dp", "ctx", None),
        P(("dp", "ctx"), None),
        P(("dp", "ctx"), None),
        P(("dp", "ctx"), None),
        P(("dp", "ctx"), None),
        P(("dp", "ctx"), None),
        P(None, ("dp", "ctx")),
        P(None, ("dp", "ctx")),
        P("ctx", None, "dp"),
        P("ctx", "dp", None),
    )
    return jax.shard_map(
        per_device, mesh=mesh, in_specs=in_specs, out_specs=out_specs, check_vma=False
    )
```

```python
import functools
import math

import jax
import jax.numpy as jnp
from jax import lax
from jax.experimental import pallas as pl
from jax.experimental.pallas import tpu as pltpu
from jax.sharding import PartitionSpec as P

HEADS = 16
HEAD_DIM = 64

EPS = 1e-05
NEG = -1e30
SCALE = 0.125
TILE = 256
BF = jnp.bfloat16
F32 = jnp.float32
MESH = pl.DeviceIdType.MESH


def layer_norm(values, gain, shift):
    center = values - jnp.mean(values, axis=-1, keepdims=True)
    spread = jnp.mean(center * center, axis=-1, keepdims=True)
    return center * lax.rsqrt(spread + EPS) * gain + shift


def gelu_tanh(values):
    return jax.nn.gelu(values, approximate=True)


def router_heads(router_logits, route_hot, experts):
    chances = jax.nn.softmax(router_logits[:, :experts], axis=-1)
    gate = jnp.sum(chances * route_hot, axis=-1)
    mixing = jax.nn.softmax(router_logits[:, experts:], axis=-1)
    return (gate, mixing[:, 0], mixing[:, 1])


def dot_f32(left, right):
    return jnp.dot(left, right, preferred_element_type=F32)


def contract_rows(left, right):
    return lax.dot_general(left, right, (((0,), (0,)), ((), ())), preferred_element_type=F32)


def contract_cols(left, right):
    return lax.dot_general(left, right, (((1,), (1,)), ((), ())), preferred_element_type=F32)


def span(i, size):
    return pl.ds(pl.multiple_of(i * size, size), size)


class Move:
    def __init__(self, step, src, dst, after=None):
        self.step, self.src, self.dst, self.after = step, src, dst, after


def exchange(name, cid, sizes, ins, outs, build, micros=20):
    two, groups, team = sizes

    def kernel(*refs):
        in_refs, out_refs = refs[: len(ins)], refs[len(ins) : len(ins) + len(outs)]
        send_sem, recv_sem, local_sem = refs[len(ins) + len(outs) :]
        c = lax.axis_index("dp")
        i = lax.axis_index("ctx")
        g, t = lax.div(i, team), lax.rem(i, team)

        def device(step):
            dc, dg, dt = step
            return (
                lax.rem(c + dc, two),
                lax.rem(g + dg, groups) * team + lax.rem(t + dt, team),
            )

        locals_, moves = build((c, g, t), in_refs, out_refs)
        steps = sorted({m.step for m in moves})
        greet = sorted(
            set(steps) | {((-a) % two, (-b) % groups, (-d) % team) for a, b, d in steps}
        )
        barrier = pltpu.get_barrier_semaphore()
        for step in greet:
            pl.semaphore_signal(barrier, inc=1, device_id=device(step), device_id_type=MESH)
        pl.semaphore_wait(barrier, len(greet))

        copies = {}
        arrived = set()
        for k, (src, dst) in enumerate(locals_):
            copies[("local", k)] = pltpu.make_async_copy(src, dst, local_sem.at[k])
        for k, m in enumerate(moves):
            copies[k] = pltpu.make_async_remote_copy(
                src_ref=m.src,
                dst_ref=m.dst,
                send_sem=send_sem.at[k],
                recv_sem=recv_sem.at[k],
                device_id=device(m.step),
                device_id_type=MESH,
            )
        for k, m in enumerate(moves):
            if m.after is None:
                copies[k].start()
        for k in range(len(locals_)):
            copies[("local", k)].start()
        for k, m in enumerate(moves):
            if m.after is not None:
                if m.after not in arrived:
                    arrived.add(m.after)
                    if isinstance(m.after, tuple):
                        copies[m.after].wait()
                    else:
                        copies[m.after].wait_recv()
                copies[k].start()
        for k in range(len(locals_)):
            if ("local", k) not in arrived:
                copies[("local", k)].wait()
        for k in range(len(moves)):
            if k not in arrived:
                copies[k].wait_recv()
        for k in range(len(moves)):
            copies[k].wait_send()

    count = []

    def trace_counts():
        class Probe:
            def __getattr__(self, name):
                return self

            def __getitem__(self, index):
                return self

        locals_, moves = build((0, 0, 0), [Probe() for _ in ins], [Probe() for _ in outs])
        count.extend((len(locals_), len(moves)))

    trace_counts()
    return pl.pallas_call(
        kernel,
        name=name,
        out_shape=tuple(jax.ShapeDtypeStruct(s, d) for s, d in outs),
        in_specs=[pl.BlockSpec(memory_space=pl.ANY)] * len(ins),
        out_specs=tuple(pl.BlockSpec(memory_space=pl.ANY) for _ in outs),
        scratch_shapes=[
            pltpu.SemaphoreType.DMA((max(1, count[1]),)),
            pltpu.SemaphoreType.DMA((max(1, count[1]),)),
            pltpu.SemaphoreType.DMA((max(1, count[0]),)),
        ],
        compiler_params=pltpu.CompilerParams(collective_id=cid, has_side_effects=True),
        cost_estimate=pl.CostEstimate(
            flops=0, bytes_accessed=int(micros * 3.0e6), transcendentals=0
        ),
    )(*ins)


def mask_of(kt, key_place, query_place, query_low):
    return (key_place <= query_place) & (key_place >= query_low)


def key_places(sorted_rows, kt, place_ref):
    if sorted_rows:
        return lax.broadcasted_iota(jnp.int32, (TILE, TILE), 0) + kt * TILE
    return place_ref[pl.ds(pl.multiple_of(kt * TILE, TILE), TILE), :]


def attend_kernel(
    sorted_rows, bounds, meta_ref, place_ref, q_ref, rows_ref, kvt_ref, out_ref, lse_ref
):
    step = pl.program_id(0)
    queries = q_ref[...]
    place, low = meta_ref[0:1, :], meta_ref[1:2, :]

    def body(kt, carry):
        peak, total, acc = carry
        at = pl.ds(pl.multiple_of(kt * TILE, TILE), TILE)
        scores = dot_f32(rows_ref[at, :], queries)
        allowed = mask_of(kt, key_places(sorted_rows, kt, place_ref), place, low)
        scores = jnp.where(allowed, scores, NEG)
        new_peak = jnp.maximum(peak, jnp.max(scores, axis=0, keepdims=True))
        weights = jnp.exp(scores - new_peak)
        fade = jnp.exp(peak - new_peak)
        total = total * fade + jnp.sum(weights, axis=0, keepdims=True)
        acc = acc * fade + dot_f32(kvt_ref[HEAD_DIM:, at], weights.astype(BF))
        return new_peak, total, acc

    start = (
        jnp.full((1, TILE), NEG, F32),
        jnp.zeros((1, TILE), F32),
        jnp.zeros((HEAD_DIM, TILE), F32),
    )
    peak, total, acc = lax.fori_loop(bounds[step, 0], bounds[step, 1], body, start)
    out_ref[...] = acc / total
    lse_ref[...] = peak + jnp.log(total)


def attend_back_kernel(
    sorted_rows,
    tiles,
    bounds,
    meta_ref,
    place_ref,
    q_ref,
    do_ref,
    out_ref,
    lse_ref,
    rows_ref,
    kvt_ref,
    dq_ref,
    dkv_ref,
    acc_ref,
):
    step = pl.program_id(0)

    @pl.when(step == 0)
    def _():
        acc_ref[...] = jnp.zeros_like(acc_ref)

    queries, flows = q_ref[...], do_ref[...]
    place, low = meta_ref[0:1, :], meta_ref[1:2, :]
    log_total = lse_ref[...]
    delta = jnp.sum(flows[HEAD_DIM:, :].astype(F32) * out_ref[...], axis=0, keepdims=True)

    def body(kt, dq):
        at = pl.ds(pl.multiple_of(kt * TILE, TILE), TILE)
        rows = rows_ref[at, :]
        scores = dot_f32(rows, queries)
        allowed = mask_of(kt, key_places(sorted_rows, kt, place_ref), place, low)
        chances = jnp.exp(jnp.where(allowed, scores - log_total, NEG))
        flow = dot_f32(rows, flows)
        score_grad = (chances * (flow - delta)).astype(BF)
        dq = dq + dot_f32(kvt_ref[:HEAD_DIM, at], score_grad)
        acc_ref[:HEAD_DIM, at] += contract_cols(queries[:HEAD_DIM, :], score_grad)
        acc_ref[HEAD_DIM:, at] += contract_cols(flows[HEAD_DIM:, :], chances.astype(BF))
        return dq

    dq = lax.fori_loop(
        bounds[step, 0], bounds[step, 1], body, jnp.zeros((HEAD_DIM, TILE), F32)
    )
    dq_ref[...] = (dq * SCALE).astype(BF)

    @pl.when(step == tiles - 1)
    def _():
        dkv_ref[...] = acc_ref[...].astype(BF)


def attention_specs(length, query_length):
    def whole(shape):
        return pl.BlockSpec(shape, lambda i: (0, 0))

    def tile(rows):
        return pl.BlockSpec((rows, TILE), lambda i: (0, i))

    return whole, tile


def attend(sorted_rows, bounds, meta, place_col, q_pad, kv_rows, kv_t):
    length, query_length = kv_rows.shape[0], q_pad.shape[1]
    whole, tile = attention_specs(length, query_length)
    return pl.pallas_call(
        functools.partial(attend_kernel, sorted_rows),
        name="attend",
        grid=(query_length // TILE,),
        in_specs=[
            pl.BlockSpec(memory_space=pltpu.SMEM),
            tile(8),
            whole(place_col.shape),
            tile(2 * HEAD_DIM),
            whole((length, 2 * HEAD_DIM)),
            whole((2 * HEAD_DIM, length)),
        ],
        out_specs=(tile(HEAD_DIM), tile(1)),
        out_shape=(
            jax.ShapeDtypeStruct((HEAD_DIM, query_length), F32),
            jax.ShapeDtypeStruct((1, query_length), F32),
        ),
        compiler_params=pltpu.CompilerParams(vmem_limit_bytes=40 * 2**20),
    )(bounds, meta, place_col, q_pad, kv_rows, kv_t)


def attend_back(sorted_rows, bounds, meta, place_col, q_pad, do_pad, out, lse, kv_rows, kv_t):
    length, query_length = kv_rows.shape[0], q_pad.shape[1]
    whole, tile = attention_specs(length, query_length)
    return pl.pallas_call(
        functools.partial(attend_back_kernel, sorted_rows, query_length // TILE),
        name="attend_back",
        grid=(query_length // TILE,),
        in_specs=[
            pl.BlockSpec(memory_space=pltpu.SMEM),
            tile(8),
            whole(place_col.shape),
            tile(2 * HEAD_DIM),
            tile(2 * HEAD_DIM),
            tile(HEAD_DIM),
            tile(1),
            whole((length, 2 * HEAD_DIM)),
            whole((2 * HEAD_DIM, length)),
        ],
        out_specs=(tile(HEAD_DIM), whole((2 * HEAD_DIM, length))),
        out_shape=(
            jax.ShapeDtypeStruct((HEAD_DIM, query_length), BF),
            jax.ShapeDtypeStruct((2 * HEAD_DIM, length), BF),
        ),
        scratch_shapes=[pltpu.VMEM((2 * HEAD_DIM, length), F32)],
        compiler_params=pltpu.CompilerParams(vmem_limit_bytes=40 * 2**20),
    )(bounds, meta, place_col, q_pad, do_pad, out, lse, kv_rows, kv_t)


BLOCK = 64


def pick_pair(load, table, d):
    first, second = table[2 * d], table[2 * d + 1]
    left = load(lax.div(first, 2))
    right = load(lax.div(second, 2))
    lane = lax.broadcasted_iota(jnp.int32, left.shape, 1)
    left = jnp.where(lax.rem(first, 2) == 0, left, pltpu.roll(left, BLOCK, 1))
    right = jnp.where(lax.rem(second, 2) == 1, right, pltpu.roll(right, BLOCK, 1))
    return jnp.where(lane < BLOCK, left, right)


def column_block(ref, k, per):
    return ref[lax.div(k, per), :, span(lax.rem(k, per), 128)].astype(F32)


def fill_inverse(order, inverse, count):
    def put(n, carry):
        inverse[order[n]] = n
        return carry

    lax.fori_loop(0, count, put, 0)


def query_lows(lengths, step):
    place = lax.broadcasted_iota(jnp.int32, (1, TILE), 1) + step * TILE
    low = jnp.zeros((1, TILE), jnp.int32)
    first, end = 0, 0
    for n in range(lengths.shape[0]):
        end = end + lengths[n]
        low = jnp.where(end <= place, end, low)
        first = jnp.where(end <= step * TILE, end, first)
    return place, low, lax.div(first, TILE)


def sorted_attend_kernel(
    lengths, order, parts_ref, low_ref, out_ref, lse_ref, q_ref, kvt_ref, rows_ref, inverse
):
    step = pl.program_id(0)
    length = q_ref.shape[1]
    per = parts_ref.shape[2] // 128

    @pl.when(step == 0)
    def _():
        fill_inverse(order, inverse, length // BLOCK)

        def place(d, carry):
            tile = pick_pair(lambda k: column_block(parts_ref, k, per), inverse, d)
            at = span(d, 128)
            q_ref[:HEAD_DIM, at] = (tile[:HEAD_DIM] * SCALE).astype(BF)
            q_ref[HEAD_DIM:, at] = jnp.zeros((HEAD_DIM, 128), BF)
            kvt_ref[:, at] = tile[HEAD_DIM:].astype(BF)
            rows_ref[at, :] = tile[HEAD_DIM:].T.astype(BF)
            return carry

        lax.fori_loop(0, length // 128, place, 0)

    here = span(step, TILE)
    queries = q_ref[:, here]
    place, low, first = query_lows(lengths, step)

    def body(kt, carry):
        peak, total, acc = carry
        at = span(kt, TILE)
        scores = dot_f32(rows_ref[at, :], queries)
        allowed = mask_of(kt, key_places(True, kt, None), place, low)
        scores = jnp.where(allowed, scores, NEG)
        new_peak = jnp.maximum(peak, jnp.max(scores, axis=0, keepdims=True))
        weights = jnp.exp(scores - new_peak)
        fade = jnp.exp(peak - new_peak)
        total = total * fade + jnp.sum(weights, axis=0, keepdims=True)
        acc = acc * fade + dot_f32(kvt_ref[HEAD_DIM:, at], weights.astype(BF))
        return new_peak, total, acc

    start = (
        jnp.full((1, TILE), NEG, F32),
        jnp.zeros((1, TILE), F32),
        jnp.zeros((HEAD_DIM, TILE), F32),
    )
    peak, total, acc = lax.fori_loop(first, step + 1, body, start)
    out_ref[:, here] = acc / total
    lse_ref[:, here] = peak + jnp.log(total)

    @pl.when(step == length // TILE - 1)
    def _():
        def home(d, carry):
            tile = pick_pair(lambda k: out_ref[:, span(k, 128)], order, d)
            low_ref[lax.div(d, per), :, span(lax.rem(d, per), 128)] = tile.astype(BF)
            return carry

        lax.fori_loop(0, length // 128, home, 0)


def sorted_back_kernel(
    lengths, order, flow_ref, out_ref, lse_ref, q_ref, kvt_ref, rows_ref,
    grad_ref, do_ref, dq_ref, acc_ref, inverse,
):
    step = pl.program_id(0)
    length = q_ref.shape[1]
    per = grad_ref.shape[3] // 128

    @pl.when(step == 0)
    def _():
        acc_ref[...] = jnp.zeros_like(acc_ref)
        fill_inverse(order, inverse, length // BLOCK)

        def place(d, carry):
            tile = pick_pair(lambda k: flow_ref[k].astype(F32), inverse, d)
            at = span(d, 128)
            do_ref[:HEAD_DIM, at] = jnp.zeros((HEAD_DIM, 128), BF)
            do_ref[HEAD_DIM:, at] = tile.astype(BF)
            return carry

        lax.fori_loop(0, length // 128, place, 0)

    here = span(step, TILE)
    queries, flows = q_ref[:, here], do_ref[:, here]
    place, low, first = query_lows(lengths, step)
    log_total = lse_ref[:, here]
    delta = jnp.sum(flows[HEAD_DIM:, :].astype(F32) * out_ref[:, here], axis=0, keepdims=True)

    def body(kt, dq):
        at = span(kt, TILE)
        rows = rows_ref[at, :]
        scores = dot_f32(rows, queries)
        allowed = mask_of(kt, key_places(True, kt, None), place, low)
        chances = jnp.exp(jnp.where(allowed, scores - log_total, NEG))
        flow = dot_f32(rows, flows)
        score_grad = (chances * (flow - delta)).astype(BF)
        dq = dq + dot_f32(kvt_ref[:HEAD_DIM, at], score_grad)
        acc_ref[:HEAD_DIM, at] += contract_cols(queries[:HEAD_DIM, :], score_grad)
        acc_ref[HEAD_DIM:, at] += contract_cols(flows[HEAD_DIM:, :], chances.astype(BF))
        return dq

    dq = lax.fori_loop(
        first, step + 1, body, jnp.zeros((HEAD_DIM, TILE), F32)
    )
    dq_ref[:, here] = dq * SCALE

    @pl.when(step == length // TILE - 1)
    def _():
        def home(d, carry):
            at = span(lax.rem(d, per), 128)
            tile = pick_pair(lambda k: dq_ref[:, span(k, 128)], order, d)
            grad_ref[lax.div(d, per), 0, :, at] = tile.astype(BF)
            tile = pick_pair(lambda k: acc_ref[:, span(k, 128)], order, d).astype(BF)
            grad_ref[lax.div(d, per), 1, :, at] = tile[:HEAD_DIM]
            grad_ref[lax.div(d, per), 2, :, at] = tile[HEAD_DIM:]
            return carry

        lax.fori_loop(0, length // 128, home, 0)


def fixed(shape):
    return pl.BlockSpec(shape, lambda i: (0,) * len(shape))


def sorted_attend(lengths, order, parts):
    groups, _, columns = parts.shape
    length = groups * columns
    shapes = (
        ((groups, HEAD_DIM, columns), BF),
        ((HEAD_DIM, length), F32),
        ((1, length), F32),
        ((2 * HEAD_DIM, length), BF),
        ((2 * HEAD_DIM, length), BF),
        ((length, 2 * HEAD_DIM), BF),
    )
    return pl.pallas_call(
        sorted_attend_kernel,
        name="attend",
        grid=(length // TILE,),
        in_specs=[pl.BlockSpec(memory_space=pltpu.SMEM)] * 2 + [fixed(parts.shape)],
        out_specs=tuple(fixed(s) for s, _ in shapes),
        out_shape=tuple(jax.ShapeDtypeStruct(s, d) for s, d in shapes),
        scratch_shapes=[pltpu.SMEM((length // BLOCK,), jnp.int32)],
        compiler_params=pltpu.CompilerParams(vmem_limit_bytes=60 * 2**20),
        cost_estimate=pl.CostEstimate(
            flops=0, bytes_accessed=42_000_000, transcendentals=0
        ),
    )(lengths, order, parts)


def sorted_back(lengths, order, flow, out, lse, q_pad, kv_t, kv_rows, groups):
    length = out.shape[1]
    grad = (groups, 3, HEAD_DIM, length // groups)
    return pl.pallas_call(
        sorted_back_kernel,
        name="attend_back",
        grid=(length // TILE,),
        in_specs=[pl.BlockSpec(memory_space=pltpu.SMEM)] * 2
        + [fixed(a.shape) for a in (flow, out, lse, q_pad, kv_t, kv_rows)],
        out_specs=fixed(grad),
        out_shape=jax.ShapeDtypeStruct(grad, BF),
        scratch_shapes=[
            pltpu.VMEM((2 * HEAD_DIM, length), BF),
            pltpu.VMEM((HEAD_DIM, length), F32),
            pltpu.VMEM((2 * HEAD_DIM, length), F32),
            pltpu.SMEM((length // BLOCK,), jnp.int32),
        ],
        compiler_params=pltpu.CompilerParams(vmem_limit_bytes=40 * 2**20),
        cost_estimate=pl.CostEstimate(
            flops=0, bytes_accessed=42_000_000, transcendentals=0
        ),
    )(lengths, order, flow, out, lse, q_pad, kv_t, kv_rows)


def normalize(values):
    center = values - jnp.mean(values, axis=-1, keepdims=True)
    spread = jnp.mean(center * center, axis=-1, keepdims=True)
    scale = lax.rsqrt(spread + EPS)
    return center * scale, scale


def mid_kernel(
    experts, team, member, att, wo, x, vec, rw, route, cot,
    second, dgrad, send_s, send_g, sel, mixes, middle_own, prob_own, hot_own, second_own, att_own, sel_own,
    egrad,
):
    rows = middle_own.shape[0]
    slots = send_s.shape[1]
    groups = send_s.shape[0]
    capacity = slots // team
    lane = lax.broadcasted_iota(jnp.int32, (rows, 128), 1)
    row = lax.broadcasted_iota(jnp.int32, (rows, rows), 0)
    col = lax.broadcasted_iota(jnp.int32, (rows, rows), 1)
    me = member[0]

    def block(b, carry):
        at = span(b, rows)
        part = att[:, at]
        middle = x[at, :].astype(F32) + contract_rows(part, wo[...])
        hat, _ = normalize(middle)
        low = (hat * vec[5:6, :] + vec[7:8, :]).astype(BF)
        second[at, :] = low
        logits = dot_f32(low, rw[...])
        is_expert = lane < experts
        is_mix = (lane >= experts) & (lane < experts + 2)
        pe = jnp.where(is_expert, logits, NEG)
        pe = jnp.exp(pe - jnp.max(pe, axis=1, keepdims=True))
        pe = pe / jnp.sum(pe, axis=1, keepdims=True)
        pm = jnp.where(is_mix, logits, NEG)
        pm = jnp.exp(pm - jnp.max(pm, axis=1, keepdims=True))
        pm = pm / jnp.sum(pm, axis=1, keepdims=True)
        route_row = jnp.broadcast_to(route[b][0:1, :], (rows, rows))
        route_col = jnp.sum(jnp.where(row == col, route_row, 0), axis=1, keepdims=True)
        hot = lane == route_col
        gate = jnp.sum(jnp.where(hot, pe, 0.0), axis=1, keepdims=True)
        mix0 = jnp.sum(jnp.where(lane == experts, pm, 0.0), axis=1, keepdims=True)
        mix1 = jnp.sum(jnp.where(lane == experts + 1, pm, 0.0), axis=1, keepdims=True)
        scaled = mix1 * gate
        flow = cot[at, :].astype(F32)
        dgrad[at, :] = (flow * mix0).astype(BF)
        egrad[at, :] = (flow * scaled).astype(BF)
        mixes[at, :] = jnp.where(lane == 0, mix0, jnp.where(lane == 1, scaled, 0.0))
        same = (route_row == route_col) & (col < row)
        rank = jnp.sum(jnp.where(same, 1, 0), axis=1, keepdims=True)
        group = lax.div(route_col, team)
        mine = lax.rem(route_col, team) == me
        target = jnp.where(mine, group * slots + b * capacity + rank, groups * slots)
        slot = lax.broadcasted_iota(jnp.int32, (rows, groups * slots), 1)
        sel[at, :] = jnp.where(slot == target, 1.0, 0.0).astype(BF)

        @pl.when(b == me)
        def _():
            middle_own[...] = middle
            prob_own[...] = jnp.where(is_expert, pe, jnp.where(is_mix, pm, 0.0))
            hot_own[...] = jnp.where(hot, 1.0, 0.0)
            second_own[...] = low
            att_own[...] = part
            place = lax.broadcasted_iota(jnp.int32, sel_own.shape, 1)
            sel_own[...] = jnp.where(place == route_col * capacity + rank, 1.0, 0.0).astype(BF)

        return carry

    lax.fori_loop(0, team, block, 0)
    send_s[...] = contract_rows(sel[...], second[...]).astype(BF).reshape(send_s.shape)
    send_g[...] = contract_rows(sel[...], egrad[...]).astype(BF).reshape(send_g.shape)


def between(experts, sizes, slots, member, att, wo, x, vec, rw, route, cot):
    two, groups, team = sizes
    group_rows, width = x.shape
    rows = group_rows // team
    shapes = (
        ((group_rows, width), BF),
        ((group_rows, width), BF),
        ((groups, slots, width), BF),
        ((groups, slots, width), BF),
        ((group_rows, groups * slots), BF),
        ((group_rows, 128), F32),
        ((rows, width), F32),
        ((rows, 128), F32),
        ((rows, 128), F32),
        ((rows, width), BF),
        ((width, rows), BF),
        ((rows, experts * (slots // team)), BF),
    )
    inside = pl.BlockSpec(memory_space=pltpu.VMEM)
    return pl.pallas_call(
        functools.partial(mid_kernel, experts, team),
        name="between",
        in_specs=[pl.BlockSpec(memory_space=pltpu.SMEM)] + [inside] * 7,
        out_specs=tuple(inside for _ in shapes),
        out_shape=tuple(jax.ShapeDtypeStruct(s, d) for s, d in shapes),
        scratch_shapes=[pltpu.VMEM((group_rows, width), BF)],
        compiler_params=pltpu.CompilerParams(vmem_limit_bytes=60 * 2**20),
    )(member, att, wo, x, vec, rw, route, cot)


def turn_kernel(
    experts, layer_sum, second_sum, sums, middle, prob, hot, second, att, cot, rw, wo, vec,
    layer, middle_grad, flow_t, out_term, small_t,
):
    rows = middle.shape[0]
    lane = lax.broadcasted_iota(jnp.int32, (rows, 128), 1)
    layer[...] = (middle[...] + layer_sum[...]).astype(BF)
    chances, chosen = prob[...], hot[...]
    s0, s1 = sums[:, 0:1], sums[:, 1:2]
    mix1 = jnp.sum(jnp.where(lane == experts + 1, chances, 0.0), axis=1, keepdims=True)
    gate = jnp.sum(chances * chosen, axis=1, keepdims=True)
    pull_gate = s1 * mix1
    pulls = jnp.where(lane == experts, s0, jnp.where(lane == experts + 1, s1 * gate, 0.0))
    mean_pull = jnp.sum(chances * pulls, axis=1, keepdims=True)
    logit_grad = chances * jnp.where(
        lane < experts, pull_gate * (chosen - gate), pulls - mean_pull
    )
    logit_grad = jnp.where(lane < experts + 2, logit_grad, 0.0).astype(BF)
    second_grad = second_sum[...] + contract_cols(logit_grad, rw[...])
    hat, scale = normalize(middle[...])
    pull = second_grad * vec[5:6, :]
    part = scale * (
        pull
        - jnp.mean(pull, axis=-1, keepdims=True)
        - hat * jnp.mean(pull * hat, axis=-1, keepdims=True)
    )
    grad = cot[...].astype(F32) + part
    middle_grad[...] = grad
    branch = grad.astype(BF)
    width = wo.shape[0]

    def tile(n, carry):
        at = span(n, TILE)
        flow_t[at, :] = contract_cols(wo[at, :], branch).astype(BF)
        out_term[at, :] = dot_f32(att[at, :], branch).astype(BF)
        return carry

    lax.fori_loop(0, width // TILE, tile, 0)
    used = small_t.shape[0]
    routed = contract_rows(logit_grad, second[...])[:used, :]
    which = lax.broadcasted_iota(jnp.int32, routed.shape, 0)
    gain = jnp.sum(second_grad * hat, axis=0, keepdims=True)
    bias = jnp.sum(second_grad, axis=0, keepdims=True)
    small_t[...] = jnp.where(
        which == experts + 3, gain, jnp.where(which == experts + 5, bias, routed)
    )


def turn(experts, layer_sum, second_sum, sums, middle, prob, hot, second, att, cot, rw, wo, vec):
    rows, width = middle.shape
    used = -(-(experts + 6) // 8) * 8
    shapes = (
        ((rows, width), BF),
        ((rows, width), F32),
        ((width, rows), BF),
        ((width, width), BF),
        ((used, width), F32),
    )
    inside = pl.BlockSpec(memory_space=pltpu.VMEM)
    return pl.pallas_call(
        functools.partial(turn_kernel, experts),
        name="turn",
        in_specs=[inside] * 12,
        out_specs=tuple(inside for _ in shapes),
        out_shape=tuple(jax.ShapeDtypeStruct(s, d) for s, d in shapes),
        compiler_params=pltpu.CompilerParams(vmem_limit_bytes=40 * 2**20),
    )(layer_sum, second_sum, sums, middle, prob, hot, second, att, cot, rw, wo, vec)


def row_sum_kernel(left, right, out):
    out[0] = contract_rows(left[...], right[...])


def row_sum(left, right, tile):
    many, high = left.shape
    wide = right.shape[1]
    return pl.pallas_call(
        row_sum_kernel,
        name="row_sum",
        grid=(high // tile,),
        in_specs=[pl.BlockSpec((many, tile), lambda i: (0, i)), fixed(right.shape)],
        out_specs=pl.BlockSpec((1, tile, wide), lambda i: (0, i, 0)),
        out_shape=jax.ShapeDtypeStruct((1, high, wide), F32),
        compiler_params=pltpu.CompilerParams(vmem_limit_bytes=40 * 2**20),
        cost_estimate=pl.CostEstimate(
            flops=2 * many * high * wide, bytes_accessed=4 * high * wide, transcendentals=0
        ),
    )(left, right)


class Net:
    def __init__(self, sizes, send_sem, recv_sem):
        self.two, self.groups, self.team = sizes
        self.send_sem, self.recv_sem = send_sem, recv_sem
        self.c = lax.axis_index("dp")
        i = lax.axis_index("ctx")
        self.g, self.t = lax.div(i, self.team), lax.rem(i, self.team)
        self.group_steps = [(0, k, 0) for k in range(1, self.groups)]
        self.team_steps = [(0, 0, k) for k in range(1, self.team)]
        self.swap = (1, 0, 0)
        self.started = []

    def device(self, step):
        dc, dg, dt = step
        return (
            lax.rem(self.c + dc, self.two),
            lax.rem(self.g + dg, self.groups) * self.team + lax.rem(self.t + dt, self.team),
        )

    def greet(self):
        barrier = pltpu.get_barrier_semaphore()
        steps = self.group_steps + self.team_steps + [self.swap]
        for step in steps:
            pl.semaphore_signal(barrier, inc=1, device_id=self.device(step), device_id_type=MESH)
        pl.semaphore_wait(barrier, len(steps))

    def send(self, src, dst, step):
        k = len(self.started)
        copy = pltpu.make_async_remote_copy(
            src_ref=src,
            dst_ref=dst,
            send_sem=self.send_sem.at[k],
            recv_sem=self.recv_sem.at[k],
            device_id=self.device(step),
            device_id_type=MESH,
        )
        copy.start()
        self.started.append(copy)
        return copy

    def other_group(self, bit, group=None):
        group = self.g if group is None else group
        return group + bit - 2 * bit * lax.rem(lax.div(group, bit), 2)

    def send_group(self, src, dst, group):
        k = len(self.started)
        copy = pltpu.make_async_remote_copy(
            src_ref=src,
            dst_ref=dst,
            send_sem=self.send_sem.at[k],
            recv_sem=self.recv_sem.at[k],
            device_id=(self.c, group * self.team + self.t),
            device_id_type=MESH,
        )
        copy.start()
        self.started.append(copy)
        return copy

    def group_to(self, step):
        return lax.rem(self.g + step[1], self.groups)

    def group_from(self, step):
        return lax.rem(self.g + self.groups - step[1], self.groups)

    def team_to(self, step):
        return lax.rem(self.t + step[2], self.team)

    def team_from(self, step):
        return lax.rem(self.t + self.team - step[2], self.team)

    def close(self):
        for copy in self.started:
            copy.wait_send()


def arrive(copies):
    for copy in copies:
        copy.wait_recv()


class Local:
    def __init__(self, sem):
        self.sem, self.count, self.open = sem, 0, []

    def copy(self, src, dst):
        made = pltpu.make_async_copy(src, dst, self.sem.at[self.count])
        made.start()
        self.count += 1
        self.open.append(made)
        return made

    def wait(self, *copies):
        for made in copies or tuple(self.open):
            made.wait()
            self.open = [other for other in self.open if other is not made]


def start_kernel(sizes, *refs):
    tokens, cot, w_qkv, w_up, w_down, w_out, router, gains, biases, routes = refs[:10]
    token_o, cot_o, heads_o, normed_o, weight_o, vec_o, out_o, ff_o, route_o, small_o = refs[10:20]
    (
        own, up, down, route, square, stage, weights, tokens_v, normed, mixed, heads, out_v,
        send_sem, recv_sem, local_sem,
    ) = refs[20:]
    net, local = Net(sizes, send_sem, recv_sem), Local(local_sem)
    c, g, t = net.c, net.g, net.t
    two, groups, team = sizes
    rows, width = tokens.shape
    used = own.shape[2] - 128
    wr = own.shape[1]
    own_tokens = local.copy(tokens, tokens_v.at[t])
    local.copy(cot, cot_o.at[t])

    square[...] = jnp.zeros_like(square)
    square[: router.shape[0], :wr] = router[...]
    square[124:126, :wr] = gains[...]
    square[126:128, :wr] = biases[...]
    small = square[...].T[:wr, :].astype(BF)
    third = used // 3
    for n in range(team):
        for k in range(3):
            at = k * width + n * third
            own[n, :, k * third : (k + 1) * third] = w_qkv[:, at : at + third].astype(BF)
        own[n, :, used:] = small
    stage[t] = own[t]
    net.greet()
    staged = [net.send(own.at[net.team_to(s)], stage.at[t], s) for s in net.team_steps]
    told = [net.send(tokens, tokens_v.at[t], s) for s in net.team_steps]
    out_v[g] = w_out[...].astype(BF)
    spread_out = [net.send(out_v.at[g], out_v.at[g], s) for s in net.group_steps]
    deep = w_down.shape[0]
    for n in range(team):
        for k in range(two * groups):
            at = (k * team + n) * deep
            up[n, :, k * deep : (k + 1) * deep] = w_up[:, at : at + deep].astype(BF)
    down[...] = w_down[...].astype(BF).reshape(down.shape)
    route[...] = jnp.broadcast_to(routes[...], route.shape)
    local.copy(up.at[t], ff_o.at[0, t])
    local.copy(down, ff_o.at[1])
    local.copy(route, route_o.at[t])
    later = [net.send(route, route_o.at[t], s) for s in net.team_steps]
    later += [net.send(up.at[net.team_to(s)], ff_o.at[0, t], s) for s in net.team_steps]
    arrive(staged)
    near, far = net.other_group(1), net.other_group(2)
    last = net.other_group(2, near)
    from_far = net.send_group(stage, weights.at[c, g], far)
    from_near = net.send_group(stage, weights.at[c, g], near)
    swapped = [net.send(stage, weights.at[c, g], net.swap)]
    mine = local.copy(stage, weights.at[c, g])
    later += [net.send(cot, cot_o.at[t], s) for s in net.team_steps]
    local.wait(mine)
    from_far.wait_recv()
    view = weights.at[c, far]
    passed = net.send_group(view, view, near)
    swapped.append(net.send(view, view, net.swap))
    from_near.wait_recv()
    view = weights.at[c, near]
    swapped.append(net.send(view, view, net.swap))
    passed.wait_recv()
    view = weights.at[c, last]
    swapped.append(net.send(view, view, net.swap))
    local.wait(own_tokens)
    arrive(told)
    local.copy(tokens_v, token_o)
    arrive(swapped)
    local.copy(weights, weight_o)

    small = weights[:, :, :, :, used:].reshape(width, 128)
    small_o[...] = small
    small = small.astype(F32).T
    vec_o[...] = small[120:, :]

    def norm(b, carry):
        hat, _ = normalize(tokens_v[b].astype(F32))
        normed[b] = (hat * vec_o[4:5, :] + vec_o[6:7, :]).astype(BF)
        return carry

    lax.fori_loop(0, team, norm, 0)
    local.copy(normed, normed_o)
    group_rows = rows * team
    per = used // 3 // 128
    pair = 128 // HEAD_DIM
    for n in range(used // 128):
        columns = weights[:, :, :, :, n * 128 : (n + 1) * 128].reshape(width, 128)
        made = dot_f32(normed[...].reshape(group_rows, width), columns).T.astype(BF)
        at = (n % per) * pair
        mixed[n // per, at : at + pair] = made.reshape(pair, HEAD_DIM, group_rows)
    given = [net.send(mixed.at[:, net.group_to(s)], heads.at[g], s) for s in net.group_steps]
    local.wait(local.copy(mixed.at[:, g], heads.at[g]))

    arrive(spread_out)
    local.copy(out_v, out_o.at[c, :, t])
    swapped = [net.send(out_v, out_o.at[c, :, t], net.swap)]
    outed = [net.send(out_v, out_o.at[c, :, t], s) for s in net.team_steps]
    for copy, s in zip(outed, net.team_steps):
        copy.wait_recv()
        view = out_o.at[c, :, net.team_from(s)]
        swapped.append(net.send(view, view, net.swap))
    arrive(given)
    local.copy(heads, heads_o)
    arrive(swapped + later)
    local.wait()
    net.close()


def start(sizes, tokens, cot, w_qkv, w_up, w_down, w_out, router, gains, biases, routes):
    two, groups, team = sizes
    rows, width = tokens.shape
    wr = w_qkv.shape[0]
    used = 3 * width // team
    cols = used + 128
    head = (3, groups, HEAD_DIM, team * rows)
    up = (team, wr, width)
    shapes = (
        ((team, rows, width), BF),
        ((team, rows, width), BF),
        ((groups, 3, HEAD_DIM, team * rows), BF),
        ((team, rows, width), BF),
        ((two, groups, team, wr, cols), BF),
        ((8, width), F32),
        ((two, groups, team, wr, width), BF),
        ((2,) + up, BF),
        ((team, 8, rows), jnp.int32),
        ((width, 128), BF),
    )
    anywhere = pl.BlockSpec(memory_space=pl.ANY)
    inside = pl.BlockSpec(memory_space=pltpu.VMEM)
    count = 6 * (team - 1) + 4 * (groups - 1) + 2 + (team - 1)
    return pl.pallas_call(
        functools.partial(start_kernel, sizes),
        name="start",
        out_shape=tuple(jax.ShapeDtypeStruct(s, d) for s, d in shapes),
        in_specs=[anywhere] * 2 + [inside] * 8,
        out_specs=tuple(inside if n in (5, 9) else anywhere for n in range(10)),
        scratch_shapes=[
            pltpu.VMEM((team, wr, cols), BF),
            pltpu.VMEM(up, BF),
            pltpu.VMEM(up, BF),
            pltpu.VMEM((8, rows), jnp.int32),
            pltpu.VMEM((128, 128), F32),
            pltpu.VMEM((team, wr, cols), BF),
            pltpu.VMEM((two, groups, team, wr, cols), BF),
            pltpu.VMEM((team, rows, width), BF),
            pltpu.VMEM((team, rows, width), BF),
            pltpu.VMEM(head, BF),
            pltpu.VMEM((groups, 3, HEAD_DIM, team * rows), BF),
            pltpu.VMEM((groups, wr, width), BF),
            pltpu.SemaphoreType.DMA((count,)),
            pltpu.SemaphoreType.DMA((count,)),
            pltpu.SemaphoreType.DMA((14,)),
        ],
        compiler_params=pltpu.CompilerParams(
            collective_id=12, has_side_effects=True, vmem_limit_bytes=60 * 2**20
        ),
        cost_estimate=pl.CostEstimate(flops=0, bytes_accessed=150_000_000, transcendentals=0),
    )(tokens, cot, w_qkv, w_up, w_down, w_out, router, gains, biases, routes)


def end_kernel(sizes, experts, *refs):
    groups = sizes[1]
    parts, refs = refs[:groups], refs[groups:]
    weight, normed, tokens, vec, middle_grad, small, up, out = refs[:8]
    grad_o, qkv_o, up_o, out_o, small_o = refs[8:13]
    (
        up_r, small_d, mixed, turned, weights, normed_v, give, got, zsend, zrecv, npart, nrecv, qsend, qrecv,
        out_r, small_a, small_b, small_c, send_sem, recv_sem, local_sem,
    ) = refs[13:]
    net, local = Net(sizes, send_sem, recv_sem), Local(local_sem)
    c, g, t = net.c, net.g, net.t
    team = sizes[2]
    rows, width = tokens.shape
    group_rows, used = turned.shape
    for k, part in enumerate(parts):
        local.copy(part, mixed.at[:, net.group_from((0, k, 0))])
    local.copy(normed, normed_v)
    local.copy(weight, weights)
    local.copy(up.at[t], up_r.at[t])
    local.copy(out.at[g], out_r.at[g])
    net.greet()
    outed = [net.send(out.at[net.group_to(s)], out_r.at[g], s) for s in net.group_steps]
    later = [net.send(up.at[net.team_to(s)], up_r.at[t], s) for s in net.team_steps]
    local.wait()
    per = used // 3 // 128
    pair = 128 // HEAD_DIM
    for n in range(used // 128):
        at = (n % per) * pair
        block = mixed[n // per, at : at + pair].reshape(128, group_rows)
        turned[:, n * 128 : (n + 1) * 128] = block.astype(F32).T.astype(BF)

    half = width // 2
    tile = 128

    def term(core, n):
        at = pl.ds(pl.multiple_of(core * half + n * tile, tile), tile)
        left = normed_v[:, :, at].reshape(group_rows, tile)
        return contract_rows(left, turned[...])

    def giving(n, carry):
        give[span(n, tile), :] = term(lax.rem(c + 1, 2), n).astype(BF)
        return carry

    lax.fori_loop(0, half // tile, giving, 0)
    crossed = net.send(give, got, net.swap)

    def part_of(r, carry):
        columns = weights[:, :, :, :, :used].reshape(width, used)
        npart[r] = contract_cols(turned[span(r, rows), :], columns).astype(BF)
        return carry

    lax.fori_loop(0, team, part_of, 0)
    owned = [net.send(npart.at[net.team_to(s)], nrecv.at[t], s) for s in net.team_steps]
    nrecv[t] = npart[t]
    crossed.wait_recv()

    def keeping(n, carry):
        at = span(n, tile)
        zsend[at, :] = (term(c, n) + got[at, :].astype(F32)).astype(BF)
        return carry

    lax.fori_loop(0, half // tile, keeping, 0)
    deep = half // groups
    near, far = net.other_group(1), net.other_group(2)
    last = net.other_group(2, near)
    for_far = net.send_group(zsend.at[span(last, deep), :], zrecv.at[0], near)
    for_me = net.send_group(zsend.at[span(near, deep), :], zrecv.at[1], near)
    for_far.wait_recv()
    zrecv[3] = (zsend[span(far, deep), :].astype(F32) + zrecv[0].astype(F32)).astype(BF)
    summed = [for_me, net.send_group(zrecv.at[3], zrecv.at[2], far)]

    arrive(owned)
    flow = jnp.sum(nrecv[...].astype(F32), axis=0)
    hat, scale = normalize(tokens[...].astype(F32))
    pull = flow * vec[4:5, :]
    pulled = scale * (
        pull
        - jnp.mean(pull, axis=-1, keepdims=True)
        - hat * jnp.mean(pull * hat, axis=-1, keepdims=True)
    )
    grad_o[...] = (middle_grad[...] + pulled).astype(BF)

    gain = jnp.sum(flow * hat, axis=0, keepdims=True)
    bias = jnp.sum(flow, axis=0, keepdims=True)
    which = lax.broadcasted_iota(jnp.int32, small.shape, 0)
    mine = jnp.where(
        which == experts + 2, gain, jnp.where(which == experts + 4, bias, small[...])
    )
    small_a[c] = mine
    crossing = net.send(small_a.at[c], small_a.at[c], net.swap)
    crossing.wait_recv()
    small_c[...] = small_a[0] + small_a[1]

    def columns_of(k):
        return span(c * groups + k, 128)

    moved = [
        net.send(small_c.at[:, columns_of(net.group_to(s))], small_b.at[g], s)
        for s in net.group_steps
    ]
    small_b[g] = small_c[:, columns_of(g)]
    arrive(moved)
    small_d[t] = jnp.sum(small_b[...], axis=0)
    later += [net.send(small_d.at[t], small_d.at[t], s) for s in net.team_steps]

    arrive(summed)
    total = zsend[span(g, deep), :].astype(F32) + zrecv[1].astype(F32) + zrecv[2].astype(F32)
    qsend[...] = total.astype(BF).reshape(qsend.shape)
    later += [net.send(qsend.at[net.team_to(s)], qrecv.at[t], s) for s in net.team_steps]
    qrecv[t] = qsend[t]
    arrive(outed)
    out_o[...] = jnp.sum(out_r[...].astype(F32), axis=0)
    arrive(later)
    small_o[...] = jnp.sum(small_d[...], axis=0)
    third = used // 3
    deep = up_o.shape[1] // (2 * groups * team)
    for n in range(team):
        for k in range(3):
            at = k * width + n * third
            qkv_o[:, at : at + third] = qrecv[n, :, k * third : (k + 1) * third].astype(F32)
        for k in range(2 * groups):
            at = (k * team + n) * deep
            up_o[:, at : at + deep] = up_r[n, :, k * deep : (k + 1) * deep].astype(F32)
    net.close()


def end(sizes, experts, parts, weight, normed, tokens, vec, middle_grad, small, up, out):
    two, groups, team = sizes
    rows, width = tokens.shape
    wr = out.shape[1]
    used = 3 * groups * HEAD_DIM
    group_rows = parts[0].shape[2]
    half = width // 2
    shapes = (
        ((rows, width), BF),
        ((wr, 3 * width), F32),
        ((wr, team * width), F32),
        ((wr, width), F32),
        ((small.shape[0], 128), F32),
    )
    anywhere = pl.BlockSpec(memory_space=pl.ANY)
    inside = pl.BlockSpec(memory_space=pltpu.VMEM)
    count = 5 * (team - 1) + 3 * (groups - 1) + 2
    return pl.pallas_call(
        functools.partial(end_kernel, sizes, experts),
        name="end",
        out_shape=tuple(jax.ShapeDtypeStruct(s, d) for s, d in shapes),
        in_specs=[anywhere] * (groups + 2) + [inside] * 4 + [anywhere] * 2,
        out_specs=tuple(inside for _ in shapes),
        scratch_shapes=[
            pltpu.VMEM((team, wr, width), BF),
            pltpu.VMEM((team, small.shape[0], 128), F32),
            pltpu.VMEM((3, groups, HEAD_DIM, group_rows), BF),
            pltpu.VMEM((group_rows, used), BF),
            pltpu.VMEM(weight.shape, BF),
            pltpu.VMEM(normed.shape, BF),
            pltpu.VMEM((half, used), BF),
            pltpu.VMEM((half, used), BF),
            pltpu.VMEM((half, used), BF),
            pltpu.VMEM((groups, half // groups, used), BF),
            pltpu.VMEM((team, rows, width), BF),
            pltpu.VMEM((team, rows, width), BF),
            pltpu.VMEM((team, wr, used), BF),
            pltpu.VMEM((team, wr, used), BF),
            pltpu.VMEM((groups, wr, width), BF),
            pltpu.VMEM((2,) + small.shape, F32),
            pltpu.VMEM((groups, small.shape[0], 128), F32),
            pltpu.VMEM(small.shape, F32),
            pltpu.SemaphoreType.DMA((count,)),
            pltpu.SemaphoreType.DMA((count,)),
            pltpu.SemaphoreType.DMA((groups + 4,)),
        ],
        compiler_params=pltpu.CompilerParams(
            collective_id=13, has_side_effects=True, vmem_limit_bytes=60 * 2**20
        ),
        cost_estimate=pl.CostEstimate(flops=0, bytes_accessed=120_000_000, transcendentals=0),
    )(*parts, weight, normed, tokens, vec, middle_grad, small, up, out)


def gelu_and_slope(x):
    k = math.sqrt(2.0 / math.pi)
    square = x * x
    bent = jnp.tanh(k * (x + 0.044715 * (square * x)))
    half = 0.5 * (1.0 + bent)
    slope = half + (0.5 * k) * x * (1.0 - bent * bent) * (1.0 + (3 * 0.044715) * square)
    return x * half, slope


def feed_kernel(sizes, copies_count, *refs):
    two, groups, team = sizes
    (send_s, send_g, eup_h, edown_h, second_h, dgrad_h, ff_h, sel_h, cot_h, mix_h) = refs[:10]
    (layer_o, grad_o, sums_o, active_o, hgrad_o, arr_s_o, arr_g_o, ffg_o) = refs[10:18]
    (
        arr_s, arr_g, eup, edown, second, dgrad, upw, downw, sel, cot, mix,
        slope, active, hgrad, acc, give, got_s, got_g, ret_s, ret_g, back_s, back_g,
        low, ugrad, dense, spart, lay, spa, sums, lay_r, spa_r, sums_r,
        term_give, term_got, send_sem, recv_sem, load_sem, out_sem,
    ) = refs[18:]
    c = lax.axis_index("dp")
    i = lax.axis_index("ctx")
    g, t = lax.div(i, team), lax.rem(i, team)
    width = second.shape[1]
    rows = lay.shape[1]
    hid, ehid = upw.shape[1], eup.shape[1]
    core = lax.rem(c + 1, two)

    def device(step):
        dc, dg, dt = step
        return (
            lax.rem(c + dc, two),
            lax.rem(g + dg, groups) * team + lax.rem(t + dt, team),
        )

    index = [0]

    def remote(src, dst, step):
        k = index[0]
        index[0] += 1
        assert k < copies_count
        return pltpu.make_async_remote_copy(
            src_ref=src,
            dst_ref=dst,
            send_sem=send_sem.at[k],
            recv_sem=recv_sem.at[k],
            device_id=device(step),
            device_id_type=MESH,
        )

    group_steps = [(0, k, 0) for k in range(1, groups)]
    team_steps = [(0, 0, k) for k in range(1, team)]
    swap = (1, 0, 0)
    deep = ff_h.shape[2]

    def block_of(core, k):
        return pl.ds(pl.multiple_of((core * groups + k) * deep, deep), deep)

    loads = []
    for k, (src, dst) in enumerate(
        [
            (second_h, second), (dgrad_h, dgrad), (eup_h, eup), (edown_h, edown), (sel_h, sel), (cot_h, cot), (mix_h, mix),
            (send_s.at[g], arr_s.at[c, g]), (send_g.at[g], arr_g.at[c, g]),
        ]
        + [
            (ff_h.at[k, n], weight.at[block_of(c, k), :])
            for k in range(groups)
            for n, weight in enumerate((upw, downw))
        ]
    ):
        load = pltpu.make_async_copy(src, dst, load_sem.at[k])
        load.start()
        loads.append(load)

    barrier = pltpu.get_barrier_semaphore()
    greet = group_steps + team_steps + [swap]
    for step in greet:
        pl.semaphore_signal(barrier, inc=1, device_id=device(step), device_id_type=MESH)
    pl.semaphore_wait(barrier, len(greet))

    every = []

    def launch(copy):
        copy.start()
        every.append(copy)
        return copy

    def to_groups(src, dst):
        return [
            launch(remote(src.at[lax.rem(g + s[1], groups)], dst.at[g], s)) for s in group_steps
        ]

    def source(s):
        return lax.rem(g + groups - s[1], groups)

    swap_w = [
        launch(remote(ff_h.at[k, n], weight.at[block_of(c, k), :], swap))
        for k in range(groups)
        for n, weight in enumerate((upw, downw))
    ]
    out_s = [
        launch(remote(send_s.at[lax.rem(g + s[1], groups)], arr_s.at[c, g], s))
        for s in group_steps
    ]
    swap_s = [launch(remote(send_s.at[g], arr_s.at[c, g], swap))]
    out_g = [
        launch(remote(send_g.at[lax.rem(g + s[1], groups)], arr_g.at[c, g], s))
        for s in group_steps
    ]
    swap_g = [launch(remote(send_g.at[g], arr_g.at[c, g], swap))]

    for load in loads[:2] + loads[9:]:
        load.wait()
    for copy in swap_w:
        copy.wait_recv()

    def dense_in(h, carry):
        at = span(h, TILE)
        value, bend = gelu_and_slope(dot_f32(second[...], upw[:, at]))
        low[:, at] = value.astype(BF)
        ugrad[:, at] = (bend * contract_cols(dgrad[...], downw[at, :])).astype(BF)
        return carry

    lax.fori_loop(0, hid // TILE, dense_in, 0)

    def dense_out(n, carry):
        at = span(n, TILE)
        dense[:, at] = dot_f32(low[...], downw[:, at])
        spart[:, at] = contract_cols(ugrad[...], upw[at, :])
        return carry

    lax.fori_loop(0, width // TILE, dense_out, 0)

    for load in loads[2:9]:
        load.wait()
    for copy, s in zip(out_s, group_steps):
        copy.wait_recv()
        swap_s.append(launch(remote(arr_s.at[c, source(s)], arr_s.at[c, source(s)], swap)))
    for copy in swap_s:
        copy.wait_recv()
    entries = 2 * groups * arr_s.shape[2]

    def expert_in(h, carry):
        at = span(h, TILE)
        value, bend = gelu_and_slope(dot_f32(arr_s[...].reshape(entries, width), eup[:, at]))
        active[:, at] = value.astype(BF)
        slope[:, at] = bend
        return carry

    lax.fori_loop(0, ehid // TILE, expert_in, 0)
    keeps = [
        pltpu.make_async_copy(active, active_o, out_sem.at[0]),
        pltpu.make_async_copy(arr_s, arr_s_o, out_sem.at[1]),
    ]
    for copy in keeps:
        copy.start()

    def expert_out(n, carry):
        at = span(n, TILE)
        acc[:, :, at] = dot_f32(active[...], edown[:, at]).reshape(2, entries // 2, TILE)
        return carry

    lax.fori_loop(0, width // TILE, expert_out, 0)
    give[0] = acc[core].astype(BF)
    other_s = launch(remote(give.at[0], got_s, swap))

    for copy, s in zip(out_g, group_steps):
        copy.wait_recv()
        swap_g.append(launch(remote(arr_g.at[c, source(s)], arr_g.at[c, source(s)], swap)))
    other_s.wait_recv()
    ret_s[...] = (acc[c] + got_s[...].astype(F32)).astype(BF).reshape(ret_s.shape)
    home_s = to_groups(ret_s, back_s)
    back_s[g] = ret_s[g]
    for copy in swap_g:
        copy.wait_recv()

    def expert_back(h, carry):
        at = span(h, TILE)
        pull = contract_cols(arr_g[...].reshape(entries, width), edown[at, :])
        hgrad[:, at] = (slope[:, at] * pull).astype(BF)
        return carry

    lax.fori_loop(0, ehid // TILE, expert_back, 0)
    keeps += [
        pltpu.make_async_copy(hgrad, hgrad_o, out_sem.at[2]),
        pltpu.make_async_copy(arr_g, arr_g_o, out_sem.at[3]),
    ]
    for copy in keeps[2:]:
        copy.start()

    def expert_back_out(n, carry):
        at = span(n, TILE)
        acc[:, :, at] = contract_cols(hgrad[...], eup[at, :]).reshape(2, entries // 2, TILE)
        return carry

    lax.fori_loop(0, width // TILE, expert_back_out, 0)
    give[1] = acc[core].astype(BF)
    other_g = launch(remote(give.at[1], got_g, swap))
    other_g.wait_recv()
    ret_g[...] = (acc[c] + got_g[...].astype(F32)).astype(BF).reshape(ret_g.shape)
    home_g = to_groups(ret_g, back_g)
    back_g[g] = ret_g[g]

    for copy in home_s:
        copy.wait_recv()
    slots = groups * back_s.shape[1]
    lane = lax.broadcasted_iota(jnp.int32, (rows, 128), 1)

    def join_layer(r, carry):
        at = span(r, rows)
        found = dot_f32(sel[at, :], back_s[...].reshape(slots, width))
        own = dense[at, :]
        flow = cot[at, :].astype(F32)
        mixes = mix[at, :]
        lay[r] = (mixes[:, 0:1] * own + mixes[:, 1:2] * found).astype(BF)
        plain = jnp.sum(flow * own, axis=1, keepdims=True)
        routed = jnp.sum(flow * found, axis=1, keepdims=True)
        sums[r] = jnp.where(lane == 0, plain, jnp.where(lane == 1, routed, 0.0))
        return carry

    lax.fori_loop(0, team, join_layer, 0)

    def to_team(src, dst):
        made = [launch(remote(src.at[lax.rem(t + s[2], team)], dst.at[t], s)) for s in team_steps]
        dst[t] = src[t]
        return made

    team_copies = to_team(lay, lay_r) + to_team(sums, sums_r)

    for copy in home_g:
        copy.wait_recv()

    def join_grad(r, carry):
        at = span(r, rows)
        found = dot_f32(sel[at, :], back_g[...].reshape(slots, width))
        spa[r] = (spart[at, :] + found).astype(BF)
        return carry

    lax.fori_loop(0, team, join_grad, 0)
    team_copies += to_team(spa, spa_r)

    half = hid // 2
    term_tile = 128

    def down_term(base, n):
        at = pl.ds(pl.multiple_of(base + n * term_tile, term_tile), term_tile)
        return contract_rows(low[:, at], dgrad[...])

    def up_term(base, n):
        at = pl.ds(pl.multiple_of(base + n * term_tile, term_tile), term_tile)
        return contract_rows(second[:, at], ugrad[...])

    terms = []
    for k, (term, size) in enumerate(((down_term, half), (up_term, width // 2))):

        def giving(n, carry, k=k, term=term, size=size):
            term_give[k, span(n, term_tile), :] = term(core * size, n).astype(BF)
            return carry

        lax.fori_loop(0, size // term_tile, giving, 0)
        terms.append(launch(remote(term_give.at[k], term_got.at[k], swap)))
    for k, (term, size) in enumerate(((down_term, half), (up_term, width // 2))):
        terms[k].wait_recv()

        def keeping(n, carry, k=k, term=term, size=size):
            at = span(n, term_tile)
            total = term(c * size, n) + term_got[k, at, :].astype(F32)
            ffg_o[at, k * width : (k + 1) * width] = total.astype(BF)
            return carry

        lax.fori_loop(0, size // term_tile, keeping, 0)

    for copy in team_copies:
        copy.wait_recv()
    layer_o[...] = jnp.sum(lay_r[...].astype(F32), axis=0)
    grad_o[...] = jnp.sum(spa_r[...].astype(F32), axis=0)
    sums_o[...] = jnp.sum(sums_r[...], axis=0)
    for copy in keeps:
        copy.wait()
    for copy in every:
        copy.wait_send()


def feed_forward(sizes, rows, send_s, send_g, eup, edown, second, dgrad, ff, sel, cot, mix):
    two, groups, team = sizes
    slots = send_s.shape[1]
    width = second.shape[1]
    hid, ehid = second.shape[1] * ff.shape[3] // width, eup.shape[1]
    entries = 2 * groups * slots
    count = 2 * (groups - 1) * 2 + 2 * groups + 2 + 3 * (team - 1) + 2 + 2 * groups
    arrived = (two, groups, slots, width)
    anywhere = pl.BlockSpec(memory_space=pl.ANY)
    inside = pl.BlockSpec(memory_space=pltpu.VMEM)
    team_rows = team * rows
    return pl.pallas_call(
        functools.partial(feed_kernel, sizes, count),
        name="feed_forward",
        out_shape=(
            jax.ShapeDtypeStruct((rows, width), F32),
            jax.ShapeDtypeStruct((rows, width), F32),
            jax.ShapeDtypeStruct((rows, 128), F32),
            jax.ShapeDtypeStruct((entries, ehid), BF),
            jax.ShapeDtypeStruct((entries, ehid), BF),
            jax.ShapeDtypeStruct(arrived, BF),
            jax.ShapeDtypeStruct(arrived, BF),
            jax.ShapeDtypeStruct((hid // 2, 2 * width), BF),
        ),
        in_specs=[anywhere] * 10,
        out_specs=(inside, inside, inside, anywhere, anywhere, anywhere, anywhere, inside),
        scratch_shapes=[
            pltpu.VMEM((two, groups, slots, width), BF),
            pltpu.VMEM((two, groups, slots, width), BF),
            pltpu.VMEM(eup.shape, BF),
            pltpu.VMEM(edown.shape, BF),
            pltpu.VMEM(second.shape, BF),
            pltpu.VMEM(dgrad.shape, BF),
            pltpu.VMEM((width, hid), BF),
            pltpu.VMEM((hid, width), BF),
            pltpu.VMEM(sel.shape, BF),
            pltpu.VMEM(cot.shape, BF),
            pltpu.VMEM(mix.shape, F32),
            pltpu.VMEM((entries, ehid), F32),
            pltpu.VMEM((entries, ehid), BF),
            pltpu.VMEM((entries, ehid), BF),
            pltpu.VMEM((2, entries // 2, width), F32),
            pltpu.VMEM((2, entries // 2, width), BF),
            pltpu.VMEM((entries // 2, width), BF),
            pltpu.VMEM((entries // 2, width), BF),
            pltpu.VMEM((groups, slots, width), BF),
            pltpu.VMEM((groups, slots, width), BF),
            pltpu.VMEM((groups, slots, width), BF),
            pltpu.VMEM((groups, slots, width), BF),
            pltpu.VMEM((team_rows, hid), BF),
            pltpu.VMEM((team_rows, hid), BF),
            pltpu.VMEM((team_rows, width), F32),
            pltpu.VMEM((team_rows, width), F32),
            pltpu.VMEM((team, rows, width), BF),
            pltpu.VMEM((team, rows, width), BF),
            pltpu.VMEM((team, rows, 128), F32),
            pltpu.VMEM((team, rows, width), BF),
            pltpu.VMEM((team, rows, width), BF),
            pltpu.VMEM((team, rows, 128), F32),
            pltpu.VMEM((2, hid // 2, width), BF),
            pltpu.VMEM((2, hid // 2, width), BF),
            pltpu.SemaphoreType.DMA((count,)),
            pltpu.SemaphoreType.DMA((count,)),
            pltpu.SemaphoreType.DMA((9 + 2 * groups,)),
            pltpu.SemaphoreType.DMA((4,)),
        ],
        compiler_params=pltpu.CompilerParams(
            collective_id=5, has_side_effects=True, vmem_limit_bytes=60 * 2**20
        ),
        cost_estimate=pl.CostEstimate(
            flops=0, bytes_accessed=240_000_000, transcendentals=0
        ),
    )(send_s, send_g, eup, edown, second, dgrad, ff, sel, cot, mix)


def tall(chunk):
    rows, cols = chunk.shape[-2:]
    factor = 1
    while (rows * factor) % 16:
        factor *= 2
    return chunk.reshape(chunk.shape[:-2] + (rows * factor, cols // factor))


def per_device_general(
    tokens,
    cotangent,
    block_order,
    doc_lengths,
    routes,
    w_qkv,
    w_out,
    w_up,
    w_down,
    router,
    norm_gains,
    norm_biases,
    expert_up,
    expert_down,
):
    rows, width = tokens.shape[1], tokens.shape[2]
    ctx_count = lax.axis_size("ctx")
    two = lax.axis_size("dp")
    team = math.gcd(4, ctx_count)
    groups = ctx_count // team
    sizes = (two, groups, team)
    team_heads = HEADS // team
    reps = groups // team_heads
    length = rows * ctx_count
    group_rows = rows * team
    experts = ctx_count * expert_up.shape[0]
    capacity = max(2, 2 * rows // experts)
    block_rows = length // block_order.shape[0]
    hidden = w_up.shape[1]
    hidden_dev = w_down.shape[0]
    wr = w_qkv.shape[0]
    qkv_cols = 3 * width // team
    up_cols = hidden // team
    core = lax.axis_index("dp")
    ctx = lax.axis_index("ctx")
    group, member = lax.div(ctx, team), lax.rem(ctx, team)
    team_steps = [(0, 0, k) for k in range(1, team)]
    group_steps = [(0, k, 0) for k in range(1, groups)]
    by_group = [[g * team + t for g in range(groups)] for t in range(team)]
    by_team = [[g * team + t for t in range(team)] for g in range(groups)]
    swap = [(d, (d + 1) % two) for d in range(two)]

    small_flat = jnp.concatenate(
        [router.reshape(-1), norm_gains.reshape(-1), norm_biases.reshape(-1)]
    )
    small_size = -(-small_flat.shape[0] // 2048) * 2048
    small = jnp.pad(small_flat, (0, small_size - small_flat.shape[0])).astype(BF)
    small = small.reshape(-1, 128)

    qkv_first = tall(
        w_qkv.astype(BF).reshape(wr, 3, team, width // team).transpose(2, 0, 1, 3).reshape(
            team, wr, qkv_cols
        )
    )
    up_first = tall(
        w_up.reshape(wr, two * groups, team, hidden_dev)
        .transpose(2, 0, 1, 3)
        .reshape(team, wr, up_cols)
        .astype(BF)
    )
    down_first = tall(w_down.astype(BF).reshape(team, wr, width))
    out_first = tall(w_out.astype(BF))
    route_row = jnp.broadcast_to(routes[0, :, 0][None, :], (8, rows))

    def first(coords, ins, outs):
        c, g, t = coords
        moves, local = [], []
        for s in team_steps:
            to = lax.rem(t + s[2], team)
            moves.append(Move(s, ins[0], outs[0].at[t]))
            moves.append(Move(s, ins[1].at[to], outs[1].at[t]))
            moves.append(Move(s, ins[3], outs[3].at[t]))
            moves.append(Move(s, ins[4], outs[4].at[t]))
            moves.append(Move(s, ins[2].at[to], outs[2].at[0, t]))
        for s in group_steps:
            moves.append(Move(s, ins[5], outs[5].at[g]))
        local.append((ins[0], outs[0].at[t]))
        local.append((ins[1].at[t], outs[1].at[t]))
        local.append((ins[2].at[t], outs[2].at[0, t]))
        local.append((ins[3], outs[3].at[t]))
        local.append((ins[4], outs[4].at[t]))
        local.append((ins[5], outs[5].at[g]))
        local.append((ins[6], outs[2].at[1]))
        return local, moves

    token_rows, qkv_part, ff_part, small_part, route_all, out_part = exchange(
        "first",
        1,
        sizes,
        (tokens[0], qkv_first, up_first, small, route_row, out_first, down_first),
        [
            ((team, rows, width), BF),
            (qkv_first.shape, BF),
            ((2,) + up_first.shape, BF),
            ((team,) + small.shape, BF),
            ((team, 8, rows), jnp.int32),
            ((groups,) + out_first.shape, BF),
        ],
        first,
    )

    def second_build(coords, ins, outs):
        c, g, t = coords
        moves, local = [], []
        for k, s in enumerate(group_steps):
            moves.append(Move(s, ins[0], outs[0].at[c, g]))
            moves.append(Move(s, ins[1], outs[1].at[c, g]))
        for s in team_steps:
            moves.append(Move(s, ins[2], outs[2].at[t]))
        local.append((ins[0], outs[0].at[c, g]))
        local.append((ins[1], outs[1].at[c, g]))
        local.append((ins[2], outs[2].at[t]))
        other = (1, 0, 0)
        for n in range(2):
            moves.append(Move(other, ins[n], outs[n].at[c, g]))
        for k, s in enumerate(group_steps):
            source = lax.rem(g + groups - s[1], groups)
            for n in range(2):
                moves.append(
                    Move(other, outs[n].at[c, source], outs[n].at[c, source], after=2 * k + n)
                )
        return local, moves

    qkv_all, small_all, cot_rows = exchange(
        "second",
        2,
        sizes,
        (qkv_part, small_part, cotangent[0]),
        [
            ((two, groups) + qkv_part.shape, BF),
            ((two, groups) + small_part.shape, BF),
            ((team, rows, width), BF),
        ],
        second_build,
    )
    qkv_weight = qkv_all.reshape(width, qkv_cols)
    small_rows = small_all.reshape(two * ctx_count, -1)
    router_cols = router.shape[1]
    router_weight = jnp.pad(
        small_rows[:, : wr * router_cols].reshape(width, router_cols),
        ((0, 0), (0, 128 - router_cols)),
    )
    vectors = small_rows[:, wr * router_cols : small_flat.shape[0]].reshape(
        two * ctx_count, 4, wr
    )
    vectors = vectors.transpose(1, 0, 2).reshape(4, width).astype(F32)
    vectors = jnp.pad(vectors, ((4, 0), (0, 0)))

    ff_half = lax.all_gather(
        ff_part.reshape(2, team * wr, width),
        "ctx",
        axis=0,
        tiled=False,
        axis_index_groups=by_group,
    )

    def core_half(term):
        halves = term.reshape((two, term.shape[0] // two) + term.shape[1:])
        keep = lax.dynamic_index_in_dim(halves, core, 0, keepdims=False)
        give = lax.dynamic_index_in_dim(halves, 1 - core, 0, keepdims=False)
        return keep + lax.ppermute(give.astype(BF), "dp", swap).astype(F32)

    def over_groups(term):
        return lax.psum_scatter(
            term, "ctx", scatter_dimension=0, tiled=True, axis_index_groups=by_group
        )

    doc_id = jnp.arange(doc_lengths.shape[1], dtype=jnp.int32)
    doc_ends = jnp.sum(
        jnp.where(doc_id[:, None] <= doc_id[None, :], doc_lengths[0][:, None], 0), axis=0
    )
    all_rows = jnp.arange(length, dtype=jnp.int32)
    marks = (all_rows // block_rows)[:, None] == jnp.arange(
        block_order.shape[0], dtype=jnp.int32
    )[None, :]
    anchor = jnp.sum(jnp.where(marks, block_order[None, :], 0), axis=1)
    all_place = anchor * block_rows + all_rows % block_rows

    def low_of(place):
        return jnp.max(
            jnp.where(doc_ends[None, :] <= place[:, None], doc_ends[None, :], 0), axis=1
        )

    query_length = length // reps
    tiles = query_length // TILE
    part = lax.rem(group, reps)
    query_place = lax.dynamic_slice(all_place, (part * query_length,), (query_length,))
    lows = low_of(query_place)
    bounds = jnp.broadcast_to(jnp.array([[0, length // TILE]], dtype=jnp.int32), (tiles, 2))
    meta = jnp.concatenate(
        [query_place[None], lows[None], jnp.zeros((6, query_length), jnp.int32)], axis=0
    )

    token_rows = token_rows.reshape(group_rows, width)
    inputs = token_rows.astype(F32)
    normed_low = layer_norm(inputs, vectors[4], vectors[6]).astype(BF)
    mixed_t = lax.dot_general(
        qkv_weight, normed_low, (((0,), (1,)), ((), ())), preferred_element_type=F32
    ).astype(BF)
    mixed_t = mixed_t.reshape(3, team_heads, HEAD_DIM, group_rows)

    def spread_heads(coords, ins, outs):
        c, g, t = coords
        moves = [
            Move(s, ins[0].at[:, lax.div(lax.rem(g + s[1], groups), reps)], outs[0].at[g])
            for s in group_steps
        ]
        local = [(ins[0].at[:, lax.div(g, reps)], outs[0].at[g])]
        other = (1, 0, 0)
        moves.append(Move(other, ins[1], outs[1].at[c, :, t]))
        local.append((ins[1], outs[1].at[c, :, t]))
        first_team = len(moves)
        for s in team_steps:
            moves.append(Move(s, ins[1], outs[1].at[c, :, t]))
        for k, s in enumerate(team_steps):
            source = lax.rem(t + team - s[2], team)
            view = outs[1].at[c, :, source]
            moves.append(Move(other, view, view, after=first_team + k))
        return local, moves

    head_parts, out_weight = exchange(
        "heads",
        3,
        sizes,
        (mixed_t, out_part),
        [
            ((groups, 3, HEAD_DIM, group_rows), BF),
            ((two, groups, team) + out_first.shape, BF),
        ],
        spread_heads,
    )
    out_weight = out_weight.reshape(width, width)
    head_parts = head_parts.reshape(groups, 3 * HEAD_DIM, group_rows)
    place_col = all_place[:, None]
    head_t = head_parts.transpose(1, 0, 2).reshape(3 * HEAD_DIM, length)
    zeros = jnp.zeros((HEAD_DIM, query_length), BF)
    kv_t = head_t[HEAD_DIM:]
    kv_rows = kv_t.T
    q_t = lax.dynamic_slice(
        head_t[:HEAD_DIM], (0, part * query_length), (HEAD_DIM, query_length)
    )
    q_pad = jnp.concatenate([q_t * jnp.asarray(SCALE, BF), zeros], axis=0)
    attention_t, log_total = attend(False, bounds, meta, place_col, q_pad, kv_rows, kv_t)
    low_t = lax.dynamic_update_slice(
        jnp.zeros((HEAD_DIM, length), BF),
        attention_t.astype(BF),
        (0, part * query_length),
    )
    low_t = low_t.reshape(HEAD_DIM, groups, group_rows).transpose(1, 0, 2)

    def gather_heads(coords, ins, outs):
        c, g, t = coords
        moves = [
            Move(s, ins[0].at[lax.rem(g + s[1], groups)], outs[0].at[t, g]) for s in group_steps
        ]
        local = [(ins[0].at[g], outs[0].at[t, g])]
        for s in team_steps:
            moves.append(Move(s, ins[0].at[g], outs[0].at[t, g]))
        for k, s in enumerate(group_steps):
            source = lax.rem(g + groups - s[1], groups)
            for e in team_steps:
                moves.append(Move(e, outs[0].at[t, source], outs[0].at[t, source], after=k))
        return local, moves

    [attended] = exchange(
        "attended",
        4,
        sizes,
        (low_t,),
        [((team, groups, HEAD_DIM, group_rows), BF)],
        gather_heads,
    )
    if reps > 1:
        attended = lax.dynamic_index_in_dim(
            attended.reshape(team, team_heads, reps, HEAD_DIM, group_rows),
            lax.div(group, groups // reps),
            2,
            keepdims=False,
        )
    attended_t = attended.reshape(width, group_rows)

    slots = team * capacity
    (
        second_low,
        dense_grad,
        send_s,
        send_g,
        select,
        mixes,
        middle_own,
        prob_own,
        hot_own,
        second_own,
        attended_own,
        _,
    ) = between(
        experts,
        sizes,
        slots,
        member[None],
        attended_t,
        out_weight,
        token_rows,
        vectors,
        router_weight,
        route_all,
        cot_rows.reshape(group_rows, width),
    )
    (
        layer_sum,
        second_sum,
        sums_own,
        expert_active,
        hidden_grad,
        arrived_in,
        arrived_grad,
        ff_terms,
    ) = feed_forward(
        sizes,
        rows,
        send_s,
        send_g,
        expert_up[0],
        expert_down[0],
        second_low,
        dense_grad,
        ff_half,
        select,
        cot_rows.reshape(group_rows, width),
        mixes,
    )
    ff_sum = over_groups(ff_terms)
    down_sum = ff_sum[:, :width].astype(F32)
    up_sum = ff_sum[:, width:].reshape(team, wr, up_cols)
    entries = two * groups * slots
    expert_down_grad = row_sum(expert_active, arrived_grad.reshape(entries, width), TILE)
    expert_up_grad = row_sum(arrived_in.reshape(entries, width), hidden_grad, 128)

    layer_out, middle_grad, flow_t, out_term, small_t = turn(
        experts,
        layer_sum,
        second_sum,
        sums_own,
        middle_own,
        prob_own,
        hot_own,
        second_own,
        attended_own,
        cotangent[0],
        router_weight,
        out_weight,
        vectors,
    )
    flow_t = flow_t.reshape(team, team_heads, HEAD_DIM, rows)
    out_halves = out_term.reshape(two, groups, team, wr, width)

    def spread_flow(coords, ins, outs):
        c, g, t = coords
        moves = []
        for dg in range(groups):
            for dt in range(team):
                if dg or dt:
                    to_g, to_t = lax.rem(g + dg, groups), lax.rem(t + dt, team)
                    moves.append(
                        Move((0, dg, dt), ins[0].at[to_t, lax.div(to_g, reps)], outs[0].at[g, t])
                    )
        moves.append(Move((1, 0, 0), ins[1].at[lax.rem(c + 1, two)], outs[1]))
        return [(ins[0].at[t, lax.div(g, reps)], outs[0].at[g, t])], moves

    flow_parts, out_got = exchange(
        "flow",
        8,
        sizes,
        (flow_t, out_halves),
        [((groups, team, HEAD_DIM, rows), BF), (out_halves.shape[1:], BF)],
        spread_flow,
    )
    flow_all = flow_parts.transpose(2, 0, 1, 3).reshape(HEAD_DIM, length)
    flow_all = lax.dynamic_slice(
        flow_all, (0, part * query_length), (HEAD_DIM, query_length)
    )
    do_pad = jnp.concatenate([zeros, flow_all], axis=0)
    query_grad, pair_grad = attend_back(
        False,
        bounds,
        meta,
        place_col,
        q_pad,
        do_pad,
        attention_t,
        log_total,
        kv_rows,
        kv_t,
    )
    query_grad = lax.dynamic_update_slice(
        jnp.zeros((HEAD_DIM, length), BF), query_grad, (0, part * query_length)
    )
    grad_parts = jnp.concatenate([query_grad, pair_grad], axis=0)
    grad_parts = grad_parts.reshape(3, HEAD_DIM, groups, group_rows).transpose(2, 0, 1, 3)
    out_keep = lax.dynamic_index_in_dim(out_halves, core, 0, keepdims=False)
    out_parts = tall(
        (out_keep.astype(F32) + out_got.astype(F32))
        .astype(BF)
        .transpose(1, 0, 2, 3)
        .reshape(team, groups * wr, width)
    )

    def mixed_build(coords, ins, outs):
        c, g, t = coords
        moves = [
            Move(s, ins[0].at[lax.rem(g + s[1], groups)], outs[0].at[:, g])
            for s in group_steps
        ]
        moves += [
            Move(s, ins[1].at[lax.rem(t + s[2], team)], outs[1].at[t]) for s in team_steps
        ]
        return [(ins[0].at[g], outs[0].at[:, g]), (ins[1].at[t], outs[1].at[t])], moves

    grad_parts, out_parts = exchange(
        "mixed",
        9,
        sizes,
        (grad_parts, out_parts),
        [((3, groups, HEAD_DIM, group_rows), BF), (out_parts.shape, BF)],
        mixed_build,
    )
    out_parts = tall(
        jnp.sum(out_parts.astype(F32), axis=0).astype(BF).reshape(groups, wr, width)
    )
    if reps > 1:
        grad_parts = jnp.sum(
            grad_parts.reshape(3, team_heads, reps, HEAD_DIM, group_rows).astype(F32), axis=2
        ).astype(BF)
    mixed_grad_t = grad_parts.reshape(qkv_cols, group_rows)
    normed_part = (
        lax.dot_general(
            mixed_grad_t, qkv_weight, (((0,), (1,)), ((), ())), preferred_element_type=F32
        )
        .astype(BF)
        .reshape(team, rows, width)
    )
    qkv_term = lax.dot_general(
        normed_low, mixed_grad_t, (((0,), (1,)), ((), ())), preferred_element_type=F32
    )
    qkv_parts = core_half(qkv_term).astype(BF).reshape(groups, team * wr, qkv_cols)

    def normed_build(coords, ins, outs):
        c, g, t = coords
        moves, local = [], [(ins[2].at[t], outs[2].at[t])]
        for n in range(2):
            for s in group_steps:
                moves.append(Move(s, ins[n].at[lax.rem(g + s[1], groups)], outs[n].at[g]))
            local.append((ins[n].at[g], outs[n].at[g]))
        for s in team_steps:
            moves.append(Move(s, ins[2].at[lax.rem(t + s[2], team)], outs[2].at[t]))
        return local, moves

    qkv_parts, out_parts, normed_own = exchange(
        "normed",
        10,
        sizes,
        (qkv_parts, out_parts, normed_part),
        [(qkv_parts.shape, BF), (out_parts.shape, BF), (normed_part.shape, BF)],
        normed_build,
    )
    qkv_sum = (
        jnp.sum(qkv_parts.astype(F32), axis=0).astype(BF).reshape(team, wr, qkv_cols)
    )
    out_sum = jnp.sum(out_parts.astype(F32), axis=0).reshape(wr, width)
    normed_grad = jnp.sum(normed_own.astype(F32), axis=0)
    input_part_grad, gain_first, bias_first = jax.vjp(
        layer_norm, tokens[0].astype(F32), vectors[4], vectors[6]
    )[1](normed_grad)
    input_grad = middle_grad + input_part_grad

    small_used = small_t.shape[0]
    small_row = jnp.arange(small_used, dtype=jnp.int32)[:, None]
    small_t = jnp.where(
        small_row == experts + 2,
        gain_first[None],
        jnp.where(small_row == experts + 4, bias_first[None], small_t),
    )
    small_cols = small_used * wr
    small_pad = -(-small_cols // 1024) * 1024
    small_parts = jnp.pad(
        small_t.reshape(small_used, two * ctx_count, wr)
        .transpose(1, 0, 2)
        .reshape(two * ctx_count, small_cols),
        ((0, 0), (0, small_pad - small_cols)),
    ).reshape(two * ctx_count, small_pad // 128, 128)

    def owners_build(coords, ins, outs):
        c, g, t = coords
        moves, local = [], []
        for n in range(2):
            for s in team_steps:
                moves.append(Move(s, ins[n].at[lax.rem(t + s[2], team)], outs[n].at[t]))
            local.append((ins[n].at[t], outs[n].at[t]))
        me = c * ctx_count + g * team + t
        for dc in range(two):
            for dg in range(groups):
                for dt in range(team):
                    if dc or dg or dt:
                        to = (
                            lax.rem(c + dc, two) * ctx_count
                            + lax.rem(g + dg, groups) * team
                            + lax.rem(t + dt, team)
                        )
                        moves.append(Move((dc, dg, dt), ins[2].at[to], outs[2].at[me]))
        local.append((ins[2].at[me], outs[2].at[me]))
        return local, moves

    up_own, qkv_own, small_own = exchange(
        "owners",
        11,
        sizes,
        (tall(up_sum), tall(qkv_sum), small_parts),
        [
            (tall(up_sum).shape, BF),
            (tall(qkv_sum).shape, BF),
            (small_parts.shape, F32),
        ],
        owners_build,
    )
    small_sum = jnp.sum(small_own, axis=0).reshape(-1)[:small_cols].reshape(small_used, wr)
    up_own = (
        up_own.reshape(team, wr, two * groups, hidden_dev)
        .transpose(1, 2, 0, 3)
        .reshape(wr, hidden)
        .astype(F32)
    )
    qkv_own = (
        qkv_own.reshape(team, wr, 3, width // team)
        .transpose(1, 2, 0, 3)
        .reshape(wr, 3 * width)
        .astype(F32)
    )
    return (
        layer_out[None],
        input_grad[None].astype(BF),
        qkv_own,
        out_sum,
        up_own,
        down_sum,
        small_sum[:router_cols].T,
        small_sum[router_cols : router_cols + 2],
        small_sum[router_cols + 2 : router_cols + 4],
        expert_up_grad,
        expert_down_grad,
    )


def whole_kernel(sizes, experts, copies_count, *refs):
    two, groups, team = sizes
    (send_s, send_g, eup_h, edown_h, second_h, dgrad_h, ff_h, sel_h, cot_h) = refs[:9]
    (middle_h, prob_h, hot_h, own_h, att_h, rw_h, wo_h, vec_h) = refs[9:17]
    (
        layer_o, middle_o, small_o, flow_o, out_o, down_o, up_o,
        active_o, hgrad_o, arr_s_o, arr_g_o,
    ) = refs[17:28]
    (
        arr_s, arr_g, eup, edown, second, dgrad, upw, downw, sel, cot,
        slope, active, hgrad, acc, give, got_s, got_g, ret_s, ret_g, back_s, back_g,
        low, ugrad, lay, spa, lay_r, spa_r,
        term_give, term_got, out_got, ffg, ff_r,
        middle, prob, hot, own, att, rw, wo, vec, flow_t, flow_1,
        send_sem, recv_sem, load_sem, out_sem,
    ) = refs[28:]
    c = lax.axis_index("dp")
    i = lax.axis_index("ctx")
    g, t = lax.div(i, team), lax.rem(i, team)
    width = second.shape[1]
    rows = lay.shape[1]
    hid, ehid = upw.shape[1], eup.shape[1]
    core = lax.rem(c + 1, two)

    def device(step):
        if not isinstance(step, tuple):
            return c, step * team + t
        dc, dg, dt = step
        return (
            lax.rem(c + dc, two),
            lax.rem(g + dg, groups) * team + lax.rem(t + dt, team),
        )

    index = [0]

    def remote(src, dst, step):
        k = index[0]
        index[0] += 1
        assert k < copies_count
        return pltpu.make_async_remote_copy(
            src_ref=src,
            dst_ref=dst,
            send_sem=send_sem.at[k],
            recv_sem=recv_sem.at[k],
            device_id=device(step),
            device_id_type=MESH,
        )

    group_steps = [(0, k, 0) for k in range(1, groups)]
    team_steps = [(0, 0, k) for k in range(1, team)]
    swap = (1, 0, 0)
    deep = ff_h.shape[2]

    def block_of(core, k):
        return pl.ds(pl.multiple_of((core * groups + k) * deep, deep), deep)

    loads = []
    for k, (src, dst) in enumerate(
        [(second_h, second), (dgrad_h, dgrad)]
        + [
            (ff_h.at[k, n], weight.at[block_of(c, k), :])
            for n, weight in enumerate((upw, downw))
            for k in range(groups)
        ]
        + [
            (send_s.at[g], arr_s.at[c, g]), (eup_h, eup), (edown_h, edown),
            (send_g.at[g], arr_g.at[c, g]), (sel_h, sel), (cot_h, cot),
            (middle_h, middle), (prob_h, prob), (hot_h, hot), (own_h, own),
            (att_h, att), (rw_h, rw), (wo_h, wo), (vec_h, vec),
        ]
    ):
        load = pltpu.make_async_copy(src, dst, load_sem.at[k])
        load.start()
        loads.append(load)

    barrier = pltpu.get_barrier_semaphore()
    home_steps = [
        (0, dg, dt) for dg in range(groups) for dt in range(team) if dg or dt
    ]
    greet = home_steps + [swap]
    for step in greet:
        pl.semaphore_signal(barrier, inc=1, device_id=device(step), device_id_type=MESH)
    pl.semaphore_wait(barrier, len(greet))

    every = []

    def launch(copy):
        copy.start()
        every.append(copy)
        return copy

    each = arr_s.shape[2] // team

    def to_home(src, dst):
        me = g * team + t
        made = []
        for s in home_steps:
            to_g, to_t = lax.rem(g + s[1], groups), lax.rem(t + s[2], team)
            made.append(launch(remote(src.at[to_g, span(to_t, each), :], dst.at[me], s)))
        dst[me] = src[g, span(t, each), :]
        return made

    def source(s):
        return lax.rem(g + groups - s[1], groups)

    swap_w = [
        launch(remote(ff_h.at[k, n], weight.at[block_of(c, k), :], swap))
        for k in range(groups)
        for n, weight in enumerate((upw, downw))
    ]
    out_s = [
        launch(remote(send_s.at[lax.rem(g + s[1], groups)], arr_s.at[c, g], s))
        for s in group_steps
    ]
    swap_s = [launch(remote(send_s.at[g], arr_s.at[c, g], swap))]
    dense_loads = 2 + 2 * groups
    for load in loads[:dense_loads]:
        load.wait()
    for copy in swap_w:
        copy.wait_recv()

    def dense_in(h, carry):
        at = span(h, TILE)
        value, bend = gelu_and_slope(dot_f32(second[...], upw[:, at]))
        low[:, at] = value.astype(BF)
        ugrad[:, at] = (bend * contract_cols(dgrad[...], downw[at, :])).astype(BF)
        return carry

    lax.fori_loop(0, hid // TILE, dense_in, 0)
    out_g = [
        launch(remote(send_g.at[lax.rem(g + s[1], groups)], arr_g.at[c, g], s))
        for s in group_steps
    ]
    swap_g = [launch(remote(send_g.at[g], arr_g.at[c, g], swap))]

    def dense_out(n, carry):
        at = span(n, TILE)
        made = dot_f32(low[...], downw[:, at])
        lay[:, :, at] = made.astype(BF).reshape(team, rows, TILE)
        made = contract_cols(ugrad[...], upw[at, :])
        spa[:, :, at] = made.astype(BF).reshape(team, rows, TILE)
        return carry

    lax.fori_loop(0, width // TILE, dense_out, 0)

    def to_team(src, dst):
        made = [launch(remote(src.at[lax.rem(t + s[2], team)], dst.at[t], s)) for s in team_steps]
        dst[t] = src[t]
        return made

    team_copies = to_team(lay, lay_r) + to_team(spa, spa_r)

    for load in loads[dense_loads : dense_loads + 4]:
        load.wait()
    for copy, s in zip(out_s, group_steps):
        copy.wait_recv()
        swap_s.append(launch(remote(arr_s.at[c, source(s)], arr_s.at[c, source(s)], swap)))
    for copy in swap_s:
        copy.wait_recv()
    entries = 2 * groups * arr_s.shape[2]

    def expert_in(h, carry):
        at = span(h, TILE)
        value, bend = gelu_and_slope(dot_f32(arr_s[...].reshape(entries, width), eup[:, at]))
        active[:, at] = value.astype(BF)
        slope[:, at] = bend
        return carry

    lax.fori_loop(0, ehid // TILE, expert_in, 0)
    keeps = [
        pltpu.make_async_copy(active, active_o, out_sem.at[0]),
        pltpu.make_async_copy(arr_s, arr_s_o, out_sem.at[1]),
    ]
    for copy in keeps:
        copy.start()

    def expert_out(n, carry):
        at = span(n, TILE)
        acc[:, :, at] = dot_f32(active[...], edown[:, at]).reshape(2, entries // 2, TILE)
        return carry

    lax.fori_loop(0, width // TILE, expert_out, 0)
    give[0] = acc[core].astype(BF)
    other_s = launch(remote(give.at[0], got_s, swap))

    for copy, s in zip(out_g, group_steps):
        copy.wait_recv()
        swap_g.append(launch(remote(arr_g.at[c, source(s)], arr_g.at[c, source(s)], swap)))
    other_s.wait_recv()
    ret_s[...] = (acc[c] + got_s[...].astype(F32)).astype(BF).reshape(ret_s.shape)
    home_s = to_home(ret_s, back_s)
    for copy in swap_g:
        copy.wait_recv()

    def expert_back(h, carry):
        at = span(h, TILE)
        pull = contract_cols(arr_g[...].reshape(entries, width), edown[at, :])
        hgrad[:, at] = (slope[:, at] * pull).astype(BF)
        return carry

    lax.fori_loop(0, ehid // TILE, expert_back, 0)
    keeps += [
        pltpu.make_async_copy(hgrad, hgrad_o, out_sem.at[2]),
        pltpu.make_async_copy(arr_g, arr_g_o, out_sem.at[3]),
    ]
    for copy in keeps[2:]:
        copy.start()

    def expert_back_out(n, carry):
        at = span(n, TILE)
        acc[:, :, at] = contract_cols(hgrad[...], eup[at, :]).reshape(2, entries // 2, TILE)
        return carry

    lax.fori_loop(0, width // TILE, expert_back_out, 0)
    give[1] = acc[core].astype(BF)
    other_g = launch(remote(give.at[1], got_g, swap))
    other_g.wait_recv()
    ret_g[...] = (acc[c] + got_g[...].astype(F32)).astype(BF).reshape(ret_g.shape)
    home_g = to_home(ret_g, back_g)

    half = hid // 2
    term_tile = 128

    def down_term(base, n):
        at = pl.ds(pl.multiple_of(base + n * term_tile, term_tile), term_tile)
        return contract_rows(low[:, at], dgrad[...])

    def up_term(base, n):
        at = pl.ds(pl.multiple_of(base + n * term_tile, term_tile), term_tile)
        return contract_rows(second[:, at], ugrad[...])

    terms = []
    for k, (term, size) in enumerate(((down_term, half), (up_term, width // 2))):

        def giving(n, carry, k=k, term=term, size=size):
            term_give[k, span(n, term_tile), :] = term(core * size, n).astype(BF)
            return carry

        lax.fori_loop(0, size // term_tile, giving, 0)
        terms.append(launch(remote(term_give.at[k], term_got.at[k], swap)))
    for k, (term, size) in enumerate(((down_term, half), (up_term, width // 2))):
        terms[k].wait_recv()

        def keeping(n, carry, k=k, term=term, size=size):
            at = span(n, term_tile)
            total = term(c * size, n) + term_got[k, at, :].astype(F32)
            ffg[k, at, :] = total.astype(BF)
            return carry

        lax.fori_loop(0, size // term_tile, keeping, 0)
    up_copy = pltpu.make_async_copy(ffg.at[1], up_o, out_sem.at[4])
    up_copy.start()

    for load in loads[dense_loads + 4 :]:
        load.wait()
    for copy in team_copies + home_s:
        copy.wait_recv()
    lane = lax.broadcasted_iota(jnp.int32, (rows, 128), 1)
    places = groups * team * each
    chances, chosen = prob[...], hot[...]
    mix0 = jnp.sum(jnp.where(lane == experts, chances, 0.0), axis=1, keepdims=True)
    mix1 = jnp.sum(jnp.where(lane == experts + 1, chances, 0.0), axis=1, keepdims=True)
    gate = jnp.sum(chances * chosen, axis=1, keepdims=True)
    flow = cot[...].astype(F32)
    plain = jnp.sum(lay_r[...].astype(F32), axis=0)
    found = dot_f32(sel[...], back_s[...].reshape(places, width))
    layer_o[...] = (middle[...] + mix0 * plain + (mix1 * gate) * found).astype(BF)
    s0 = jnp.sum(flow * plain, axis=1, keepdims=True)
    s1 = jnp.sum(flow * found, axis=1, keepdims=True)
    pulls = jnp.where(lane == experts, s0, jnp.where(lane == experts + 1, s1 * gate, 0.0))
    mean_pull = jnp.sum(chances * pulls, axis=1, keepdims=True)
    logit_grad = chances * jnp.where(
        lane < experts, (s1 * mix1) * (chosen - gate), pulls - mean_pull
    )
    logit_grad = jnp.where(lane < experts + 2, logit_grad, 0.0).astype(BF)
    hat, scale = normalize(middle[...])
    early = jnp.sum(spa_r[...].astype(F32), axis=0) + contract_cols(logit_grad, rw[...])
    for copy in home_g:
        copy.wait_recv()
    piece = half // groups

    def other_group(bit, group):
        return group + bit - 2 * bit * lax.rem(lax.div(group, bit), 2)

    near, far = other_group(1, g), other_group(2, g)
    last = other_group(2, near)
    for_far = launch(remote(ffg.at[0, span(last, piece), :], ff_r.at[0], near))
    downs = [launch(remote(ffg.at[0, span(near, piece), :], ff_r.at[1], near))]

    second_grad = early + dot_f32(sel[...], back_g[...].reshape(places, width))
    pull = second_grad * vec[5:6, :]
    moved = scale * (
        pull
        - jnp.mean(pull, axis=-1, keepdims=True)
        - hat * jnp.mean(pull * hat, axis=-1, keepdims=True)
    )
    middle_grad = flow + moved
    middle_o[...] = middle_grad
    branch = middle_grad.astype(BF)

    for n in range(team):
        at = slice(n * (width // team), (n + 1) * (width // team))
        flow_t[n] = contract_cols(wo[at, :], branch).astype(BF).reshape(flow_t.shape[1:])
    flowed = [
        launch(remote(flow_t.at[lax.rem(t + s[2], team)], flow_1.at[t], s)) for s in team_steps
    ]
    flow_1[t] = flow_t[t]

    def out_term(base, n):
        at = pl.ds(pl.multiple_of(base + n * term_tile, term_tile), term_tile)
        return dot_f32(att[at, :], branch)

    def out_giving(n, carry):
        term_give[0, span(n, term_tile), :] = out_term(core * (width // 2), n).astype(BF)
        return carry

    terms[0].wait_send()
    every[:] = [copy for copy in every if copy is not terms[0]]
    lax.fori_loop(0, width // 2 // term_tile, out_giving, 0)
    out_cross = launch(remote(term_give.at[0], out_got, swap))
    for copy in flowed:
        copy.wait_recv()
    flowed = [
        launch(remote(flow_1.at[:, lax.rem(g + s[1], groups)], flow_o.at[g], s))
        for s in group_steps
    ]
    own_flow = pltpu.make_async_copy(flow_1.at[:, g], flow_o.at[g], out_sem.at[5])
    own_flow.start()
    for_far.wait_recv()
    ff_r[3] = (ffg[0, span(far, piece), :].astype(F32) + ff_r[0].astype(F32)).astype(BF)
    downs.append(launch(remote(ff_r.at[3], ff_r.at[2], far)))
    out_cross.wait_recv()
    wr = out_o.shape[2]

    def out_keeping(n, carry):
        at = span(n, term_tile)
        total = out_term(c * (width // 2), n) + out_got[at, :].astype(F32)
        out_o[:, n] = total.astype(BF).reshape(team, wr, width)
        return carry

    lax.fori_loop(0, groups, out_keeping, 0)

    routed = contract_rows(logit_grad, own[...])[: small_o.shape[0], :]
    which = lax.broadcasted_iota(jnp.int32, routed.shape, 0)
    gain = jnp.sum(second_grad * hat, axis=0, keepdims=True)
    bias = jnp.sum(second_grad, axis=0, keepdims=True)
    small_o[...] = jnp.where(
        which == experts + 3, gain, jnp.where(which == experts + 5, bias, routed)
    )
    for copy in downs:
        copy.wait_recv()
    down_o[...] = (
        ffg[0, span(g, piece), :].astype(F32) + ff_r[1].astype(F32) + ff_r[2].astype(F32)
    )
    for copy in flowed:
        copy.wait_recv()
    for copy in keeps + [up_copy, own_flow]:
        copy.wait()
    for copy in every:
        copy.wait_send()


def whole(
    sizes, rows, experts, wr, send_s, send_g, eup, edown, second, dgrad, ff, sel, cot,
    middle, prob, hot, own, att, rw, wo, vec,
):
    two, groups, team = sizes
    slots = send_s.shape[1]
    width = second.shape[1]
    hid, ehid = ff.shape[3], eup.shape[1]
    entries = 2 * groups * slots
    used = -(-(experts + 6) // 8) * 8
    homes = groups * team - 1
    count = 3 * (groups - 1) + 4 * groups + 5 + 3 * (team - 1) + 2 * homes + 3
    each = slots // team
    arrived = (two, groups, slots, width)
    anywhere = pl.BlockSpec(memory_space=pl.ANY)
    inside = pl.BlockSpec(memory_space=pltpu.VMEM)
    team_rows = team * rows
    heads = (groups, HEAD_DIM, rows)
    shapes = (
        ((rows, width), BF),
        ((rows, width), F32),
        ((used, width), F32),
        ((groups, team, HEAD_DIM, rows), BF),
        ((team, groups, wr, width), BF),
        ((hid // 2 // groups, width), F32),
        ((width // 2, hid), BF),
        ((entries, ehid), BF),
        ((entries, ehid), BF),
        (arrived, BF),
        (arrived, BF),
    )
    scratch = (
        (arrived, BF), (arrived, BF), (eup.shape, BF), (edown.shape, BF), (second.shape, BF),
        (dgrad.shape, BF), ((width, hid), BF), ((hid, width), BF), (sel.shape, BF),
        (cot.shape, BF),
        ((entries, ehid), F32), ((entries, ehid), BF), ((entries, ehid), BF),
        ((2, entries // 2, width), F32), ((2, entries // 2, width), BF),
        ((entries // 2, width), BF), ((entries // 2, width), BF),
        ((groups, slots, width), BF), ((groups, slots, width), BF),
        ((groups * team, each, width), BF), ((groups * team, each, width), BF),
        ((team_rows, hid), BF), ((team_rows, hid), BF),
        ((team, rows, width), BF), ((team, rows, width), BF),
        ((team, rows, width), BF), ((team, rows, width), BF),
        ((2, hid // 2, width), BF), ((2, hid // 2, width), BF), ((width // 2, width), BF),
        ((2, hid // 2, width), BF),
        ((groups, hid // 2 // groups, width), BF),
        (middle.shape, F32), (prob.shape, F32), (hot.shape, F32), (own.shape, BF),
        (att.shape, BF), (rw.shape, BF), (wo.shape, BF), (vec.shape, F32),
        ((team,) + heads, BF), ((team,) + heads, BF),
    )
    return pl.pallas_call(
        functools.partial(whole_kernel, sizes, experts, count),
        name="feed_forward",
        out_shape=tuple(jax.ShapeDtypeStruct(s, d) for s, d in shapes),
        in_specs=[anywhere] * 17,
        out_specs=tuple(inside if n in (0, 1, 2, 4, 5) else anywhere for n in range(11)),
        scratch_shapes=[pltpu.VMEM(s, d) for s, d in scratch]
        + [
            pltpu.SemaphoreType.DMA((count,)),
            pltpu.SemaphoreType.DMA((count,)),
            pltpu.SemaphoreType.DMA((16 + 2 * groups,)),
            pltpu.SemaphoreType.DMA((6,)),
        ],
        compiler_params=pltpu.CompilerParams(
            collective_id=14, has_side_effects=True, vmem_limit_bytes=60 * 2**20
        ),
        cost_estimate=pl.CostEstimate(flops=0, bytes_accessed=300_000_000, transcendentals=0),
    )(
        send_s, send_g, eup, edown, second, dgrad, ff, sel, cot,
        middle, prob, hot, own, att, rw, wo, vec,
    )


def deliver_kernel(experts, count, shift, small, *refs):
    ins, outs = refs[:count], refs[count : 2 * count]
    router, vectors = refs[2 * count : 2 * count + 2]
    sem = refs[2 * count + 2]
    copies = [pltpu.make_async_copy(a, b, sem.at[n]) for n, (a, b) in enumerate(zip(ins, outs))]
    for copy in copies:
        copy.start()
    wr = router.shape[1]
    mine = pltpu.roll(small[...], lax.rem(128 - shift[0], 128), 1)[:, :wr]
    router[...] = mine[: experts + 2, :]
    vectors[...] = mine[experts + 2 : experts + 6, :]
    for copy in copies:
        copy.wait()


def deliver(experts, shift, small, arrays):
    wr = arrays[2].shape[0]
    anywhere = pl.BlockSpec(memory_space=pl.ANY)
    inside = pl.BlockSpec(memory_space=pltpu.VMEM)
    count = len(arrays)
    return pl.pallas_call(
        functools.partial(deliver_kernel, experts, count),
        name="deliver",
        in_specs=[pl.BlockSpec(memory_space=pltpu.SMEM)] + [inside] * (count + 1),
        out_specs=tuple([anywhere] * count + [inside] * 2),
        out_shape=tuple(jax.ShapeDtypeStruct(a.shape, a.dtype) for a in arrays)
        + (
            jax.ShapeDtypeStruct((experts + 2, wr), F32),
            jax.ShapeDtypeStruct((4, wr), F32),
        ),
        scratch_shapes=[pltpu.SemaphoreType.DMA((count,))],
        compiler_params=pltpu.CompilerParams(vmem_limit_bytes=60 * 2**20),
    )(shift, small, *arrays)


def per_device(
    tokens,
    cotangent,
    block_order,
    doc_lengths,
    routes,
    w_qkv,
    w_out,
    w_up,
    w_down,
    router,
    norm_gains,
    norm_biases,
    expert_up,
    expert_down,
):
    rows, width = tokens.shape[1], tokens.shape[2]
    ctx_count = lax.axis_size("ctx")
    two = lax.axis_size("dp")
    team = math.gcd(4, ctx_count)
    groups = ctx_count // team
    sizes = (two, groups, team)
    length = rows * ctx_count
    wr = w_qkv.shape[0]
    experts = ctx_count * expert_up.shape[0]
    fits = groups == team == 4 and groups * team == HEADS and team * wr == 128 and w_up.shape[1] == team * width
    if not fits or length // block_order.shape[0] != BLOCK:
        return per_device_general(
            tokens, cotangent, block_order, doc_lengths, routes, w_qkv, w_out, w_up, w_down,
            router, norm_gains, norm_biases, expert_up, expert_down,
        )
    group_rows = rows * team
    capacity = max(2, 2 * rows // experts)
    slots = team * capacity
    hidden = w_up.shape[1]
    hidden_dev = w_down.shape[0]
    up_cols = hidden // team
    ctx = lax.axis_index("ctx")
    core = lax.axis_index("dp")
    group, member = lax.div(ctx, team), lax.rem(ctx, team)
    by_group = [[g * team + t for g in range(groups)] for t in range(team)]
    team_steps = [(0, 0, k) for k in range(1, team)]

    router_cols = router.shape[1]
    (
        token_rows,
        cot_rows,
        head_parts,
        normed,
        weights,
        vectors,
        out_weight,
        ff_part,
        route_all,
        router_weight,
    ) = start(
        sizes,
        tokens[0],
        cotangent[0],
        w_qkv,
        w_up,
        w_down,
        w_out,
        router.T,
        norm_gains,
        norm_biases,
        routes[0].reshape(1, rows),
    )
    out_weight = out_weight.reshape(width, width)
    token_rows = token_rows.reshape(group_rows, width)
    cot_rows = cot_rows.reshape(group_rows, width)

    ff_half = lax.all_gather(
        ff_part.reshape(2, team * wr, width),
        "ctx",
        axis=0,
        tiled=False,
        axis_index_groups=by_group,
    )
    low_t, attention_t, log_total, q_pad, kv_t, kv_rows = sorted_attend(
        doc_lengths[0], block_order, head_parts.reshape(groups, 3 * HEAD_DIM, group_rows)
    )

    def gather_heads(coords, ins, outs):
        c, g, t = coords
        steps = [(0, k, 0) for k in range(1, groups)]
        moves = [Move(s, ins[0].at[lax.rem(g + s[1], groups)], outs[0].at[t, g]) for s in steps]
        local = [(ins[0].at[g], outs[0].at[t, g])]
        for s in team_steps:
            moves.append(Move(s, ins[0].at[g], outs[0].at[t, g]))
        for k, s in enumerate(steps):
            source = lax.rem(g + groups - s[1], groups)
            for e in team_steps:
                moves.append(Move(e, outs[0].at[t, source], outs[0].at[t, source], after=k))
        return local, moves

    [attended] = exchange(
        "attended",
        4,
        sizes,
        (low_t,),
        [((team, groups, HEAD_DIM, group_rows), BF)],
        gather_heads,
    )
    (
        second_low,
        dense_grad,
        send_s,
        send_g,
        select,
        mixes,
        middle_own,
        prob_own,
        hot_own,
        second_own,
        attended_own,
        select_own,
    ) = between(
        experts,
        sizes,
        slots,
        member[None],
        attended.reshape(width, group_rows),
        out_weight,
        token_rows,
        vectors,
        router_weight,
        route_all,
        cot_rows,
    )
    (
        layer_out,
        middle_grad,
        small_t,
        flow_parts,
        out_half,
        down_sum,
        up_half,
        expert_active,
        hidden_grad,
        arrived_in,
        arrived_grad,
    ) = whole(
        sizes,
        rows,
        experts,
        wr,
        send_s,
        send_g,
        expert_up[0],
        expert_down[0],
        second_low,
        dense_grad,
        ff_half,
        select_own,
        cotangent[0],
        middle_own,
        prob_own,
        hot_own,
        second_own,
        attended_own,
        router_weight,
        out_weight,
        vectors,
    )

    def pieces_of(array, along):
        count = groups if along == "g" else team
        me = group if along == "g" else member
        found = [lax.dynamic_index_in_dim(array, me, 0, keepdims=False)]
        for step in range(1, count):
            if along == "g":
                pairs = [
                    (g * team + t, (g + step) % groups * team + t)
                    for g in range(groups)
                    for t in range(team)
                ]
            else:
                pairs = [
                    (g * team + t, g * team + (t + step) % team)
                    for g in range(groups)
                    for t in range(team)
                ]
            chunk = lax.dynamic_index_in_dim(array, lax.rem(me + step, count), 0, keepdims=False)
            found.append(lax.ppermute(chunk, "ctx", pairs))
        return found

    up_sum = lax.psum_scatter(
        up_half, "ctx", scatter_dimension=0, tiled=True, axis_index_groups=by_group
    ).reshape(team, wr, up_cols)
    out_pieces = pieces_of(out_half, "t")
    grad_parts = sorted_back(
        doc_lengths[0],
        block_order,
        flow_parts.reshape(ctx_count, HEAD_DIM, rows),
        attention_t,
        log_total,
        q_pad,
        kv_t,
        kv_rows,
        groups,
    )

    grad_parts, expert_active, hidden_grad = lax.optimization_barrier(
        (grad_parts, expert_active, hidden_grad)
    )

    pieces = pieces_of(grad_parts, "g")
    out_sum = sum(piece.astype(F32) for piece in out_pieces).astype(BF)
    entries = two * groups * slots
    expert_down_grad = row_sum(expert_active, arrived_grad.reshape(entries, width), TILE)
    expert_up_grad = row_sum(arrived_in.reshape(entries, width), hidden_grad, 128)
    input_grad, qkv_own, up_own, out_own, small_own = end(
        sizes,
        experts,
        pieces,
        weights,
        normed,
        tokens[0],
        vectors,
        middle_grad,
        small_t,
        up_sum,
        out_sum,
    )
    delivered = deliver(
        experts,
        member[None] * wr,
        small_own,
        (layer_out, input_grad, qkv_own, out_own, up_own, down_sum),
    )
    layer_out, input_grad, qkv_own, out_own, up_own, down_sum, router_own, vectors_own = delivered
    return (
        layer_out[None],
        input_grad[None],
        qkv_own,
        out_own,
        up_own,
        down_sum,
        router_own.T,
        vectors_own[:2],
        vectors_own[2:],
        expert_up_grad,
        expert_down_grad,
    )


def solution(mesh):
    in_specs = (
        P("dp", "ctx", None),
        P("dp", "ctx", None),
        P(),
        P("dp", None),
        P("dp", "ctx", None),
        P(("dp", "ctx"), None),
        P(("dp", "ctx"), None),
        P(("dp", "ctx"), None),
        P(("dp", "ctx"), None),
        P(("dp", "ctx"), None),
        P(None, ("dp", "ctx")),
        P(None, ("dp", "ctx")),
        P("ctx", None, "dp"),
        P("ctx", "dp", None),
    )
    out_specs = (
        P("dp", "ctx", None),
        P("dp", "ctx", None),
        P(("dp", "ctx"), None),
        P(("dp", "ctx"), None),
        P(("dp", "ctx"), None),
        P(("dp", "ctx"), None),
        P(("dp", "ctx"), None),
        P(None, ("dp", "ctx")),
        P(None, ("dp", "ctx")),
        P("ctx", None, "dp"),
        P("ctx", "dp", None),
    )
    return jax.shard_map(
        per_device, mesh=mesh, in_specs=in_specs, out_specs=out_specs, check_vma=False
    )
```

```python
import functools
import math

import jax
import jax.numpy as jnp
from jax import lax
from jax.experimental import pallas as pl
from jax.experimental.pallas import tpu as pltpu
from jax.sharding import PartitionSpec as P

HEADS = 16
HEAD_DIM = 64

EPS = 1e-05
NEG = -1e30
SCALE = 0.125
TILE = 256
BF = jnp.bfloat16
F32 = jnp.float32
MESH = pl.DeviceIdType.MESH


def layer_norm(values, gain, shift):
    center = values - jnp.mean(values, axis=-1, keepdims=True)
    spread = jnp.mean(center * center, axis=-1, keepdims=True)
    return center * lax.rsqrt(spread + EPS) * gain + shift


def gelu_tanh(values):
    return jax.nn.gelu(values, approximate=True)


def router_heads(router_logits, route_hot, experts):
    chances = jax.nn.softmax(router_logits[:, :experts], axis=-1)
    gate = jnp.sum(chances * route_hot, axis=-1)
    mixing = jax.nn.softmax(router_logits[:, experts:], axis=-1)
    return (gate, mixing[:, 0], mixing[:, 1])


def dot_f32(left, right):
    return jnp.dot(left, right, preferred_element_type=F32)


def contract_rows(left, right):
    return lax.dot_general(left, right, (((0,), (0,)), ((), ())), preferred_element_type=F32)


def contract_cols(left, right):
    return lax.dot_general(left, right, (((1,), (1,)), ((), ())), preferred_element_type=F32)


def span(i, size):
    return pl.ds(pl.multiple_of(i * size, size), size)


class Move:
    def __init__(self, step, src, dst, after=None):
        self.step, self.src, self.dst, self.after = step, src, dst, after


def exchange(name, cid, sizes, ins, outs, build, micros=20):
    two, groups, team = sizes

    def kernel(*refs):
        in_refs, out_refs = refs[: len(ins)], refs[len(ins) : len(ins) + len(outs)]
        send_sem, recv_sem, local_sem = refs[len(ins) + len(outs) :]
        c = lax.axis_index("dp")
        i = lax.axis_index("ctx")
        g, t = lax.div(i, team), lax.rem(i, team)

        def device(step):
            dc, dg, dt = step
            return (
                lax.rem(c + dc, two),
                lax.rem(g + dg, groups) * team + lax.rem(t + dt, team),
            )

        locals_, moves = build((c, g, t), in_refs, out_refs)
        steps = sorted({m.step for m in moves})
        greet = sorted(
            set(steps) | {((-a) % two, (-b) % groups, (-d) % team) for a, b, d in steps}
        )
        barrier = pltpu.get_barrier_semaphore()
        for step in greet:
            pl.semaphore_signal(barrier, inc=1, device_id=device(step), device_id_type=MESH)
        pl.semaphore_wait(barrier, len(greet))

        copies = {}
        arrived = set()
        for k, (src, dst) in enumerate(locals_):
            copies[("local", k)] = pltpu.make_async_copy(src, dst, local_sem.at[k])
        for k, m in enumerate(moves):
            copies[k] = pltpu.make_async_remote_copy(
                src_ref=m.src,
                dst_ref=m.dst,
                send_sem=send_sem.at[k],
                recv_sem=recv_sem.at[k],
                device_id=device(m.step),
                device_id_type=MESH,
            )
        for k, m in enumerate(moves):
            if m.after is None:
                copies[k].start()
        for k in range(len(locals_)):
            copies[("local", k)].start()
        for k, m in enumerate(moves):
            if m.after is not None:
                if m.after not in arrived:
                    arrived.add(m.after)
                    if isinstance(m.after, tuple):
                        copies[m.after].wait()
                    else:
                        copies[m.after].wait_recv()
                copies[k].start()
        for k in range(len(locals_)):
            if ("local", k) not in arrived:
                copies[("local", k)].wait()
        for k in range(len(moves)):
            if k not in arrived:
                copies[k].wait_recv()
        for k in range(len(moves)):
            copies[k].wait_send()

    count = []

    def trace_counts():
        class Probe:
            def __getattr__(self, name):
                return self

            def __getitem__(self, index):
                return self

        locals_, moves = build((0, 0, 0), [Probe() for _ in ins], [Probe() for _ in outs])
        count.extend((len(locals_), len(moves)))

    trace_counts()
    return pl.pallas_call(
        kernel,
        name=name,
        out_shape=tuple(jax.ShapeDtypeStruct(s, d) for s, d in outs),
        in_specs=[pl.BlockSpec(memory_space=pl.ANY)] * len(ins),
        out_specs=tuple(pl.BlockSpec(memory_space=pl.ANY) for _ in outs),
        scratch_shapes=[
            pltpu.SemaphoreType.DMA((max(1, count[1]),)),
            pltpu.SemaphoreType.DMA((max(1, count[1]),)),
            pltpu.SemaphoreType.DMA((max(1, count[0]),)),
        ],
        compiler_params=pltpu.CompilerParams(collective_id=cid, has_side_effects=True),
        cost_estimate=pl.CostEstimate(
            flops=0, bytes_accessed=int(micros * 3.0e6), transcendentals=0
        ),
    )(*ins)


def mask_of(kt, key_place, query_place, query_low):
    return (key_place <= query_place) & (key_place >= query_low)


def key_places(sorted_rows, kt, place_ref):
    if sorted_rows:
        return lax.broadcasted_iota(jnp.int32, (TILE, TILE), 0) + kt * TILE
    return place_ref[pl.ds(pl.multiple_of(kt * TILE, TILE), TILE), :]


def attend_kernel(
    sorted_rows, bounds, meta_ref, place_ref, q_ref, rows_ref, kvt_ref, out_ref, lse_ref
):
    step = pl.program_id(0)
    queries = q_ref[...]
    place, low = meta_ref[0:1, :], meta_ref[1:2, :]

    def body(kt, carry):
        peak, total, acc = carry
        at = pl.ds(pl.multiple_of(kt * TILE, TILE), TILE)
        scores = dot_f32(rows_ref[at, :], queries)
        allowed = mask_of(kt, key_places(sorted_rows, kt, place_ref), place, low)
        scores = jnp.where(allowed, scores, NEG)
        new_peak = jnp.maximum(peak, jnp.max(scores, axis=0, keepdims=True))
        weights = jnp.exp(scores - new_peak)
        fade = jnp.exp(peak - new_peak)
        total = total * fade + jnp.sum(weights, axis=0, keepdims=True)
        acc = acc * fade + dot_f32(kvt_ref[HEAD_DIM:, at], weights.astype(BF))
        return new_peak, total, acc

    start = (
        jnp.full((1, TILE), NEG, F32),
        jnp.zeros((1, TILE), F32),
        jnp.zeros((HEAD_DIM, TILE), F32),
    )
    peak, total, acc = lax.fori_loop(bounds[step, 0], bounds[step, 1], body, start)
    out_ref[...] = acc / total
    lse_ref[...] = peak + jnp.log(total)


def attend_back_kernel(
    sorted_rows,
    tiles,
    bounds,
    meta_ref,
    place_ref,
    q_ref,
    do_ref,
    out_ref,
    lse_ref,
    rows_ref,
    kvt_ref,
    dq_ref,
    dkv_ref,
    acc_ref,
):
    step = pl.program_id(0)

    @pl.when(step == 0)
    def _():
        acc_ref[...] = jnp.zeros_like(acc_ref)

    queries, flows = q_ref[...], do_ref[...]
    place, low = meta_ref[0:1, :], meta_ref[1:2, :]
    log_total = lse_ref[...]
    delta = jnp.sum(flows[HEAD_DIM:, :].astype(F32) * out_ref[...], axis=0, keepdims=True)

    def body(kt, dq):
        at = pl.ds(pl.multiple_of(kt * TILE, TILE), TILE)
        rows = rows_ref[at, :]
        scores = dot_f32(rows, queries)
        allowed = mask_of(kt, key_places(sorted_rows, kt, place_ref), place, low)
        chances = jnp.exp(jnp.where(allowed, scores - log_total, NEG))
        flow = dot_f32(rows, flows)
        score_grad = (chances * (flow - delta)).astype(BF)
        dq = dq + dot_f32(kvt_ref[:HEAD_DIM, at], score_grad)
        acc_ref[:HEAD_DIM, at] += contract_cols(queries[:HEAD_DIM, :], score_grad)
        acc_ref[HEAD_DIM:, at] += contract_cols(flows[HEAD_DIM:, :], chances.astype(BF))
        return dq

    dq = lax.fori_loop(
        bounds[step, 0], bounds[step, 1], body, jnp.zeros((HEAD_DIM, TILE), F32)
    )
    dq_ref[...] = (dq * SCALE).astype(BF)

    @pl.when(step == tiles - 1)
    def _():
        dkv_ref[...] = acc_ref[...].astype(BF)


def attention_specs(length, query_length):
    def whole(shape):
        return pl.BlockSpec(shape, lambda i: (0, 0))

    def tile(rows):
        return pl.BlockSpec((rows, TILE), lambda i: (0, i))

    return whole, tile


def attend(sorted_rows, bounds, meta, place_col, q_pad, kv_rows, kv_t):
    length, query_length = kv_rows.shape[0], q_pad.shape[1]
    whole, tile = attention_specs(length, query_length)
    return pl.pallas_call(
        functools.partial(attend_kernel, sorted_rows),
        name="attend",
        grid=(query_length // TILE,),
        in_specs=[
            pl.BlockSpec(memory_space=pltpu.SMEM),
            tile(8),
            whole(place_col.shape),
            tile(2 * HEAD_DIM),
            whole((length, 2 * HEAD_DIM)),
            whole((2 * HEAD_DIM, length)),
        ],
        out_specs=(tile(HEAD_DIM), tile(1)),
        out_shape=(
            jax.ShapeDtypeStruct((HEAD_DIM, query_length), F32),
            jax.ShapeDtypeStruct((1, query_length), F32),
        ),
        compiler_params=pltpu.CompilerParams(vmem_limit_bytes=40 * 2**20),
    )(bounds, meta, place_col, q_pad, kv_rows, kv_t)


def attend_back(sorted_rows, bounds, meta, place_col, q_pad, do_pad, out, lse, kv_rows, kv_t):
    length, query_length = kv_rows.shape[0], q_pad.shape[1]
    whole, tile = attention_specs(length, query_length)
    return pl.pallas_call(
        functools.partial(attend_back_kernel, sorted_rows, query_length // TILE),
        name="attend_back",
        grid=(query_length // TILE,),
        in_specs=[
            pl.BlockSpec(memory_space=pltpu.SMEM),
            tile(8),
            whole(place_col.shape),
            tile(2 * HEAD_DIM),
            tile(2 * HEAD_DIM),
            tile(HEAD_DIM),
            tile(1),
            whole((length, 2 * HEAD_DIM)),
            whole((2 * HEAD_DIM, length)),
        ],
        out_specs=(tile(HEAD_DIM), whole((2 * HEAD_DIM, length))),
        out_shape=(
            jax.ShapeDtypeStruct((HEAD_DIM, query_length), BF),
            jax.ShapeDtypeStruct((2 * HEAD_DIM, length), BF),
        ),
        scratch_shapes=[pltpu.VMEM((2 * HEAD_DIM, length), F32)],
        compiler_params=pltpu.CompilerParams(vmem_limit_bytes=40 * 2**20),
    )(bounds, meta, place_col, q_pad, do_pad, out, lse, kv_rows, kv_t)


BLOCK = 64


def pick_pair(load, table, d):
    first, second = table[2 * d], table[2 * d + 1]
    left = load(lax.div(first, 2))
    right = load(lax.div(second, 2))
    lane = lax.broadcasted_iota(jnp.int32, left.shape, 1)
    left = jnp.where(lax.rem(first, 2) == 0, left, pltpu.roll(left, BLOCK, 1))
    right = jnp.where(lax.rem(second, 2) == 1, right, pltpu.roll(right, BLOCK, 1))
    return jnp.where(lane < BLOCK, left, right)


def column_block(ref, k, per):
    return ref[lax.div(k, per), :, span(lax.rem(k, per), 128)].astype(F32)


def fill_inverse(order, inverse, count):
    def put(n, carry):
        inverse[order[n]] = n
        return carry

    lax.fori_loop(0, count, put, 0)


def query_lows(lengths, step):
    place = lax.broadcasted_iota(jnp.int32, (1, TILE), 1) + step * TILE
    low = jnp.zeros((1, TILE), jnp.int32)
    first, end = 0, 0
    for n in range(lengths.shape[0]):
        end = end + lengths[n]
        low = jnp.where(end <= place, end, low)
        first = jnp.where(end <= step * TILE, end, first)
    return place, low, lax.div(first, TILE)


def sorted_attend_kernel(
    lengths, order, parts_ref, low_ref, out_ref, lse_ref, q_ref, kvt_ref, rows_ref, inverse
):
    step = pl.program_id(0)
    length = q_ref.shape[1]
    per = parts_ref.shape[2] // 128

    @pl.when(step == 0)
    def _():
        fill_inverse(order, inverse, length // BLOCK)

        def place(d, carry):
            tile = pick_pair(lambda k: column_block(parts_ref, k, per), inverse, d)
            at = span(d, 128)
            q_ref[:HEAD_DIM, at] = (tile[:HEAD_DIM] * SCALE).astype(BF)
            q_ref[HEAD_DIM:, at] = jnp.zeros((HEAD_DIM, 128), BF)
            kvt_ref[:, at] = tile[HEAD_DIM:].astype(BF)
            rows_ref[at, :] = tile[HEAD_DIM:].T.astype(BF)
            return carry

        lax.fori_loop(0, length // 128, place, 0)

    here = span(step, TILE)
    queries = q_ref[:, here]
    place, low, first = query_lows(lengths, step)

    def body(kt, carry):
        peak, total, acc = carry
        at = span(kt, TILE)
        scores = dot_f32(rows_ref[at, :], queries)
        allowed = mask_of(kt, key_places(True, kt, None), place, low)
        scores = jnp.where(allowed, scores, NEG)
        new_peak = jnp.maximum(peak, jnp.max(scores, axis=0, keepdims=True))
        weights = jnp.exp(scores - new_peak)
        fade = jnp.exp(peak - new_peak)
        total = total * fade + jnp.sum(weights, axis=0, keepdims=True)
        acc = acc * fade + dot_f32(kvt_ref[HEAD_DIM:, at], weights.astype(BF))
        return new_peak, total, acc

    start = (
        jnp.full((1, TILE), NEG, F32),
        jnp.zeros((1, TILE), F32),
        jnp.zeros((HEAD_DIM, TILE), F32),
    )
    peak, total, acc = lax.fori_loop(first, step + 1, body, start)
    out_ref[:, here] = acc / total
    lse_ref[:, here] = peak + jnp.log(total)

    @pl.when(step == length // TILE - 1)
    def _():
        def home(d, carry):
            tile = pick_pair(lambda k: out_ref[:, span(k, 128)], order, d)
            low_ref[lax.div(d, per), :, span(lax.rem(d, per), 128)] = tile.astype(BF)
            return carry

        lax.fori_loop(0, length // 128, home, 0)


def sorted_back_kernel(
    lengths, order, flow_ref, out_ref, lse_ref, q_ref, kvt_ref, rows_ref,
    grad_ref, do_ref, dq_ref, acc_ref, inverse,
):
    step = pl.program_id(0)
    length = q_ref.shape[1]
    per = grad_ref.shape[3] // 128

    @pl.when(step == 0)
    def _():
        acc_ref[...] = jnp.zeros_like(acc_ref)
        fill_inverse(order, inverse, length // BLOCK)

        def place(d, carry):
            tile = pick_pair(lambda k: flow_ref[k].astype(F32), inverse, d)
            at = span(d, 128)
            do_ref[:HEAD_DIM, at] = jnp.zeros((HEAD_DIM, 128), BF)
            do_ref[HEAD_DIM:, at] = tile.astype(BF)
            return carry

        lax.fori_loop(0, length // 128, place, 0)

    here = span(step, TILE)
    queries, flows = q_ref[:, here], do_ref[:, here]
    place, low, first = query_lows(lengths, step)
    log_total = lse_ref[:, here]
    delta = jnp.sum(flows[HEAD_DIM:, :].astype(F32) * out_ref[:, here], axis=0, keepdims=True)

    def body(kt, dq):
        at = span(kt, TILE)
        rows = rows_ref[at, :]
        scores = dot_f32(rows, queries)
        allowed = mask_of(kt, key_places(True, kt, None), place, low)
        chances = jnp.exp(jnp.where(allowed, scores - log_total, NEG))
        flow = dot_f32(rows, flows)
        score_grad = (chances * (flow - delta)).astype(BF)
        dq = dq + dot_f32(kvt_ref[:HEAD_DIM, at], score_grad)
        acc_ref[:HEAD_DIM, at] += contract_cols(queries[:HEAD_DIM, :], score_grad)
        acc_ref[HEAD_DIM:, at] += contract_cols(flows[HEAD_DIM:, :], chances.astype(BF))
        return dq

    dq = lax.fori_loop(
        first, step + 1, body, jnp.zeros((HEAD_DIM, TILE), F32)
    )
    dq_ref[:, here] = dq * SCALE

    @pl.when(step == length // TILE - 1)
    def _():
        def home(d, carry):
            at = span(lax.rem(d, per), 128)
            tile = pick_pair(lambda k: dq_ref[:, span(k, 128)], order, d)
            grad_ref[lax.div(d, per), 0, :, at] = tile.astype(BF)
            tile = pick_pair(lambda k: acc_ref[:, span(k, 128)], order, d).astype(BF)
            grad_ref[lax.div(d, per), 1, :, at] = tile[:HEAD_DIM]
            grad_ref[lax.div(d, per), 2, :, at] = tile[HEAD_DIM:]
            return carry

        lax.fori_loop(0, length // 128, home, 0)


def fixed(shape):
    return pl.BlockSpec(shape, lambda i: (0,) * len(shape))


def sorted_attend(lengths, order, parts):
    groups, _, columns = parts.shape
    length = groups * columns
    shapes = (
        ((groups, HEAD_DIM, columns), BF),
        ((HEAD_DIM, length), F32),
        ((1, length), F32),
        ((2 * HEAD_DIM, length), BF),
        ((2 * HEAD_DIM, length), BF),
        ((length, 2 * HEAD_DIM), BF),
    )
    return pl.pallas_call(
        sorted_attend_kernel,
        name="attend",
        grid=(length // TILE,),
        in_specs=[pl.BlockSpec(memory_space=pltpu.SMEM)] * 2 + [fixed(parts.shape)],
        out_specs=tuple(fixed(s) for s, _ in shapes),
        out_shape=tuple(jax.ShapeDtypeStruct(s, d) for s, d in shapes),
        scratch_shapes=[pltpu.SMEM((length // BLOCK,), jnp.int32)],
        compiler_params=pltpu.CompilerParams(vmem_limit_bytes=60 * 2**20),
        cost_estimate=pl.CostEstimate(
            flops=0, bytes_accessed=42_000_000, transcendentals=0
        ),
    )(lengths, order, parts)


def sorted_back(lengths, order, flow, out, lse, q_pad, kv_t, kv_rows, groups):
    length = out.shape[1]
    grad = (groups, 3, HEAD_DIM, length // groups)
    return pl.pallas_call(
        sorted_back_kernel,
        name="attend_back",
        grid=(length // TILE,),
        in_specs=[pl.BlockSpec(memory_space=pltpu.SMEM)] * 2
        + [fixed(a.shape) for a in (flow, out, lse, q_pad, kv_t, kv_rows)],
        out_specs=fixed(grad),
        out_shape=jax.ShapeDtypeStruct(grad, BF),
        scratch_shapes=[
            pltpu.VMEM((2 * HEAD_DIM, length), BF),
            pltpu.VMEM((HEAD_DIM, length), F32),
            pltpu.VMEM((2 * HEAD_DIM, length), F32),
            pltpu.SMEM((length // BLOCK,), jnp.int32),
        ],
        compiler_params=pltpu.CompilerParams(vmem_limit_bytes=40 * 2**20),
        cost_estimate=pl.CostEstimate(
            flops=0, bytes_accessed=42_000_000, transcendentals=0
        ),
    )(lengths, order, flow, out, lse, q_pad, kv_t, kv_rows)


def normalize(values):
    center = values - jnp.mean(values, axis=-1, keepdims=True)
    spread = jnp.mean(center * center, axis=-1, keepdims=True)
    scale = lax.rsqrt(spread + EPS)
    return center * scale, scale


def mid_kernel(
    experts, team, member, att, wo, x, vec, rw, route, cot,
    second, dgrad, send_s, send_g, sel, mixes, middle_own, prob_own, hot_own, second_own, att_own, sel_own,
    egrad,
):
    rows = middle_own.shape[0]
    slots = send_s.shape[1]
    groups = send_s.shape[0]
    capacity = slots // team
    lane = lax.broadcasted_iota(jnp.int32, (rows, 128), 1)
    row = lax.broadcasted_iota(jnp.int32, (rows, rows), 0)
    col = lax.broadcasted_iota(jnp.int32, (rows, rows), 1)
    me = member[0]

    def block(b, carry):
        at = span(b, rows)
        part = att[:, at]
        middle = x[at, :].astype(F32) + contract_rows(part, wo[...])
        hat, _ = normalize(middle)
        low = (hat * vec[5:6, :] + vec[7:8, :]).astype(BF)
        second[at, :] = low
        logits = dot_f32(low, rw[...])
        is_expert = lane < experts
        is_mix = (lane >= experts) & (lane < experts + 2)
        pe = jnp.where(is_expert, logits, NEG)
        pe = jnp.exp(pe - jnp.max(pe, axis=1, keepdims=True))
        pe = pe / jnp.sum(pe, axis=1, keepdims=True)
        pm = jnp.where(is_mix, logits, NEG)
        pm = jnp.exp(pm - jnp.max(pm, axis=1, keepdims=True))
        pm = pm / jnp.sum(pm, axis=1, keepdims=True)
        route_row = jnp.broadcast_to(route[b][0:1, :], (rows, rows))
        route_col = jnp.sum(jnp.where(row == col, route_row, 0), axis=1, keepdims=True)
        hot = lane == route_col
        gate = jnp.sum(jnp.where(hot, pe, 0.0), axis=1, keepdims=True)
        mix0 = jnp.sum(jnp.where(lane == experts, pm, 0.0), axis=1, keepdims=True)
        mix1 = jnp.sum(jnp.where(lane == experts + 1, pm, 0.0), axis=1, keepdims=True)
        scaled = mix1 * gate
        flow = cot[at, :].astype(F32)
        dgrad[at, :] = (flow * mix0).astype(BF)
        egrad[at, :] = (flow * scaled).astype(BF)
        mixes[at, :] = jnp.where(lane == 0, mix0, jnp.where(lane == 1, scaled, 0.0))
        same = (route_row == route_col) & (col < row)
        rank = jnp.sum(jnp.where(same, 1, 0), axis=1, keepdims=True)
        group = lax.div(route_col, team)
        mine = lax.rem(route_col, team) == me
        target = jnp.where(mine, group * slots + b * capacity + rank, groups * slots)
        slot = lax.broadcasted_iota(jnp.int32, (rows, groups * slots), 1)
        sel[at, :] = jnp.where(slot == target, 1.0, 0.0).astype(BF)

        @pl.when(b == me)
        def _():
            middle_own[...] = middle
            prob_own[...] = jnp.where(is_expert, pe, jnp.where(is_mix, pm, 0.0))
            hot_own[...] = jnp.where(hot, 1.0, 0.0)
            second_own[...] = low
            att_own[...] = part
            place = lax.broadcasted_iota(jnp.int32, sel_own.shape, 1)
            sel_own[...] = jnp.where(place == route_col * capacity + rank, 1.0, 0.0).astype(BF)

        return carry

    lax.fori_loop(0, team, block, 0)
    send_s[...] = contract_rows(sel[...], second[...]).astype(BF).reshape(send_s.shape)
    send_g[...] = contract_rows(sel[...], egrad[...]).astype(BF).reshape(send_g.shape)


def between(experts, sizes, slots, member, att, wo, x, vec, rw, route, cot):
    two, groups, team = sizes
    group_rows, width = x.shape
    rows = group_rows // team
    shapes = (
        ((group_rows, width), BF),
        ((group_rows, width), BF),
        ((groups, slots, width), BF),
        ((groups, slots, width), BF),
        ((group_rows, groups * slots), BF),
        ((group_rows, 128), F32),
        ((rows, width), F32),
        ((rows, 128), F32),
        ((rows, 128), F32),
        ((rows, width), BF),
        ((width, rows), BF),
        ((rows, experts * (slots // team)), BF),
    )
    inside = pl.BlockSpec(memory_space=pltpu.VMEM)
    return pl.pallas_call(
        functools.partial(mid_kernel, experts, team),
        name="between",
        in_specs=[pl.BlockSpec(memory_space=pltpu.SMEM)] + [inside] * 7,
        out_specs=tuple(inside for _ in shapes),
        out_shape=tuple(jax.ShapeDtypeStruct(s, d) for s, d in shapes),
        scratch_shapes=[pltpu.VMEM((group_rows, width), BF)],
        compiler_params=pltpu.CompilerParams(vmem_limit_bytes=60 * 2**20),
    )(member, att, wo, x, vec, rw, route, cot)


def turn_kernel(
    experts, layer_sum, second_sum, sums, middle, prob, hot, second, att, cot, rw, wo, vec,
    layer, middle_grad, flow_t, out_term, small_t,
):
    rows = middle.shape[0]
    lane = lax.broadcasted_iota(jnp.int32, (rows, 128), 1)
    layer[...] = (middle[...] + layer_sum[...]).astype(BF)
    chances, chosen = prob[...], hot[...]
    s0, s1 = sums[:, 0:1], sums[:, 1:2]
    mix1 = jnp.sum(jnp.where(lane == experts + 1, chances, 0.0), axis=1, keepdims=True)
    gate = jnp.sum(chances * chosen, axis=1, keepdims=True)
    pull_gate = s1 * mix1
    pulls = jnp.where(lane == experts, s0, jnp.where(lane == experts + 1, s1 * gate, 0.0))
    mean_pull = jnp.sum(chances * pulls, axis=1, keepdims=True)
    logit_grad = chances * jnp.where(
        lane < experts, pull_gate * (chosen - gate), pulls - mean_pull
    )
    logit_grad = jnp.where(lane < experts + 2, logit_grad, 0.0).astype(BF)
    second_grad = second_sum[...] + contract_cols(logit_grad, rw[...])
    hat, scale = normalize(middle[...])
    pull = second_grad * vec[5:6, :]
    part = scale * (
        pull
        - jnp.mean(pull, axis=-1, keepdims=True)
        - hat * jnp.mean(pull * hat, axis=-1, keepdims=True)
    )
    grad = cot[...].astype(F32) + part
    middle_grad[...] = grad
    branch = grad.astype(BF)
    width = wo.shape[0]

    def tile(n, carry):
        at = span(n, TILE)
        flow_t[at, :] = contract_cols(wo[at, :], branch).astype(BF)
        out_term[at, :] = dot_f32(att[at, :], branch).astype(BF)
        return carry

    lax.fori_loop(0, width // TILE, tile, 0)
    used = small_t.shape[0]
    routed = contract_rows(logit_grad, second[...])[:used, :]
    which = lax.broadcasted_iota(jnp.int32, routed.shape, 0)
    gain = jnp.sum(second_grad * hat, axis=0, keepdims=True)
    bias = jnp.sum(second_grad, axis=0, keepdims=True)
    small_t[...] = jnp.where(
        which == experts + 3, gain, jnp.where(which == experts + 5, bias, routed)
    )


def turn(experts, layer_sum, second_sum, sums, middle, prob, hot, second, att, cot, rw, wo, vec):
    rows, width = middle.shape
    used = -(-(experts + 6) // 8) * 8
    shapes = (
        ((rows, width), BF),
        ((rows, width), F32),
        ((width, rows), BF),
        ((width, width), BF),
        ((used, width), F32),
    )
    inside = pl.BlockSpec(memory_space=pltpu.VMEM)
    return pl.pallas_call(
        functools.partial(turn_kernel, experts),
        name="turn",
        in_specs=[inside] * 12,
        out_specs=tuple(inside for _ in shapes),
        out_shape=tuple(jax.ShapeDtypeStruct(s, d) for s, d in shapes),
        compiler_params=pltpu.CompilerParams(vmem_limit_bytes=40 * 2**20),
    )(layer_sum, second_sum, sums, middle, prob, hot, second, att, cot, rw, wo, vec)


def row_sum_kernel(left, right, out):
    out[0] = contract_rows(left[...], right[...])


def row_sum(left, right, tile):
    many, high = left.shape
    wide = right.shape[1]
    return pl.pallas_call(
        row_sum_kernel,
        name="row_sum",
        grid=(high // tile,),
        in_specs=[pl.BlockSpec((many, tile), lambda i: (0, i)), fixed(right.shape)],
        out_specs=pl.BlockSpec((1, tile, wide), lambda i: (0, i, 0)),
        out_shape=jax.ShapeDtypeStruct((1, high, wide), F32),
        compiler_params=pltpu.CompilerParams(vmem_limit_bytes=40 * 2**20),
        cost_estimate=pl.CostEstimate(
            flops=2 * many * high * wide, bytes_accessed=4 * high * wide, transcendentals=0
        ),
    )(left, right)


class Net:
    def __init__(self, sizes, send_sem, recv_sem):
        self.two, self.groups, self.team = sizes
        self.send_sem, self.recv_sem = send_sem, recv_sem
        self.c = lax.axis_index("dp")
        i = lax.axis_index("ctx")
        self.g, self.t = lax.div(i, self.team), lax.rem(i, self.team)
        self.group_steps = [(0, k, 0) for k in range(1, self.groups)]
        self.team_steps = [(0, 0, k) for k in range(1, self.team)]
        self.swap = (1, 0, 0)
        self.started = []

    def device(self, step):
        dc, dg, dt = step
        return (
            lax.rem(self.c + dc, self.two),
            lax.rem(self.g + dg, self.groups) * self.team + lax.rem(self.t + dt, self.team),
        )

    def greet(self):
        barrier = pltpu.get_barrier_semaphore()
        steps = self.group_steps + self.team_steps + [self.swap]
        for step in steps:
            pl.semaphore_signal(barrier, inc=1, device_id=self.device(step), device_id_type=MESH)
        pl.semaphore_wait(barrier, len(steps))

    def send(self, src, dst, step):
        k = len(self.started)
        copy = pltpu.make_async_remote_copy(
            src_ref=src,
            dst_ref=dst,
            send_sem=self.send_sem.at[k],
            recv_sem=self.recv_sem.at[k],
            device_id=self.device(step),
            device_id_type=MESH,
        )
        copy.start()
        self.started.append(copy)
        return copy

    def other_group(self, bit, group=None):
        group = self.g if group is None else group
        return group + bit - 2 * bit * lax.rem(lax.div(group, bit), 2)

    def other_member(self, bit):
        return self.t + bit - 2 * bit * lax.rem(lax.div(self.t, bit), 2)

    def send_member(self, src, dst, member):
        k = len(self.started)
        copy = pltpu.make_async_remote_copy(
            src_ref=src,
            dst_ref=dst,
            send_sem=self.send_sem.at[k],
            recv_sem=self.recv_sem.at[k],
            device_id=(self.c, self.g * self.team + member),
            device_id_type=MESH,
        )
        copy.start()
        self.started.append(copy)
        return copy

    def send_group(self, src, dst, group):
        k = len(self.started)
        copy = pltpu.make_async_remote_copy(
            src_ref=src,
            dst_ref=dst,
            send_sem=self.send_sem.at[k],
            recv_sem=self.recv_sem.at[k],
            device_id=(self.c, group * self.team + self.t),
            device_id_type=MESH,
        )
        copy.start()
        self.started.append(copy)
        return copy

    def group_to(self, step):
        return lax.rem(self.g + step[1], self.groups)

    def group_from(self, step):
        return lax.rem(self.g + self.groups - step[1], self.groups)

    def team_to(self, step):
        return lax.rem(self.t + step[2], self.team)

    def team_from(self, step):
        return lax.rem(self.t + self.team - step[2], self.team)

    def close(self):
        for copy in self.started:
            copy.wait_send()


def arrive(copies):
    for copy in copies:
        copy.wait_recv()


class Local:
    def __init__(self, sem):
        self.sem, self.count, self.open = sem, 0, []

    def copy(self, src, dst):
        made = pltpu.make_async_copy(src, dst, self.sem.at[self.count])
        made.start()
        self.count += 1
        self.open.append(made)
        return made

    def wait(self, *copies):
        for made in copies or tuple(self.open):
            made.wait()
            self.open = [other for other in self.open if other is not made]


def start_kernel(sizes, *refs):
    tokens, cot, w_qkv, w_up, w_down, w_out, router, gains, biases, routes = refs[:10]
    token_o, cot_o, heads_o, normed_o, weight_o, vec_o, out_o, ff_o, route_o, small_o = refs[10:20]
    (
        own, up, down, route, square, stage, weights, tokens_v, normed, mixed, heads, out_v,
        send_sem, recv_sem, local_sem,
    ) = refs[20:]
    net, local = Net(sizes, send_sem, recv_sem), Local(local_sem)
    c, g, t = net.c, net.g, net.t
    two, groups, team = sizes
    rows, width = tokens.shape
    used = own.shape[2] - 128
    wr = own.shape[1]
    own_tokens = local.copy(tokens, tokens_v.at[t])
    local.copy(cot, cot_o.at[t])

    square[...] = jnp.zeros_like(square)
    square[: router.shape[0], :wr] = router[...]
    square[124:126, :wr] = gains[...]
    square[126:128, :wr] = biases[...]
    small = square[...].T[:wr, :].astype(BF)
    third = used // 3
    for n in range(team):
        for k in range(3):
            at = k * width + n * third
            own[n, :, k * third : (k + 1) * third] = w_qkv[:, at : at + third].astype(BF)
        own[n, :, used:] = small
    stage[t] = own[t]
    net.greet()
    staged = [net.send(own.at[net.team_to(s)], stage.at[t], s) for s in net.team_steps]
    out_v[g] = w_out[...].astype(BF)
    spread_out = [net.send(out_v.at[g], out_v.at[g], s) for s in net.group_steps]
    deep = w_down.shape[0]
    for n in range(team):
        for k in range(two * groups):
            at = (k * team + n) * deep
            up[n, :, k * deep : (k + 1) * deep] = w_up[:, at : at + deep].astype(BF)
    down[...] = w_down[...].astype(BF).reshape(down.shape)
    route[...] = jnp.broadcast_to(routes[...], route.shape)
    local.copy(up.at[t], ff_o.at[0, t])
    local.copy(down, ff_o.at[1])
    local.copy(route, route_o.at[t])
    arrive(staged)
    near, far = net.other_group(1), net.other_group(2)
    last = net.other_group(2, near)
    from_far = net.send_group(stage, weights.at[c, g], far)
    from_near = net.send_group(stage, weights.at[c, g], near)
    swapped = [net.send(stage, weights.at[c, g], net.swap)]
    mine = local.copy(stage, weights.at[c, g])

    side, other = net.other_member(1), net.other_member(2)
    part = rows // 2

    def to_sides(src, dst):
        return [net.send_member(src, dst.at[t], member) for member in (side, other)]

    def pass_on(copies, dst):
        made = []
        for n, (copy, at, to) in enumerate(zip(copies, (side, other), (other, side))):
            copy.wait_recv()
            view = dst.at[at, pl.ds(n * part, part)]
            made.append(net.send_member(view, view, to))
        return made

    told = to_sides(tokens, tokens_v)
    later = [net.send(route, route_o.at[t], s) for s in net.team_steps]
    local.wait(mine)
    told = pass_on(told, tokens_v)
    turned = to_sides(cot, cot_o)
    later += [net.send(up.at[net.team_to(s)], ff_o.at[0, t], s) for s in net.team_steps]
    from_far.wait_recv()
    view = weights.at[c, far]
    passed = net.send_group(view, view, near)
    swapped.append(net.send(view, view, net.swap))
    from_near.wait_recv()
    view = weights.at[c, near]
    swapped.append(net.send(view, view, net.swap))
    passed.wait_recv()
    view = weights.at[c, last]
    swapped.append(net.send(view, view, net.swap))
    local.wait(own_tokens)
    arrive(told)
    local.copy(tokens_v, token_o)
    arrive(swapped)
    local.copy(weights, weight_o)

    small = weights[:, :, :, :, used:].reshape(width, 128)
    small_o[...] = small
    small = small.astype(F32).T
    vec_o[...] = small[120:, :]

    def norm(b, carry):
        hat, _ = normalize(tokens_v[b].astype(F32))
        normed[b] = (hat * vec_o[4:5, :] + vec_o[6:7, :]).astype(BF)
        return carry

    lax.fori_loop(0, team, norm, 0)
    local.copy(normed, normed_o)
    group_rows = rows * team
    per = used // 3 // 128
    pair = 128 // HEAD_DIM
    for n in range(used // 128):
        columns = weights[:, :, :, :, n * 128 : (n + 1) * 128].reshape(width, 128)
        made = dot_f32(normed[...].reshape(group_rows, width), columns).T.astype(BF)
        at = (n % per) * pair
        mixed[n // per, at : at + pair] = made.reshape(pair, HEAD_DIM, group_rows)
    given = [net.send(mixed.at[:, net.group_to(s)], heads.at[g], s) for s in net.group_steps]
    later += pass_on(turned, cot_o)
    local.wait(local.copy(mixed.at[:, g], heads.at[g]))

    arrive(spread_out)
    local.copy(out_v, out_o.at[c, :, t])
    swapped = [net.send(out_v, out_o.at[c, :, t], net.swap)]
    outed = [net.send(out_v, out_o.at[c, :, t], s) for s in net.team_steps]
    for copy, s in zip(outed, net.team_steps):
        copy.wait_recv()
        view = out_o.at[c, :, net.team_from(s)]
        swapped.append(net.send(view, view, net.swap))
    arrive(given)
    local.copy(heads, heads_o)
    arrive(swapped + later)
    local.wait()
    net.close()


def start(sizes, tokens, cot, w_qkv, w_up, w_down, w_out, router, gains, biases, routes):
    two, groups, team = sizes
    rows, width = tokens.shape
    wr = w_qkv.shape[0]
    used = 3 * width // team
    cols = used + 128
    head = (3, groups, HEAD_DIM, team * rows)
    up = (team, wr, width)
    shapes = (
        ((team, rows, width), BF),
        ((team, rows, width), BF),
        ((groups, 3, HEAD_DIM, team * rows), BF),
        ((team, rows, width), BF),
        ((two, groups, team, wr, cols), BF),
        ((8, width), F32),
        ((two, groups, team, wr, width), BF),
        ((2,) + up, BF),
        ((team, 8, rows), jnp.int32),
        ((width, 128), BF),
    )
    anywhere = pl.BlockSpec(memory_space=pl.ANY)
    inside = pl.BlockSpec(memory_space=pltpu.VMEM)
    count = 6 * (team - 1) + 4 * (groups - 1) + 4 + (team - 1)
    return pl.pallas_call(
        functools.partial(start_kernel, sizes),
        name="start",
        out_shape=tuple(jax.ShapeDtypeStruct(s, d) for s, d in shapes),
        in_specs=[anywhere] * 2 + [inside] * 8,
        out_specs=tuple(inside if n in (5, 9) else anywhere for n in range(10)),
        scratch_shapes=[
            pltpu.VMEM((team, wr, cols), BF),
            pltpu.VMEM(up, BF),
            pltpu.VMEM(up, BF),
            pltpu.VMEM((8, rows), jnp.int32),
            pltpu.VMEM((128, 128), F32),
            pltpu.VMEM((team, wr, cols), BF),
            pltpu.VMEM((two, groups, team, wr, cols), BF),
            pltpu.VMEM((team, rows, width), BF),
            pltpu.VMEM((team, rows, width), BF),
            pltpu.VMEM(head, BF),
            pltpu.VMEM((groups, 3, HEAD_DIM, team * rows), BF),
            pltpu.VMEM((groups, wr, width), BF),
            pltpu.SemaphoreType.DMA((count,)),
            pltpu.SemaphoreType.DMA((count,)),
            pltpu.SemaphoreType.DMA((14,)),
        ],
        compiler_params=pltpu.CompilerParams(
            collective_id=12, has_side_effects=True, vmem_limit_bytes=60 * 2**20
        ),
        cost_estimate=pl.CostEstimate(flops=0, bytes_accessed=150_000_000, transcendentals=0),
    )(tokens, cot, w_qkv, w_up, w_down, w_out, router, gains, biases, routes)


def end_kernel(sizes, experts, *refs):
    groups = sizes[1]
    parts, refs = refs[:groups], refs[groups:]
    weight, normed, tokens, vec, middle_grad, small, up, out = refs[:8]
    grad_o, qkv_o, up_o, out_o, small_o = refs[8:13]
    (
        up_r, small_d, mixed, turned, weights, normed_v, give, got, zsend, zrecv, npart, nrecv, qsend, qrecv,
        out_r, small_a, small_b, small_c, send_sem, recv_sem, local_sem,
    ) = refs[13:]
    net, local = Net(sizes, send_sem, recv_sem), Local(local_sem)
    c, g, t = net.c, net.g, net.t
    team = sizes[2]
    rows, width = tokens.shape
    group_rows, used = turned.shape
    for k, part in enumerate(parts):
        local.copy(part, mixed.at[:, net.group_from((0, k, 0))])
    local.copy(normed, normed_v)
    local.copy(weight, weights)
    local.copy(up.at[t], up_r.at[t])
    local.copy(out.at[g], out_r.at[g])
    net.greet()
    outed = [net.send(out.at[net.group_to(s)], out_r.at[g], s) for s in net.group_steps]
    later = [net.send(up.at[net.team_to(s)], up_r.at[t], s) for s in net.team_steps]
    local.wait()
    per = used // 3 // 128
    pair = 128 // HEAD_DIM
    for n in range(used // 128):
        at = (n % per) * pair
        block = mixed[n // per, at : at + pair].reshape(128, group_rows)
        turned[:, n * 128 : (n + 1) * 128] = block.astype(F32).T.astype(BF)

    half = width // 2
    tile = 128

    def term(core, n):
        at = pl.ds(pl.multiple_of(core * half + n * tile, tile), tile)
        left = normed_v[:, :, at].reshape(group_rows, tile)
        return contract_rows(left, turned[...])

    def giving(n, carry):
        give[span(n, tile), :] = term(lax.rem(c + 1, 2), n).astype(BF)
        return carry

    lax.fori_loop(0, half // tile, giving, 0)
    crossed = net.send(give, got, net.swap)

    def part_of(r, carry):
        columns = weights[:, :, :, :, :used].reshape(width, used)
        npart[r] = contract_cols(turned[span(r, rows), :], columns).astype(BF)
        return carry

    lax.fori_loop(0, team, part_of, 0)
    owned = [net.send(npart.at[net.team_to(s)], nrecv.at[t], s) for s in net.team_steps]
    nrecv[t] = npart[t]
    crossed.wait_recv()

    def keeping(n, carry):
        at = span(n, tile)
        zsend[at, :] = (term(c, n) + got[at, :].astype(F32)).astype(BF)
        return carry

    lax.fori_loop(0, half // tile, keeping, 0)
    deep = half // groups
    near, far = net.other_group(1), net.other_group(2)
    last = net.other_group(2, near)
    for_far = net.send_group(zsend.at[span(last, deep), :], zrecv.at[0], near)
    for_me = net.send_group(zsend.at[span(near, deep), :], zrecv.at[1], near)
    for_far.wait_recv()
    zrecv[3] = (zsend[span(far, deep), :].astype(F32) + zrecv[0].astype(F32)).astype(BF)
    summed = [for_me, net.send_group(zrecv.at[3], zrecv.at[2], far)]

    arrive(owned)
    flow = jnp.sum(nrecv[...].astype(F32), axis=0)
    hat, scale = normalize(tokens[...].astype(F32))
    pull = flow * vec[4:5, :]
    pulled = scale * (
        pull
        - jnp.mean(pull, axis=-1, keepdims=True)
        - hat * jnp.mean(pull * hat, axis=-1, keepdims=True)
    )
    grad_o[...] = (middle_grad[...] + pulled).astype(BF)

    gain = jnp.sum(flow * hat, axis=0, keepdims=True)
    bias = jnp.sum(flow, axis=0, keepdims=True)
    which = lax.broadcasted_iota(jnp.int32, small.shape, 0)
    mine = jnp.where(
        which == experts + 2, gain, jnp.where(which == experts + 4, bias, small[...])
    )
    small_a[c] = mine
    crossing = net.send(small_a.at[c], small_a.at[c], net.swap)
    crossing.wait_recv()
    small_c[...] = small_a[0] + small_a[1]

    def columns_of(k):
        return span(c * groups + k, 128)

    moved = [
        net.send(small_c.at[:, columns_of(net.group_to(s))], small_b.at[g], s)
        for s in net.group_steps
    ]
    small_b[g] = small_c[:, columns_of(g)]
    arrive(moved)
    small_d[t] = jnp.sum(small_b[...], axis=0)
    later += [net.send(small_d.at[t], small_d.at[t], s) for s in net.team_steps]

    arrive(summed)
    total = zsend[span(g, deep), :].astype(F32) + zrecv[1].astype(F32) + zrecv[2].astype(F32)
    qsend[...] = total.astype(BF).reshape(qsend.shape)
    later += [net.send(qsend.at[net.team_to(s)], qrecv.at[t], s) for s in net.team_steps]
    qrecv[t] = qsend[t]
    arrive(outed)
    out_o[...] = jnp.sum(out_r[...].astype(F32), axis=0)
    arrive(later)
    small_o[...] = jnp.sum(small_d[...], axis=0)
    third = used // 3
    deep = up_o.shape[1] // (2 * groups * team)
    for n in range(team):
        for k in range(3):
            at = k * width + n * third
            qkv_o[:, at : at + third] = qrecv[n, :, k * third : (k + 1) * third].astype(F32)
        for k in range(2 * groups):
            at = (k * team + n) * deep
            up_o[:, at : at + deep] = up_r[n, :, k * deep : (k + 1) * deep].astype(F32)
    net.close()


def end(sizes, experts, parts, weight, normed, tokens, vec, middle_grad, small, up, out):
    two, groups, team = sizes
    rows, width = tokens.shape
    wr = out.shape[1]
    used = 3 * groups * HEAD_DIM
    group_rows = parts[0].shape[2]
    half = width // 2
    shapes = (
        ((rows, width), BF),
        ((wr, 3 * width), F32),
        ((wr, team * width), F32),
        ((wr, width), F32),
        ((small.shape[0], 128), F32),
    )
    anywhere = pl.BlockSpec(memory_space=pl.ANY)
    inside = pl.BlockSpec(memory_space=pltpu.VMEM)
    count = 5 * (team - 1) + 3 * (groups - 1) + 2
    return pl.pallas_call(
        functools.partial(end_kernel, sizes, experts),
        name="end",
        out_shape=tuple(jax.ShapeDtypeStruct(s, d) for s, d in shapes),
        in_specs=[anywhere] * (groups + 2) + [inside] * 4 + [anywhere] * 2,
        out_specs=tuple(inside for _ in shapes),
        scratch_shapes=[
            pltpu.VMEM((team, wr, width), BF),
            pltpu.VMEM((team, small.shape[0], 128), F32),
            pltpu.VMEM((3, groups, HEAD_DIM, group_rows), BF),
            pltpu.VMEM((group_rows, used), BF),
            pltpu.VMEM(weight.shape, BF),
            pltpu.VMEM(normed.shape, BF),
            pltpu.VMEM((half, used), BF),
            pltpu.VMEM((half, used), BF),
            pltpu.VMEM((half, used), BF),
            pltpu.VMEM((groups, half // groups, used), BF),
            pltpu.VMEM((team, rows, width), BF),
            pltpu.VMEM((team, rows, width), BF),
            pltpu.VMEM((team, wr, used), BF),
            pltpu.VMEM((team, wr, used), BF),
            pltpu.VMEM((groups, wr, width), BF),
            pltpu.VMEM((2,) + small.shape, F32),
            pltpu.VMEM((groups, small.shape[0], 128), F32),
            pltpu.VMEM(small.shape, F32),
            pltpu.SemaphoreType.DMA((count,)),
            pltpu.SemaphoreType.DMA((count,)),
            pltpu.SemaphoreType.DMA((groups + 4,)),
        ],
        compiler_params=pltpu.CompilerParams(
            collective_id=13, has_side_effects=True, vmem_limit_bytes=60 * 2**20
        ),
        cost_estimate=pl.CostEstimate(flops=0, bytes_accessed=120_000_000, transcendentals=0),
    )(*parts, weight, normed, tokens, vec, middle_grad, small, up, out)


def gelu_and_slope(x):
    k = math.sqrt(2.0 / math.pi)
    square = x * x
    bent = jnp.tanh(k * (x + 0.044715 * (square * x)))
    half = 0.5 * (1.0 + bent)
    slope = half + (0.5 * k) * x * (1.0 - bent * bent) * (1.0 + (3 * 0.044715) * square)
    return x * half, slope


def feed_kernel(sizes, copies_count, *refs):
    two, groups, team = sizes
    (send_s, send_g, eup_h, edown_h, second_h, dgrad_h, ff_h, sel_h, cot_h, mix_h) = refs[:10]
    (layer_o, grad_o, sums_o, active_o, hgrad_o, arr_s_o, arr_g_o, ffg_o) = refs[10:18]
    (
        arr_s, arr_g, eup, edown, second, dgrad, upw, downw, sel, cot, mix,
        slope, active, hgrad, acc, give, got_s, got_g, ret_s, ret_g, back_s, back_g,
        low, ugrad, dense, spart, lay, spa, sums, lay_r, spa_r, sums_r,
        term_give, term_got, send_sem, recv_sem, load_sem, out_sem,
    ) = refs[18:]
    c = lax.axis_index("dp")
    i = lax.axis_index("ctx")
    g, t = lax.div(i, team), lax.rem(i, team)
    width = second.shape[1]
    rows = lay.shape[1]
    hid, ehid = upw.shape[1], eup.shape[1]
    core = lax.rem(c + 1, two)

    def device(step):
        dc, dg, dt = step
        return (
            lax.rem(c + dc, two),
            lax.rem(g + dg, groups) * team + lax.rem(t + dt, team),
        )

    index = [0]

    def remote(src, dst, step):
        k = index[0]
        index[0] += 1
        assert k < copies_count
        return pltpu.make_async_remote_copy(
            src_ref=src,
            dst_ref=dst,
            send_sem=send_sem.at[k],
            recv_sem=recv_sem.at[k],
            device_id=device(step),
            device_id_type=MESH,
        )

    group_steps = [(0, k, 0) for k in range(1, groups)]
    team_steps = [(0, 0, k) for k in range(1, team)]
    swap = (1, 0, 0)
    deep = ff_h.shape[2]

    def block_of(core, k):
        return pl.ds(pl.multiple_of((core * groups + k) * deep, deep), deep)

    loads = []
    for k, (src, dst) in enumerate(
        [
            (second_h, second), (dgrad_h, dgrad), (eup_h, eup), (edown_h, edown), (sel_h, sel), (cot_h, cot), (mix_h, mix),
            (send_s.at[g], arr_s.at[c, g]), (send_g.at[g], arr_g.at[c, g]),
        ]
        + [
            (ff_h.at[k, n], weight.at[block_of(c, k), :])
            for k in range(groups)
            for n, weight in enumerate((upw, downw))
        ]
    ):
        load = pltpu.make_async_copy(src, dst, load_sem.at[k])
        load.start()
        loads.append(load)

    barrier = pltpu.get_barrier_semaphore()
    greet = group_steps + team_steps + [swap]
    for step in greet:
        pl.semaphore_signal(barrier, inc=1, device_id=device(step), device_id_type=MESH)
    pl.semaphore_wait(barrier, len(greet))

    every = []

    def launch(copy):
        copy.start()
        every.append(copy)
        return copy

    def to_groups(src, dst):
        return [
            launch(remote(src.at[lax.rem(g + s[1], groups)], dst.at[g], s)) for s in group_steps
        ]

    def source(s):
        return lax.rem(g + groups - s[1], groups)

    swap_w = [
        launch(remote(ff_h.at[k, n], weight.at[block_of(c, k), :], swap))
        for k in range(groups)
        for n, weight in enumerate((upw, downw))
    ]
    out_s = [
        launch(remote(send_s.at[lax.rem(g + s[1], groups)], arr_s.at[c, g], s))
        for s in group_steps
    ]
    swap_s = [launch(remote(send_s.at[g], arr_s.at[c, g], swap))]
    out_g = [
        launch(remote(send_g.at[lax.rem(g + s[1], groups)], arr_g.at[c, g], s))
        for s in group_steps
    ]
    swap_g = [launch(remote(send_g.at[g], arr_g.at[c, g], swap))]

    for load in loads[:2] + loads[9:]:
        load.wait()
    for copy in swap_w:
        copy.wait_recv()

    def dense_in(h, carry):
        at = span(h, TILE)
        value, bend = gelu_and_slope(dot_f32(second[...], upw[:, at]))
        low[:, at] = value.astype(BF)
        ugrad[:, at] = (bend * contract_cols(dgrad[...], downw[at, :])).astype(BF)
        return carry

    lax.fori_loop(0, hid // TILE, dense_in, 0)

    def dense_out(n, carry):
        at = span(n, TILE)
        dense[:, at] = dot_f32(low[...], downw[:, at])
        spart[:, at] = contract_cols(ugrad[...], upw[at, :])
        return carry

    lax.fori_loop(0, width // TILE, dense_out, 0)

    for load in loads[2:9]:
        load.wait()
    for copy, s in zip(out_s, group_steps):
        copy.wait_recv()
        swap_s.append(launch(remote(arr_s.at[c, source(s)], arr_s.at[c, source(s)], swap)))
    for copy in swap_s:
        copy.wait_recv()
    entries = 2 * groups * arr_s.shape[2]

    def expert_in(h, carry):
        at = span(h, TILE)
        value, bend = gelu_and_slope(dot_f32(arr_s[...].reshape(entries, width), eup[:, at]))
        active[:, at] = value.astype(BF)
        slope[:, at] = bend
        return carry

    lax.fori_loop(0, ehid // TILE, expert_in, 0)
    keeps = [
        pltpu.make_async_copy(active, active_o, out_sem.at[0]),
        pltpu.make_async_copy(arr_s, arr_s_o, out_sem.at[1]),
    ]
    for copy in keeps:
        copy.start()

    def expert_out(n, carry):
        at = span(n, TILE)
        acc[:, :, at] = dot_f32(active[...], edown[:, at]).reshape(2, entries // 2, TILE)
        return carry

    lax.fori_loop(0, width // TILE, expert_out, 0)
    give[0] = acc[core].astype(BF)
    other_s = launch(remote(give.at[0], got_s, swap))

    for copy, s in zip(out_g, group_steps):
        copy.wait_recv()
        swap_g.append(launch(remote(arr_g.at[c, source(s)], arr_g.at[c, source(s)], swap)))
    other_s.wait_recv()
    ret_s[...] = (acc[c] + got_s[...].astype(F32)).astype(BF).reshape(ret_s.shape)
    home_s = to_groups(ret_s, back_s)
    back_s[g] = ret_s[g]
    for copy in swap_g:
        copy.wait_recv()

    def expert_back(h, carry):
        at = span(h, TILE)
        pull = contract_cols(arr_g[...].reshape(entries, width), edown[at, :])
        hgrad[:, at] = (slope[:, at] * pull).astype(BF)
        return carry

    lax.fori_loop(0, ehid // TILE, expert_back, 0)
    keeps += [
        pltpu.make_async_copy(hgrad, hgrad_o, out_sem.at[2]),
        pltpu.make_async_copy(arr_g, arr_g_o, out_sem.at[3]),
    ]
    for copy in keeps[2:]:
        copy.start()

    def expert_back_out(n, carry):
        at = span(n, TILE)
        acc[:, :, at] = contract_cols(hgrad[...], eup[at, :]).reshape(2, entries // 2, TILE)
        return carry

    lax.fori_loop(0, width // TILE, expert_back_out, 0)
    give[1] = acc[core].astype(BF)
    other_g = launch(remote(give.at[1], got_g, swap))
    other_g.wait_recv()
    ret_g[...] = (acc[c] + got_g[...].astype(F32)).astype(BF).reshape(ret_g.shape)
    home_g = to_groups(ret_g, back_g)
    back_g[g] = ret_g[g]

    for copy in home_s:
        copy.wait_recv()
    slots = groups * back_s.shape[1]
    lane = lax.broadcasted_iota(jnp.int32, (rows, 128), 1)

    def join_layer(r, carry):
        at = span(r, rows)
        found = dot_f32(sel[at, :], back_s[...].reshape(slots, width))
        own = dense[at, :]
        flow = cot[at, :].astype(F32)
        mixes = mix[at, :]
        lay[r] = (mixes[:, 0:1] * own + mixes[:, 1:2] * found).astype(BF)
        plain = jnp.sum(flow * own, axis=1, keepdims=True)
        routed = jnp.sum(flow * found, axis=1, keepdims=True)
        sums[r] = jnp.where(lane == 0, plain, jnp.where(lane == 1, routed, 0.0))
        return carry

    lax.fori_loop(0, team, join_layer, 0)

    def to_team(src, dst):
        made = [launch(remote(src.at[lax.rem(t + s[2], team)], dst.at[t], s)) for s in team_steps]
        dst[t] = src[t]
        return made

    team_copies = to_team(lay, lay_r) + to_team(sums, sums_r)

    for copy in home_g:
        copy.wait_recv()

    def join_grad(r, carry):
        at = span(r, rows)
        found = dot_f32(sel[at, :], back_g[...].reshape(slots, width))
        spa[r] = (spart[at, :] + found).astype(BF)
        return carry

    lax.fori_loop(0, team, join_grad, 0)
    team_copies += to_team(spa, spa_r)

    half = hid // 2
    term_tile = 128

    def down_term(base, n):
        at = pl.ds(pl.multiple_of(base + n * term_tile, term_tile), term_tile)
        return contract_rows(low[:, at], dgrad[...])

    def up_term(base, n):
        at = pl.ds(pl.multiple_of(base + n * term_tile, term_tile), term_tile)
        return contract_rows(second[:, at], ugrad[...])

    terms = []
    for k, (term, size) in enumerate(((down_term, half), (up_term, width // 2))):

        def giving(n, carry, k=k, term=term, size=size):
            term_give[k, span(n, term_tile), :] = term(core * size, n).astype(BF)
            return carry

        lax.fori_loop(0, size // term_tile, giving, 0)
        terms.append(launch(remote(term_give.at[k], term_got.at[k], swap)))
    for k, (term, size) in enumerate(((down_term, half), (up_term, width // 2))):
        terms[k].wait_recv()

        def keeping(n, carry, k=k, term=term, size=size):
            at = span(n, term_tile)
            total = term(c * size, n) + term_got[k, at, :].astype(F32)
            ffg_o[at, k * width : (k + 1) * width] = total.astype(BF)
            return carry

        lax.fori_loop(0, size // term_tile, keeping, 0)

    for copy in team_copies:
        copy.wait_recv()
    layer_o[...] = jnp.sum(lay_r[...].astype(F32), axis=0)
    grad_o[...] = jnp.sum(spa_r[...].astype(F32), axis=0)
    sums_o[...] = jnp.sum(sums_r[...], axis=0)
    for copy in keeps:
        copy.wait()
    for copy in every:
        copy.wait_send()


def feed_forward(sizes, rows, send_s, send_g, eup, edown, second, dgrad, ff, sel, cot, mix):
    two, groups, team = sizes
    slots = send_s.shape[1]
    width = second.shape[1]
    hid, ehid = second.shape[1] * ff.shape[3] // width, eup.shape[1]
    entries = 2 * groups * slots
    count = 2 * (groups - 1) * 2 + 2 * groups + 2 + 3 * (team - 1) + 2 + 2 * groups
    arrived = (two, groups, slots, width)
    anywhere = pl.BlockSpec(memory_space=pl.ANY)
    inside = pl.BlockSpec(memory_space=pltpu.VMEM)
    team_rows = team * rows
    return pl.pallas_call(
        functools.partial(feed_kernel, sizes, count),
        name="feed_forward",
        out_shape=(
            jax.ShapeDtypeStruct((rows, width), F32),
            jax.ShapeDtypeStruct((rows, width), F32),
            jax.ShapeDtypeStruct((rows, 128), F32),
            jax.ShapeDtypeStruct((entries, ehid), BF),
            jax.ShapeDtypeStruct((entries, ehid), BF),
            jax.ShapeDtypeStruct(arrived, BF),
            jax.ShapeDtypeStruct(arrived, BF),
            jax.ShapeDtypeStruct((hid // 2, 2 * width), BF),
        ),
        in_specs=[anywhere] * 10,
        out_specs=(inside, inside, inside, anywhere, anywhere, anywhere, anywhere, inside),
        scratch_shapes=[
            pltpu.VMEM((two, groups, slots, width), BF),
            pltpu.VMEM((two, groups, slots, width), BF),
            pltpu.VMEM(eup.shape, BF),
            pltpu.VMEM(edown.shape, BF),
            pltpu.VMEM(second.shape, BF),
            pltpu.VMEM(dgrad.shape, BF),
            pltpu.VMEM((width, hid), BF),
            pltpu.VMEM((hid, width), BF),
            pltpu.VMEM(sel.shape, BF),
            pltpu.VMEM(cot.shape, BF),
            pltpu.VMEM(mix.shape, F32),
            pltpu.VMEM((entries, ehid), F32),
            pltpu.VMEM((entries, ehid), BF),
            pltpu.VMEM((entries, ehid), BF),
            pltpu.VMEM((2, entries // 2, width), F32),
            pltpu.VMEM((2, entries // 2, width), BF),
            pltpu.VMEM((entries // 2, width), BF),
            pltpu.VMEM((entries // 2, width), BF),
            pltpu.VMEM((groups, slots, width), BF),
            pltpu.VMEM((groups, slots, width), BF),
            pltpu.VMEM((groups, slots, width), BF),
            pltpu.VMEM((groups, slots, width), BF),
            pltpu.VMEM((team_rows, hid), BF),
            pltpu.VMEM((team_rows, hid), BF),
            pltpu.VMEM((team_rows, width), F32),
            pltpu.VMEM((team_rows, width), F32),
            pltpu.VMEM((team, rows, width), BF),
            pltpu.VMEM((team, rows, width), BF),
            pltpu.VMEM((team, rows, 128), F32),
            pltpu.VMEM((team, rows, width), BF),
            pltpu.VMEM((team, rows, width), BF),
            pltpu.VMEM((team, rows, 128), F32),
            pltpu.VMEM((2, hid // 2, width), BF),
            pltpu.VMEM((2, hid // 2, width), BF),
            pltpu.SemaphoreType.DMA((count,)),
            pltpu.SemaphoreType.DMA((count,)),
            pltpu.SemaphoreType.DMA((9 + 2 * groups,)),
            pltpu.SemaphoreType.DMA((4,)),
        ],
        compiler_params=pltpu.CompilerParams(
            collective_id=5, has_side_effects=True, vmem_limit_bytes=60 * 2**20
        ),
        cost_estimate=pl.CostEstimate(
            flops=0, bytes_accessed=240_000_000, transcendentals=0
        ),
    )(send_s, send_g, eup, edown, second, dgrad, ff, sel, cot, mix)


def tall(chunk):
    rows, cols = chunk.shape[-2:]
    factor = 1
    while (rows * factor) % 16:
        factor *= 2
    return chunk.reshape(chunk.shape[:-2] + (rows * factor, cols // factor))


def per_device_general(
    tokens,
    cotangent,
    block_order,
    doc_lengths,
    routes,
    w_qkv,
    w_out,
    w_up,
    w_down,
    router,
    norm_gains,
    norm_biases,
    expert_up,
    expert_down,
):
    rows, width = tokens.shape[1], tokens.shape[2]
    ctx_count = lax.axis_size("ctx")
    two = lax.axis_size("dp")
    team = math.gcd(4, ctx_count)
    groups = ctx_count // team
    sizes = (two, groups, team)
    team_heads = HEADS // team
    reps = groups // team_heads
    length = rows * ctx_count
    group_rows = rows * team
    experts = ctx_count * expert_up.shape[0]
    capacity = max(2, 2 * rows // experts)
    block_rows = length // block_order.shape[0]
    hidden = w_up.shape[1]
    hidden_dev = w_down.shape[0]
    wr = w_qkv.shape[0]
    qkv_cols = 3 * width // team
    up_cols = hidden // team
    core = lax.axis_index("dp")
    ctx = lax.axis_index("ctx")
    group, member = lax.div(ctx, team), lax.rem(ctx, team)
    team_steps = [(0, 0, k) for k in range(1, team)]
    group_steps = [(0, k, 0) for k in range(1, groups)]
    by_group = [[g * team + t for g in range(groups)] for t in range(team)]
    by_team = [[g * team + t for t in range(team)] for g in range(groups)]
    swap = [(d, (d + 1) % two) for d in range(two)]

    small_flat = jnp.concatenate(
        [router.reshape(-1), norm_gains.reshape(-1), norm_biases.reshape(-1)]
    )
    small_size = -(-small_flat.shape[0] // 2048) * 2048
    small = jnp.pad(small_flat, (0, small_size - small_flat.shape[0])).astype(BF)
    small = small.reshape(-1, 128)

    qkv_first = tall(
        w_qkv.astype(BF).reshape(wr, 3, team, width // team).transpose(2, 0, 1, 3).reshape(
            team, wr, qkv_cols
        )
    )
    up_first = tall(
        w_up.reshape(wr, two * groups, team, hidden_dev)
        .transpose(2, 0, 1, 3)
        .reshape(team, wr, up_cols)
        .astype(BF)
    )
    down_first = tall(w_down.astype(BF).reshape(team, wr, width))
    out_first = tall(w_out.astype(BF))
    route_row = jnp.broadcast_to(routes[0, :, 0][None, :], (8, rows))

    def first(coords, ins, outs):
        c, g, t = coords
        moves, local = [], []
        for s in team_steps:
            to = lax.rem(t + s[2], team)
            moves.append(Move(s, ins[0], outs[0].at[t]))
            moves.append(Move(s, ins[1].at[to], outs[1].at[t]))
            moves.append(Move(s, ins[3], outs[3].at[t]))
            moves.append(Move(s, ins[4], outs[4].at[t]))
            moves.append(Move(s, ins[2].at[to], outs[2].at[0, t]))
        for s in group_steps:
            moves.append(Move(s, ins[5], outs[5].at[g]))
        local.append((ins[0], outs[0].at[t]))
        local.append((ins[1].at[t], outs[1].at[t]))
        local.append((ins[2].at[t], outs[2].at[0, t]))
        local.append((ins[3], outs[3].at[t]))
        local.append((ins[4], outs[4].at[t]))
        local.append((ins[5], outs[5].at[g]))
        local.append((ins[6], outs[2].at[1]))
        return local, moves

    token_rows, qkv_part, ff_part, small_part, route_all, out_part = exchange(
        "first",
        1,
        sizes,
        (tokens[0], qkv_first, up_first, small, route_row, out_first, down_first),
        [
            ((team, rows, width), BF),
            (qkv_first.shape, BF),
            ((2,) + up_first.shape, BF),
            ((team,) + small.shape, BF),
            ((team, 8, rows), jnp.int32),
            ((groups,) + out_first.shape, BF),
        ],
        first,
    )

    def second_build(coords, ins, outs):
        c, g, t = coords
        moves, local = [], []
        for k, s in enumerate(group_steps):
            moves.append(Move(s, ins[0], outs[0].at[c, g]))
            moves.append(Move(s, ins[1], outs[1].at[c, g]))
        for s in team_steps:
            moves.append(Move(s, ins[2], outs[2].at[t]))
        local.append((ins[0], outs[0].at[c, g]))
        local.append((ins[1], outs[1].at[c, g]))
        local.append((ins[2], outs[2].at[t]))
        other = (1, 0, 0)
        for n in range(2):
            moves.append(Move(other, ins[n], outs[n].at[c, g]))
        for k, s in enumerate(group_steps):
            source = lax.rem(g + groups - s[1], groups)
            for n in range(2):
                moves.append(
                    Move(other, outs[n].at[c, source], outs[n].at[c, source], after=2 * k + n)
                )
        return local, moves

    qkv_all, small_all, cot_rows = exchange(
        "second",
        2,
        sizes,
        (qkv_part, small_part, cotangent[0]),
        [
            ((two, groups) + qkv_part.shape, BF),
            ((two, groups) + small_part.shape, BF),
            ((team, rows, width), BF),
        ],
        second_build,
    )
    qkv_weight = qkv_all.reshape(width, qkv_cols)
    small_rows = small_all.reshape(two * ctx_count, -1)
    router_cols = router.shape[1]
    router_weight = jnp.pad(
        small_rows[:, : wr * router_cols].reshape(width, router_cols),
        ((0, 0), (0, 128 - router_cols)),
    )
    vectors = small_rows[:, wr * router_cols : small_flat.shape[0]].reshape(
        two * ctx_count, 4, wr
    )
    vectors = vectors.transpose(1, 0, 2).reshape(4, width).astype(F32)
    vectors = jnp.pad(vectors, ((4, 0), (0, 0)))

    ff_half = lax.all_gather(
        ff_part.reshape(2, team * wr, width),
        "ctx",
        axis=0,
        tiled=False,
        axis_index_groups=by_group,
    )

    def core_half(term):
        halves = term.reshape((two, term.shape[0] // two) + term.shape[1:])
        keep = lax.dynamic_index_in_dim(halves, core, 0, keepdims=False)
        give = lax.dynamic_index_in_dim(halves, 1 - core, 0, keepdims=False)
        return keep + lax.ppermute(give.astype(BF), "dp", swap).astype(F32)

    def over_groups(term):
        return lax.psum_scatter(
            term, "ctx", scatter_dimension=0, tiled=True, axis_index_groups=by_group
        )

    doc_id = jnp.arange(doc_lengths.shape[1], dtype=jnp.int32)
    doc_ends = jnp.sum(
        jnp.where(doc_id[:, None] <= doc_id[None, :], doc_lengths[0][:, None], 0), axis=0
    )
    all_rows = jnp.arange(length, dtype=jnp.int32)
    marks = (all_rows // block_rows)[:, None] == jnp.arange(
        block_order.shape[0], dtype=jnp.int32
    )[None, :]
    anchor = jnp.sum(jnp.where(marks, block_order[None, :], 0), axis=1)
    all_place = anchor * block_rows + all_rows % block_rows

    def low_of(place):
        return jnp.max(
            jnp.where(doc_ends[None, :] <= place[:, None], doc_ends[None, :], 0), axis=1
        )

    query_length = length // reps
    tiles = query_length // TILE
    part = lax.rem(group, reps)
    query_place = lax.dynamic_slice(all_place, (part * query_length,), (query_length,))
    lows = low_of(query_place)
    bounds = jnp.broadcast_to(jnp.array([[0, length // TILE]], dtype=jnp.int32), (tiles, 2))
    meta = jnp.concatenate(
        [query_place[None], lows[None], jnp.zeros((6, query_length), jnp.int32)], axis=0
    )

    token_rows = token_rows.reshape(group_rows, width)
    inputs = token_rows.astype(F32)
    normed_low = layer_norm(inputs, vectors[4], vectors[6]).astype(BF)
    mixed_t = lax.dot_general(
        qkv_weight, normed_low, (((0,), (1,)), ((), ())), preferred_element_type=F32
    ).astype(BF)
    mixed_t = mixed_t.reshape(3, team_heads, HEAD_DIM, group_rows)

    def spread_heads(coords, ins, outs):
        c, g, t = coords
        moves = [
            Move(s, ins[0].at[:, lax.div(lax.rem(g + s[1], groups), reps)], outs[0].at[g])
            for s in group_steps
        ]
        local = [(ins[0].at[:, lax.div(g, reps)], outs[0].at[g])]
        other = (1, 0, 0)
        moves.append(Move(other, ins[1], outs[1].at[c, :, t]))
        local.append((ins[1], outs[1].at[c, :, t]))
        first_team = len(moves)
        for s in team_steps:
            moves.append(Move(s, ins[1], outs[1].at[c, :, t]))
        for k, s in enumerate(team_steps):
            source = lax.rem(t + team - s[2], team)
            view = outs[1].at[c, :, source]
            moves.append(Move(other, view, view, after=first_team + k))
        return local, moves

    head_parts, out_weight = exchange(
        "heads",
        3,
        sizes,
        (mixed_t, out_part),
        [
            ((groups, 3, HEAD_DIM, group_rows), BF),
            ((two, groups, team) + out_first.shape, BF),
        ],
        spread_heads,
    )
    out_weight = out_weight.reshape(width, width)
    head_parts = head_parts.reshape(groups, 3 * HEAD_DIM, group_rows)
    place_col = all_place[:, None]
    head_t = head_parts.transpose(1, 0, 2).reshape(3 * HEAD_DIM, length)
    zeros = jnp.zeros((HEAD_DIM, query_length), BF)
    kv_t = head_t[HEAD_DIM:]
    kv_rows = kv_t.T
    q_t = lax.dynamic_slice(
        head_t[:HEAD_DIM], (0, part * query_length), (HEAD_DIM, query_length)
    )
    q_pad = jnp.concatenate([q_t * jnp.asarray(SCALE, BF), zeros], axis=0)
    attention_t, log_total = attend(False, bounds, meta, place_col, q_pad, kv_rows, kv_t)
    low_t = lax.dynamic_update_slice(
        jnp.zeros((HEAD_DIM, length), BF),
        attention_t.astype(BF),
        (0, part * query_length),
    )
    low_t = low_t.reshape(HEAD_DIM, groups, group_rows).transpose(1, 0, 2)

    def gather_heads(coords, ins, outs):
        c, g, t = coords
        moves = [
            Move(s, ins[0].at[lax.rem(g + s[1], groups)], outs[0].at[t, g]) for s in group_steps
        ]
        local = [(ins[0].at[g], outs[0].at[t, g])]
        for s in team_steps:
            moves.append(Move(s, ins[0].at[g], outs[0].at[t, g]))
        for k, s in enumerate(group_steps):
            source = lax.rem(g + groups - s[1], groups)
            for e in team_steps:
                moves.append(Move(e, outs[0].at[t, source], outs[0].at[t, source], after=k))
        return local, moves

    [attended] = exchange(
        "attended",
        4,
        sizes,
        (low_t,),
        [((team, groups, HEAD_DIM, group_rows), BF)],
        gather_heads,
    )
    if reps > 1:
        attended = lax.dynamic_index_in_dim(
            attended.reshape(team, team_heads, reps, HEAD_DIM, group_rows),
            lax.div(group, groups // reps),
            2,
            keepdims=False,
        )
    attended_t = attended.reshape(width, group_rows)

    slots = team * capacity
    (
        second_low,
        dense_grad,
        send_s,
        send_g,
        select,
        mixes,
        middle_own,
        prob_own,
        hot_own,
        second_own,
        attended_own,
        _,
    ) = between(
        experts,
        sizes,
        slots,
        member[None],
        attended_t,
        out_weight,
        token_rows,
        vectors,
        router_weight,
        route_all,
        cot_rows.reshape(group_rows, width),
    )
    (
        layer_sum,
        second_sum,
        sums_own,
        expert_active,
        hidden_grad,
        arrived_in,
        arrived_grad,
        ff_terms,
    ) = feed_forward(
        sizes,
        rows,
        send_s,
        send_g,
        expert_up[0],
        expert_down[0],
        second_low,
        dense_grad,
        ff_half,
        select,
        cot_rows.reshape(group_rows, width),
        mixes,
    )
    ff_sum = over_groups(ff_terms)
    down_sum = ff_sum[:, :width].astype(F32)
    up_sum = ff_sum[:, width:].reshape(team, wr, up_cols)
    entries = two * groups * slots
    expert_down_grad = row_sum(expert_active, arrived_grad.reshape(entries, width), TILE)
    expert_up_grad = row_sum(arrived_in.reshape(entries, width), hidden_grad, 128)

    layer_out, middle_grad, flow_t, out_term, small_t = turn(
        experts,
        layer_sum,
        second_sum,
        sums_own,
        middle_own,
        prob_own,
        hot_own,
        second_own,
        attended_own,
        cotangent[0],
        router_weight,
        out_weight,
        vectors,
    )
    flow_t = flow_t.reshape(team, team_heads, HEAD_DIM, rows)
    out_halves = out_term.reshape(two, groups, team, wr, width)

    def spread_flow(coords, ins, outs):
        c, g, t = coords
        moves = []
        for dg in range(groups):
            for dt in range(team):
                if dg or dt:
                    to_g, to_t = lax.rem(g + dg, groups), lax.rem(t + dt, team)
                    moves.append(
                        Move((0, dg, dt), ins[0].at[to_t, lax.div(to_g, reps)], outs[0].at[g, t])
                    )
        moves.append(Move((1, 0, 0), ins[1].at[lax.rem(c + 1, two)], outs[1]))
        return [(ins[0].at[t, lax.div(g, reps)], outs[0].at[g, t])], moves

    flow_parts, out_got = exchange(
        "flow",
        8,
        sizes,
        (flow_t, out_halves),
        [((groups, team, HEAD_DIM, rows), BF), (out_halves.shape[1:], BF)],
        spread_flow,
    )
    flow_all = flow_parts.transpose(2, 0, 1, 3).reshape(HEAD_DIM, length)
    flow_all = lax.dynamic_slice(
        flow_all, (0, part * query_length), (HEAD_DIM, query_length)
    )
    do_pad = jnp.concatenate([zeros, flow_all], axis=0)
    query_grad, pair_grad = attend_back(
        False,
        bounds,
        meta,
        place_col,
        q_pad,
        do_pad,
        attention_t,
        log_total,
        kv_rows,
        kv_t,
    )
    query_grad = lax.dynamic_update_slice(
        jnp.zeros((HEAD_DIM, length), BF), query_grad, (0, part * query_length)
    )
    grad_parts = jnp.concatenate([query_grad, pair_grad], axis=0)
    grad_parts = grad_parts.reshape(3, HEAD_DIM, groups, group_rows).transpose(2, 0, 1, 3)
    out_keep = lax.dynamic_index_in_dim(out_halves, core, 0, keepdims=False)
    out_parts = tall(
        (out_keep.astype(F32) + out_got.astype(F32))
        .astype(BF)
        .transpose(1, 0, 2, 3)
        .reshape(team, groups * wr, width)
    )

    def mixed_build(coords, ins, outs):
        c, g, t = coords
        moves = [
            Move(s, ins[0].at[lax.rem(g + s[1], groups)], outs[0].at[:, g])
            for s in group_steps
        ]
        moves += [
            Move(s, ins[1].at[lax.rem(t + s[2], team)], outs[1].at[t]) for s in team_steps
        ]
        return [(ins[0].at[g], outs[0].at[:, g]), (ins[1].at[t], outs[1].at[t])], moves

    grad_parts, out_parts = exchange(
        "mixed",
        9,
        sizes,
        (grad_parts, out_parts),
        [((3, groups, HEAD_DIM, group_rows), BF), (out_parts.shape, BF)],
        mixed_build,
    )
    out_parts = tall(
        jnp.sum(out_parts.astype(F32), axis=0).astype(BF).reshape(groups, wr, width)
    )
    if reps > 1:
        grad_parts = jnp.sum(
            grad_parts.reshape(3, team_heads, reps, HEAD_DIM, group_rows).astype(F32), axis=2
        ).astype(BF)
    mixed_grad_t = grad_parts.reshape(qkv_cols, group_rows)
    normed_part = (
        lax.dot_general(
            mixed_grad_t, qkv_weight, (((0,), (1,)), ((), ())), preferred_element_type=F32
        )
        .astype(BF)
        .reshape(team, rows, width)
    )
    qkv_term = lax.dot_general(
        normed_low, mixed_grad_t, (((0,), (1,)), ((), ())), preferred_element_type=F32
    )
    qkv_parts = core_half(qkv_term).astype(BF).reshape(groups, team * wr, qkv_cols)

    def normed_build(coords, ins, outs):
        c, g, t = coords
        moves, local = [], [(ins[2].at[t], outs[2].at[t])]
        for n in range(2):
            for s in group_steps:
                moves.append(Move(s, ins[n].at[lax.rem(g + s[1], groups)], outs[n].at[g]))
            local.append((ins[n].at[g], outs[n].at[g]))
        for s in team_steps:
            moves.append(Move(s, ins[2].at[lax.rem(t + s[2], team)], outs[2].at[t]))
        return local, moves

    qkv_parts, out_parts, normed_own = exchange(
        "normed",
        10,
        sizes,
        (qkv_parts, out_parts, normed_part),
        [(qkv_parts.shape, BF), (out_parts.shape, BF), (normed_part.shape, BF)],
        normed_build,
    )
    qkv_sum = (
        jnp.sum(qkv_parts.astype(F32), axis=0).astype(BF).reshape(team, wr, qkv_cols)
    )
    out_sum = jnp.sum(out_parts.astype(F32), axis=0).reshape(wr, width)
    normed_grad = jnp.sum(normed_own.astype(F32), axis=0)
    input_part_grad, gain_first, bias_first = jax.vjp(
        layer_norm, tokens[0].astype(F32), vectors[4], vectors[6]
    )[1](normed_grad)
    input_grad = middle_grad + input_part_grad

    small_used = small_t.shape[0]
    small_row = jnp.arange(small_used, dtype=jnp.int32)[:, None]
    small_t = jnp.where(
        small_row == experts + 2,
        gain_first[None],
        jnp.where(small_row == experts + 4, bias_first[None], small_t),
    )
    small_cols = small_used * wr
    small_pad = -(-small_cols // 1024) * 1024
    small_parts = jnp.pad(
        small_t.reshape(small_used, two * ctx_count, wr)
        .transpose(1, 0, 2)
        .reshape(two * ctx_count, small_cols),
        ((0, 0), (0, small_pad - small_cols)),
    ).reshape(two * ctx_count, small_pad // 128, 128)

    def owners_build(coords, ins, outs):
        c, g, t = coords
        moves, local = [], []
        for n in range(2):
            for s in team_steps:
                moves.append(Move(s, ins[n].at[lax.rem(t + s[2], team)], outs[n].at[t]))
            local.append((ins[n].at[t], outs[n].at[t]))
        me = c * ctx_count + g * team + t
        for dc in range(two):
            for dg in range(groups):
                for dt in range(team):
                    if dc or dg or dt:
                        to = (
                            lax.rem(c + dc, two) * ctx_count
                            + lax.rem(g + dg, groups) * team
                            + lax.rem(t + dt, team)
                        )
                        moves.append(Move((dc, dg, dt), ins[2].at[to], outs[2].at[me]))
        local.append((ins[2].at[me], outs[2].at[me]))
        return local, moves

    up_own, qkv_own, small_own = exchange(
        "owners",
        11,
        sizes,
        (tall(up_sum), tall(qkv_sum), small_parts),
        [
            (tall(up_sum).shape, BF),
            (tall(qkv_sum).shape, BF),
            (small_parts.shape, F32),
        ],
        owners_build,
    )
    small_sum = jnp.sum(small_own, axis=0).reshape(-1)[:small_cols].reshape(small_used, wr)
    up_own = (
        up_own.reshape(team, wr, two * groups, hidden_dev)
        .transpose(1, 2, 0, 3)
        .reshape(wr, hidden)
        .astype(F32)
    )
    qkv_own = (
        qkv_own.reshape(team, wr, 3, width // team)
        .transpose(1, 2, 0, 3)
        .reshape(wr, 3 * width)
        .astype(F32)
    )
    return (
        layer_out[None],
        input_grad[None].astype(BF),
        qkv_own,
        out_sum,
        up_own,
        down_sum,
        small_sum[:router_cols].T,
        small_sum[router_cols : router_cols + 2],
        small_sum[router_cols + 2 : router_cols + 4],
        expert_up_grad,
        expert_down_grad,
    )


def whole_kernel(sizes, experts, copies_count, *refs):
    two, groups, team = sizes
    (send_s, send_g, eup_h, edown_h, second_h, dgrad_h, ff_h, sel_h, cot_h) = refs[:9]
    (middle_h, prob_h, hot_h, own_h, att_h, rw_h, wo_h, vec_h) = refs[9:17]
    (
        layer_o, middle_o, small_o, flow_o, out_o, down_o, up_o,
        active_o, hgrad_o, arr_s_o, arr_g_o,
    ) = refs[17:28]
    (
        arr_s, arr_g, eup, edown, second, dgrad, upw, downw, sel, cot,
        slope, active, hgrad, acc, give, got_s, got_g, ret_s, ret_g, back_s, back_g,
        low, ugrad, lay, spa, lay_r, spa_r,
        term_give, term_got, out_got, ffg, ff_r,
        middle, prob, hot, own, att, rw, wo, vec, flow_t, flow_1, wo_s, wo_r,
        send_sem, recv_sem, load_sem, out_sem,
    ) = refs[28:]
    c = lax.axis_index("dp")
    i = lax.axis_index("ctx")
    g, t = lax.div(i, team), lax.rem(i, team)
    width = second.shape[1]
    rows = lay.shape[1]
    hid, ehid = upw.shape[1], eup.shape[1]
    core = lax.rem(c + 1, two)

    def device(step):
        if not isinstance(step, tuple):
            return c, step * team + t
        dc, dg, dt = step
        return (
            lax.rem(c + dc, two),
            lax.rem(g + dg, groups) * team + lax.rem(t + dt, team),
        )

    index = [0]

    def remote(src, dst, step):
        k = index[0]
        index[0] += 1
        assert k < copies_count
        return pltpu.make_async_remote_copy(
            src_ref=src,
            dst_ref=dst,
            send_sem=send_sem.at[k],
            recv_sem=recv_sem.at[k],
            device_id=device(step),
            device_id_type=MESH,
        )

    group_steps = [(0, k, 0) for k in range(1, groups)]
    team_steps = [(0, 0, k) for k in range(1, team)]
    swap = (1, 0, 0)
    deep = ff_h.shape[2]

    def block_of(core, k):
        return pl.ds(pl.multiple_of((core * groups + k) * deep, deep), deep)

    loads = []
    for k, (src, dst) in enumerate(
        [(second_h, second), (dgrad_h, dgrad)]
        + [
            (ff_h.at[k, n], weight.at[block_of(c, k), :])
            for n, weight in enumerate((upw, downw))
            for k in range(groups)
        ]
        + [
            (send_s.at[g], arr_s.at[c, g]), (eup_h, eup), (edown_h, edown),
            (send_g.at[g], arr_g.at[c, g]), (sel_h, sel), (cot_h, cot),
            (middle_h, middle), (prob_h, prob), (hot_h, hot), (own_h, own),
            (att_h, att), (rw_h, rw), (wo_h, wo), (vec_h, vec),
        ]
    ):
        load = pltpu.make_async_copy(src, dst, load_sem.at[k])
        load.start()
        loads.append(load)

    barrier = pltpu.get_barrier_semaphore()
    home_steps = [
        (0, dg, dt) for dg in range(groups) for dt in range(team) if dg or dt
    ]
    greet = home_steps + [swap]
    for step in greet:
        pl.semaphore_signal(barrier, inc=1, device_id=device(step), device_id_type=MESH)
    pl.semaphore_wait(barrier, len(greet))

    every = []

    def launch(copy):
        copy.start()
        every.append(copy)
        return copy

    each = arr_s.shape[2] // team

    def to_home(src, dst):
        me = g * team + t
        made = []
        for s in home_steps:
            to_g, to_t = lax.rem(g + s[1], groups), lax.rem(t + s[2], team)
            made.append(launch(remote(src.at[to_g, span(to_t, each), :], dst.at[me], s)))
        dst[me] = src[g, span(t, each), :]
        return made

    def source(s):
        return lax.rem(g + groups - s[1], groups)

    swap_w = [
        launch(remote(ff_h.at[k, n], weight.at[block_of(c, k), :], swap))
        for k in range(groups)
        for n, weight in enumerate((upw, downw))
    ]
    out_s = [
        launch(remote(send_s.at[lax.rem(g + s[1], groups)], arr_s.at[c, g], s))
        for s in group_steps
    ]
    swap_s = [launch(remote(send_s.at[g], arr_s.at[c, g], swap))]
    dense_loads = 2 + 2 * groups
    for load in loads[:dense_loads]:
        load.wait()
    for copy in swap_w:
        copy.wait_recv()

    def dense_in(h, carry):
        at = span(h, TILE)
        value, bend = gelu_and_slope(dot_f32(second[...], upw[:, at]))
        low[:, at] = value.astype(BF)
        ugrad[:, at] = (bend * contract_cols(dgrad[...], downw[at, :])).astype(BF)
        return carry

    lax.fori_loop(0, hid // TILE, dense_in, 0)
    out_g = [
        launch(remote(send_g.at[lax.rem(g + s[1], groups)], arr_g.at[c, g], s))
        for s in group_steps
    ]
    swap_g = [launch(remote(send_g.at[g], arr_g.at[c, g], swap))]

    def dense_out(n, carry):
        at = span(n, TILE)
        made = dot_f32(low[...], downw[:, at])
        lay[:, :, at] = made.astype(BF).reshape(team, rows, TILE)
        made = contract_cols(ugrad[...], upw[at, :])
        spa[:, :, at] = made.astype(BF).reshape(team, rows, TILE)
        return carry

    lax.fori_loop(0, width // TILE, dense_out, 0)

    def to_team(src, dst):
        made = [launch(remote(src.at[lax.rem(t + s[2], team)], dst.at[t], s)) for s in team_steps]
        dst[t] = src[t]
        return made

    team_copies = to_team(lay, lay_r) + to_team(spa, spa_r)

    for load in loads[dense_loads : dense_loads + 4]:
        load.wait()
    for copy, s in zip(out_s, group_steps):
        copy.wait_recv()
        swap_s.append(launch(remote(arr_s.at[c, source(s)], arr_s.at[c, source(s)], swap)))
    for copy in swap_s:
        copy.wait_recv()
    entries = 2 * groups * arr_s.shape[2]

    def expert_in(h, carry):
        at = span(h, TILE)
        value, bend = gelu_and_slope(dot_f32(arr_s[...].reshape(entries, width), eup[:, at]))
        active[:, at] = value.astype(BF)
        slope[:, at] = bend
        return carry

    lax.fori_loop(0, ehid // TILE, expert_in, 0)
    keeps = [
        pltpu.make_async_copy(active, active_o, out_sem.at[0]),
        pltpu.make_async_copy(arr_s, arr_s_o, out_sem.at[1]),
    ]
    for copy in keeps:
        copy.start()

    def expert_out(n, carry):
        at = span(n, TILE)
        acc[:, :, at] = dot_f32(active[...], edown[:, at]).reshape(2, entries // 2, TILE)
        return carry

    lax.fori_loop(0, width // TILE, expert_out, 0)
    give[0] = acc[core].astype(BF)
    other_s = launch(remote(give.at[0], got_s, swap))

    for copy, s in zip(out_g, group_steps):
        copy.wait_recv()
        swap_g.append(launch(remote(arr_g.at[c, source(s)], arr_g.at[c, source(s)], swap)))
    other_s.wait_recv()
    ret_s[...] = (acc[c] + got_s[...].astype(F32)).astype(BF).reshape(ret_s.shape)
    home_s = to_home(ret_s, back_s)
    for copy in swap_g:
        copy.wait_recv()

    def expert_back(h, carry):
        at = span(h, TILE)
        pull = contract_cols(arr_g[...].reshape(entries, width), edown[at, :])
        hgrad[:, at] = (slope[:, at] * pull).astype(BF)
        return carry

    lax.fori_loop(0, ehid // TILE, expert_back, 0)
    keeps += [
        pltpu.make_async_copy(hgrad, hgrad_o, out_sem.at[2]),
        pltpu.make_async_copy(arr_g, arr_g_o, out_sem.at[3]),
    ]
    for copy in keeps[2:]:
        copy.start()

    def expert_back_out(n, carry):
        at = span(n, TILE)
        acc[:, :, at] = contract_cols(hgrad[...], eup[at, :]).reshape(2, entries // 2, TILE)
        return carry

    lax.fori_loop(0, width // TILE, expert_back_out, 0)
    give[1] = acc[core].astype(BF)
    other_g = launch(remote(give.at[1], got_g, swap))
    other_g.wait_recv()
    ret_g[...] = (acc[c] + got_g[...].astype(F32)).astype(BF).reshape(ret_g.shape)
    home_g = to_home(ret_g, back_g)

    half = hid // 2
    term_tile = 128

    def down_term(base, n):
        at = pl.ds(pl.multiple_of(base + n * term_tile, term_tile), term_tile)
        return contract_rows(low[:, at], dgrad[...])

    def up_term(base, n):
        at = pl.ds(pl.multiple_of(base + n * term_tile, term_tile), term_tile)
        return contract_rows(second[:, at], ugrad[...])

    terms = []
    for k, (term, size) in enumerate(((down_term, half), (up_term, width // 2))):

        def giving(n, carry, k=k, term=term, size=size):
            term_give[k, span(n, term_tile), :] = term(core * size, n).astype(BF)
            return carry

        lax.fori_loop(0, size // term_tile, giving, 0)
        terms.append(launch(remote(term_give.at[k], term_got.at[k], swap)))
    for k, (term, size) in enumerate(((down_term, half), (up_term, width // 2))):
        terms[k].wait_recv()

        def keeping(n, carry, k=k, term=term, size=size):
            at = span(n, term_tile)
            total = term(c * size, n) + term_got[k, at, :].astype(F32)
            ffg[k, at, :] = total.astype(BF)
            return carry

        lax.fori_loop(0, size // term_tile, keeping, 0)
    up_copy = pltpu.make_async_copy(ffg.at[1], up_o, out_sem.at[4])
    up_copy.start()

    for load in loads[dense_loads + 4 :]:
        load.wait()
    for copy in team_copies + home_s:
        copy.wait_recv()
    lane = lax.broadcasted_iota(jnp.int32, (rows, 128), 1)
    places = groups * team * each
    chances, chosen = prob[...], hot[...]
    mix0 = jnp.sum(jnp.where(lane == experts, chances, 0.0), axis=1, keepdims=True)
    mix1 = jnp.sum(jnp.where(lane == experts + 1, chances, 0.0), axis=1, keepdims=True)
    gate = jnp.sum(chances * chosen, axis=1, keepdims=True)
    flow = cot[...].astype(F32)
    plain = jnp.sum(lay_r[...].astype(F32), axis=0)
    found = dot_f32(sel[...], back_s[...].reshape(places, width))
    layer_o[...] = (middle[...] + mix0 * plain + (mix1 * gate) * found).astype(BF)
    s0 = jnp.sum(flow * plain, axis=1, keepdims=True)
    s1 = jnp.sum(flow * found, axis=1, keepdims=True)
    pulls = jnp.where(lane == experts, s0, jnp.where(lane == experts + 1, s1 * gate, 0.0))
    mean_pull = jnp.sum(chances * pulls, axis=1, keepdims=True)
    logit_grad = chances * jnp.where(
        lane < experts, (s1 * mix1) * (chosen - gate), pulls - mean_pull
    )
    logit_grad = jnp.where(lane < experts + 2, logit_grad, 0.0).astype(BF)
    hat, scale = normalize(middle[...])
    early = jnp.sum(spa_r[...].astype(F32), axis=0) + contract_cols(logit_grad, rw[...])
    for copy in home_g:
        copy.wait_recv()
    piece = half // groups

    def other_group(bit, group):
        return group + bit - 2 * bit * lax.rem(lax.div(group, bit), 2)

    near, far = other_group(1, g), other_group(2, g)
    last = other_group(2, near)
    for_far = launch(remote(ffg.at[0, span(last, piece), :], ff_r.at[0], near))
    downs = [launch(remote(ffg.at[0, span(near, piece), :], ff_r.at[1], near))]

    second_grad = early + dot_f32(sel[...], back_g[...].reshape(places, width))
    pull = second_grad * vec[5:6, :]
    moved = scale * (
        pull
        - jnp.mean(pull, axis=-1, keepdims=True)
        - hat * jnp.mean(pull * hat, axis=-1, keepdims=True)
    )
    middle_grad = flow + moved
    middle_o[...] = middle_grad
    branch = middle_grad.astype(BF)

    for n in range(team):
        at = slice(n * (width // team), (n + 1) * (width // team))
        flow_t[n] = contract_cols(wo[at, :], branch).astype(BF).reshape(flow_t.shape[1:])
    flowed = [
        launch(remote(flow_t.at[lax.rem(t + s[2], team)], flow_1.at[t], s)) for s in team_steps
    ]
    flow_1[t] = flow_t[t]

    def out_term(base, n):
        at = pl.ds(pl.multiple_of(base + n * term_tile, term_tile), term_tile)
        return dot_f32(att[at, :], branch)

    def out_giving(n, carry):
        term_give[0, span(n, term_tile), :] = out_term(core * (width // 2), n).astype(BF)
        return carry

    terms[0].wait_send()
    every[:] = [copy for copy in every if copy is not terms[0]]
    lax.fori_loop(0, width // 2 // term_tile, out_giving, 0)
    out_cross = launch(remote(term_give.at[0], out_got, swap))
    for copy in flowed:
        copy.wait_recv()
    flowed = [
        launch(remote(flow_1.at[:, lax.rem(g + s[1], groups)], flow_o.at[g], s))
        for s in group_steps
    ]
    own_flow = pltpu.make_async_copy(flow_1.at[:, g], flow_o.at[g], out_sem.at[5])
    own_flow.start()
    for_far.wait_recv()
    ff_r[3] = (ffg[0, span(far, piece), :].astype(F32) + ff_r[0].astype(F32)).astype(BF)
    downs.append(launch(remote(ff_r.at[3], ff_r.at[2], far)))
    out_cross.wait_recv()
    wr = wo_s.shape[2]

    def out_keeping(n, carry):
        at = span(n, term_tile)
        total = out_term(c * (width // 2), n) + out_got[at, :].astype(F32)
        wo_s[:, n] = total.astype(BF).reshape(team, wr, width)
        return carry

    lax.fori_loop(0, groups, out_keeping, 0)
    outs = to_team(wo_s, wo_r)

    routed = contract_rows(logit_grad, own[...])[: small_o.shape[0], :]
    which = lax.broadcasted_iota(jnp.int32, routed.shape, 0)
    gain = jnp.sum(second_grad * hat, axis=0, keepdims=True)
    bias = jnp.sum(second_grad, axis=0, keepdims=True)
    small_o[...] = jnp.where(
        which == experts + 3, gain, jnp.where(which == experts + 5, bias, routed)
    )
    for copy in outs:
        copy.wait_recv()
    out_o[...] = jnp.sum(wo_r[...].astype(F32), axis=0).astype(BF)
    for copy in downs:
        copy.wait_recv()
    down_o[...] = (
        ffg[0, span(g, piece), :].astype(F32) + ff_r[1].astype(F32) + ff_r[2].astype(F32)
    )
    for copy in flowed:
        copy.wait_recv()
    for copy in keeps + [up_copy, own_flow]:
        copy.wait()
    for copy in every:
        copy.wait_send()


def whole(
    sizes, rows, experts, wr, send_s, send_g, eup, edown, second, dgrad, ff, sel, cot,
    middle, prob, hot, own, att, rw, wo, vec,
):
    two, groups, team = sizes
    slots = send_s.shape[1]
    width = second.shape[1]
    hid, ehid = ff.shape[3], eup.shape[1]
    entries = 2 * groups * slots
    used = -(-(experts + 6) // 8) * 8
    homes = groups * team - 1
    count = 3 * (groups - 1) + 4 * groups + 5 + 4 * (team - 1) + 2 * homes + 3
    each = slots // team
    arrived = (two, groups, slots, width)
    anywhere = pl.BlockSpec(memory_space=pl.ANY)
    inside = pl.BlockSpec(memory_space=pltpu.VMEM)
    team_rows = team * rows
    heads = (groups, HEAD_DIM, rows)
    shapes = (
        ((rows, width), BF),
        ((rows, width), F32),
        ((used, width), F32),
        ((groups, team, HEAD_DIM, rows), BF),
        ((groups, wr, width), BF),
        ((hid // 2 // groups, width), F32),
        ((width // 2, hid), BF),
        ((entries, ehid), BF),
        ((entries, ehid), BF),
        (arrived, BF),
        (arrived, BF),
    )
    scratch = (
        (arrived, BF), (arrived, BF), (eup.shape, BF), (edown.shape, BF), (second.shape, BF),
        (dgrad.shape, BF), ((width, hid), BF), ((hid, width), BF), (sel.shape, BF),
        (cot.shape, BF),
        ((entries, ehid), F32), ((entries, ehid), BF), ((entries, ehid), BF),
        ((2, entries // 2, width), F32), ((2, entries // 2, width), BF),
        ((entries // 2, width), BF), ((entries // 2, width), BF),
        ((groups, slots, width), BF), ((groups, slots, width), BF),
        ((groups * team, each, width), BF), ((groups * team, each, width), BF),
        ((team_rows, hid), BF), ((team_rows, hid), BF),
        ((team, rows, width), BF), ((team, rows, width), BF),
        ((team, rows, width), BF), ((team, rows, width), BF),
        ((2, hid // 2, width), BF), ((2, hid // 2, width), BF), ((width // 2, width), BF),
        ((2, hid // 2, width), BF),
        ((groups, hid // 2 // groups, width), BF),
        (middle.shape, F32), (prob.shape, F32), (hot.shape, F32), (own.shape, BF),
        (att.shape, BF), (rw.shape, BF), (wo.shape, BF), (vec.shape, F32),
        ((team,) + heads, BF), ((team,) + heads, BF),
        ((team, groups, wr, width), BF), ((team, groups, wr, width), BF),
    )
    return pl.pallas_call(
        functools.partial(whole_kernel, sizes, experts, count),
        name="feed_forward",
        out_shape=tuple(jax.ShapeDtypeStruct(s, d) for s, d in shapes),
        in_specs=[anywhere] * 17,
        out_specs=tuple(inside if n in (0, 1, 2, 4, 5) else anywhere for n in range(11)),
        scratch_shapes=[pltpu.VMEM(s, d) for s, d in scratch]
        + [
            pltpu.SemaphoreType.DMA((count,)),
            pltpu.SemaphoreType.DMA((count,)),
            pltpu.SemaphoreType.DMA((16 + 2 * groups,)),
            pltpu.SemaphoreType.DMA((6,)),
        ],
        compiler_params=pltpu.CompilerParams(
            collective_id=14, has_side_effects=True, vmem_limit_bytes=60 * 2**20
        ),
        cost_estimate=pl.CostEstimate(flops=0, bytes_accessed=300_000_000, transcendentals=0),
    )(
        send_s, send_g, eup, edown, second, dgrad, ff, sel, cot,
        middle, prob, hot, own, att, rw, wo, vec,
    )


def deliver_kernel(experts, count, shift, small, *refs):
    ins, outs = refs[:count], refs[count : 2 * count]
    router, gains, biases, sem = refs[2 * count :]
    copies = [pltpu.make_async_copy(a, b, sem.at[n]) for n, (a, b) in enumerate(zip(ins, outs))]
    for copy in copies:
        copy.start()
    wr = router.shape[1]
    mine = pltpu.roll(small[...], lax.rem(128 - shift[0], 128), 1)[:, :wr]
    router[...] = mine[: experts + 2, :]
    gains[...] = mine[experts + 2 : experts + 4, :]
    biases[...] = mine[experts + 4 : experts + 6, :]
    for copy in copies:
        copy.wait()


def deliver(experts, shift, small, arrays):
    wr = arrays[2].shape[0]
    anywhere = pl.BlockSpec(memory_space=pl.ANY)
    inside = pl.BlockSpec(memory_space=pltpu.VMEM)
    count = len(arrays)
    return pl.pallas_call(
        functools.partial(deliver_kernel, experts, count),
        name="deliver",
        in_specs=[pl.BlockSpec(memory_space=pltpu.SMEM)] + [inside] * (count + 1),
        out_specs=tuple([anywhere] * count + [inside] * 3),
        out_shape=tuple(jax.ShapeDtypeStruct(a.shape, a.dtype) for a in arrays)
        + (
            jax.ShapeDtypeStruct((experts + 2, wr), F32),
            jax.ShapeDtypeStruct((2, wr), F32),
            jax.ShapeDtypeStruct((2, wr), F32),
        ),
        scratch_shapes=[pltpu.SemaphoreType.DMA((count,))],
        compiler_params=pltpu.CompilerParams(vmem_limit_bytes=60 * 2**20),
    )(shift, small, *arrays)


def per_device(
    tokens,
    cotangent,
    block_order,
    doc_lengths,
    routes,
    w_qkv,
    w_out,
    w_up,
    w_down,
    router,
    norm_gains,
    norm_biases,
    expert_up,
    expert_down,
):
    rows, width = tokens.shape[1], tokens.shape[2]
    ctx_count = lax.axis_size("ctx")
    two = lax.axis_size("dp")
    team = math.gcd(4, ctx_count)
    groups = ctx_count // team
    sizes = (two, groups, team)
    length = rows * ctx_count
    wr = w_qkv.shape[0]
    experts = ctx_count * expert_up.shape[0]
    fits = groups == team == 4 and groups * team == HEADS and team * wr == 128 and w_up.shape[1] == team * width
    if not fits or length // block_order.shape[0] != BLOCK:
        return per_device_general(
            tokens, cotangent, block_order, doc_lengths, routes, w_qkv, w_out, w_up, w_down,
            router, norm_gains, norm_biases, expert_up, expert_down,
        )
    group_rows = rows * team
    capacity = max(2, 2 * rows // experts)
    slots = team * capacity
    hidden = w_up.shape[1]
    hidden_dev = w_down.shape[0]
    up_cols = hidden // team
    ctx = lax.axis_index("ctx")
    core = lax.axis_index("dp")
    group, member = lax.div(ctx, team), lax.rem(ctx, team)
    by_group = [[g * team + t for g in range(groups)] for t in range(team)]
    team_steps = [(0, 0, k) for k in range(1, team)]

    router_cols = router.shape[1]
    (
        token_rows,
        cot_rows,
        head_parts,
        normed,
        weights,
        vectors,
        out_weight,
        ff_part,
        route_all,
        router_weight,
    ) = start(
        sizes,
        tokens[0],
        cotangent[0],
        w_qkv,
        w_up,
        w_down,
        w_out,
        router.T,
        norm_gains,
        norm_biases,
        routes[0].reshape(1, rows),
    )
    out_weight = out_weight.reshape(width, width)
    token_rows = token_rows.reshape(group_rows, width)
    cot_rows = cot_rows.reshape(group_rows, width)

    ff_half = lax.all_gather(
        ff_part.reshape(2, team * wr, width),
        "ctx",
        axis=0,
        tiled=False,
        axis_index_groups=by_group,
    )
    low_t, attention_t, log_total, q_pad, kv_t, kv_rows = sorted_attend(
        doc_lengths[0], block_order, head_parts.reshape(groups, 3 * HEAD_DIM, group_rows)
    )

    def gather_heads(coords, ins, outs):
        c, g, t = coords
        steps = [(0, k, 0) for k in range(1, groups)]
        moves = [Move(s, ins[0].at[lax.rem(g + s[1], groups)], outs[0].at[t, g]) for s in steps]
        local = [(ins[0].at[g], outs[0].at[t, g])]
        for s in team_steps:
            moves.append(Move(s, ins[0].at[g], outs[0].at[t, g]))
        for k, s in enumerate(steps):
            source = lax.rem(g + groups - s[1], groups)
            for e in team_steps:
                moves.append(Move(e, outs[0].at[t, source], outs[0].at[t, source], after=k))
        return local, moves

    [attended] = exchange(
        "attended",
        4,
        sizes,
        (low_t,),
        [((team, groups, HEAD_DIM, group_rows), BF)],
        gather_heads,
    )
    (
        second_low,
        dense_grad,
        send_s,
        send_g,
        select,
        mixes,
        middle_own,
        prob_own,
        hot_own,
        second_own,
        attended_own,
        select_own,
    ) = between(
        experts,
        sizes,
        slots,
        member[None],
        attended.reshape(width, group_rows),
        out_weight,
        token_rows,
        vectors,
        router_weight,
        route_all,
        cot_rows,
    )
    (
        layer_out,
        middle_grad,
        small_t,
        flow_parts,
        out_sum,
        down_sum,
        up_half,
        expert_active,
        hidden_grad,
        arrived_in,
        arrived_grad,
    ) = whole(
        sizes,
        rows,
        experts,
        wr,
        send_s,
        send_g,
        expert_up[0],
        expert_down[0],
        second_low,
        dense_grad,
        ff_half,
        select_own,
        cotangent[0],
        middle_own,
        prob_own,
        hot_own,
        second_own,
        attended_own,
        router_weight,
        out_weight,
        vectors,
    )

    def pieces_of(array, along):
        count = groups if along == "g" else team
        me = group if along == "g" else member
        found = [lax.dynamic_index_in_dim(array, me, 0, keepdims=False)]
        for step in range(1, count):
            if along == "g":
                pairs = [
                    (g * team + t, (g + step) % groups * team + t)
                    for g in range(groups)
                    for t in range(team)
                ]
            else:
                pairs = [
                    (g * team + t, g * team + (t + step) % team)
                    for g in range(groups)
                    for t in range(team)
                ]
            chunk = lax.dynamic_index_in_dim(array, lax.rem(me + step, count), 0, keepdims=False)
            found.append(lax.ppermute(chunk, "ctx", pairs))
        return found

    up_sum = lax.psum_scatter(
        up_half, "ctx", scatter_dimension=0, tiled=True, axis_index_groups=by_group
    ).reshape(team, wr, up_cols)
    grad_parts = sorted_back(
        doc_lengths[0],
        block_order,
        flow_parts.reshape(ctx_count, HEAD_DIM, rows),
        attention_t,
        log_total,
        q_pad,
        kv_t,
        kv_rows,
        groups,
    )

    grad_parts, expert_active, hidden_grad = lax.optimization_barrier(
        (grad_parts, expert_active, hidden_grad)
    )

    pieces = pieces_of(grad_parts, "g")
    entries = two * groups * slots
    expert_down_grad = row_sum(expert_active, arrived_grad.reshape(entries, width), TILE)
    expert_up_grad = row_sum(arrived_in.reshape(entries, width), hidden_grad, 128)
    input_grad, qkv_own, up_own, out_own, small_own = end(
        sizes,
        experts,
        pieces,
        weights,
        normed,
        tokens[0],
        vectors,
        middle_grad,
        small_t,
        up_sum,
        out_sum,
    )
    delivered = deliver(
        experts,
        member[None] * wr,
        small_own,
        (layer_out, input_grad, qkv_own, out_own, up_own, down_sum),
    )
    layer_out, input_grad, qkv_own, out_own, up_own, down_sum = delivered[:6]
    router_own, gains_own, biases_own = delivered[6:]
    return (
        layer_out[None],
        input_grad[None],
        qkv_own,
        out_own,
        up_own,
        down_sum,
        router_own.T,
        gains_own,
        biases_own,
        expert_up_grad,
        expert_down_grad,
    )


def solution(mesh):
    in_specs = (
        P("dp", "ctx", None),
        P("dp", "ctx", None),
        P(),
        P("dp", None),
        P("dp", "ctx", None),
        P(("dp", "ctx"), None),
        P(("dp", "ctx"), None),
        P(("dp", "ctx"), None),
        P(("dp", "ctx"), None),
        P(("dp", "ctx"), None),
        P(None, ("dp", "ctx")),
        P(None, ("dp", "ctx")),
        P("ctx", None, "dp"),
        P("ctx", "dp", None),
    )
    out_specs = (
        P("dp", "ctx", None),
        P("dp", "ctx", None),
        P(("dp", "ctx"), None),
        P(("dp", "ctx"), None),
        P(("dp", "ctx"), None),
        P(("dp", "ctx"), None),
        P(("dp", "ctx"), None),
        P(None, ("dp", "ctx")),
        P(None, ("dp", "ctx")),
        P("ctx", None, "dp"),
        P("ctx", "dp", None),
    )
    return jax.shard_map(
        per_device, mesh=mesh, in_specs=in_specs, out_specs=out_specs, check_vma=False
    )
```

```python
import functools
import math

import jax
import jax.numpy as jnp
from jax import lax
from jax.experimental import pallas as pl
from jax.experimental.pallas import tpu as pltpu
from jax.sharding import PartitionSpec as P

HEADS = 16
HEAD_DIM = 64

EPS = 1e-05
NEG = -1e30
SCALE = 0.125
TILE = 256
BF = jnp.bfloat16
F32 = jnp.float32
MESH = pl.DeviceIdType.MESH


def layer_norm(values, gain, shift):
    center = values - jnp.mean(values, axis=-1, keepdims=True)
    spread = jnp.mean(center * center, axis=-1, keepdims=True)
    return center * lax.rsqrt(spread + EPS) * gain + shift


def gelu_tanh(values):
    return jax.nn.gelu(values, approximate=True)


def router_heads(router_logits, route_hot, experts):
    chances = jax.nn.softmax(router_logits[:, :experts], axis=-1)
    gate = jnp.sum(chances * route_hot, axis=-1)
    mixing = jax.nn.softmax(router_logits[:, experts:], axis=-1)
    return (gate, mixing[:, 0], mixing[:, 1])


def dot_f32(left, right):
    return jnp.dot(left, right, preferred_element_type=F32)


def contract_rows(left, right):
    return lax.dot_general(left, right, (((0,), (0,)), ((), ())), preferred_element_type=F32)


def contract_cols(left, right):
    return lax.dot_general(left, right, (((1,), (1,)), ((), ())), preferred_element_type=F32)


def span(i, size):
    return pl.ds(pl.multiple_of(i * size, size), size)


class Move:
    def __init__(self, step, src, dst, after=None):
        self.step, self.src, self.dst, self.after = step, src, dst, after


def exchange(name, cid, sizes, ins, outs, build, micros=20):
    two, groups, team = sizes

    def kernel(*refs):
        in_refs, out_refs = refs[: len(ins)], refs[len(ins) : len(ins) + len(outs)]
        send_sem, recv_sem, local_sem = refs[len(ins) + len(outs) :]
        c = lax.axis_index("dp")
        i = lax.axis_index("ctx")
        g, t = lax.div(i, team), lax.rem(i, team)

        def device(step):
            dc, dg, dt = step
            return (
                lax.rem(c + dc, two),
                lax.rem(g + dg, groups) * team + lax.rem(t + dt, team),
            )

        locals_, moves = build((c, g, t), in_refs, out_refs)
        steps = sorted({m.step for m in moves})
        greet = sorted(
            set(steps) | {((-a) % two, (-b) % groups, (-d) % team) for a, b, d in steps}
        )
        barrier = pltpu.get_barrier_semaphore()
        for step in greet:
            pl.semaphore_signal(barrier, inc=1, device_id=device(step), device_id_type=MESH)
        pl.semaphore_wait(barrier, len(greet))

        copies = {}
        arrived = set()
        for k, (src, dst) in enumerate(locals_):
            copies[("local", k)] = pltpu.make_async_copy(src, dst, local_sem.at[k])
        for k, m in enumerate(moves):
            copies[k] = pltpu.make_async_remote_copy(
                src_ref=m.src,
                dst_ref=m.dst,
                send_sem=send_sem.at[k],
                recv_sem=recv_sem.at[k],
                device_id=device(m.step),
                device_id_type=MESH,
            )
        for k, m in enumerate(moves):
            if m.after is None:
                copies[k].start()
        for k in range(len(locals_)):
            copies[("local", k)].start()
        for k, m in enumerate(moves):
            if m.after is not None:
                if m.after not in arrived:
                    arrived.add(m.after)
                    if isinstance(m.after, tuple):
                        copies[m.after].wait()
                    else:
                        copies[m.after].wait_recv()
                copies[k].start()
        for k in range(len(locals_)):
            if ("local", k) not in arrived:
                copies[("local", k)].wait()
        for k in range(len(moves)):
            if k not in arrived:
                copies[k].wait_recv()
        for k in range(len(moves)):
            copies[k].wait_send()

    count = []

    def trace_counts():
        class Probe:
            def __getattr__(self, name):
                return self

            def __getitem__(self, index):
                return self

        locals_, moves = build((0, 0, 0), [Probe() for _ in ins], [Probe() for _ in outs])
        count.extend((len(locals_), len(moves)))

    trace_counts()
    return pl.pallas_call(
        kernel,
        name=name,
        out_shape=tuple(jax.ShapeDtypeStruct(s, d) for s, d in outs),
        in_specs=[pl.BlockSpec(memory_space=pl.ANY)] * len(ins),
        out_specs=tuple(pl.BlockSpec(memory_space=pl.ANY) for _ in outs),
        scratch_shapes=[
            pltpu.SemaphoreType.DMA((max(1, count[1]),)),
            pltpu.SemaphoreType.DMA((max(1, count[1]),)),
            pltpu.SemaphoreType.DMA((max(1, count[0]),)),
        ],
        compiler_params=pltpu.CompilerParams(collective_id=cid, has_side_effects=True),
        cost_estimate=pl.CostEstimate(
            flops=0, bytes_accessed=int(micros * 3.0e6), transcendentals=0
        ),
    )(*ins)


def mask_of(kt, key_place, query_place, query_low):
    return (key_place <= query_place) & (key_place >= query_low)


def key_places(sorted_rows, kt, place_ref):
    if sorted_rows:
        return lax.broadcasted_iota(jnp.int32, (TILE, TILE), 0) + kt * TILE
    return place_ref[pl.ds(pl.multiple_of(kt * TILE, TILE), TILE), :]


def attend_kernel(
    sorted_rows, bounds, meta_ref, place_ref, q_ref, rows_ref, kvt_ref, out_ref, lse_ref
):
    step = pl.program_id(0)
    queries = q_ref[...]
    place, low = meta_ref[0:1, :], meta_ref[1:2, :]

    def body(kt, carry):
        peak, total, acc = carry
        at = pl.ds(pl.multiple_of(kt * TILE, TILE), TILE)
        scores = dot_f32(rows_ref[at, :], queries)
        allowed = mask_of(kt, key_places(sorted_rows, kt, place_ref), place, low)
        scores = jnp.where(allowed, scores, NEG)
        new_peak = jnp.maximum(peak, jnp.max(scores, axis=0, keepdims=True))
        weights = jnp.exp(scores - new_peak)
        fade = jnp.exp(peak - new_peak)
        total = total * fade + jnp.sum(weights, axis=0, keepdims=True)
        acc = acc * fade + dot_f32(kvt_ref[HEAD_DIM:, at], weights.astype(BF))
        return new_peak, total, acc

    start = (
        jnp.full((1, TILE), NEG, F32),
        jnp.zeros((1, TILE), F32),
        jnp.zeros((HEAD_DIM, TILE), F32),
    )
    peak, total, acc = lax.fori_loop(bounds[step, 0], bounds[step, 1], body, start)
    out_ref[...] = acc / total
    lse_ref[...] = peak + jnp.log(total)


def attend_back_kernel(
    sorted_rows,
    tiles,
    bounds,
    meta_ref,
    place_ref,
    q_ref,
    do_ref,
    out_ref,
    lse_ref,
    rows_ref,
    kvt_ref,
    dq_ref,
    dkv_ref,
    acc_ref,
):
    step = pl.program_id(0)

    @pl.when(step == 0)
    def _():
        acc_ref[...] = jnp.zeros_like(acc_ref)

    queries, flows = q_ref[...], do_ref[...]
    place, low = meta_ref[0:1, :], meta_ref[1:2, :]
    log_total = lse_ref[...]
    delta = jnp.sum(flows[HEAD_DIM:, :].astype(F32) * out_ref[...], axis=0, keepdims=True)

    def body(kt, dq):
        at = pl.ds(pl.multiple_of(kt * TILE, TILE), TILE)
        rows = rows_ref[at, :]
        scores = dot_f32(rows, queries)
        allowed = mask_of(kt, key_places(sorted_rows, kt, place_ref), place, low)
        chances = jnp.exp(jnp.where(allowed, scores - log_total, NEG))
        flow = dot_f32(rows, flows)
        score_grad = (chances * (flow - delta)).astype(BF)
        dq = dq + dot_f32(kvt_ref[:HEAD_DIM, at], score_grad)
        acc_ref[:HEAD_DIM, at] += contract_cols(queries[:HEAD_DIM, :], score_grad)
        acc_ref[HEAD_DIM:, at] += contract_cols(flows[HEAD_DIM:, :], chances.astype(BF))
        return dq

    dq = lax.fori_loop(
        bounds[step, 0], bounds[step, 1], body, jnp.zeros((HEAD_DIM, TILE), F32)
    )
    dq_ref[...] = (dq * SCALE).astype(BF)

    @pl.when(step == tiles - 1)
    def _():
        dkv_ref[...] = acc_ref[...].astype(BF)


def attention_specs(length, query_length):
    def whole(shape):
        return pl.BlockSpec(shape, lambda i: (0, 0))

    def tile(rows):
        return pl.BlockSpec((rows, TILE), lambda i: (0, i))

    return whole, tile


def attend(sorted_rows, bounds, meta, place_col, q_pad, kv_rows, kv_t):
    length, query_length = kv_rows.shape[0], q_pad.shape[1]
    whole, tile = attention_specs(length, query_length)
    return pl.pallas_call(
        functools.partial(attend_kernel, sorted_rows),
        name="attend",
        grid=(query_length // TILE,),
        in_specs=[
            pl.BlockSpec(memory_space=pltpu.SMEM),
            tile(8),
            whole(place_col.shape),
            tile(2 * HEAD_DIM),
            whole((length, 2 * HEAD_DIM)),
            whole((2 * HEAD_DIM, length)),
        ],
        out_specs=(tile(HEAD_DIM), tile(1)),
        out_shape=(
            jax.ShapeDtypeStruct((HEAD_DIM, query_length), F32),
            jax.ShapeDtypeStruct((1, query_length), F32),
        ),
        compiler_params=pltpu.CompilerParams(vmem_limit_bytes=40 * 2**20),
    )(bounds, meta, place_col, q_pad, kv_rows, kv_t)


def attend_back(sorted_rows, bounds, meta, place_col, q_pad, do_pad, out, lse, kv_rows, kv_t):
    length, query_length = kv_rows.shape[0], q_pad.shape[1]
    whole, tile = attention_specs(length, query_length)
    return pl.pallas_call(
        functools.partial(attend_back_kernel, sorted_rows, query_length // TILE),
        name="attend_back",
        grid=(query_length // TILE,),
        in_specs=[
            pl.BlockSpec(memory_space=pltpu.SMEM),
            tile(8),
            whole(place_col.shape),
            tile(2 * HEAD_DIM),
            tile(2 * HEAD_DIM),
            tile(HEAD_DIM),
            tile(1),
            whole((length, 2 * HEAD_DIM)),
            whole((2 * HEAD_DIM, length)),
        ],
        out_specs=(tile(HEAD_DIM), whole((2 * HEAD_DIM, length))),
        out_shape=(
            jax.ShapeDtypeStruct((HEAD_DIM, query_length), BF),
            jax.ShapeDtypeStruct((2 * HEAD_DIM, length), BF),
        ),
        scratch_shapes=[pltpu.VMEM((2 * HEAD_DIM, length), F32)],
        compiler_params=pltpu.CompilerParams(vmem_limit_bytes=40 * 2**20),
    )(bounds, meta, place_col, q_pad, do_pad, out, lse, kv_rows, kv_t)


BLOCK = 64


def pick_pair(load, table, d):
    first, second = table[2 * d], table[2 * d + 1]
    left = load(lax.div(first, 2))
    right = load(lax.div(second, 2))
    lane = lax.broadcasted_iota(jnp.int32, left.shape, 1)
    left = jnp.where(lax.rem(first, 2) == 0, left, pltpu.roll(left, BLOCK, 1))
    right = jnp.where(lax.rem(second, 2) == 1, right, pltpu.roll(right, BLOCK, 1))
    return jnp.where(lane < BLOCK, left, right)


def column_block(ref, k, per):
    return ref[lax.div(k, per), :, span(lax.rem(k, per), 128)].astype(F32)


def fill_inverse(order, inverse, count):
    def put(n, carry):
        inverse[order[n]] = n
        return carry

    lax.fori_loop(0, count, put, 0)


def query_lows(lengths, step):
    place = lax.broadcasted_iota(jnp.int32, (1, TILE), 1) + step * TILE
    low = jnp.zeros((1, TILE), jnp.int32)
    first, end = 0, 0
    for n in range(lengths.shape[0]):
        end = end + lengths[n]
        low = jnp.where(end <= place, end, low)
        first = jnp.where(end <= step * TILE, end, first)
    return place, low, lax.div(first, TILE)


def sorted_attend_kernel(
    lengths, order, parts_ref, low_ref, out_ref, lse_ref, q_ref, kvt_ref, rows_ref, inverse
):
    step = pl.program_id(0)
    length = q_ref.shape[1]
    per = parts_ref.shape[2] // 128

    @pl.when(step == 0)
    def _():
        fill_inverse(order, inverse, length // BLOCK)

        def place(d, carry):
            tile = pick_pair(lambda k: column_block(parts_ref, k, per), inverse, d)
            at = span(d, 128)
            q_ref[:HEAD_DIM, at] = (tile[:HEAD_DIM] * SCALE).astype(BF)
            q_ref[HEAD_DIM:, at] = jnp.zeros((HEAD_DIM, 128), BF)
            kvt_ref[:, at] = tile[HEAD_DIM:].astype(BF)
            rows_ref[at, :] = tile[HEAD_DIM:].T.astype(BF)
            return carry

        lax.fori_loop(0, length // 128, place, 0)

    here = span(step, TILE)
    queries = q_ref[:, here]
    place, low, first = query_lows(lengths, step)

    def body(kt, carry):
        peak, total, acc = carry
        at = span(kt, TILE)
        scores = dot_f32(rows_ref[at, :], queries)
        allowed = mask_of(kt, key_places(True, kt, None), place, low)
        scores = jnp.where(allowed, scores, NEG)
        new_peak = jnp.maximum(peak, jnp.max(scores, axis=0, keepdims=True))
        weights = jnp.exp(scores - new_peak)
        fade = jnp.exp(peak - new_peak)
        total = total * fade + jnp.sum(weights, axis=0, keepdims=True)
        acc = acc * fade + dot_f32(kvt_ref[HEAD_DIM:, at], weights.astype(BF))
        return new_peak, total, acc

    start = (
        jnp.full((1, TILE), NEG, F32),
        jnp.zeros((1, TILE), F32),
        jnp.zeros((HEAD_DIM, TILE), F32),
    )
    peak, total, acc = lax.fori_loop(first, step + 1, body, start)
    out_ref[:, here] = acc / total
    lse_ref[:, here] = peak + jnp.log(total)

    @pl.when(step == length // TILE - 1)
    def _():
        def home(d, carry):
            tile = pick_pair(lambda k: out_ref[:, span(k, 128)], order, d)
            low_ref[lax.div(d, per), :, span(lax.rem(d, per), 128)] = tile.astype(BF)
            return carry

        lax.fori_loop(0, length // 128, home, 0)


def sorted_back_kernel(
    lengths, order, flow_ref, out_ref, lse_ref, q_ref, kvt_ref, rows_ref,
    grad_ref, do_ref, dq_ref, acc_ref, inverse,
):
    step = pl.program_id(0)
    length = q_ref.shape[1]
    per = grad_ref.shape[3] // 128

    @pl.when(step == 0)
    def _():
        acc_ref[...] = jnp.zeros_like(acc_ref)
        fill_inverse(order, inverse, length // BLOCK)

        def place(d, carry):
            tile = pick_pair(lambda k: flow_ref[k].astype(F32), inverse, d)
            at = span(d, 128)
            do_ref[:HEAD_DIM, at] = jnp.zeros((HEAD_DIM, 128), BF)
            do_ref[HEAD_DIM:, at] = tile.astype(BF)
            return carry

        lax.fori_loop(0, length // 128, place, 0)

    here = span(step, TILE)
    queries, flows = q_ref[:, here], do_ref[:, here]
    place, low, first = query_lows(lengths, step)
    log_total = lse_ref[:, here]
    delta = jnp.sum(flows[HEAD_DIM:, :].astype(F32) * out_ref[:, here], axis=0, keepdims=True)

    def body(kt, dq):
        at = span(kt, TILE)
        rows = rows_ref[at, :]
        scores = dot_f32(rows, queries)
        allowed = mask_of(kt, key_places(True, kt, None), place, low)
        chances = jnp.exp(jnp.where(allowed, scores - log_total, NEG))
        flow = dot_f32(rows, flows)
        score_grad = (chances * (flow - delta)).astype(BF)
        dq = dq + dot_f32(kvt_ref[:HEAD_DIM, at], score_grad)
        acc_ref[:HEAD_DIM, at] += contract_cols(queries[:HEAD_DIM, :], score_grad)
        acc_ref[HEAD_DIM:, at] += contract_cols(flows[HEAD_DIM:, :], chances.astype(BF))
        return dq

    dq = lax.fori_loop(
        first, step + 1, body, jnp.zeros((HEAD_DIM, TILE), F32)
    )
    dq_ref[:, here] = dq * SCALE

    @pl.when(step == length // TILE - 1)
    def _():
        def home(d, carry):
            at = span(lax.rem(d, per), 128)
            tile = pick_pair(lambda k: dq_ref[:, span(k, 128)], order, d)
            grad_ref[lax.div(d, per), 0, :, at] = tile.astype(BF)
            tile = pick_pair(lambda k: acc_ref[:, span(k, 128)], order, d).astype(BF)
            grad_ref[lax.div(d, per), 1, :, at] = tile[:HEAD_DIM]
            grad_ref[lax.div(d, per), 2, :, at] = tile[HEAD_DIM:]
            return carry

        lax.fori_loop(0, length // 128, home, 0)


def fixed(shape):
    return pl.BlockSpec(shape, lambda i: (0,) * len(shape))


def sorted_attend(lengths, order, parts):
    groups, _, columns = parts.shape
    length = groups * columns
    shapes = (
        ((groups, HEAD_DIM, columns), BF),
        ((HEAD_DIM, length), F32),
        ((1, length), F32),
        ((2 * HEAD_DIM, length), BF),
        ((2 * HEAD_DIM, length), BF),
        ((length, 2 * HEAD_DIM), BF),
    )
    return pl.pallas_call(
        sorted_attend_kernel,
        name="attend",
        grid=(length // TILE,),
        in_specs=[pl.BlockSpec(memory_space=pltpu.SMEM)] * 2 + [fixed(parts.shape)],
        out_specs=tuple(fixed(s) for s, _ in shapes),
        out_shape=tuple(jax.ShapeDtypeStruct(s, d) for s, d in shapes),
        scratch_shapes=[pltpu.SMEM((length // BLOCK,), jnp.int32)],
        compiler_params=pltpu.CompilerParams(vmem_limit_bytes=60 * 2**20),
        cost_estimate=pl.CostEstimate(
            flops=0, bytes_accessed=42_000_000, transcendentals=0
        ),
    )(lengths, order, parts)


def sorted_back(lengths, order, flow, out, lse, q_pad, kv_t, kv_rows, groups):
    length = out.shape[1]
    grad = (groups, 3, HEAD_DIM, length // groups)
    return pl.pallas_call(
        sorted_back_kernel,
        name="attend_back",
        grid=(length // TILE,),
        in_specs=[pl.BlockSpec(memory_space=pltpu.SMEM)] * 2
        + [fixed(a.shape) for a in (flow, out, lse, q_pad, kv_t, kv_rows)],
        out_specs=fixed(grad),
        out_shape=jax.ShapeDtypeStruct(grad, BF),
        scratch_shapes=[
            pltpu.VMEM((2 * HEAD_DIM, length), BF),
            pltpu.VMEM((HEAD_DIM, length), F32),
            pltpu.VMEM((2 * HEAD_DIM, length), F32),
            pltpu.SMEM((length // BLOCK,), jnp.int32),
        ],
        compiler_params=pltpu.CompilerParams(vmem_limit_bytes=40 * 2**20),
        cost_estimate=pl.CostEstimate(
            flops=0, bytes_accessed=42_000_000, transcendentals=0
        ),
    )(lengths, order, flow, out, lse, q_pad, kv_t, kv_rows)


def normalize(values):
    center = values - jnp.mean(values, axis=-1, keepdims=True)
    spread = jnp.mean(center * center, axis=-1, keepdims=True)
    scale = lax.rsqrt(spread + EPS)
    return center * scale, scale


def mid_kernel(
    experts, team, member, att, wo, x, vec, rw, route, cot,
    second, dgrad, send_s, send_g, sel, mixes, middle_own, prob_own, hot_own, second_own, att_own, sel_own,
    egrad,
):
    rows = middle_own.shape[0]
    slots = send_s.shape[1]
    groups = send_s.shape[0]
    capacity = slots // team
    lane = lax.broadcasted_iota(jnp.int32, (rows, 128), 1)
    row = lax.broadcasted_iota(jnp.int32, (rows, rows), 0)
    col = lax.broadcasted_iota(jnp.int32, (rows, rows), 1)
    me = member[0]

    def block(b, carry):
        at = span(b, rows)
        part = att[:, at]
        middle = x[at, :].astype(F32) + contract_rows(part, wo[...])
        hat, _ = normalize(middle)
        low = (hat * vec[5:6, :] + vec[7:8, :]).astype(BF)
        second[at, :] = low
        logits = dot_f32(low, rw[...])
        is_expert = lane < experts
        is_mix = (lane >= experts) & (lane < experts + 2)
        pe = jnp.where(is_expert, logits, NEG)
        pe = jnp.exp(pe - jnp.max(pe, axis=1, keepdims=True))
        pe = pe / jnp.sum(pe, axis=1, keepdims=True)
        pm = jnp.where(is_mix, logits, NEG)
        pm = jnp.exp(pm - jnp.max(pm, axis=1, keepdims=True))
        pm = pm / jnp.sum(pm, axis=1, keepdims=True)
        route_row = jnp.broadcast_to(route[b][0:1, :], (rows, rows))
        route_col = jnp.sum(jnp.where(row == col, route_row, 0), axis=1, keepdims=True)
        hot = lane == route_col
        gate = jnp.sum(jnp.where(hot, pe, 0.0), axis=1, keepdims=True)
        mix0 = jnp.sum(jnp.where(lane == experts, pm, 0.0), axis=1, keepdims=True)
        mix1 = jnp.sum(jnp.where(lane == experts + 1, pm, 0.0), axis=1, keepdims=True)
        scaled = mix1 * gate
        flow = cot[at, :].astype(F32)
        dgrad[at, :] = (flow * mix0).astype(BF)
        egrad[at, :] = (flow * scaled).astype(BF)
        mixes[at, :] = jnp.where(lane == 0, mix0, jnp.where(lane == 1, scaled, 0.0))
        same = (route_row == route_col) & (col < row)
        rank = jnp.sum(jnp.where(same, 1, 0), axis=1, keepdims=True)
        group = lax.div(route_col, team)
        mine = lax.rem(route_col, team) == me
        target = jnp.where(mine, group * slots + b * capacity + rank, groups * slots)
        slot = lax.broadcasted_iota(jnp.int32, (rows, groups * slots), 1)
        sel[at, :] = jnp.where(slot == target, 1.0, 0.0).astype(BF)

        @pl.when(b == me)
        def _():
            middle_own[...] = middle
            prob_own[...] = jnp.where(is_expert, pe, jnp.where(is_mix, pm, 0.0))
            hot_own[...] = jnp.where(hot, 1.0, 0.0)
            second_own[...] = low
            att_own[...] = part
            place = lax.broadcasted_iota(jnp.int32, sel_own.shape, 1)
            sel_own[...] = jnp.where(place == route_col * capacity + rank, 1.0, 0.0).astype(BF)

        return carry

    lax.fori_loop(0, team, block, 0)
    send_s[...] = contract_rows(sel[...], second[...]).astype(BF).reshape(send_s.shape)
    send_g[...] = contract_rows(sel[...], egrad[...]).astype(BF).reshape(send_g.shape)


def between(experts, sizes, slots, member, att, wo, x, vec, rw, route, cot):
    two, groups, team = sizes
    group_rows, width = x.shape
    rows = group_rows // team
    shapes = (
        ((group_rows, width), BF),
        ((group_rows, width), BF),
        ((groups, slots, width), BF),
        ((groups, slots, width), BF),
        ((group_rows, groups * slots), BF),
        ((group_rows, 128), F32),
        ((rows, width), F32),
        ((rows, 128), F32),
        ((rows, 128), F32),
        ((rows, width), BF),
        ((width, rows), BF),
        ((rows, experts * (slots // team)), BF),
    )
    inside = pl.BlockSpec(memory_space=pltpu.VMEM)
    return pl.pallas_call(
        functools.partial(mid_kernel, experts, team),
        name="between",
        in_specs=[pl.BlockSpec(memory_space=pltpu.SMEM)] + [inside] * 7,
        out_specs=tuple(inside for _ in shapes),
        out_shape=tuple(jax.ShapeDtypeStruct(s, d) for s, d in shapes),
        scratch_shapes=[pltpu.VMEM((group_rows, width), BF)],
        compiler_params=pltpu.CompilerParams(vmem_limit_bytes=60 * 2**20),
    )(member, att, wo, x, vec, rw, route, cot)


def turn_kernel(
    experts, layer_sum, second_sum, sums, middle, prob, hot, second, att, cot, rw, wo, vec,
    layer, middle_grad, flow_t, out_term, small_t,
):
    rows = middle.shape[0]
    lane = lax.broadcasted_iota(jnp.int32, (rows, 128), 1)
    layer[...] = (middle[...] + layer_sum[...]).astype(BF)
    chances, chosen = prob[...], hot[...]
    s0, s1 = sums[:, 0:1], sums[:, 1:2]
    mix1 = jnp.sum(jnp.where(lane == experts + 1, chances, 0.0), axis=1, keepdims=True)
    gate = jnp.sum(chances * chosen, axis=1, keepdims=True)
    pull_gate = s1 * mix1
    pulls = jnp.where(lane == experts, s0, jnp.where(lane == experts + 1, s1 * gate, 0.0))
    mean_pull = jnp.sum(chances * pulls, axis=1, keepdims=True)
    logit_grad = chances * jnp.where(
        lane < experts, pull_gate * (chosen - gate), pulls - mean_pull
    )
    logit_grad = jnp.where(lane < experts + 2, logit_grad, 0.0).astype(BF)
    second_grad = second_sum[...] + contract_cols(logit_grad, rw[...])
    hat, scale = normalize(middle[...])
    pull = second_grad * vec[5:6, :]
    part = scale * (
        pull
        - jnp.mean(pull, axis=-1, keepdims=True)
        - hat * jnp.mean(pull * hat, axis=-1, keepdims=True)
    )
    grad = cot[...].astype(F32) + part
    middle_grad[...] = grad
    branch = grad.astype(BF)
    width = wo.shape[0]

    def tile(n, carry):
        at = span(n, TILE)
        flow_t[at, :] = contract_cols(wo[at, :], branch).astype(BF)
        out_term[at, :] = dot_f32(att[at, :], branch).astype(BF)
        return carry

    lax.fori_loop(0, width // TILE, tile, 0)
    used = small_t.shape[0]
    routed = contract_rows(logit_grad, second[...])[:used, :]
    which = lax.broadcasted_iota(jnp.int32, routed.shape, 0)
    gain = jnp.sum(second_grad * hat, axis=0, keepdims=True)
    bias = jnp.sum(second_grad, axis=0, keepdims=True)
    small_t[...] = jnp.where(
        which == experts + 3, gain, jnp.where(which == experts + 5, bias, routed)
    )


def turn(experts, layer_sum, second_sum, sums, middle, prob, hot, second, att, cot, rw, wo, vec):
    rows, width = middle.shape
    used = -(-(experts + 6) // 8) * 8
    shapes = (
        ((rows, width), BF),
        ((rows, width), F32),
        ((width, rows), BF),
        ((width, width), BF),
        ((used, width), F32),
    )
    inside = pl.BlockSpec(memory_space=pltpu.VMEM)
    return pl.pallas_call(
        functools.partial(turn_kernel, experts),
        name="turn",
        in_specs=[inside] * 12,
        out_specs=tuple(inside for _ in shapes),
        out_shape=tuple(jax.ShapeDtypeStruct(s, d) for s, d in shapes),
        compiler_params=pltpu.CompilerParams(vmem_limit_bytes=40 * 2**20),
    )(layer_sum, second_sum, sums, middle, prob, hot, second, att, cot, rw, wo, vec)


def row_sum_kernel(left, right, out):
    out[0] = contract_rows(left[...], right[...])


def row_sum(left, right, tile):
    many, high = left.shape
    wide = right.shape[1]
    return pl.pallas_call(
        row_sum_kernel,
        name="row_sum",
        grid=(high // tile,),
        in_specs=[pl.BlockSpec((many, tile), lambda i: (0, i)), fixed(right.shape)],
        out_specs=pl.BlockSpec((1, tile, wide), lambda i: (0, i, 0)),
        out_shape=jax.ShapeDtypeStruct((1, high, wide), F32),
        compiler_params=pltpu.CompilerParams(vmem_limit_bytes=40 * 2**20),
        cost_estimate=pl.CostEstimate(
            flops=2 * many * high * wide, bytes_accessed=4 * high * wide, transcendentals=0
        ),
    )(left, right)


class Net:
    def __init__(self, sizes, send_sem, recv_sem):
        self.two, self.groups, self.team = sizes
        self.send_sem, self.recv_sem = send_sem, recv_sem
        self.c = lax.axis_index("dp")
        i = lax.axis_index("ctx")
        self.g, self.t = lax.div(i, self.team), lax.rem(i, self.team)
        self.group_steps = [(0, k, 0) for k in range(1, self.groups)]
        self.team_steps = [(0, 0, k) for k in range(1, self.team)]
        self.swap = (1, 0, 0)
        self.started = []

    def device(self, step):
        dc, dg, dt = step
        return (
            lax.rem(self.c + dc, self.two),
            lax.rem(self.g + dg, self.groups) * self.team + lax.rem(self.t + dt, self.team),
        )

    def greet(self):
        barrier = pltpu.get_barrier_semaphore()
        steps = self.group_steps + self.team_steps + [self.swap]
        for step in steps:
            pl.semaphore_signal(barrier, inc=1, device_id=self.device(step), device_id_type=MESH)
        pl.semaphore_wait(barrier, len(steps))

    def send(self, src, dst, step):
        k = len(self.started)
        copy = pltpu.make_async_remote_copy(
            src_ref=src,
            dst_ref=dst,
            send_sem=self.send_sem.at[k],
            recv_sem=self.recv_sem.at[k],
            device_id=self.device(step),
            device_id_type=MESH,
        )
        copy.start()
        self.started.append(copy)
        return copy

    def other_group(self, bit, group=None):
        group = self.g if group is None else group
        return group + bit - 2 * bit * lax.rem(lax.div(group, bit), 2)

    def other_member(self, bit):
        return self.t + bit - 2 * bit * lax.rem(lax.div(self.t, bit), 2)

    def send_member(self, src, dst, member):
        k = len(self.started)
        copy = pltpu.make_async_remote_copy(
            src_ref=src,
            dst_ref=dst,
            send_sem=self.send_sem.at[k],
            recv_sem=self.recv_sem.at[k],
            device_id=(self.c, self.g * self.team + member),
            device_id_type=MESH,
        )
        copy.start()
        self.started.append(copy)
        return copy

    def send_group(self, src, dst, group):
        k = len(self.started)
        copy = pltpu.make_async_remote_copy(
            src_ref=src,
            dst_ref=dst,
            send_sem=self.send_sem.at[k],
            recv_sem=self.recv_sem.at[k],
            device_id=(self.c, group * self.team + self.t),
            device_id_type=MESH,
        )
        copy.start()
        self.started.append(copy)
        return copy

    def group_to(self, step):
        return lax.rem(self.g + step[1], self.groups)

    def group_from(self, step):
        return lax.rem(self.g + self.groups - step[1], self.groups)

    def team_to(self, step):
        return lax.rem(self.t + step[2], self.team)

    def team_from(self, step):
        return lax.rem(self.t + self.team - step[2], self.team)

    def close(self):
        for copy in self.started:
            copy.wait_send()


def arrive(copies):
    for copy in copies:
        copy.wait_recv()


class Local:
    def __init__(self, sem):
        self.sem, self.count, self.open = sem, 0, []

    def copy(self, src, dst):
        made = pltpu.make_async_copy(src, dst, self.sem.at[self.count])
        made.start()
        self.count += 1
        self.open.append(made)
        return made

    def wait(self, *copies):
        for made in copies or tuple(self.open):
            made.wait()
            self.open = [other for other in self.open if other is not made]


def start_kernel(sizes, *refs):
    tokens, cot, w_qkv, w_up, w_down, w_out, router, gains, biases, routes = refs[:10]
    token_o, cot_o, heads_o, normed_o, weight_o, vec_o, out_o, ff_o, route_o, small_o = refs[10:20]
    (
        own, up, down, route, square, hats, stage, weights, tokens_v, normed, mixed, heads, out_v,
        send_sem, recv_sem, local_sem,
    ) = refs[20:]
    net, local = Net(sizes, send_sem, recv_sem), Local(local_sem)
    c, g, t = net.c, net.g, net.t
    two, groups, team = sizes
    rows, width = tokens.shape
    used = own.shape[2] - 128
    wr = own.shape[1]
    own_tokens = local.copy(tokens, tokens_v.at[t])
    local.copy(cot, cot_o.at[t])

    square[...] = jnp.zeros_like(square)
    square[: router.shape[0], :wr] = router[...]
    square[124:126, :wr] = gains[...]
    square[126:128, :wr] = biases[...]
    small = square[...].T[:wr, :].astype(BF)
    third = used // 3
    for n in range(team):
        for k in range(3):
            at = k * width + n * third
            own[n, :, k * third : (k + 1) * third] = w_qkv[:, at : at + third].astype(BF)
        own[n, :, used:] = small
    stage[t] = own[t]
    net.greet()
    staged = [net.send(own.at[net.team_to(s)], stage.at[t], s) for s in net.team_steps]
    out_v[g] = w_out[...].astype(BF)
    spread_out = [net.send(out_v.at[g], out_v.at[g], s) for s in net.group_steps]
    deep = w_down.shape[0]
    for n in range(team):
        for k in range(two * groups):
            at = (k * team + n) * deep
            up[n, :, k * deep : (k + 1) * deep] = w_up[:, at : at + deep].astype(BF)
    down[...] = w_down[...].astype(BF).reshape(down.shape)
    route[...] = jnp.broadcast_to(routes[...], route.shape)
    local.copy(up.at[t], ff_o.at[0, t])
    local.copy(down, ff_o.at[1])
    local.copy(route, route_o.at[t])
    arrive(staged)
    near, far = net.other_group(1), net.other_group(2)
    last = net.other_group(2, near)
    from_far = net.send_group(stage, weights.at[c, g], far)
    from_near = net.send_group(stage, weights.at[c, g], near)
    swapped = [net.send(stage, weights.at[c, g], net.swap)]
    mine = local.copy(stage, weights.at[c, g])

    side, other = net.other_member(1), net.other_member(2)
    part = rows // 2

    def to_sides(src, dst):
        return [net.send_member(src, dst.at[t], member) for member in (side, other)]

    def pass_on(copies, dst):
        made = []
        for n, (copy, at, to) in enumerate(zip(copies, (side, other), (other, side))):
            copy.wait_recv()
            view = dst.at[at, pl.ds(n * part, part)]
            made.append(net.send_member(view, view, to))
        return made

    told = to_sides(tokens, tokens_v)
    later = [net.send(route, route_o.at[t], s) for s in net.team_steps]
    local.wait(mine)
    told = pass_on(told, tokens_v)
    turned = to_sides(cot, cot_o)
    later += [net.send(up.at[net.team_to(s)], ff_o.at[0, t], s) for s in net.team_steps]
    from_far.wait_recv()
    view = weights.at[c, far]
    passed = net.send_group(view, view, near)
    swapped.append(net.send(view, view, net.swap))
    from_near.wait_recv()
    view = weights.at[c, near]
    swapped.append(net.send(view, view, net.swap))
    local.wait(own_tokens)
    arrive(told)
    local.copy(tokens_v, token_o)

    def center(b, carry):
        hats[b] = normalize(tokens_v[b].astype(F32))[0]
        return carry

    lax.fori_loop(0, team, center, 0)
    passed.wait_recv()
    view = weights.at[c, last]
    swapped.append(net.send(view, view, net.swap))
    arrive(swapped)
    local.copy(weights, weight_o)

    small = weights[:, :, :, :, used:].reshape(width, 128)
    small_o[...] = small
    small = small.astype(F32).T
    vec_o[...] = small[120:, :]

    def norm(b, carry):
        normed[b] = (hats[b] * vec_o[4:5, :] + vec_o[6:7, :]).astype(BF)
        return carry

    lax.fori_loop(0, team, norm, 0)
    local.copy(normed, normed_o)
    group_rows = rows * team
    per = used // 3 // 128
    pair = 128 // HEAD_DIM
    for n in range(used // 128):
        columns = weights[:, :, :, :, n * 128 : (n + 1) * 128].reshape(width, 128)
        made = dot_f32(normed[...].reshape(group_rows, width), columns).T.astype(BF)
        at = (n % per) * pair
        mixed[n // per, at : at + pair] = made.reshape(pair, HEAD_DIM, group_rows)
    given = [net.send(mixed.at[:, net.group_to(s)], heads.at[g], s) for s in net.group_steps]
    later += pass_on(turned, cot_o)
    local.wait(local.copy(mixed.at[:, g], heads.at[g]))

    arrive(spread_out)
    local.copy(out_v, out_o.at[c, :, t])
    swapped = [net.send(out_v, out_o.at[c, :, t], net.swap)]
    outed = [net.send(out_v, out_o.at[c, :, t], s) for s in net.team_steps]
    for copy, s in zip(outed, net.team_steps):
        copy.wait_recv()
        view = out_o.at[c, :, net.team_from(s)]
        swapped.append(net.send(view, view, net.swap))
    arrive(given)
    local.copy(heads, heads_o)
    arrive(swapped + later)
    local.wait()
    net.close()


def start(sizes, tokens, cot, w_qkv, w_up, w_down, w_out, router, gains, biases, routes):
    two, groups, team = sizes
    rows, width = tokens.shape
    wr = w_qkv.shape[0]
    used = 3 * width // team
    cols = used + 128
    head = (3, groups, HEAD_DIM, team * rows)
    up = (team, wr, width)
    shapes = (
        ((team, rows, width), BF),
        ((team, rows, width), BF),
        ((groups, 3, HEAD_DIM, team * rows), BF),
        ((team, rows, width), BF),
        ((two, groups, team, wr, cols), BF),
        ((8, width), F32),
        ((two, groups, team, wr, width), BF),
        ((2,) + up, BF),
        ((team, 8, rows), jnp.int32),
        ((width, 128), BF),
    )
    anywhere = pl.BlockSpec(memory_space=pl.ANY)
    inside = pl.BlockSpec(memory_space=pltpu.VMEM)
    count = 6 * (team - 1) + 4 * (groups - 1) + 4 + (team - 1)
    return pl.pallas_call(
        functools.partial(start_kernel, sizes),
        name="start",
        out_shape=tuple(jax.ShapeDtypeStruct(s, d) for s, d in shapes),
        in_specs=[anywhere] * 2 + [inside] * 8,
        out_specs=tuple(inside if n in (5, 9) else anywhere for n in range(10)),
        scratch_shapes=[
            pltpu.VMEM((team, wr, cols), BF),
            pltpu.VMEM(up, BF),
            pltpu.VMEM(up, BF),
            pltpu.VMEM((8, rows), jnp.int32),
            pltpu.VMEM((128, 128), F32),
            pltpu.VMEM((team, rows, width), F32),
            pltpu.VMEM((team, wr, cols), BF),
            pltpu.VMEM((two, groups, team, wr, cols), BF),
            pltpu.VMEM((team, rows, width), BF),
            pltpu.VMEM((team, rows, width), BF),
            pltpu.VMEM(head, BF),
            pltpu.VMEM((groups, 3, HEAD_DIM, team * rows), BF),
            pltpu.VMEM((groups, wr, width), BF),
            pltpu.SemaphoreType.DMA((count,)),
            pltpu.SemaphoreType.DMA((count,)),
            pltpu.SemaphoreType.DMA((14,)),
        ],
        compiler_params=pltpu.CompilerParams(
            collective_id=12, has_side_effects=True, vmem_limit_bytes=60 * 2**20
        ),
        cost_estimate=pl.CostEstimate(flops=0, bytes_accessed=150_000_000, transcendentals=0),
    )(tokens, cot, w_qkv, w_up, w_down, w_out, router, gains, biases, routes)


def end_kernel(sizes, experts, *refs):
    groups = sizes[1]
    parts, refs = refs[:groups], refs[groups:]
    weight, normed, tokens, vec, middle_grad, small, up, out = refs[:8]
    grad_o, qkv_o, up_o, out_o, small_o = refs[8:13]
    (
        up_r, small_d, mixed, turned, weights, normed_v, give, got, zsend, zrecv, npart, nrecv, qsend, qrecv,
        out_r, small_a, small_b, small_c, send_sem, recv_sem, local_sem,
    ) = refs[13:]
    net, local = Net(sizes, send_sem, recv_sem), Local(local_sem)
    c, g, t = net.c, net.g, net.t
    team = sizes[2]
    rows, width = tokens.shape
    group_rows, used = turned.shape
    for k, part in enumerate(parts):
        local.copy(part, mixed.at[:, net.group_from((0, k, 0))])
    local.copy(normed, normed_v)
    local.copy(weight, weights)
    local.copy(up.at[t], up_r.at[t])
    local.copy(out.at[g], out_r.at[g])
    net.greet()
    outed = [net.send(out.at[net.group_to(s)], out_r.at[g], s) for s in net.group_steps]
    later = [net.send(up.at[net.team_to(s)], up_r.at[t], s) for s in net.team_steps]
    local.wait()
    per = used // 3 // 128
    pair = 128 // HEAD_DIM
    for n in range(used // 128):
        at = (n % per) * pair
        block = mixed[n // per, at : at + pair].reshape(128, group_rows)
        turned[:, n * 128 : (n + 1) * 128] = block.astype(F32).T.astype(BF)

    half = width // 2
    tile = 128

    def term(core, n):
        at = pl.ds(pl.multiple_of(core * half + n * tile, tile), tile)
        left = normed_v[:, :, at].reshape(group_rows, tile)
        return contract_rows(left, turned[...])

    def giving(n, carry):
        give[span(n, tile), :] = term(lax.rem(c + 1, 2), n).astype(BF)
        return carry

    lax.fori_loop(0, half // tile, giving, 0)
    crossed = net.send(give, got, net.swap)

    def part_of(r, carry):
        columns = weights[:, :, :, :, :used].reshape(width, used)
        npart[r] = contract_cols(turned[span(r, rows), :], columns).astype(BF)
        return carry

    lax.fori_loop(0, team, part_of, 0)
    owned = [net.send(npart.at[net.team_to(s)], nrecv.at[t], s) for s in net.team_steps]
    nrecv[t] = npart[t]
    crossed.wait_recv()

    def keeping(n, carry):
        at = span(n, tile)
        zsend[at, :] = (term(c, n) + got[at, :].astype(F32)).astype(BF)
        return carry

    lax.fori_loop(0, half // tile, keeping, 0)
    deep = half // groups
    near, far = net.other_group(1), net.other_group(2)
    last = net.other_group(2, near)
    for_far = net.send_group(zsend.at[span(last, deep), :], zrecv.at[0], near)
    for_me = net.send_group(zsend.at[span(near, deep), :], zrecv.at[1], near)
    for_far.wait_recv()
    zrecv[3] = (zsend[span(far, deep), :].astype(F32) + zrecv[0].astype(F32)).astype(BF)
    summed = [for_me, net.send_group(zrecv.at[3], zrecv.at[2], far)]

    arrive(owned)
    flow = jnp.sum(nrecv[...].astype(F32), axis=0)
    hat, scale = normalize(tokens[...].astype(F32))
    pull = flow * vec[4:5, :]
    pulled = scale * (
        pull
        - jnp.mean(pull, axis=-1, keepdims=True)
        - hat * jnp.mean(pull * hat, axis=-1, keepdims=True)
    )
    grad_o[...] = (middle_grad[...] + pulled).astype(BF)

    gain = jnp.sum(flow * hat, axis=0, keepdims=True)
    bias = jnp.sum(flow, axis=0, keepdims=True)
    which = lax.broadcasted_iota(jnp.int32, small.shape, 0)
    mine = jnp.where(
        which == experts + 2, gain, jnp.where(which == experts + 4, bias, small[...])
    )
    small_a[c] = mine
    crossing = net.send(small_a.at[c], small_a.at[c], net.swap)
    crossing.wait_recv()
    small_c[...] = small_a[0] + small_a[1]

    def columns_of(k):
        return span(c * groups + k, 128)

    moved = [
        net.send(small_c.at[:, columns_of(net.group_to(s))], small_b.at[g], s)
        for s in net.group_steps
    ]
    small_b[g] = small_c[:, columns_of(g)]
    arrive(moved)
    small_d[t] = jnp.sum(small_b[...], axis=0)
    later += [net.send(small_d.at[t], small_d.at[t], s) for s in net.team_steps]

    arrive(summed)
    total = zsend[span(g, deep), :].astype(F32) + zrecv[1].astype(F32) + zrecv[2].astype(F32)
    qsend[...] = total.astype(BF).reshape(qsend.shape)
    later += [net.send(qsend.at[net.team_to(s)], qrecv.at[t], s) for s in net.team_steps]
    qrecv[t] = qsend[t]
    arrive(outed)
    out_o[...] = jnp.sum(out_r[...].astype(F32), axis=0)
    arrive(later)
    small_o[...] = jnp.sum(small_d[...], axis=0)
    third = used // 3
    deep = up_o.shape[1] // (2 * groups * team)
    for n in range(team):
        for k in range(3):
            at = k * width + n * third
            qkv_o[:, at : at + third] = qrecv[n, :, k * third : (k + 1) * third].astype(F32)
        for k in range(2 * groups):
            at = (k * team + n) * deep
            up_o[:, at : at + deep] = up_r[n, :, k * deep : (k + 1) * deep].astype(F32)
    net.close()


def end(sizes, experts, parts, weight, normed, tokens, vec, middle_grad, small, up, out):
    two, groups, team = sizes
    rows, width = tokens.shape
    wr = out.shape[1]
    used = 3 * groups * HEAD_DIM
    group_rows = parts[0].shape[2]
    half = width // 2
    shapes = (
        ((rows, width), BF),
        ((wr, 3 * width), F32),
        ((wr, team * width), F32),
        ((wr, width), F32),
        ((small.shape[0], 128), F32),
    )
    anywhere = pl.BlockSpec(memory_space=pl.ANY)
    inside = pl.BlockSpec(memory_space=pltpu.VMEM)
    count = 5 * (team - 1) + 3 * (groups - 1) + 2
    return pl.pallas_call(
        functools.partial(end_kernel, sizes, experts),
        name="end",
        out_shape=tuple(jax.ShapeDtypeStruct(s, d) for s, d in shapes),
        in_specs=[anywhere] * (groups + 2) + [inside] * 4 + [anywhere] * 2,
        out_specs=tuple(inside for _ in shapes),
        scratch_shapes=[
            pltpu.VMEM((team, wr, width), BF),
            pltpu.VMEM((team, small.shape[0], 128), F32),
            pltpu.VMEM((3, groups, HEAD_DIM, group_rows), BF),
            pltpu.VMEM((group_rows, used), BF),
            pltpu.VMEM(weight.shape, BF),
            pltpu.VMEM(normed.shape, BF),
            pltpu.VMEM((half, used), BF),
            pltpu.VMEM((half, used), BF),
            pltpu.VMEM((half, used), BF),
            pltpu.VMEM((groups, half // groups, used), BF),
            pltpu.VMEM((team, rows, width), BF),
            pltpu.VMEM((team, rows, width), BF),
            pltpu.VMEM((team, wr, used), BF),
            pltpu.VMEM((team, wr, used), BF),
            pltpu.VMEM((groups, wr, width), BF),
            pltpu.VMEM((2,) + small.shape, F32),
            pltpu.VMEM((groups, small.shape[0], 128), F32),
            pltpu.VMEM(small.shape, F32),
            pltpu.SemaphoreType.DMA((count,)),
            pltpu.SemaphoreType.DMA((count,)),
            pltpu.SemaphoreType.DMA((groups + 4,)),
        ],
        compiler_params=pltpu.CompilerParams(
            collective_id=13, has_side_effects=True, vmem_limit_bytes=60 * 2**20
        ),
        cost_estimate=pl.CostEstimate(flops=0, bytes_accessed=120_000_000, transcendentals=0),
    )(*parts, weight, normed, tokens, vec, middle_grad, small, up, out)


def gelu_and_slope(x):
    k = math.sqrt(2.0 / math.pi)
    square = x * x
    bent = jnp.tanh(k * (x + 0.044715 * (square * x)))
    half = 0.5 * (1.0 + bent)
    slope = half + (0.5 * k) * x * (1.0 - bent * bent) * (1.0 + (3 * 0.044715) * square)
    return x * half, slope


def feed_kernel(sizes, copies_count, *refs):
    two, groups, team = sizes
    (send_s, send_g, eup_h, edown_h, second_h, dgrad_h, ff_h, sel_h, cot_h, mix_h) = refs[:10]
    (layer_o, grad_o, sums_o, active_o, hgrad_o, arr_s_o, arr_g_o, ffg_o) = refs[10:18]
    (
        arr_s, arr_g, eup, edown, second, dgrad, upw, downw, sel, cot, mix,
        slope, active, hgrad, acc, give, got_s, got_g, ret_s, ret_g, back_s, back_g,
        low, ugrad, dense, spart, lay, spa, sums, lay_r, spa_r, sums_r,
        term_give, term_got, send_sem, recv_sem, load_sem, out_sem,
    ) = refs[18:]
    c = lax.axis_index("dp")
    i = lax.axis_index("ctx")
    g, t = lax.div(i, team), lax.rem(i, team)
    width = second.shape[1]
    rows = lay.shape[1]
    hid, ehid = upw.shape[1], eup.shape[1]
    core = lax.rem(c + 1, two)

    def device(step):
        dc, dg, dt = step
        return (
            lax.rem(c + dc, two),
            lax.rem(g + dg, groups) * team + lax.rem(t + dt, team),
        )

    index = [0]

    def remote(src, dst, step):
        k = index[0]
        index[0] += 1
        assert k < copies_count
        return pltpu.make_async_remote_copy(
            src_ref=src,
            dst_ref=dst,
            send_sem=send_sem.at[k],
            recv_sem=recv_sem.at[k],
            device_id=device(step),
            device_id_type=MESH,
        )

    group_steps = [(0, k, 0) for k in range(1, groups)]
    team_steps = [(0, 0, k) for k in range(1, team)]
    swap = (1, 0, 0)
    deep = ff_h.shape[2]

    def block_of(core, k):
        return pl.ds(pl.multiple_of((core * groups + k) * deep, deep), deep)

    loads = []
    for k, (src, dst) in enumerate(
        [
            (second_h, second), (dgrad_h, dgrad), (eup_h, eup), (edown_h, edown), (sel_h, sel), (cot_h, cot), (mix_h, mix),
            (send_s.at[g], arr_s.at[c, g]), (send_g.at[g], arr_g.at[c, g]),
        ]
        + [
            (ff_h.at[k, n], weight.at[block_of(c, k), :])
            for k in range(groups)
            for n, weight in enumerate((upw, downw))
        ]
    ):
        load = pltpu.make_async_copy(src, dst, load_sem.at[k])
        load.start()
        loads.append(load)

    barrier = pltpu.get_barrier_semaphore()
    greet = group_steps + team_steps + [swap]
    for step in greet:
        pl.semaphore_signal(barrier, inc=1, device_id=device(step), device_id_type=MESH)
    pl.semaphore_wait(barrier, len(greet))

    every = []

    def launch(copy):
        copy.start()
        every.append(copy)
        return copy

    def to_groups(src, dst):
        return [
            launch(remote(src.at[lax.rem(g + s[1], groups)], dst.at[g], s)) for s in group_steps
        ]

    def source(s):
        return lax.rem(g + groups - s[1], groups)

    swap_w = [
        launch(remote(ff_h.at[k, n], weight.at[block_of(c, k), :], swap))
        for k in range(groups)
        for n, weight in enumerate((upw, downw))
    ]
    out_s = [
        launch(remote(send_s.at[lax.rem(g + s[1], groups)], arr_s.at[c, g], s))
        for s in group_steps
    ]
    swap_s = [launch(remote(send_s.at[g], arr_s.at[c, g], swap))]
    out_g = [
        launch(remote(send_g.at[lax.rem(g + s[1], groups)], arr_g.at[c, g], s))
        for s in group_steps
    ]
    swap_g = [launch(remote(send_g.at[g], arr_g.at[c, g], swap))]

    for load in loads[:2] + loads[9:]:
        load.wait()
    for copy in swap_w:
        copy.wait_recv()

    def dense_in(h, carry):
        at = span(h, TILE)
        value, bend = gelu_and_slope(dot_f32(second[...], upw[:, at]))
        low[:, at] = value.astype(BF)
        ugrad[:, at] = (bend * contract_cols(dgrad[...], downw[at, :])).astype(BF)
        return carry

    lax.fori_loop(0, hid // TILE, dense_in, 0)

    def dense_out(n, carry):
        at = span(n, TILE)
        dense[:, at] = dot_f32(low[...], downw[:, at])
        spart[:, at] = contract_cols(ugrad[...], upw[at, :])
        return carry

    lax.fori_loop(0, width // TILE, dense_out, 0)

    for load in loads[2:9]:
        load.wait()
    for copy, s in zip(out_s, group_steps):
        copy.wait_recv()
        swap_s.append(launch(remote(arr_s.at[c, source(s)], arr_s.at[c, source(s)], swap)))
    for copy in swap_s:
        copy.wait_recv()
    entries = 2 * groups * arr_s.shape[2]

    def expert_in(h, carry):
        at = span(h, TILE)
        value, bend = gelu_and_slope(dot_f32(arr_s[...].reshape(entries, width), eup[:, at]))
        active[:, at] = value.astype(BF)
        slope[:, at] = bend
        return carry

    lax.fori_loop(0, ehid // TILE, expert_in, 0)
    keeps = [
        pltpu.make_async_copy(active, active_o, out_sem.at[0]),
        pltpu.make_async_copy(arr_s, arr_s_o, out_sem.at[1]),
    ]
    for copy in keeps:
        copy.start()

    def expert_out(n, carry):
        at = span(n, TILE)
        acc[:, :, at] = dot_f32(active[...], edown[:, at]).reshape(2, entries // 2, TILE)
        return carry

    lax.fori_loop(0, width // TILE, expert_out, 0)
    give[0] = acc[core].astype(BF)
    other_s = launch(remote(give.at[0], got_s, swap))

    for copy, s in zip(out_g, group_steps):
        copy.wait_recv()
        swap_g.append(launch(remote(arr_g.at[c, source(s)], arr_g.at[c, source(s)], swap)))
    other_s.wait_recv()
    ret_s[...] = (acc[c] + got_s[...].astype(F32)).astype(BF).reshape(ret_s.shape)
    home_s = to_groups(ret_s, back_s)
    back_s[g] = ret_s[g]
    for copy in swap_g:
        copy.wait_recv()

    def expert_back(h, carry):
        at = span(h, TILE)
        pull = contract_cols(arr_g[...].reshape(entries, width), edown[at, :])
        hgrad[:, at] = (slope[:, at] * pull).astype(BF)
        return carry

    lax.fori_loop(0, ehid // TILE, expert_back, 0)
    keeps += [
        pltpu.make_async_copy(hgrad, hgrad_o, out_sem.at[2]),
        pltpu.make_async_copy(arr_g, arr_g_o, out_sem.at[3]),
    ]
    for copy in keeps[2:]:
        copy.start()

    def expert_back_out(n, carry):
        at = span(n, TILE)
        acc[:, :, at] = contract_cols(hgrad[...], eup[at, :]).reshape(2, entries // 2, TILE)
        return carry

    lax.fori_loop(0, width // TILE, expert_back_out, 0)
    give[1] = acc[core].astype(BF)
    other_g = launch(remote(give.at[1], got_g, swap))
    other_g.wait_recv()
    ret_g[...] = (acc[c] + got_g[...].astype(F32)).astype(BF).reshape(ret_g.shape)
    home_g = to_groups(ret_g, back_g)
    back_g[g] = ret_g[g]

    for copy in home_s:
        copy.wait_recv()
    slots = groups * back_s.shape[1]
    lane = lax.broadcasted_iota(jnp.int32, (rows, 128), 1)

    def join_layer(r, carry):
        at = span(r, rows)
        found = dot_f32(sel[at, :], back_s[...].reshape(slots, width))
        own = dense[at, :]
        flow = cot[at, :].astype(F32)
        mixes = mix[at, :]
        lay[r] = (mixes[:, 0:1] * own + mixes[:, 1:2] * found).astype(BF)
        plain = jnp.sum(flow * own, axis=1, keepdims=True)
        routed = jnp.sum(flow * found, axis=1, keepdims=True)
        sums[r] = jnp.where(lane == 0, plain, jnp.where(lane == 1, routed, 0.0))
        return carry

    lax.fori_loop(0, team, join_layer, 0)

    def to_team(src, dst):
        made = [launch(remote(src.at[lax.rem(t + s[2], team)], dst.at[t], s)) for s in team_steps]
        dst[t] = src[t]
        return made

    team_copies = to_team(lay, lay_r) + to_team(sums, sums_r)

    for copy in home_g:
        copy.wait_recv()

    def join_grad(r, carry):
        at = span(r, rows)
        found = dot_f32(sel[at, :], back_g[...].reshape(slots, width))
        spa[r] = (spart[at, :] + found).astype(BF)
        return carry

    lax.fori_loop(0, team, join_grad, 0)
    team_copies += to_team(spa, spa_r)

    half = hid // 2
    term_tile = 128

    def down_term(base, n):
        at = pl.ds(pl.multiple_of(base + n * term_tile, term_tile), term_tile)
        return contract_rows(low[:, at], dgrad[...])

    def up_term(base, n):
        at = pl.ds(pl.multiple_of(base + n * term_tile, term_tile), term_tile)
        return contract_rows(second[:, at], ugrad[...])

    terms = []
    for k, (term, size) in enumerate(((down_term, half), (up_term, width // 2))):

        def giving(n, carry, k=k, term=term, size=size):
            term_give[k, span(n, term_tile), :] = term(core * size, n).astype(BF)
            return carry

        lax.fori_loop(0, size // term_tile, giving, 0)
        terms.append(launch(remote(term_give.at[k], term_got.at[k], swap)))
    for k, (term, size) in enumerate(((down_term, half), (up_term, width // 2))):
        terms[k].wait_recv()

        def keeping(n, carry, k=k, term=term, size=size):
            at = span(n, term_tile)
            total = term(c * size, n) + term_got[k, at, :].astype(F32)
            ffg_o[at, k * width : (k + 1) * width] = total.astype(BF)
            return carry

        lax.fori_loop(0, size // term_tile, keeping, 0)

    for copy in team_copies:
        copy.wait_recv()
    layer_o[...] = jnp.sum(lay_r[...].astype(F32), axis=0)
    grad_o[...] = jnp.sum(spa_r[...].astype(F32), axis=0)
    sums_o[...] = jnp.sum(sums_r[...], axis=0)
    for copy in keeps:
        copy.wait()
    for copy in every:
        copy.wait_send()


def feed_forward(sizes, rows, send_s, send_g, eup, edown, second, dgrad, ff, sel, cot, mix):
    two, groups, team = sizes
    slots = send_s.shape[1]
    width = second.shape[1]
    hid, ehid = second.shape[1] * ff.shape[3] // width, eup.shape[1]
    entries = 2 * groups * slots
    count = 2 * (groups - 1) * 2 + 2 * groups + 2 + 3 * (team - 1) + 2 + 2 * groups
    arrived = (two, groups, slots, width)
    anywhere = pl.BlockSpec(memory_space=pl.ANY)
    inside = pl.BlockSpec(memory_space=pltpu.VMEM)
    team_rows = team * rows
    return pl.pallas_call(
        functools.partial(feed_kernel, sizes, count),
        name="feed_forward",
        out_shape=(
            jax.ShapeDtypeStruct((rows, width), F32),
            jax.ShapeDtypeStruct((rows, width), F32),
            jax.ShapeDtypeStruct((rows, 128), F32),
            jax.ShapeDtypeStruct((entries, ehid), BF),
            jax.ShapeDtypeStruct((entries, ehid), BF),
            jax.ShapeDtypeStruct(arrived, BF),
            jax.ShapeDtypeStruct(arrived, BF),
            jax.ShapeDtypeStruct((hid // 2, 2 * width), BF),
        ),
        in_specs=[anywhere] * 10,
        out_specs=(inside, inside, inside, anywhere, anywhere, anywhere, anywhere, inside),
        scratch_shapes=[
            pltpu.VMEM((two, groups, slots, width), BF),
            pltpu.VMEM((two, groups, slots, width), BF),
            pltpu.VMEM(eup.shape, BF),
            pltpu.VMEM(edown.shape, BF),
            pltpu.VMEM(second.shape, BF),
            pltpu.VMEM(dgrad.shape, BF),
            pltpu.VMEM((width, hid), BF),
            pltpu.VMEM((hid, width), BF),
            pltpu.VMEM(sel.shape, BF),
            pltpu.VMEM(cot.shape, BF),
            pltpu.VMEM(mix.shape, F32),
            pltpu.VMEM((entries, ehid), F32),
            pltpu.VMEM((entries, ehid), BF),
            pltpu.VMEM((entries, ehid), BF),
            pltpu.VMEM((2, entries // 2, width), F32),
            pltpu.VMEM((2, entries // 2, width), BF),
            pltpu.VMEM((entries // 2, width), BF),
            pltpu.VMEM((entries // 2, width), BF),
            pltpu.VMEM((groups, slots, width), BF),
            pltpu.VMEM((groups, slots, width), BF),
            pltpu.VMEM((groups, slots, width), BF),
            pltpu.VMEM((groups, slots, width), BF),
            pltpu.VMEM((team_rows, hid), BF),
            pltpu.VMEM((team_rows, hid), BF),
            pltpu.VMEM((team_rows, width), F32),
            pltpu.VMEM((team_rows, width), F32),
            pltpu.VMEM((team, rows, width), BF),
            pltpu.VMEM((team, rows, width), BF),
            pltpu.VMEM((team, rows, 128), F32),
            pltpu.VMEM((team, rows, width), BF),
            pltpu.VMEM((team, rows, width), BF),
            pltpu.VMEM((team, rows, 128), F32),
            pltpu.VMEM((2, hid // 2, width), BF),
            pltpu.VMEM((2, hid // 2, width), BF),
            pltpu.SemaphoreType.DMA((count,)),
            pltpu.SemaphoreType.DMA((count,)),
            pltpu.SemaphoreType.DMA((9 + 2 * groups,)),
            pltpu.SemaphoreType.DMA((4,)),
        ],
        compiler_params=pltpu.CompilerParams(
            collective_id=5, has_side_effects=True, vmem_limit_bytes=60 * 2**20
        ),
        cost_estimate=pl.CostEstimate(
            flops=0, bytes_accessed=240_000_000, transcendentals=0
        ),
    )(send_s, send_g, eup, edown, second, dgrad, ff, sel, cot, mix)


def tall(chunk):
    rows, cols = chunk.shape[-2:]
    factor = 1
    while (rows * factor) % 16:
        factor *= 2
    return chunk.reshape(chunk.shape[:-2] + (rows * factor, cols // factor))


def per_device_general(
    tokens,
    cotangent,
    block_order,
    doc_lengths,
    routes,
    w_qkv,
    w_out,
    w_up,
    w_down,
    router,
    norm_gains,
    norm_biases,
    expert_up,
    expert_down,
):
    rows, width = tokens.shape[1], tokens.shape[2]
    ctx_count = lax.axis_size("ctx")
    two = lax.axis_size("dp")
    team = math.gcd(4, ctx_count)
    groups = ctx_count // team
    sizes = (two, groups, team)
    team_heads = HEADS // team
    reps = groups // team_heads
    length = rows * ctx_count
    group_rows = rows * team
    experts = ctx_count * expert_up.shape[0]
    capacity = max(2, 2 * rows // experts)
    block_rows = length // block_order.shape[0]
    hidden = w_up.shape[1]
    hidden_dev = w_down.shape[0]
    wr = w_qkv.shape[0]
    qkv_cols = 3 * width // team
    up_cols = hidden // team
    core = lax.axis_index("dp")
    ctx = lax.axis_index("ctx")
    group, member = lax.div(ctx, team), lax.rem(ctx, team)
    team_steps = [(0, 0, k) for k in range(1, team)]
    group_steps = [(0, k, 0) for k in range(1, groups)]
    by_group = [[g * team + t for g in range(groups)] for t in range(team)]
    by_team = [[g * team + t for t in range(team)] for g in range(groups)]
    swap = [(d, (d + 1) % two) for d in range(two)]

    small_flat = jnp.concatenate(
        [router.reshape(-1), norm_gains.reshape(-1), norm_biases.reshape(-1)]
    )
    small_size = -(-small_flat.shape[0] // 2048) * 2048
    small = jnp.pad(small_flat, (0, small_size - small_flat.shape[0])).astype(BF)
    small = small.reshape(-1, 128)

    qkv_first = tall(
        w_qkv.astype(BF).reshape(wr, 3, team, width // team).transpose(2, 0, 1, 3).reshape(
            team, wr, qkv_cols
        )
    )
    up_first = tall(
        w_up.reshape(wr, two * groups, team, hidden_dev)
        .transpose(2, 0, 1, 3)
        .reshape(team, wr, up_cols)
        .astype(BF)
    )
    down_first = tall(w_down.astype(BF).reshape(team, wr, width))
    out_first = tall(w_out.astype(BF))
    route_row = jnp.broadcast_to(routes[0, :, 0][None, :], (8, rows))

    def first(coords, ins, outs):
        c, g, t = coords
        moves, local = [], []
        for s in team_steps:
            to = lax.rem(t + s[2], team)
            moves.append(Move(s, ins[0], outs[0].at[t]))
            moves.append(Move(s, ins[1].at[to], outs[1].at[t]))
            moves.append(Move(s, ins[3], outs[3].at[t]))
            moves.append(Move(s, ins[4], outs[4].at[t]))
            moves.append(Move(s, ins[2].at[to], outs[2].at[0, t]))
        for s in group_steps:
            moves.append(Move(s, ins[5], outs[5].at[g]))
        local.append((ins[0], outs[0].at[t]))
        local.append((ins[1].at[t], outs[1].at[t]))
        local.append((ins[2].at[t], outs[2].at[0, t]))
        local.append((ins[3], outs[3].at[t]))
        local.append((ins[4], outs[4].at[t]))
        local.append((ins[5], outs[5].at[g]))
        local.append((ins[6], outs[2].at[1]))
        return local, moves

    token_rows, qkv_part, ff_part, small_part, route_all, out_part = exchange(
        "first",
        1,
        sizes,
        (tokens[0], qkv_first, up_first, small, route_row, out_first, down_first),
        [
            ((team, rows, width), BF),
            (qkv_first.shape, BF),
            ((2,) + up_first.shape, BF),
            ((team,) + small.shape, BF),
            ((team, 8, rows), jnp.int32),
            ((groups,) + out_first.shape, BF),
        ],
        first,
    )

    def second_build(coords, ins, outs):
        c, g, t = coords
        moves, local = [], []
        for k, s in enumerate(group_steps):
            moves.append(Move(s, ins[0], outs[0].at[c, g]))
            moves.append(Move(s, ins[1], outs[1].at[c, g]))
        for s in team_steps:
            moves.append(Move(s, ins[2], outs[2].at[t]))
        local.append((ins[0], outs[0].at[c, g]))
        local.append((ins[1], outs[1].at[c, g]))
        local.append((ins[2], outs[2].at[t]))
        other = (1, 0, 0)
        for n in range(2):
            moves.append(Move(other, ins[n], outs[n].at[c, g]))
        for k, s in enumerate(group_steps):
            source = lax.rem(g + groups - s[1], groups)
            for n in range(2):
                moves.append(
                    Move(other, outs[n].at[c, source], outs[n].at[c, source], after=2 * k + n)
                )
        return local, moves

    qkv_all, small_all, cot_rows = exchange(
        "second",
        2,
        sizes,
        (qkv_part, small_part, cotangent[0]),
        [
            ((two, groups) + qkv_part.shape, BF),
            ((two, groups) + small_part.shape, BF),
            ((team, rows, width), BF),
        ],
        second_build,
    )
    qkv_weight = qkv_all.reshape(width, qkv_cols)
    small_rows = small_all.reshape(two * ctx_count, -1)
    router_cols = router.shape[1]
    router_weight = jnp.pad(
        small_rows[:, : wr * router_cols].reshape(width, router_cols),
        ((0, 0), (0, 128 - router_cols)),
    )
    vectors = small_rows[:, wr * router_cols : small_flat.shape[0]].reshape(
        two * ctx_count, 4, wr
    )
    vectors = vectors.transpose(1, 0, 2).reshape(4, width).astype(F32)
    vectors = jnp.pad(vectors, ((4, 0), (0, 0)))

    ff_half = lax.all_gather(
        ff_part.reshape(2, team * wr, width),
        "ctx",
        axis=0,
        tiled=False,
        axis_index_groups=by_group,
    )

    def core_half(term):
        halves = term.reshape((two, term.shape[0] // two) + term.shape[1:])
        keep = lax.dynamic_index_in_dim(halves, core, 0, keepdims=False)
        give = lax.dynamic_index_in_dim(halves, 1 - core, 0, keepdims=False)
        return keep + lax.ppermute(give.astype(BF), "dp", swap).astype(F32)

    def over_groups(term):
        return lax.psum_scatter(
            term, "ctx", scatter_dimension=0, tiled=True, axis_index_groups=by_group
        )

    doc_id = jnp.arange(doc_lengths.shape[1], dtype=jnp.int32)
    doc_ends = jnp.sum(
        jnp.where(doc_id[:, None] <= doc_id[None, :], doc_lengths[0][:, None], 0), axis=0
    )
    all_rows = jnp.arange(length, dtype=jnp.int32)
    marks = (all_rows // block_rows)[:, None] == jnp.arange(
        block_order.shape[0], dtype=jnp.int32
    )[None, :]
    anchor = jnp.sum(jnp.where(marks, block_order[None, :], 0), axis=1)
    all_place = anchor * block_rows + all_rows % block_rows

    def low_of(place):
        return jnp.max(
            jnp.where(doc_ends[None, :] <= place[:, None], doc_ends[None, :], 0), axis=1
        )

    query_length = length // reps
    tiles = query_length // TILE
    part = lax.rem(group, reps)
    query_place = lax.dynamic_slice(all_place, (part * query_length,), (query_length,))
    lows = low_of(query_place)
    bounds = jnp.broadcast_to(jnp.array([[0, length // TILE]], dtype=jnp.int32), (tiles, 2))
    meta = jnp.concatenate(
        [query_place[None], lows[None], jnp.zeros((6, query_length), jnp.int32)], axis=0
    )

    token_rows = token_rows.reshape(group_rows, width)
    inputs = token_rows.astype(F32)
    normed_low = layer_norm(inputs, vectors[4], vectors[6]).astype(BF)
    mixed_t = lax.dot_general(
        qkv_weight, normed_low, (((0,), (1,)), ((), ())), preferred_element_type=F32
    ).astype(BF)
    mixed_t = mixed_t.reshape(3, team_heads, HEAD_DIM, group_rows)

    def spread_heads(coords, ins, outs):
        c, g, t = coords
        moves = [
            Move(s, ins[0].at[:, lax.div(lax.rem(g + s[1], groups), reps)], outs[0].at[g])
            for s in group_steps
        ]
        local = [(ins[0].at[:, lax.div(g, reps)], outs[0].at[g])]
        other = (1, 0, 0)
        moves.append(Move(other, ins[1], outs[1].at[c, :, t]))
        local.append((ins[1], outs[1].at[c, :, t]))
        first_team = len(moves)
        for s in team_steps:
            moves.append(Move(s, ins[1], outs[1].at[c, :, t]))
        for k, s in enumerate(team_steps):
            source = lax.rem(t + team - s[2], team)
            view = outs[1].at[c, :, source]
            moves.append(Move(other, view, view, after=first_team + k))
        return local, moves

    head_parts, out_weight = exchange(
        "heads",
        3,
        sizes,
        (mixed_t, out_part),
        [
            ((groups, 3, HEAD_DIM, group_rows), BF),
            ((two, groups, team) + out_first.shape, BF),
        ],
        spread_heads,
    )
    out_weight = out_weight.reshape(width, width)
    head_parts = head_parts.reshape(groups, 3 * HEAD_DIM, group_rows)
    place_col = all_place[:, None]
    head_t = head_parts.transpose(1, 0, 2).reshape(3 * HEAD_DIM, length)
    zeros = jnp.zeros((HEAD_DIM, query_length), BF)
    kv_t = head_t[HEAD_DIM:]
    kv_rows = kv_t.T
    q_t = lax.dynamic_slice(
        head_t[:HEAD_DIM], (0, part * query_length), (HEAD_DIM, query_length)
    )
    q_pad = jnp.concatenate([q_t * jnp.asarray(SCALE, BF), zeros], axis=0)
    attention_t, log_total = attend(False, bounds, meta, place_col, q_pad, kv_rows, kv_t)
    low_t = lax.dynamic_update_slice(
        jnp.zeros((HEAD_DIM, length), BF),
        attention_t.astype(BF),
        (0, part * query_length),
    )
    low_t = low_t.reshape(HEAD_DIM, groups, group_rows).transpose(1, 0, 2)

    def gather_heads(coords, ins, outs):
        c, g, t = coords
        moves = [
            Move(s, ins[0].at[lax.rem(g + s[1], groups)], outs[0].at[t, g]) for s in group_steps
        ]
        local = [(ins[0].at[g], outs[0].at[t, g])]
        for s in team_steps:
            moves.append(Move(s, ins[0].at[g], outs[0].at[t, g]))
        for k, s in enumerate(group_steps):
            source = lax.rem(g + groups - s[1], groups)
            for e in team_steps:
                moves.append(Move(e, outs[0].at[t, source], outs[0].at[t, source], after=k))
        return local, moves

    [attended] = exchange(
        "attended",
        4,
        sizes,
        (low_t,),
        [((team, groups, HEAD_DIM, group_rows), BF)],
        gather_heads,
    )
    if reps > 1:
        attended = lax.dynamic_index_in_dim(
            attended.reshape(team, team_heads, reps, HEAD_DIM, group_rows),
            lax.div(group, groups // reps),
            2,
            keepdims=False,
        )
    attended_t = attended.reshape(width, group_rows)

    slots = team * capacity
    (
        second_low,
        dense_grad,
        send_s,
        send_g,
        select,
        mixes,
        middle_own,
        prob_own,
        hot_own,
        second_own,
        attended_own,
        _,
    ) = between(
        experts,
        sizes,
        slots,
        member[None],
        attended_t,
        out_weight,
        token_rows,
        vectors,
        router_weight,
        route_all,
        cot_rows.reshape(group_rows, width),
    )
    (
        layer_sum,
        second_sum,
        sums_own,
        expert_active,
        hidden_grad,
        arrived_in,
        arrived_grad,
        ff_terms,
    ) = feed_forward(
        sizes,
        rows,
        send_s,
        send_g,
        expert_up[0],
        expert_down[0],
        second_low,
        dense_grad,
        ff_half,
        select,
        cot_rows.reshape(group_rows, width),
        mixes,
    )
    ff_sum = over_groups(ff_terms)
    down_sum = ff_sum[:, :width].astype(F32)
    up_sum = ff_sum[:, width:].reshape(team, wr, up_cols)
    entries = two * groups * slots
    expert_down_grad = row_sum(expert_active, arrived_grad.reshape(entries, width), TILE)
    expert_up_grad = row_sum(arrived_in.reshape(entries, width), hidden_grad, 128)

    layer_out, middle_grad, flow_t, out_term, small_t = turn(
        experts,
        layer_sum,
        second_sum,
        sums_own,
        middle_own,
        prob_own,
        hot_own,
        second_own,
        attended_own,
        cotangent[0],
        router_weight,
        out_weight,
        vectors,
    )
    flow_t = flow_t.reshape(team, team_heads, HEAD_DIM, rows)
    out_halves = out_term.reshape(two, groups, team, wr, width)

    def spread_flow(coords, ins, outs):
        c, g, t = coords
        moves = []
        for dg in range(groups):
            for dt in range(team):
                if dg or dt:
                    to_g, to_t = lax.rem(g + dg, groups), lax.rem(t + dt, team)
                    moves.append(
                        Move((0, dg, dt), ins[0].at[to_t, lax.div(to_g, reps)], outs[0].at[g, t])
                    )
        moves.append(Move((1, 0, 0), ins[1].at[lax.rem(c + 1, two)], outs[1]))
        return [(ins[0].at[t, lax.div(g, reps)], outs[0].at[g, t])], moves

    flow_parts, out_got = exchange(
        "flow",
        8,
        sizes,
        (flow_t, out_halves),
        [((groups, team, HEAD_DIM, rows), BF), (out_halves.shape[1:], BF)],
        spread_flow,
    )
    flow_all = flow_parts.transpose(2, 0, 1, 3).reshape(HEAD_DIM, length)
    flow_all = lax.dynamic_slice(
        flow_all, (0, part * query_length), (HEAD_DIM, query_length)
    )
    do_pad = jnp.concatenate([zeros, flow_all], axis=0)
    query_grad, pair_grad = attend_back(
        False,
        bounds,
        meta,
        place_col,
        q_pad,
        do_pad,
        attention_t,
        log_total,
        kv_rows,
        kv_t,
    )
    query_grad = lax.dynamic_update_slice(
        jnp.zeros((HEAD_DIM, length), BF), query_grad, (0, part * query_length)
    )
    grad_parts = jnp.concatenate([query_grad, pair_grad], axis=0)
    grad_parts = grad_parts.reshape(3, HEAD_DIM, groups, group_rows).transpose(2, 0, 1, 3)
    out_keep = lax.dynamic_index_in_dim(out_halves, core, 0, keepdims=False)
    out_parts = tall(
        (out_keep.astype(F32) + out_got.astype(F32))
        .astype(BF)
        .transpose(1, 0, 2, 3)
        .reshape(team, groups * wr, width)
    )

    def mixed_build(coords, ins, outs):
        c, g, t = coords
        moves = [
            Move(s, ins[0].at[lax.rem(g + s[1], groups)], outs[0].at[:, g])
            for s in group_steps
        ]
        moves += [
            Move(s, ins[1].at[lax.rem(t + s[2], team)], outs[1].at[t]) for s in team_steps
        ]
        return [(ins[0].at[g], outs[0].at[:, g]), (ins[1].at[t], outs[1].at[t])], moves

    grad_parts, out_parts = exchange(
        "mixed",
        9,
        sizes,
        (grad_parts, out_parts),
        [((3, groups, HEAD_DIM, group_rows), BF), (out_parts.shape, BF)],
        mixed_build,
    )
    out_parts = tall(
        jnp.sum(out_parts.astype(F32), axis=0).astype(BF).reshape(groups, wr, width)
    )
    if reps > 1:
        grad_parts = jnp.sum(
            grad_parts.reshape(3, team_heads, reps, HEAD_DIM, group_rows).astype(F32), axis=2
        ).astype(BF)
    mixed_grad_t = grad_parts.reshape(qkv_cols, group_rows)
    normed_part = (
        lax.dot_general(
            mixed_grad_t, qkv_weight, (((0,), (1,)), ((), ())), preferred_element_type=F32
        )
        .astype(BF)
        .reshape(team, rows, width)
    )
    qkv_term = lax.dot_general(
        normed_low, mixed_grad_t, (((0,), (1,)), ((), ())), preferred_element_type=F32
    )
    qkv_parts = core_half(qkv_term).astype(BF).reshape(groups, team * wr, qkv_cols)

    def normed_build(coords, ins, outs):
        c, g, t = coords
        moves, local = [], [(ins[2].at[t], outs[2].at[t])]
        for n in range(2):
            for s in group_steps:
                moves.append(Move(s, ins[n].at[lax.rem(g + s[1], groups)], outs[n].at[g]))
            local.append((ins[n].at[g], outs[n].at[g]))
        for s in team_steps:
            moves.append(Move(s, ins[2].at[lax.rem(t + s[2], team)], outs[2].at[t]))
        return local, moves

    qkv_parts, out_parts, normed_own = exchange(
        "normed",
        10,
        sizes,
        (qkv_parts, out_parts, normed_part),
        [(qkv_parts.shape, BF), (out_parts.shape, BF), (normed_part.shape, BF)],
        normed_build,
    )
    qkv_sum = (
        jnp.sum(qkv_parts.astype(F32), axis=0).astype(BF).reshape(team, wr, qkv_cols)
    )
    out_sum = jnp.sum(out_parts.astype(F32), axis=0).reshape(wr, width)
    normed_grad = jnp.sum(normed_own.astype(F32), axis=0)
    input_part_grad, gain_first, bias_first = jax.vjp(
        layer_norm, tokens[0].astype(F32), vectors[4], vectors[6]
    )[1](normed_grad)
    input_grad = middle_grad + input_part_grad

    small_used = small_t.shape[0]
    small_row = jnp.arange(small_used, dtype=jnp.int32)[:, None]
    small_t = jnp.where(
        small_row == experts + 2,
        gain_first[None],
        jnp.where(small_row == experts + 4, bias_first[None], small_t),
    )
    small_cols = small_used * wr
    small_pad = -(-small_cols // 1024) * 1024
    small_parts = jnp.pad(
        small_t.reshape(small_used, two * ctx_count, wr)
        .transpose(1, 0, 2)
        .reshape(two * ctx_count, small_cols),
        ((0, 0), (0, small_pad - small_cols)),
    ).reshape(two * ctx_count, small_pad // 128, 128)

    def owners_build(coords, ins, outs):
        c, g, t = coords
        moves, local = [], []
        for n in range(2):
            for s in team_steps:
                moves.append(Move(s, ins[n].at[lax.rem(t + s[2], team)], outs[n].at[t]))
            local.append((ins[n].at[t], outs[n].at[t]))
        me = c * ctx_count + g * team + t
        for dc in range(two):
            for dg in range(groups):
                for dt in range(team):
                    if dc or dg or dt:
                        to = (
                            lax.rem(c + dc, two) * ctx_count
                            + lax.rem(g + dg, groups) * team
                            + lax.rem(t + dt, team)
                        )
                        moves.append(Move((dc, dg, dt), ins[2].at[to], outs[2].at[me]))
        local.append((ins[2].at[me], outs[2].at[me]))
        return local, moves

    up_own, qkv_own, small_own = exchange(
        "owners",
        11,
        sizes,
        (tall(up_sum), tall(qkv_sum), small_parts),
        [
            (tall(up_sum).shape, BF),
            (tall(qkv_sum).shape, BF),
            (small_parts.shape, F32),
        ],
        owners_build,
    )
    small_sum = jnp.sum(small_own, axis=0).reshape(-1)[:small_cols].reshape(small_used, wr)
    up_own = (
        up_own.reshape(team, wr, two * groups, hidden_dev)
        .transpose(1, 2, 0, 3)
        .reshape(wr, hidden)
        .astype(F32)
    )
    qkv_own = (
        qkv_own.reshape(team, wr, 3, width // team)
        .transpose(1, 2, 0, 3)
        .reshape(wr, 3 * width)
        .astype(F32)
    )
    return (
        layer_out[None],
        input_grad[None].astype(BF),
        qkv_own,
        out_sum,
        up_own,
        down_sum,
        small_sum[:router_cols].T,
        small_sum[router_cols : router_cols + 2],
        small_sum[router_cols + 2 : router_cols + 4],
        expert_up_grad,
        expert_down_grad,
    )


def whole_kernel(sizes, experts, copies_count, *refs):
    two, groups, team = sizes
    (send_s, send_g, eup_h, edown_h, second_h, dgrad_h, ff_h, sel_h, cot_h) = refs[:9]
    (middle_h, prob_h, hot_h, own_h, att_h, rw_h, wo_h, vec_h) = refs[9:17]
    (
        layer_o, middle_o, small_o, flow_o, out_o, down_o, up_o,
        active_o, hgrad_o, arr_s_o, arr_g_o,
    ) = refs[17:28]
    (
        arr_s, arr_g, eup, edown, second, dgrad, upw, downw, sel, cot,
        slope, active, hgrad, acc, give, got_s, got_g, ret_s, ret_g, back_s, back_g,
        low, ugrad, lay, spa, lay_r, spa_r,
        term_give, term_got, out_got, ffg, ff_r,
        middle, prob, hot, own, att, rw, wo, vec, flow_t, flow_1, wo_s, wo_r,
        send_sem, recv_sem, load_sem, out_sem,
    ) = refs[28:]
    c = lax.axis_index("dp")
    i = lax.axis_index("ctx")
    g, t = lax.div(i, team), lax.rem(i, team)
    width = second.shape[1]
    rows = lay.shape[1]
    hid, ehid = upw.shape[1], eup.shape[1]
    core = lax.rem(c + 1, two)

    def device(step):
        if not isinstance(step, tuple):
            return c, step * team + t
        dc, dg, dt = step
        return (
            lax.rem(c + dc, two),
            lax.rem(g + dg, groups) * team + lax.rem(t + dt, team),
        )

    index = [0]

    def remote(src, dst, step):
        k = index[0]
        index[0] += 1
        assert k < copies_count
        return pltpu.make_async_remote_copy(
            src_ref=src,
            dst_ref=dst,
            send_sem=send_sem.at[k],
            recv_sem=recv_sem.at[k],
            device_id=device(step),
            device_id_type=MESH,
        )

    group_steps = [(0, k, 0) for k in range(1, groups)]
    team_steps = [(0, 0, k) for k in range(1, team)]
    swap = (1, 0, 0)
    deep = ff_h.shape[2]

    def block_of(core, k):
        return pl.ds(pl.multiple_of((core * groups + k) * deep, deep), deep)

    loads = []
    for k, (src, dst) in enumerate(
        [(second_h, second), (dgrad_h, dgrad)]
        + [
            (ff_h.at[k, n], weight.at[block_of(c, k), :])
            for n, weight in enumerate((upw, downw))
            for k in range(groups)
        ]
        + [
            (send_s.at[g], arr_s.at[c, g]), (eup_h, eup), (edown_h, edown),
            (send_g.at[g], arr_g.at[c, g]), (sel_h, sel), (cot_h, cot),
            (middle_h, middle), (prob_h, prob), (hot_h, hot), (own_h, own),
            (att_h, att), (rw_h, rw), (wo_h, wo), (vec_h, vec),
        ]
    ):
        load = pltpu.make_async_copy(src, dst, load_sem.at[k])
        load.start()
        loads.append(load)

    barrier = pltpu.get_barrier_semaphore()
    home_steps = [
        (0, dg, dt) for dg in range(groups) for dt in range(team) if dg or dt
    ]
    greet = home_steps + [swap]
    for step in greet:
        pl.semaphore_signal(barrier, inc=1, device_id=device(step), device_id_type=MESH)
    pl.semaphore_wait(barrier, len(greet))

    every = []

    def launch(copy):
        copy.start()
        every.append(copy)
        return copy

    each = arr_s.shape[2] // team

    def to_home(src, dst):
        me = g * team + t
        made = []
        for s in home_steps:
            to_g, to_t = lax.rem(g + s[1], groups), lax.rem(t + s[2], team)
            made.append(launch(remote(src.at[to_g, span(to_t, each), :], dst.at[me], s)))
        dst[me] = src[g, span(t, each), :]
        return made

    def source(s):
        return lax.rem(g + groups - s[1], groups)

    swap_w = [
        launch(remote(ff_h.at[k, n], weight.at[block_of(c, k), :], swap))
        for k in range(groups)
        for n, weight in enumerate((upw, downw))
    ]
    out_s = [
        launch(remote(send_s.at[lax.rem(g + s[1], groups)], arr_s.at[c, g], s))
        for s in group_steps
    ]
    swap_s = [launch(remote(send_s.at[g], arr_s.at[c, g], swap))]
    dense_loads = 2 + 2 * groups
    for load in loads[:dense_loads]:
        load.wait()
    for copy in swap_w:
        copy.wait_recv()

    def dense_in(h, carry):
        at = span(h, TILE)
        value, bend = gelu_and_slope(dot_f32(second[...], upw[:, at]))
        low[:, at] = value.astype(BF)
        ugrad[:, at] = (bend * contract_cols(dgrad[...], downw[at, :])).astype(BF)
        return carry

    lax.fori_loop(0, hid // TILE, dense_in, 0)
    out_g = [
        launch(remote(send_g.at[lax.rem(g + s[1], groups)], arr_g.at[c, g], s))
        for s in group_steps
    ]
    swap_g = [launch(remote(send_g.at[g], arr_g.at[c, g], swap))]

    def dense_out(n, carry):
        at = span(n, TILE)
        made = dot_f32(low[...], downw[:, at])
        lay[:, :, at] = made.astype(BF).reshape(team, rows, TILE)
        made = contract_cols(ugrad[...], upw[at, :])
        spa[:, :, at] = made.astype(BF).reshape(team, rows, TILE)
        return carry

    lax.fori_loop(0, width // TILE, dense_out, 0)

    def to_team(src, dst):
        made = [launch(remote(src.at[lax.rem(t + s[2], team)], dst.at[t], s)) for s in team_steps]
        dst[t] = src[t]
        return made

    team_copies = to_team(lay, lay_r) + to_team(spa, spa_r)

    for load in loads[dense_loads : dense_loads + 4]:
        load.wait()
    for copy, s in zip(out_s, group_steps):
        copy.wait_recv()
        swap_s.append(launch(remote(arr_s.at[c, source(s)], arr_s.at[c, source(s)], swap)))
    for copy in swap_s:
        copy.wait_recv()
    entries = 2 * groups * arr_s.shape[2]

    def expert_in(h, carry):
        at = span(h, TILE)
        value, bend = gelu_and_slope(dot_f32(arr_s[...].reshape(entries, width), eup[:, at]))
        active[:, at] = value.astype(BF)
        slope[:, at] = bend
        return carry

    lax.fori_loop(0, ehid // TILE, expert_in, 0)
    keeps = [
        pltpu.make_async_copy(active, active_o, out_sem.at[0]),
        pltpu.make_async_copy(arr_s, arr_s_o, out_sem.at[1]),
    ]
    for copy in keeps:
        copy.start()

    def expert_out(n, carry):
        at = span(n, TILE)
        acc[:, :, at] = dot_f32(active[...], edown[:, at]).reshape(2, entries // 2, TILE)
        return carry

    lax.fori_loop(0, width // TILE, expert_out, 0)
    give[0] = acc[core].astype(BF)
    other_s = launch(remote(give.at[0], got_s, swap))

    for copy, s in zip(out_g, group_steps):
        copy.wait_recv()
        swap_g.append(launch(remote(arr_g.at[c, source(s)], arr_g.at[c, source(s)], swap)))
    other_s.wait_recv()
    ret_s[...] = (acc[c] + got_s[...].astype(F32)).astype(BF).reshape(ret_s.shape)
    home_s = to_home(ret_s, back_s)
    for copy in swap_g:
        copy.wait_recv()

    def expert_back(h, carry):
        at = span(h, TILE)
        pull = contract_cols(arr_g[...].reshape(entries, width), edown[at, :])
        hgrad[:, at] = (slope[:, at] * pull).astype(BF)
        return carry

    lax.fori_loop(0, ehid // TILE, expert_back, 0)
    keeps += [
        pltpu.make_async_copy(hgrad, hgrad_o, out_sem.at[2]),
        pltpu.make_async_copy(arr_g, arr_g_o, out_sem.at[3]),
    ]
    for copy in keeps[2:]:
        copy.start()

    def expert_back_out(n, carry):
        at = span(n, TILE)
        acc[:, :, at] = contract_cols(hgrad[...], eup[at, :]).reshape(2, entries // 2, TILE)
        return carry

    lax.fori_loop(0, width // TILE, expert_back_out, 0)
    give[1] = acc[core].astype(BF)
    other_g = launch(remote(give.at[1], got_g, swap))
    other_g.wait_recv()
    ret_g[...] = (acc[c] + got_g[...].astype(F32)).astype(BF).reshape(ret_g.shape)
    home_g = to_home(ret_g, back_g)

    half = hid // 2
    term_tile = 128

    def down_term(base, n):
        at = pl.ds(pl.multiple_of(base + n * term_tile, term_tile), term_tile)
        return contract_rows(low[:, at], dgrad[...])

    def up_term(base, n):
        at = pl.ds(pl.multiple_of(base + n * term_tile, term_tile), term_tile)
        return contract_rows(second[:, at], ugrad[...])

    terms = []
    for k, (term, size) in enumerate(((down_term, half), (up_term, width // 2))):

        def giving(n, carry, k=k, term=term, size=size):
            term_give[k, span(n, term_tile), :] = term(core * size, n).astype(BF)
            return carry

        lax.fori_loop(0, size // term_tile, giving, 0)
        terms.append(launch(remote(term_give.at[k], term_got.at[k], swap)))
    for k, (term, size) in enumerate(((down_term, half), (up_term, width // 2))):
        terms[k].wait_recv()

        def keeping(n, carry, k=k, term=term, size=size):
            at = span(n, term_tile)
            total = term(c * size, n) + term_got[k, at, :].astype(F32)
            ffg[k, at, :] = total.astype(BF)
            return carry

        lax.fori_loop(0, size // term_tile, keeping, 0)
    up_copy = pltpu.make_async_copy(ffg.at[1], up_o, out_sem.at[4])
    up_copy.start()

    for load in loads[dense_loads + 4 :]:
        load.wait()
    for copy in team_copies + home_s:
        copy.wait_recv()
    lane = lax.broadcasted_iota(jnp.int32, (rows, 128), 1)
    places = groups * team * each
    chances, chosen = prob[...], hot[...]
    mix0 = jnp.sum(jnp.where(lane == experts, chances, 0.0), axis=1, keepdims=True)
    mix1 = jnp.sum(jnp.where(lane == experts + 1, chances, 0.0), axis=1, keepdims=True)
    gate = jnp.sum(chances * chosen, axis=1, keepdims=True)
    flow = cot[...].astype(F32)
    plain = jnp.sum(lay_r[...].astype(F32), axis=0)
    found = dot_f32(sel[...], back_s[...].reshape(places, width))
    layer_o[...] = (middle[...] + mix0 * plain + (mix1 * gate) * found).astype(BF)
    s0 = jnp.sum(flow * plain, axis=1, keepdims=True)
    s1 = jnp.sum(flow * found, axis=1, keepdims=True)
    pulls = jnp.where(lane == experts, s0, jnp.where(lane == experts + 1, s1 * gate, 0.0))
    mean_pull = jnp.sum(chances * pulls, axis=1, keepdims=True)
    logit_grad = chances * jnp.where(
        lane < experts, (s1 * mix1) * (chosen - gate), pulls - mean_pull
    )
    logit_grad = jnp.where(lane < experts + 2, logit_grad, 0.0).astype(BF)
    hat, scale = normalize(middle[...])
    early = jnp.sum(spa_r[...].astype(F32), axis=0) + contract_cols(logit_grad, rw[...])
    for copy in home_g:
        copy.wait_recv()
    piece = half // groups

    def other_group(bit, group):
        return group + bit - 2 * bit * lax.rem(lax.div(group, bit), 2)

    near, far = other_group(1, g), other_group(2, g)
    last = other_group(2, near)
    for_far = launch(remote(ffg.at[0, span(last, piece), :], ff_r.at[0], near))
    downs = [launch(remote(ffg.at[0, span(near, piece), :], ff_r.at[1], near))]

    second_grad = early + dot_f32(sel[...], back_g[...].reshape(places, width))
    pull = second_grad * vec[5:6, :]
    moved = scale * (
        pull
        - jnp.mean(pull, axis=-1, keepdims=True)
        - hat * jnp.mean(pull * hat, axis=-1, keepdims=True)
    )
    middle_grad = flow + moved
    middle_o[...] = middle_grad
    branch = middle_grad.astype(BF)

    for n in range(team):
        at = slice(n * (width // team), (n + 1) * (width // team))
        flow_t[n] = contract_cols(wo[at, :], branch).astype(BF).reshape(flow_t.shape[1:])
    flowed = [
        launch(remote(flow_t.at[lax.rem(t + s[2], team)], flow_1.at[t], s)) for s in team_steps
    ]
    flow_1[t] = flow_t[t]

    def out_term(base, n):
        at = pl.ds(pl.multiple_of(base + n * term_tile, term_tile), term_tile)
        return dot_f32(att[at, :], branch)

    def out_giving(n, carry):
        term_give[0, span(n, term_tile), :] = out_term(core * (width // 2), n).astype(BF)
        return carry

    terms[0].wait_send()
    every[:] = [copy for copy in every if copy is not terms[0]]
    lax.fori_loop(0, width // 2 // term_tile, out_giving, 0)
    out_cross = launch(remote(term_give.at[0], out_got, swap))
    for copy in flowed:
        copy.wait_recv()
    flowed = [
        launch(remote(flow_1.at[:, lax.rem(g + s[1], groups)], flow_o.at[g], s))
        for s in group_steps
    ]
    own_flow = pltpu.make_async_copy(flow_1.at[:, g], flow_o.at[g], out_sem.at[5])
    own_flow.start()
    for_far.wait_recv()
    ff_r[3] = (ffg[0, span(far, piece), :].astype(F32) + ff_r[0].astype(F32)).astype(BF)
    downs.append(launch(remote(ff_r.at[3], ff_r.at[2], far)))
    out_cross.wait_recv()
    wr = wo_s.shape[2]

    def out_keeping(n, carry):
        at = span(n, term_tile)
        total = out_term(c * (width // 2), n) + out_got[at, :].astype(F32)
        wo_s[:, n] = total.astype(BF).reshape(team, wr, width)
        return carry

    lax.fori_loop(0, groups, out_keeping, 0)
    outs = to_team(wo_s, wo_r)

    routed = contract_rows(logit_grad, own[...])[: small_o.shape[0], :]
    which = lax.broadcasted_iota(jnp.int32, routed.shape, 0)
    gain = jnp.sum(second_grad * hat, axis=0, keepdims=True)
    bias = jnp.sum(second_grad, axis=0, keepdims=True)
    small_o[...] = jnp.where(
        which == experts + 3, gain, jnp.where(which == experts + 5, bias, routed)
    )
    for copy in outs:
        copy.wait_recv()
    out_o[...] = jnp.sum(wo_r[...].astype(F32), axis=0).astype(BF)
    for copy in downs:
        copy.wait_recv()
    down_o[...] = (
        ffg[0, span(g, piece), :].astype(F32) + ff_r[1].astype(F32) + ff_r[2].astype(F32)
    )
    for copy in flowed:
        copy.wait_recv()
    for copy in keeps + [up_copy, own_flow]:
        copy.wait()
    for copy in every:
        copy.wait_send()


def whole(
    sizes, rows, experts, wr, send_s, send_g, eup, edown, second, dgrad, ff, sel, cot,
    middle, prob, hot, own, att, rw, wo, vec,
):
    two, groups, team = sizes
    slots = send_s.shape[1]
    width = second.shape[1]
    hid, ehid = ff.shape[3], eup.shape[1]
    entries = 2 * groups * slots
    used = -(-(experts + 6) // 8) * 8
    homes = groups * team - 1
    count = 3 * (groups - 1) + 4 * groups + 5 + 4 * (team - 1) + 2 * homes + 3
    each = slots // team
    arrived = (two, groups, slots, width)
    anywhere = pl.BlockSpec(memory_space=pl.ANY)
    inside = pl.BlockSpec(memory_space=pltpu.VMEM)
    team_rows = team * rows
    heads = (groups, HEAD_DIM, rows)
    shapes = (
        ((rows, width), BF),
        ((rows, width), F32),
        ((used, width), F32),
        ((groups, team, HEAD_DIM, rows), BF),
        ((groups, wr, width), BF),
        ((hid // 2 // groups, width), F32),
        ((width // 2, hid), BF),
        ((entries, ehid), BF),
        ((entries, ehid), BF),
        (arrived, BF),
        (arrived, BF),
    )
    scratch = (
        (arrived, BF), (arrived, BF), (eup.shape, BF), (edown.shape, BF), (second.shape, BF),
        (dgrad.shape, BF), ((width, hid), BF), ((hid, width), BF), (sel.shape, BF),
        (cot.shape, BF),
        ((entries, ehid), F32), ((entries, ehid), BF), ((entries, ehid), BF),
        ((2, entries // 2, width), F32), ((2, entries // 2, width), BF),
        ((entries // 2, width), BF), ((entries // 2, width), BF),
        ((groups, slots, width), BF), ((groups, slots, width), BF),
        ((groups * team, each, width), BF), ((groups * team, each, width), BF),
        ((team_rows, hid), BF), ((team_rows, hid), BF),
        ((team, rows, width), BF), ((team, rows, width), BF),
        ((team, rows, width), BF), ((team, rows, width), BF),
        ((2, hid // 2, width), BF), ((2, hid // 2, width), BF), ((width // 2, width), BF),
        ((2, hid // 2, width), BF),
        ((groups, hid // 2 // groups, width), BF),
        (middle.shape, F32), (prob.shape, F32), (hot.shape, F32), (own.shape, BF),
        (att.shape, BF), (rw.shape, BF), (wo.shape, BF), (vec.shape, F32),
        ((team,) + heads, BF), ((team,) + heads, BF),
        ((team, groups, wr, width), BF), ((team, groups, wr, width), BF),
    )
    return pl.pallas_call(
        functools.partial(whole_kernel, sizes, experts, count),
        name="feed_forward",
        out_shape=tuple(jax.ShapeDtypeStruct(s, d) for s, d in shapes),
        in_specs=[anywhere] * 17,
        out_specs=tuple(inside if n in (0, 1, 2, 4, 5) else anywhere for n in range(11)),
        scratch_shapes=[pltpu.VMEM(s, d) for s, d in scratch]
        + [
            pltpu.SemaphoreType.DMA((count,)),
            pltpu.SemaphoreType.DMA((count,)),
            pltpu.SemaphoreType.DMA((16 + 2 * groups,)),
            pltpu.SemaphoreType.DMA((6,)),
        ],
        compiler_params=pltpu.CompilerParams(
            collective_id=14, has_side_effects=True, vmem_limit_bytes=60 * 2**20
        ),
        cost_estimate=pl.CostEstimate(flops=0, bytes_accessed=300_000_000, transcendentals=0),
    )(
        send_s, send_g, eup, edown, second, dgrad, ff, sel, cot,
        middle, prob, hot, own, att, rw, wo, vec,
    )


def deliver_kernel(experts, count, shift, small, *refs):
    ins, outs = refs[:count], refs[count : 2 * count]
    router, gains, biases, sem = refs[2 * count :]
    copies = [pltpu.make_async_copy(a, b, sem.at[n]) for n, (a, b) in enumerate(zip(ins, outs))]
    for copy in copies:
        copy.start()
    wr = router.shape[1]
    mine = pltpu.roll(small[...], lax.rem(128 - shift[0], 128), 1)[:, :wr]
    router[...] = mine[: experts + 2, :]
    gains[...] = mine[experts + 2 : experts + 4, :]
    biases[...] = mine[experts + 4 : experts + 6, :]
    for copy in copies:
        copy.wait()


def deliver(experts, shift, small, arrays):
    wr = arrays[2].shape[0]
    anywhere = pl.BlockSpec(memory_space=pl.ANY)
    inside = pl.BlockSpec(memory_space=pltpu.VMEM)
    count = len(arrays)
    return pl.pallas_call(
        functools.partial(deliver_kernel, experts, count),
        name="deliver",
        in_specs=[pl.BlockSpec(memory_space=pltpu.SMEM)] + [inside] * (count + 1),
        out_specs=tuple([anywhere] * count + [inside] * 3),
        out_shape=tuple(jax.ShapeDtypeStruct(a.shape, a.dtype) for a in arrays)
        + (
            jax.ShapeDtypeStruct((experts + 2, wr), F32),
            jax.ShapeDtypeStruct((2, wr), F32),
            jax.ShapeDtypeStruct((2, wr), F32),
        ),
        scratch_shapes=[pltpu.SemaphoreType.DMA((count,))],
        compiler_params=pltpu.CompilerParams(vmem_limit_bytes=60 * 2**20),
    )(shift, small, *arrays)


def per_device(
    tokens,
    cotangent,
    block_order,
    doc_lengths,
    routes,
    w_qkv,
    w_out,
    w_up,
    w_down,
    router,
    norm_gains,
    norm_biases,
    expert_up,
    expert_down,
):
    rows, width = tokens.shape[1], tokens.shape[2]
    ctx_count = lax.axis_size("ctx")
    two = lax.axis_size("dp")
    team = math.gcd(4, ctx_count)
    groups = ctx_count // team
    sizes = (two, groups, team)
    length = rows * ctx_count
    wr = w_qkv.shape[0]
    experts = ctx_count * expert_up.shape[0]
    fits = groups == team == 4 and groups * team == HEADS and team * wr == 128 and w_up.shape[1] == team * width
    if not fits or length // block_order.shape[0] != BLOCK:
        return per_device_general(
            tokens, cotangent, block_order, doc_lengths, routes, w_qkv, w_out, w_up, w_down,
            router, norm_gains, norm_biases, expert_up, expert_down,
        )
    group_rows = rows * team
    capacity = max(2, 2 * rows // experts)
    slots = team * capacity
    hidden = w_up.shape[1]
    hidden_dev = w_down.shape[0]
    up_cols = hidden // team
    ctx = lax.axis_index("ctx")
    core = lax.axis_index("dp")
    group, member = lax.div(ctx, team), lax.rem(ctx, team)
    by_group = [[g * team + t for g in range(groups)] for t in range(team)]
    team_steps = [(0, 0, k) for k in range(1, team)]

    router_cols = router.shape[1]
    (
        token_rows,
        cot_rows,
        head_parts,
        normed,
        weights,
        vectors,
        out_weight,
        ff_part,
        route_all,
        router_weight,
    ) = start(
        sizes,
        tokens[0],
        cotangent[0],
        w_qkv,
        w_up,
        w_down,
        w_out,
        router.T,
        norm_gains,
        norm_biases,
        routes[0].reshape(1, rows),
    )
    out_weight = out_weight.reshape(width, width)
    token_rows = token_rows.reshape(group_rows, width)
    cot_rows = cot_rows.reshape(group_rows, width)

    ff_half = lax.all_gather(
        ff_part.reshape(2, team * wr, width),
        "ctx",
        axis=0,
        tiled=False,
        axis_index_groups=by_group,
    )
    low_t, attention_t, log_total, q_pad, kv_t, kv_rows = sorted_attend(
        doc_lengths[0], block_order, head_parts.reshape(groups, 3 * HEAD_DIM, group_rows)
    )

    def gather_heads(coords, ins, outs):
        c, g, t = coords
        steps = [(0, k, 0) for k in range(1, groups)]
        moves = [Move(s, ins[0].at[lax.rem(g + s[1], groups)], outs[0].at[t, g]) for s in steps]
        local = [(ins[0].at[g], outs[0].at[t, g])]
        for s in team_steps:
            moves.append(Move(s, ins[0].at[g], outs[0].at[t, g]))
        for k, s in enumerate(steps):
            source = lax.rem(g + groups - s[1], groups)
            for e in team_steps:
                moves.append(Move(e, outs[0].at[t, source], outs[0].at[t, source], after=k))
        return local, moves

    [attended] = exchange(
        "attended",
        4,
        sizes,
        (low_t,),
        [((team, groups, HEAD_DIM, group_rows), BF)],
        gather_heads,
    )
    (
        second_low,
        dense_grad,
        send_s,
        send_g,
        select,
        mixes,
        middle_own,
        prob_own,
        hot_own,
        second_own,
        attended_own,
        select_own,
    ) = between(
        experts,
        sizes,
        slots,
        member[None],
        attended.reshape(width, group_rows),
        out_weight,
        token_rows,
        vectors,
        router_weight,
        route_all,
        cot_rows,
    )
    (
        layer_out,
        middle_grad,
        small_t,
        flow_parts,
        out_sum,
        down_sum,
        up_half,
        expert_active,
        hidden_grad,
        arrived_in,
        arrived_grad,
    ) = whole(
        sizes,
        rows,
        experts,
        wr,
        send_s,
        send_g,
        expert_up[0],
        expert_down[0],
        second_low,
        dense_grad,
        ff_half,
        select_own,
        cotangent[0],
        middle_own,
        prob_own,
        hot_own,
        second_own,
        attended_own,
        router_weight,
        out_weight,
        vectors,
    )

    def pieces_of(array, along):
        count = groups if along == "g" else team
        me = group if along == "g" else member
        found = [lax.dynamic_index_in_dim(array, me, 0, keepdims=False)]
        for step in range(1, count):
            if along == "g":
                pairs = [
                    (g * team + t, (g + step) % groups * team + t)
                    for g in range(groups)
                    for t in range(team)
                ]
            else:
                pairs = [
                    (g * team + t, g * team + (t + step) % team)
                    for g in range(groups)
                    for t in range(team)
                ]
            chunk = lax.dynamic_index_in_dim(array, lax.rem(me + step, count), 0, keepdims=False)
            found.append(lax.ppermute(chunk, "ctx", pairs))
        return found

    up_sum = lax.psum_scatter(
        up_half, "ctx", scatter_dimension=0, tiled=True, axis_index_groups=by_group
    ).reshape(team, wr, up_cols)
    grad_parts = sorted_back(
        doc_lengths[0],
        block_order,
        flow_parts.reshape(ctx_count, HEAD_DIM, rows),
        attention_t,
        log_total,
        q_pad,
        kv_t,
        kv_rows,
        groups,
    )

    grad_parts, expert_active, hidden_grad = lax.optimization_barrier(
        (grad_parts, expert_active, hidden_grad)
    )

    pieces = pieces_of(grad_parts, "g")
    entries = two * groups * slots
    expert_down_grad = row_sum(expert_active, arrived_grad.reshape(entries, width), TILE)
    expert_up_grad = row_sum(arrived_in.reshape(entries, width), hidden_grad, 128)
    input_grad, qkv_own, up_own, out_own, small_own = end(
        sizes,
        experts,
        pieces,
        weights,
        normed,
        tokens[0],
        vectors,
        middle_grad,
        small_t,
        up_sum,
        out_sum,
    )
    delivered = deliver(
        experts,
        member[None] * wr,
        small_own,
        (layer_out, input_grad, qkv_own, out_own, up_own, down_sum),
    )
    layer_out, input_grad, qkv_own, out_own, up_own, down_sum = delivered[:6]
    router_own, gains_own, biases_own = delivered[6:]
    return (
        layer_out[None],
        input_grad[None],
        qkv_own,
        out_own,
        up_own,
        down_sum,
        router_own.T,
        gains_own,
        biases_own,
        expert_up_grad,
        expert_down_grad,
    )


def solution(mesh):
    in_specs = (
        P("dp", "ctx", None),
        P("dp", "ctx", None),
        P(),
        P("dp", None),
        P("dp", "ctx", None),
        P(("dp", "ctx"), None),
        P(("dp", "ctx"), None),
        P(("dp", "ctx"), None),
        P(("dp", "ctx"), None),
        P(("dp", "ctx"), None),
        P(None, ("dp", "ctx")),
        P(None, ("dp", "ctx")),
        P("ctx", None, "dp"),
        P("ctx", "dp", None),
    )
    out_specs = (
        P("dp", "ctx", None),
        P("dp", "ctx", None),
        P(("dp", "ctx"), None),
        P(("dp", "ctx"), None),
        P(("dp", "ctx"), None),
        P(("dp", "ctx"), None),
        P(("dp", "ctx"), None),
        P(None, ("dp", "ctx")),
        P(None, ("dp", "ctx")),
        P("ctx", None, "dp"),
        P("ctx", "dp", None),
    )
    return jax.shard_map(
        per_device, mesh=mesh, in_specs=in_specs, out_specs=out_specs, check_vma=False
    )
```
